32 devices in a mesh: groups: 2 (over x), region: 16 (over z, y, core).
Axes of the slice: x: 2, y: 2, z: 4, core: 2. Of those that a mesh axis runs over, the one named last changes fastest.
Arguments:
- patch_tiles: bfloat16 [512, 2, 4, 14336], P(('groups', 'region')), parts along dimension 0, may hold values from -6 to 6
- slot_lists: int32 [512, 2, 3], P(('groups', 'region')), parts along dimension 0, may hold values from -1 to 448, as said below
- blend_table: float32 [14, 14336], replicated, may hold values from 0.2 to 2
- smoothing: float32 [512, 896], P('region'), may hold values from 0.02 to 0.2
- analysis: bfloat16 [4, 1024, 896], P(None, 'groups', 'region'), parts along dimension 1, may hold values from -6 to 6
Outputs:
- crps_score: bfloat16 [4, 1024, 896], P(None, 'groups', 'region'), parts along dimension 1
- spread_skill: bfloat16 [2, 4, 1024, 896], P(None, None, 'groups', 'region'), parts along dimension 2
The draws below stay inside these ranges and needn't reach their ends.
There are 2 independent parts, one for each index of `groups`. The reference program is written for one: setup_inputs(seed, part) draws one part's arguments, and reference() takes and returns one part's arrays. A program takes and returns all parts, laid end to end along the dimension named above; an argument that names none is the same for every part. Nothing has to cross between parts.
Inputs may be any that keep to these rules, and one draw needn't show every extreme that they name: `slot_lists`: row p * 16 + r lists device p's slots for region r: sample (-1 marks an empty slot), first column, blend_table row. Device p lists only tiles of sample p // 2. In a region every sample has tiles at the same columns with the same table rows; a quarter of the regions, drawn, hold 4 tiles a sample and the others 2; in each region one tile starts at column 0 and one at 448. Slot 0 of every row is live; slot 1 is live exactly in the regions with 4 tiles.
All inputs are finite; a program needn't handle non-finite values.
Results may differ from the reference program's by a relative error of at most 0.0022.
The reference program's roundings to bfloat16 on the way (of `ensemble`) count: a program that leaves them out, or rounds other values in their place, can miss the bound.
Values may be sent and summed in bfloat16 or wider, within the bound.
No kernel may reach another device: no remote copies, remote signals or barrier semaphores. Data moves between devices by JAX's collectives and lax.ppermute only.
A program may use at most 192 MiB of HBM per device.

```python
import math
import jax
import jax.numpy as jnp
from jax import lax

SAMPLES = 8
FIELDS = 4
PATCH = 448
CAP = 2
ROWS = 32
COLS = 896
N_REGION = 16


def draw_slot_lists(key, part):
    key = jax.random.fold_in(key, 11)
    regions = N_REGION
    makers = N_REGION // SAMPLES
    most_tiles = 2 * makers
    shuffled = jax.random.permutation(jax.random.fold_in(key, 1), regions)
    is_heavy = shuffled < regions // 4
    counts = jnp.where(is_heavy, most_tiles, makers)
    last_column = COLS - PATCH
    columns = jax.random.randint(jax.random.fold_in(key, 2), (regions, most_tiles), 0, last_column + 1)
    slot_index = jnp.arange(most_tiles, dtype=jnp.int32)[None, :]
    columns = jnp.where(slot_index == 0, 0, columns)
    columns = jnp.where(slot_index == counts[:, None] - 1, last_column, columns)
    tables = jax.random.randint(jax.random.fold_in(key, 3), (regions, most_tiles), 0, PATCH // ROWS)
    sample = jnp.arange(SAMPLES, dtype=jnp.int32)[:, None, None]
    region = jnp.arange(regions, dtype=jnp.int32)[None, :, None]
    tile_index = jnp.arange(most_tiles, dtype=jnp.int32)[None, None, :]
    producer = sample * makers + (tile_index + region) % makers
    slot_place = tile_index // makers
    is_live = tile_index < counts[None, :, None]
    position = (producer * regions + region) * CAP + slot_place
    position = jnp.where(is_live, position, regions * regions * CAP)
    grid_shape = (SAMPLES, regions, most_tiles)
    values = jnp.stack([jnp.broadcast_to(sample, grid_shape), jnp.broadcast_to(columns[None], grid_shape), jnp.broadcast_to(tables[None], grid_shape)], axis=-1)
    lists = jnp.zeros((regions * regions * CAP, 3), jnp.int32).at[:, 0].set(-1)
    lists = lists.at[position.reshape(-1)].set(values.reshape(-1, 3).astype(jnp.int32), mode='drop')
    return lists.reshape(regions * regions, CAP, 3)


def shard_levels(key, extent, shards, least, high):
    level, own = 1.0, jax.random.fold_in(key, 6)
    for dim, parts in shards:
        steps = jnp.exp(jax.random.uniform(jax.random.fold_in(own, dim), (parts,), jnp.float32, least / len(shards), high / len(shards)))
        level = level * jnp.repeat(steps, extent[dim] // parts).reshape([-1 if axis == dim else 1 for axis in range(len(extent))])
    return level


def bell_draw(key, shape, deviation, most, pieces=(), kind=jnp.bfloat16):
    array = deviation * jax.random.normal(key, shape, jnp.float32)
    if pieces:
        array = array * shard_levels(key, shape, pieces, -0.22, 0.18)
    return jnp.clip(array, -most, most).astype(kind)


def setup_inputs(seed: int = 0, part: int = 0) -> dict:
    keys = jax.random.split(jax.random.key(seed), 6)
    part_splits = jax.random.split(jax.random.fold_in(keys[5], part), 6)
    return {
        "patch_tiles": bell_draw(part_splits[0], (N_REGION * N_REGION, CAP, FIELDS, ROWS * PATCH), 1.0, 6.0, ((0, 16),)),
        "slot_lists": draw_slot_lists(jax.random.fold_in(jax.random.fold_in(keys[5], part), 71), part),
        "blend_table": jnp.clip(jnp.exp(jax.random.uniform(keys[2], (PATCH // ROWS, ROWS * PATCH), jnp.float32, math.log(0.2), math.log(2.0))), 0.2, 2.0),
        "smoothing": jnp.clip(0.02 + 0.18 * jax.random.uniform(keys[3], (N_REGION * ROWS, COLS), jnp.float32) ** shard_levels(keys[3], (N_REGION * ROWS, COLS), ((0, 16),), -0.2, 0.2), 0.02, 0.2),
        "analysis": bell_draw(part_splits[4], (FIELDS, N_REGION * ROWS, COLS), 1.0, 6.0, ((2, 16),)),
    }


def place_tile(tile_piece, column):
    empty_frame = jnp.zeros(tile_piece.shape[:-1] + (COLS,), tile_piece.dtype)
    return lax.dynamic_update_slice_in_dim(empty_frame, tile_piece, column.astype(jnp.int32), tile_piece.ndim - 1)


def blend_set(set_tiles, set_lists, blend_table):
    slot_count = set_tiles.shape[0]
    table_pick = (set_lists[:, 2][:, None] == jnp.arange(blend_table.shape[0])[None, :]).astype(jnp.float32)
    weights = jnp.dot(table_pick, blend_table, precision=lax.Precision.HIGHEST).reshape(slot_count, ROWS, PATCH)
    member = (set_lists[:, 0][:, None] == jnp.arange(SAMPLES)[None, :]).astype(jnp.float32)
    weighted = set_tiles.reshape(slot_count, FIELDS, ROWS, PATCH).astype(jnp.float32) * weights[:, None]
    framed = jax.vmap(place_tile)(weighted, set_lists[:, 1])
    weight_frames = jax.vmap(place_tile)(weights, set_lists[:, 1])
    numer = jnp.dot(member.T, framed.reshape(slot_count, -1), precision=lax.Precision.HIGHEST)
    weight_sum = jnp.dot(member.T, weight_frames.reshape(slot_count, -1), precision=lax.Precision.HIGHEST)
    return numer.reshape(SAMPLES, FIELDS, ROWS, COLS), weight_sum.reshape(SAMPLES, ROWS, COLS)


def smooth_field(blended, smoothing, upper_row, lower_row, left_col, right_col):
    rows_ext = jnp.concatenate([upper_row, blended, lower_row], 2)
    cols_ext = jnp.concatenate([left_col, blended, right_col], 3)
    laplace = rows_ext[:, :, :-2] + rows_ext[:, :, 2:] + cols_ext[..., :-2] + cols_ext[..., 2:] - 4.0 * blended
    return (blended + smoothing * laplace).astype(jnp.bfloat16)


def score_fields(ensemble, analysis):
    members = ensemble.astype(jnp.float32)
    target = analysis.astype(jnp.float32)
    abs_error = jnp.mean(jnp.abs(members - target[None]), axis=0)
    pair_total = jnp.zeros(target.shape, jnp.float32)
    for member_index in range(SAMPLES):
        pair_total = pair_total + jnp.sum(jnp.abs(members - members[member_index][None]), axis=0)
    crps_field = abs_error - pair_total / (2.0 * SAMPLES * SAMPLES)
    average = jnp.mean(members, axis=0)
    variance = jnp.sum((members - average[None]) ** 2, axis=0) / (SAMPLES - 1.0)
    sq_error = (average - target) ** 2
    return crps_field, variance, sq_error


def reference(patch_tiles, slot_lists, blend_table, smoothing, analysis):
    regions = N_REGION
    tile_grid = jnp.swapaxes(patch_tiles.reshape(regions, regions, CAP, FIELDS, ROWS * PATCH), 0, 1)
    list_grid = jnp.swapaxes(slot_lists.reshape(regions, regions, CAP, 3), 0, 1)

    def blend_region(region_parts):
        region_tiles, region_lists = region_parts
        return blend_set(region_tiles.reshape(regions * CAP, FIELDS, ROWS * PATCH), region_lists.reshape(regions * CAP, 3), blend_table)

    numer, weight_sum = lax.map(blend_region, (tile_grid, list_grid))
    numer = jnp.transpose(numer, (1, 2, 0, 3, 4)).reshape(SAMPLES, FIELDS, regions * ROWS, COLS)
    weight_sum = jnp.transpose(weight_sum, (1, 0, 2, 3)).reshape(SAMPLES, regions * ROWS, COLS)
    blended = numer / weight_sum[:, None]
    ensemble = smooth_field(blended, smoothing, blended[:, :, :1], blended[:, :, -1:], blended[..., :1], blended[..., -1:])
    crps_field, variance, sq_error = score_fields(ensemble, analysis)
    return crps_field.astype(jnp.bfloat16), jnp.stack([variance, sq_error]).astype(jnp.bfloat16)
```

```python
import functools

import jax
import jax.numpy as jnp
from jax import lax
from jax.experimental import pallas as pl
from jax.experimental.pallas import tpu as pltpu
from jax.sharding import PartitionSpec as P

SAMPLES = 8
FIELDS = 4
PATCH = 448
CAP = 2
ROWS = 32
COLS = 896
PAIRS = ROWS // 2
FLAT = ROWS * PATCH
LANES = 128
TILES = COLS // LANES
PER_CHUNK = 2
CHUNKS = FIELDS // PER_CHUNK
MID = 0.11
VMEM = 48 * 1024 * 1024


def round_up(value, step):
    return -(-value // step) * step


class Sizes:
    def __init__(self, regions):
        self.regions = regions
        self.makers = regions // SAMPLES
        self.block = regions // self.makers
        self.heavy = min(self.block, regions // 4)
        self.part = self.block * ROWS
        self.width = COLS // regions
        self.span = round_up(self.width, 8)
        self.rows = regions * ROWS
        self.main = PER_CHUNK * self.span

    def chunk_rows(self, chunk):
        return self.main + (16 if chunk == 0 else 8)


def slot_field(region, slot, field):
    return (region * CAP + slot) * 3 + field


def pack_kernel(z, lists, tiles, packed, sems):
    part = lax.rem(lax.axis_index("region"), z.makers)
    for k in range(1, z.makers):
        first = lax.rem(part + k, z.makers) * z.block
        bulk = pltpu.make_async_copy(
            tiles.at[pl.ds(first, z.block), 0], packed.at[k - 1, pl.ds(0, z.block)], sems.at[k - 1, 0]
        )
        bulk.start()
        rank = jnp.int32(0)
        for j in range(z.block):
            live = lists[slot_field(first + j, 1, 0)] >= 0

            @pl.when(live)
            def _(j=j, rank=rank):
                pltpu.make_async_copy(
                    tiles.at[first + j, 1], packed.at[k - 1, z.block + rank], sems.at[k - 1, 1 + j]
                ).start()

            rank = jnp.minimum(rank + live.astype(jnp.int32), z.heavy - 1)
    for k in range(1, z.makers):
        first = lax.rem(part + k, z.makers) * z.block
        pltpu.make_async_copy(
            tiles.at[pl.ds(first, z.block), 0], packed.at[k - 1, pl.ds(0, z.block)], sems.at[k - 1, 0]
        ).wait()
        for j in range(z.block):

            @pl.when(lists[slot_field(first + j, 1, 0)] >= 0)
            def _(j=j):
                pltpu.make_async_copy(
                    tiles.at[first + j, 1], packed.at[k - 1, z.block], sems.at[k - 1, 1 + j]
                ).wait()


def pack_tiles(z, lists, tiles):
    return pl.pallas_call(
        functools.partial(pack_kernel, z),
        out_shape=jax.ShapeDtypeStruct((z.makers - 1, z.block + z.heavy, FIELDS, FLAT), jnp.bfloat16),
        in_specs=[pl.BlockSpec(memory_space=pltpu.SMEM), pl.BlockSpec(memory_space=pl.ANY)],
        out_specs=pl.BlockSpec(memory_space=pl.ANY),
        scratch_shapes=[pltpu.SemaphoreType.DMA((z.makers - 1, 1 + z.block))],
        name="pack_tiles",
    )(lists, tiles)


def blend_kernel(z, meta, *refs):
    slots = refs[: 2 * z.makers]
    table, smoothing = refs[2 * z.makers : 2 * z.makers + 2]
    outs = refs[2 * z.makers + 2 : 2 * z.makers + 2 + CHUNKS]
    staged, lines, turned, strength = refs[2 * z.makers + 2 + CHUNKS :]
    j = pl.program_id(0)
    quad = LANES // ROWS
    region = meta[0] * z.block + j

    def entry(maker, slot, field):
        return meta[1 + maker * z.regions * CAP * 3 + slot_field(region, slot, field)]

    heavy = entry(0, 1, 0) >= 0
    lane = lax.broadcasted_iota(jnp.int32, (PAIRS, COLS), 1)

    def stage(index):
        ref = slots[index]
        for k in range(PAIRS):
            for t in range(TILES):
                at = COLS * k + LANES * t
                staged[index, t, FIELDS * k : FIELDS * (k + 1), :] = ref[0, 0, :, at : at + LANES].astype(
                    jnp.float32
                )

    def pairs_of(index, field):
        return jnp.concatenate(
            [staged[index, t, pl.ds(field, PAIRS, stride=FIELDS), :] for t in range(TILES)], 1
        )

    def put(field, even, odd):
        at = lax.rem(j, quad) * ROWS
        for t in range(TILES):
            here = slice(LANES * t, LANES * (t + 1))
            lines[field, t, pl.ds(at, PAIRS, stride=2), :] = even[:, here]
            lines[field, t, pl.ds(at + 1, PAIRS, stride=2), :] = odd[:, here]

    for maker in range(z.makers):
        stage(2 * maker)

    def general(live_slots):
        def placed(pairs, column):
            turn = pltpu.roll(pairs, column, 1)
            other = pltpu.roll(turn, PATCH, 1)
            inside = (lane >= column) & (lane < column + PATCH)
            return jnp.where(inside, turn, 0.0), jnp.where(inside, other, 0.0)

        columns = [entry(i // 2, i % 2, 1) for i in live_slots]
        weights = [table[entry(i // 2, i % 2, 2)] for i in live_slots]
        even, odd = 0.0, 0.0
        for column, weight in zip(columns, weights):
            a, b = placed(weight, column)
            even, odd = even + a, odd + b
        even_inv, odd_inv = 1.0 / even, 1.0 / odd

        def one_field(field, carry):
            even, odd = 0.0, 0.0
            for i, column, weight in zip(live_slots, columns, weights):
                a, b = placed(pairs_of(i, field) * weight, column)
                even, odd = even + a, odd + b
            put(field, even * even_inv, odd * odd_inv)
            return carry

        lax.fori_loop(0, FIELDS, one_field, 0)

    @pl.when(heavy)
    def _():
        for maker in range(z.makers):
            stage(2 * maker + 1)
        general(list(range(2 * z.makers)))

    @pl.when(jnp.logical_not(heavy))
    def _():
        if z.makers != 2:
            general([2 * maker for maker in range(z.makers)])
            return
        left_maker = (entry(0, 0, 1) != 0).astype(jnp.int32)
        left, right = 2 * left_maker, 2 - 2 * left_maker
        left_weight = table[entry(left_maker, 0, 2)]
        right_weight = table[entry(1 - left_maker, 0, 2)]

        def merged(a, b):
            even = jnp.where(lane < PATCH, a, pltpu.roll(b, PATCH, 1))
            odd = jnp.where(lane < PATCH, pltpu.roll(a, PATCH, 1), b)
            return even, odd

        even_sum, odd_sum = merged(left_weight, right_weight)
        even_inv, odd_inv = 1.0 / even_sum, 1.0 / odd_sum

        def one_field(field, carry):
            even, odd = merged(
                pairs_of(left, field) * left_weight,
                pairs_of(right, field) * right_weight,
            )
            put(field, even * even_inv, odd * odd_inv)
            return carry

        lax.fori_loop(0, FIELDS, one_field, 0)

    @pl.when(j == 0)
    def _():
        turned_strength = jnp.transpose(smoothing[...] - MID)
        for dest in range(z.regions):
            for g in range(z.span // 8):
                top = z.width * dest + 8 * g
                rows = min(8, COLS - top)
                strength[dest, 0:rows, ROWS * g : ROWS * (g + 1)] = turned_strength[top : top + rows]

    @pl.when(lax.rem(j, quad) == quad - 1)
    def _():
        at = pl.multiple_of(lax.div(j, quad) * LANES, LANES)
        for field in range(FIELDS):
            for t in range(TILES):
                turned[field, LANES * t : LANES * (t + 1), :] = jnp.transpose(lines[field, t])
        for chunk in range(CHUNKS):
            fields = range(chunk * PER_CHUNK, (chunk + 1) * PER_CHUNK)
            for dest in range(z.regions):
                first = z.width * dest
                block = [turned[field, first : first + z.span, :] for field in fields]
                outs[chunk][dest, 0 : z.main, pl.ds(at, LANES)] = jnp.concatenate(block, 0).astype(jnp.bfloat16)
                low, high = max(first - 1, 0), min(first + z.width, COLS - 1)
                edge = [turned[field, at_row : at_row + 1, :] for field in fields for at_row in (low, high)]
                edge.append(jnp.zeros((8 - len(edge), LANES), jnp.float32))
                if chunk == 0:
                    edge.append(strength[dest, :, pl.ds(at, LANES)])
                outs[chunk][dest, z.main : z.chunk_rows(chunk), pl.ds(at, LANES)] = jnp.concatenate(
                    edge, 0
                ).astype(jnp.bfloat16)


def blend(z, meta, tiles, received, table, smoothing):
    tile_block = (1, 1, FIELDS, FLAT)

    def rank(j, meta):
        first = meta[0] * z.block
        total = jnp.int32(0)
        for before in range(z.block):
            live = meta[1 + slot_field(first + before, 1, 0)] >= 0
            total = total + jnp.where(live & (before < j), 1, 0)
        return z.block + jnp.minimum(total, z.heavy - 1)

    in_specs = [
        pl.BlockSpec(tile_block, lambda j, meta: (meta[0] * z.block + j, 0, 0, 0)),
        pl.BlockSpec(tile_block, lambda j, meta: (meta[0] * z.block + j, 1, 0, 0)),
    ]
    operands = [tiles, tiles]
    for item in received:
        in_specs += [
            pl.BlockSpec(tile_block, lambda j, meta: (0, j, 0, 0)),
            pl.BlockSpec(tile_block, lambda j, meta: (0, rank(j, meta), 0, 0)),
        ]
        operands += [item, item]
    in_specs += [
        pl.BlockSpec(table.shape, lambda j, meta: (0, 0, 0)),
        pl.BlockSpec(smoothing.shape, lambda j, meta: (0, 0)),
    ]
    shapes = [(z.regions, z.chunk_rows(chunk), z.part) for chunk in range(CHUNKS)]
    return pl.pallas_call(
        functools.partial(blend_kernel, z),
        out_shape=[jax.ShapeDtypeStruct(shape, jnp.bfloat16) for shape in shapes],
        grid_spec=pltpu.PrefetchScalarGridSpec(
            num_scalar_prefetch=1,
            grid=(z.block,),
            in_specs=in_specs,
            out_specs=[pl.BlockSpec(shape, lambda j, meta: (0, 0, 0)) for shape in shapes],
            scratch_shapes=[
                pltpu.VMEM((2 * z.makers, TILES, PAIRS * FIELDS, LANES), jnp.float32),
                pltpu.VMEM((FIELDS, TILES, LANES, LANES), jnp.float32),
                pltpu.VMEM((FIELDS, COLS + 8, LANES), jnp.float32),
                pltpu.VMEM((z.regions, 8, z.part), jnp.float32),
            ],
        ),
        compiler_params=pltpu.CompilerParams(vmem_limit_bytes=VMEM),
        name="blend",
    )(meta, *operands, table, smoothing)


SORT_STEPS = (
    ((0, 1), (2, 3), (4, 5), (6, 7)),
    ((0, 2), (1, 3), (4, 6), (5, 7)),
    ((1, 2), (5, 6)),
    ((0, 4), (1, 5), (2, 6), (3, 7)),
    ((2, 4), (3, 5)),
    ((1, 2), (3, 4), (5, 6)),
)


def score_kernel(z, chunk, block, strength_block, analysis, *refs):
    crps, spread = refs[-6:-4]
    strength, padded, members, results = refs[-4:]
    rows = z.rows
    for source in range(z.regions):
        piece = strength_block[source].astype(jnp.float32)[8:16]
        for g in range(z.span // 8):
            strength[8 * g : 8 * (g + 1), ROWS * source : ROWS * (source + 1)] = (
                piece[:, ROWS * g : ROWS * (g + 1)] + MID
            )
    lane = lax.broadcasted_iota(jnp.int32, (8, rows), 1)
    for f in range(PER_CHUNK):
        for sample in range(SAMPLES):
            for part in range(z.makers):
                source = sample * z.makers + part
                lanes = slice(part * z.part, (part + 1) * z.part)
                values = block[source, 0 : z.main, :].astype(jnp.float32)
                padded[8 : 8 + z.span, lanes] = values[f * z.span : (f + 1) * z.span]
                edge = block[source, z.main : z.main + 8, :].astype(jnp.float32)
                padded[7:8, lanes] = edge[2 * f : 2 * f + 1]
                padded[8 + z.width : 9 + z.width, lanes] = edge[2 * f + 1 : 2 * f + 2]
            for g in range(z.span // 8):
                here = padded[8 + 8 * g : 16 + 8 * g, :]
                sides = padded[7 + 8 * g : 15 + 8 * g, :] + padded[9 + 8 * g : 17 + 8 * g, :]
                above = jnp.where(lane == 0, here, pltpu.roll(here, 1, 1))
                below = jnp.where(lane == rows - 1, here, pltpu.roll(here, rows - 1, 1))
                laplace = above + below + sides - 4.0 * here
                smooth = here + strength[8 * g : 8 * (g + 1), :] * laplace
                members[sample, 8 * g : 8 * (g + 1), :] = smooth.astype(jnp.bfloat16).astype(jnp.float32)
        target_field = analysis[f].astype(jnp.float32)
        for g in range(z.span // 8):
            here = slice(8 * g, min(8 * (g + 1), z.width))
            values = [members[sample, here, :] for sample in range(SAMPLES)]
            target = target_field[here]
            error = sum(jnp.abs(value - target) for value in values) * (1.0 / SAMPLES)
            average = sum(values) * (1.0 / SAMPLES)
            variance = sum((value - average) ** 2 for value in values) * (1.0 / (SAMPLES - 1.0))
            ranked = list(values)
            for step in SORT_STEPS:
                for low, high in step:
                    a, b = ranked[low], ranked[high]
                    ranked[low], ranked[high] = jnp.minimum(a, b), jnp.maximum(a, b)
            half = SAMPLES // 2
            pairs = sum(
                (2 * k - SAMPLES + 1.0) * (ranked[k] - ranked[SAMPLES - 1 - k]) for k in range(half, SAMPLES)
            )
            results[0, here, :] = error - pairs * (1.0 / (SAMPLES * SAMPLES))
            results[1, here, :] = variance
            results[2, here, :] = (average - target) ** 2
        crps[f] = results[0, 0 : z.width, :].astype(jnp.bfloat16)
        spread[0, f] = results[1, 0 : z.width, :].astype(jnp.bfloat16)
        spread[1, f] = results[2, 0 : z.width, :].astype(jnp.bfloat16)


def score(z, chunk, block, first_block, analysis, earlier):
    width, rows = z.width, z.rows
    tail = z.main // 16
    in_specs = [
        pl.BlockSpec(block.shape, lambda i: (0, 0, 0)),
        pl.BlockSpec((z.regions, 16, z.part), lambda i: (0, tail, 0)),
        pl.BlockSpec((PER_CHUNK, width, rows), lambda i: (chunk, 0, 0)),
    ]
    in_specs += [pl.BlockSpec(memory_space=pl.ANY)] * len(earlier)
    return pl.pallas_call(
        functools.partial(score_kernel, z, chunk),
        out_shape=[
            jax.ShapeDtypeStruct((FIELDS, width, rows), jnp.bfloat16),
            jax.ShapeDtypeStruct((2, FIELDS, width, rows), jnp.bfloat16),
        ],
        grid=(1,),
        in_specs=in_specs,
        out_specs=[
            pl.BlockSpec((PER_CHUNK, width, rows), lambda i: (chunk, 0, 0)),
            pl.BlockSpec((2, PER_CHUNK, width, rows), lambda i: (0, chunk, 0, 0)),
        ],
        scratch_shapes=[
            pltpu.VMEM((z.span, rows), jnp.float32),
            pltpu.VMEM((z.span + 16, rows), jnp.float32),
            pltpu.VMEM((SAMPLES, z.span, rows), jnp.float32),
            pltpu.VMEM((3, z.span, rows), jnp.float32),
        ],
        input_output_aliases={3 + i: i for i in range(len(earlier))},
        compiler_params=pltpu.CompilerParams(vmem_limit_bytes=VMEM),
        cost_estimate=pl.CostEstimate(flops=30_000_000, bytes_accessed=3_000_000, transcendentals=0),
        name="score",
    )(block, first_block, analysis, *earlier)


def shards(patch_tiles, slot_lists, blend_table, smoothing, analysis):
    z = Sizes(lax.axis_size("region"))
    part = lax.rem(lax.axis_index("region"), z.makers)
    turns = [
        [(i, i - i % z.makers + (i + k) % z.makers) for i in range(z.regions)] for k in range(1, z.makers)
    ]
    other_lists = [lax.ppermute(slot_lists, "region", turn) for turn in turns]
    packed = pack_tiles(z, slot_lists.reshape(-1), patch_tiles)
    received = [lax.ppermute(packed[k : k + 1], "region", turn) for k, turn in enumerate(turns)]
    meta = jnp.concatenate([part.reshape(1)] + [item.reshape(-1) for item in [slot_lists, *other_lists]])
    table = blend_table.reshape(blend_table.shape[0], PAIRS, COLS)
    blocks = blend(z, meta, patch_tiles, received, table, smoothing)
    moved = [lax.all_to_all(item, "region", split_axis=0, concat_axis=0, tiled=True) for item in blocks]
    analysis = jnp.swapaxes(analysis, 1, 2)
    outs = ()
    for chunk in range(CHUNKS):
        outs = score(z, chunk, moved[chunk], moved[0], analysis, outs)
    return tuple(jnp.swapaxes(item, -1, -2) for item in outs)


def solution(mesh):
    return jax.shard_map(
        shards,
        mesh=mesh,
        in_specs=(
            P(("groups", "region"), None, None, None),
            P(("groups", "region"), None, None),
            P(),
            P("region", None),
            P(None, "groups", "region"),
        ),
        out_specs=(P(None, "groups", "region"), P(None, None, "groups", "region")),
        check_vma=False,
    )
```

```python
import functools

import jax
import jax.numpy as jnp
from jax import lax
from jax.experimental import pallas as pl
from jax.experimental.pallas import tpu as pltpu
from jax.sharding import PartitionSpec as P

SAMPLES = 8
FIELDS = 4
PATCH = 448
CAP = 2
ROWS = 32
COLS = 896
PAIRS = ROWS // 2
FLAT = ROWS * PATCH
LANES = 128
TILES = COLS // LANES
PER_CHUNK = 2
CHUNKS = FIELDS // PER_CHUNK
MID = 0.11
VMEM = 48 * 1024 * 1024


def round_up(value, step):
    return -(-value // step) * step


class Sizes:
    def __init__(self, regions):
        self.regions = regions
        self.makers = regions // SAMPLES
        self.block = regions // self.makers
        self.heavy = min(self.block, regions // 4)
        self.part = self.block * ROWS
        self.width = COLS // regions
        self.span = round_up(self.width, 8)
        self.rows = regions * ROWS
        self.main = PER_CHUNK * self.span

    def chunk_rows(self, chunk):
        return self.main + (16 if chunk == 0 else 8)


def pack_kernel(z, lists, tiles, packed, sems):
    part = lax.rem(lax.axis_index("region"), z.makers)
    for k in range(1, z.makers):
        first = lax.rem(part + k, z.makers) * z.block
        bulk = pltpu.make_async_copy(
            tiles.at[pl.ds(first, z.block), 0], packed.at[k - 1, pl.ds(0, z.block)], sems.at[k - 1, 0]
        )
        bulk.start()
        rank = jnp.int32(0)
        for j in range(z.block):
            live = lists[0, 1, first + j] >= 0

            @pl.when(live)
            def _(j=j, rank=rank):
                pltpu.make_async_copy(
                    tiles.at[first + j, 1], packed.at[k - 1, z.block + rank], sems.at[k - 1, 1 + j]
                ).start()

            rank = jnp.minimum(rank + live.astype(jnp.int32), z.heavy - 1)
    for k in range(1, z.makers):
        first = lax.rem(part + k, z.makers) * z.block
        pltpu.make_async_copy(
            tiles.at[pl.ds(first, z.block), 0], packed.at[k - 1, pl.ds(0, z.block)], sems.at[k - 1, 0]
        ).wait()
        for j in range(z.block):

            @pl.when(lists[0, 1, first + j] >= 0)
            def _(j=j):
                pltpu.make_async_copy(
                    tiles.at[first + j, 1], packed.at[k - 1, z.block], sems.at[k - 1, 1 + j]
                ).wait()


def pack_tiles(z, lists, tiles):
    return pl.pallas_call(
        functools.partial(pack_kernel, z),
        out_shape=jax.ShapeDtypeStruct((z.makers - 1, z.block + z.heavy, FIELDS, FLAT), jnp.bfloat16),
        in_specs=[pl.BlockSpec(memory_space=pltpu.SMEM), pl.BlockSpec(memory_space=pl.ANY)],
        out_specs=pl.BlockSpec(memory_space=pltpu.VMEM),
        scratch_shapes=[pltpu.SemaphoreType.DMA((z.makers - 1, 1 + z.block))],
        compiler_params=pltpu.CompilerParams(vmem_limit_bytes=VMEM),
        name="pack_tiles",
    )(lists, tiles)


def blend_kernel(z, chunk, part, *refs):
    lists, refs = refs[: z.makers], refs[z.makers :]
    slots = refs[: 2 * z.makers]
    table, smoothing, out, staged, lines, turned, strength = refs[2 * z.makers :]
    fields = range(chunk * PER_CHUNK, (chunk + 1) * PER_CHUNK)
    j = pl.program_id(0)
    quad = LANES // ROWS
    region = part[0] * z.block + j

    def entry(maker, slot, field):
        return lists[maker][field, slot, region]

    heavy = entry(0, 1, 0) >= 0
    lane = lax.broadcasted_iota(jnp.int32, (PAIRS, COLS), 1)

    def stage(index):
        ref = slots[index]
        for k in range(PAIRS):
            for t in range(TILES):
                at = COLS * k + LANES * t
                staged[index, t, FIELDS * k : FIELDS * (k + 1), :] = ref[0, 0, :, at : at + LANES].astype(
                    jnp.float32
                )

    def pairs_of(index, field):
        return jnp.concatenate(
            [staged[index, t, pl.ds(field, PAIRS, stride=FIELDS), :] for t in range(TILES)], 1
        )

    def put(field, even, odd):
        at = lax.rem(j, quad) * ROWS
        for t in range(TILES):
            here = slice(LANES * t, LANES * (t + 1))
            lines[field - fields.start, t, pl.ds(at, PAIRS, stride=2), :] = even[:, here]
            lines[field - fields.start, t, pl.ds(at + 1, PAIRS, stride=2), :] = odd[:, here]

    for maker in range(z.makers):
        stage(2 * maker)

    def general(live_slots):
        def placed(pairs, column):
            turn = pltpu.roll(pairs, column, 1)
            other = pltpu.roll(turn, PATCH, 1)
            inside = (lane >= column) & (lane < column + PATCH)
            return jnp.where(inside, turn, 0.0), jnp.where(inside, other, 0.0)

        columns = [entry(i // 2, i % 2, 1) for i in live_slots]
        weights = [table[entry(i // 2, i % 2, 2)] for i in live_slots]
        even, odd = 0.0, 0.0
        for column, weight in zip(columns, weights):
            a, b = placed(weight, column)
            even, odd = even + a, odd + b
        even_inv, odd_inv = 1.0 / even, 1.0 / odd

        def one_field(field, carry):
            even, odd = 0.0, 0.0
            for i, column, weight in zip(live_slots, columns, weights):
                a, b = placed(pairs_of(i, field) * weight, column)
                even, odd = even + a, odd + b
            put(field, even * even_inv, odd * odd_inv)
            return carry

        lax.fori_loop(fields.start, fields.stop, one_field, 0)

    @pl.when(heavy)
    def _():
        for maker in range(z.makers):
            stage(2 * maker + 1)
        general(list(range(2 * z.makers)))

    @pl.when(jnp.logical_not(heavy))
    def _():
        if z.makers != 2:
            general([2 * maker for maker in range(z.makers)])
            return
        left_maker = (entry(0, 0, 1) != 0).astype(jnp.int32)
        left, right = 2 * left_maker, 2 - 2 * left_maker
        own, other = entry(0, 0, 2), entry(1, 0, 2)
        left_weight = table[jnp.where(left_maker == 0, own, other)]
        right_weight = table[jnp.where(left_maker == 0, other, own)]

        def merged(a, b):
            even = jnp.where(lane < PATCH, a, pltpu.roll(b, PATCH, 1))
            odd = jnp.where(lane < PATCH, pltpu.roll(a, PATCH, 1), b)
            return even, odd

        even_sum, odd_sum = merged(left_weight, right_weight)
        even_inv, odd_inv = 1.0 / even_sum, 1.0 / odd_sum

        def one_field(field, carry):
            even, odd = merged(
                pairs_of(left, field) * left_weight,
                pairs_of(right, field) * right_weight,
            )
            put(field, even * even_inv, odd * odd_inv)
            return carry

        lax.fori_loop(fields.start, fields.stop, one_field, 0)

    @pl.when((j == 0) & (chunk == 0))
    def _():
        turned_strength = jnp.transpose(smoothing[...] - MID)
        for dest in range(z.regions):
            for g in range(z.span // 8):
                top = z.width * dest + 8 * g
                rows = min(8, COLS - top)
                strength[dest, 0:rows, ROWS * g : ROWS * (g + 1)] = turned_strength[top : top + rows]

    @pl.when(lax.rem(j, quad) == quad - 1)
    def _():
        at = pl.multiple_of(lax.div(j, quad) * LANES, LANES)
        for f in range(PER_CHUNK):
            for t in range(TILES):
                turned[f, LANES * t : LANES * (t + 1), :] = jnp.transpose(lines[f, t])
        for dest in range(z.regions):
            first = z.width * dest
            block = [turned[f, first : first + z.span, :] for f in range(PER_CHUNK)]
            out[dest, 0 : z.main, pl.ds(at, LANES)] = jnp.concatenate(block, 0).astype(jnp.bfloat16)
            ends = (max(first - 1, 0), min(first + z.width, COLS - 1))
            edge = [turned[f, end : end + 1, :] for f in range(PER_CHUNK) for end in ends]
            edge.append(jnp.zeros((8 - len(edge), LANES), jnp.float32))
            if chunk == 0:
                edge.append(strength[dest, :, pl.ds(at, LANES)])
            edge = jnp.concatenate(edge, 0).astype(jnp.bfloat16)
            out[dest, z.main : z.chunk_rows(chunk), pl.ds(at, LANES)] = edge


def blend(z, chunk, part, lists, tiles, received, table, smoothing):
    tile_block = (1, 1, FIELDS, FLAT)

    def rank(j, part, own, *others):
        total = jnp.int32(0)
        for before in range(z.block):
            live = own[0, 1, part[0] * z.block + before] >= 0
            total = total + jnp.where(live & (before < j), 1, 0)
        return z.block + jnp.minimum(total, z.heavy - 1)

    in_specs = [
        pl.BlockSpec(tile_block, lambda j, part, *lists: (part[0] * z.block + j, 0, 0, 0)),
        pl.BlockSpec(tile_block, lambda j, part, *lists: (part[0] * z.block + j, 1, 0, 0)),
    ]
    operands = [tiles, tiles]
    for item in received:
        in_specs += [
            pl.BlockSpec(tile_block, lambda j, *scalars: (0, j, 0, 0)),
            pl.BlockSpec(tile_block, lambda j, *scalars: (0, rank(j, *scalars), 0, 0)),
        ]
        operands += [item, item]
    in_specs += [
        pl.BlockSpec(table.shape, lambda j, *scalars: (0, 0, 0)),
        pl.BlockSpec(smoothing.shape, lambda j, *scalars: (0, 0)),
    ]
    shape = (z.regions, z.chunk_rows(chunk), z.part)
    return pl.pallas_call(
        functools.partial(blend_kernel, z, chunk),
        out_shape=jax.ShapeDtypeStruct(shape, jnp.bfloat16),
        grid_spec=pltpu.PrefetchScalarGridSpec(
            num_scalar_prefetch=1 + z.makers,
            grid=(z.block,),
            in_specs=in_specs,
            out_specs=pl.BlockSpec(shape, lambda j, *scalars: (0, 0, 0)),
            scratch_shapes=[
                pltpu.VMEM((2 * z.makers, TILES, PAIRS * FIELDS, LANES), jnp.float32),
                pltpu.VMEM((PER_CHUNK, TILES, LANES, LANES), jnp.float32),
                pltpu.VMEM((PER_CHUNK, COLS + 8, LANES), jnp.float32),
                pltpu.VMEM((z.regions, 8, z.part), jnp.float32),
            ],
        ),
        compiler_params=pltpu.CompilerParams(vmem_limit_bytes=VMEM),
        cost_estimate=pl.CostEstimate(flops=50_000_000, bytes_accessed=4_000_000, transcendentals=0),
        name="blend",
    )(part, *lists, *operands, table, smoothing)


SORT_STEPS = (
    ((0, 1), (2, 3), (4, 5), (6, 7)),
    ((0, 2), (1, 3), (4, 6), (5, 7)),
    ((1, 2), (5, 6)),
    ((0, 4), (1, 5), (2, 6), (3, 7)),
    ((2, 4), (3, 5)),
    ((1, 2), (3, 4), (5, 6)),
)


def score_kernel(z, chunk, block, strength_block, analysis, *refs):
    crps, spread = refs[-6:-4]
    strength, padded, members, results = refs[-4:]
    rows = z.rows
    for source in range(z.regions):
        piece = strength_block[source].astype(jnp.float32)[8:16]
        for g in range(z.span // 8):
            strength[8 * g : 8 * (g + 1), ROWS * source : ROWS * (source + 1)] = (
                piece[:, ROWS * g : ROWS * (g + 1)] + MID
            )
    lane = lax.broadcasted_iota(jnp.int32, (8, rows), 1)
    for f in range(PER_CHUNK):
        for sample in range(SAMPLES):
            for part in range(z.makers):
                source = sample * z.makers + part
                lanes = slice(part * z.part, (part + 1) * z.part)
                values = block[source, 0 : z.main, :].astype(jnp.float32)
                padded[8 : 8 + z.span, lanes] = values[f * z.span : (f + 1) * z.span]
                edge = block[source, z.main : z.main + 8, :].astype(jnp.float32)
                padded[7:8, lanes] = edge[2 * f : 2 * f + 1]
                padded[8 + z.width : 9 + z.width, lanes] = edge[2 * f + 1 : 2 * f + 2]
            for g in range(z.span // 8):
                here = padded[8 + 8 * g : 16 + 8 * g, :]
                sides = padded[7 + 8 * g : 15 + 8 * g, :] + padded[9 + 8 * g : 17 + 8 * g, :]
                above = jnp.where(lane == 0, here, pltpu.roll(here, 1, 1))
                below = jnp.where(lane == rows - 1, here, pltpu.roll(here, rows - 1, 1))
                laplace = above + below + sides - 4.0 * here
                smooth = here + strength[8 * g : 8 * (g + 1), :] * laplace
                members[sample, 8 * g : 8 * (g + 1), :] = smooth.astype(jnp.bfloat16).astype(jnp.float32)
        target_field = analysis[f].astype(jnp.float32)
        for g in range(z.span // 8):
            here = slice(8 * g, min(8 * (g + 1), z.width))
            values = [members[sample, here, :] for sample in range(SAMPLES)]
            target = target_field[here]
            error = sum(jnp.abs(value - target) for value in values) * (1.0 / SAMPLES)
            average = sum(values) * (1.0 / SAMPLES)
            variance = sum((value - average) ** 2 for value in values) * (1.0 / (SAMPLES - 1.0))
            ranked = list(values)
            for step in SORT_STEPS:
                for low, high in step:
                    a, b = ranked[low], ranked[high]
                    ranked[low], ranked[high] = jnp.minimum(a, b), jnp.maximum(a, b)
            half = SAMPLES // 2
            pairs = sum(
                (2 * k - SAMPLES + 1.0) * (ranked[k] - ranked[SAMPLES - 1 - k]) for k in range(half, SAMPLES)
            )
            results[0, here, :] = error - pairs * (1.0 / (SAMPLES * SAMPLES))
            results[1, here, :] = variance
            results[2, here, :] = (average - target) ** 2
        crps[f] = results[0, 0 : z.width, :].astype(jnp.bfloat16)
        spread[0, f] = results[1, 0 : z.width, :].astype(jnp.bfloat16)
        spread[1, f] = results[2, 0 : z.width, :].astype(jnp.bfloat16)


def score(z, chunk, block, first_block, analysis, earlier):
    width, rows = z.width, z.rows
    tail = z.main // 16
    in_specs = [
        pl.BlockSpec(block.shape, lambda i: (0, 0, 0)),
        pl.BlockSpec((z.regions, 16, z.part), lambda i: (0, tail, 0)),
        pl.BlockSpec((PER_CHUNK, width, rows), lambda i: (chunk, 0, 0)),
    ]
    in_specs += [pl.BlockSpec(memory_space=pl.ANY)] * len(earlier)
    return pl.pallas_call(
        functools.partial(score_kernel, z, chunk),
        out_shape=[
            jax.ShapeDtypeStruct((FIELDS, width, rows), jnp.bfloat16),
            jax.ShapeDtypeStruct((2, FIELDS, width, rows), jnp.bfloat16),
        ],
        grid=(1,),
        in_specs=in_specs,
        out_specs=[
            pl.BlockSpec((PER_CHUNK, width, rows), lambda i: (chunk, 0, 0)),
            pl.BlockSpec((2, PER_CHUNK, width, rows), lambda i: (0, chunk, 0, 0)),
        ],
        scratch_shapes=[
            pltpu.VMEM((z.span, rows), jnp.float32),
            pltpu.VMEM((z.span + 16, rows), jnp.float32),
            pltpu.VMEM((SAMPLES, z.span, rows), jnp.float32),
            pltpu.VMEM((3, z.span, rows), jnp.float32),
        ],
        input_output_aliases={3 + i: i for i in range(len(earlier))},
        compiler_params=pltpu.CompilerParams(vmem_limit_bytes=VMEM),
        cost_estimate=pl.CostEstimate(flops=30_000_000, bytes_accessed=3_000_000, transcendentals=0),
        name="score",
    )(block, first_block, analysis, *earlier)


def shards(patch_tiles, slot_lists, blend_table, smoothing, analysis):
    z = Sizes(lax.axis_size("region"))
    part = lax.rem(lax.axis_index("region"), z.makers)
    turns = [
        [(i, i - i % z.makers + (i + k) % z.makers) for i in range(z.regions)] for k in range(1, z.makers)
    ]
    lists = jnp.transpose(slot_lists, (2, 1, 0))
    lists = [lists] + [lax.ppermute(lists, "region", turn) for turn in turns]
    packed = pack_tiles(z, lists[0], patch_tiles)
    received = [lax.ppermute(packed[k : k + 1], "region", turn) for k, turn in enumerate(turns)]
    table = blend_table.reshape(blend_table.shape[0], PAIRS, COLS)
    blocks = [
        blend(z, chunk, part.reshape(1), lists, patch_tiles, received, table, smoothing)
        for chunk in range(CHUNKS)
    ]
    moved = [lax.all_to_all(item, "region", split_axis=0, concat_axis=0, tiled=True) for item in blocks]
    analysis = jnp.swapaxes(analysis, 1, 2)
    outs = ()
    for chunk in range(CHUNKS):
        outs = score(z, chunk, moved[chunk], moved[0], analysis, outs)
    return tuple(jnp.swapaxes(item, -1, -2) for item in outs)


def solution(mesh):
    return jax.shard_map(
        shards,
        mesh=mesh,
        in_specs=(
            P(("groups", "region"), None, None, None),
            P(("groups", "region"), None, None),
            P(),
            P("region", None),
            P(None, "groups", "region"),
        ),
        out_specs=(P(None, "groups", "region"), P(None, None, "groups", "region")),
        check_vma=False,
    )
```

```python
import functools

import jax
import jax.numpy as jnp
from jax import lax
from jax.experimental import pallas as pl
from jax.experimental.pallas import tpu as pltpu
from jax.sharding import PartitionSpec as P

SAMPLES = 8
FIELDS = 4
PATCH = 448
CAP = 2
ROWS = 32
COLS = 896
PAIRS = ROWS // 2
FLAT = ROWS * PATCH
LANES = 128
TILES = COLS // LANES
PER_CHUNK = 2
CHUNKS = FIELDS // PER_CHUNK
MID = 0.11
VMEM = 48 * 1024 * 1024
WHOLE_VMEM = 62 * 1024 * 1024


def round_up(value, step):
    return -(-value // step) * step


class Sizes:
    def __init__(self, regions):
        self.regions = regions
        self.makers = regions // SAMPLES
        self.block = regions // self.makers
        self.heavy = min(self.block, regions // 4)
        self.part = self.block * ROWS
        self.width = COLS // regions
        self.span = round_up(self.width, 8)
        self.rows = regions * ROWS
        self.main = PER_CHUNK * self.span

    def chunk_rows(self, chunk):
        return self.main + (16 if chunk == 0 else 8)


def pack_kernel(z, lists, tiles, packed, sems):
    part = lax.rem(lax.axis_index("region"), z.makers)
    for k in range(1, z.makers):
        first = lax.rem(part + k, z.makers) * z.block
        bulk = pltpu.make_async_copy(
            tiles.at[pl.ds(first, z.block), 0], packed.at[k - 1, pl.ds(0, z.block)], sems.at[k - 1, 0]
        )
        bulk.start()
        rank = jnp.int32(0)
        for j in range(z.block):
            live = lists[0, 1, first + j] >= 0

            @pl.when(live)
            def _(j=j, rank=rank):
                pltpu.make_async_copy(
                    tiles.at[first + j, 1], packed.at[k - 1, z.block + rank], sems.at[k - 1, 1 + j]
                ).start()

            rank = jnp.minimum(rank + live.astype(jnp.int32), z.heavy - 1)
    for k in range(1, z.makers):
        first = lax.rem(part + k, z.makers) * z.block
        pltpu.make_async_copy(
            tiles.at[pl.ds(first, z.block), 0], packed.at[k - 1, pl.ds(0, z.block)], sems.at[k - 1, 0]
        ).wait()
        for j in range(z.block):

            @pl.when(lists[0, 1, first + j] >= 0)
            def _(j=j):
                pltpu.make_async_copy(
                    tiles.at[first + j, 1], packed.at[k - 1, z.block], sems.at[k - 1, 1 + j]
                ).wait()


def pack_tiles(z, lists, tiles):
    return pl.pallas_call(
        functools.partial(pack_kernel, z),
        out_shape=jax.ShapeDtypeStruct((z.makers - 1, z.block + z.heavy, FIELDS, FLAT), jnp.bfloat16),
        in_specs=[pl.BlockSpec(memory_space=pltpu.SMEM), pl.BlockSpec(memory_space=pltpu.HBM)],
        out_specs=pl.BlockSpec(memory_space=pltpu.VMEM),
        scratch_shapes=[pltpu.SemaphoreType.DMA((z.makers - 1, 1 + z.block))],
        compiler_params=pltpu.CompilerParams(vmem_limit_bytes=WHOLE_VMEM),
        name="pack_tiles",
    )(lists, tiles)


def blend_kernel(z, chunk, place, *refs):
    lists, refs = refs[: z.makers], refs[z.makers :]
    slots = refs[: 2 * z.makers]
    table, smoothing = refs[2 * z.makers : 2 * z.makers + 2]
    outs, (staged, lines, turned, strength) = refs[-4 - z.regions : -4], refs[-4:]
    fields = range(chunk * PER_CHUNK, (chunk + 1) * PER_CHUNK)
    j = pl.program_id(0)
    quad = LANES // ROWS
    me = place[0]
    region = lax.rem(me, z.makers) * z.block + j

    def entry(maker, slot, field):
        return lists[maker][field, slot, region]

    heavy = entry(0, 1, 0) >= 0
    lane = lax.broadcasted_iota(jnp.int32, (PAIRS, COLS), 1)

    def stage(index):
        ref = slots[index]
        for k in range(PAIRS):
            for t in range(TILES):
                at = COLS * k + LANES * t
                staged[index, t, FIELDS * k : FIELDS * (k + 1), :] = ref[0, 0, :, at : at + LANES].astype(
                    jnp.float32
                )

    def pairs_of(index, field):
        return jnp.concatenate(
            [staged[index, t, pl.ds(field, PAIRS, stride=FIELDS), :] for t in range(TILES)], 1
        )

    def put(field, even, odd):
        at = lax.rem(j, quad) * ROWS
        for t in range(TILES):
            here = slice(LANES * t, LANES * (t + 1))
            lines[field - fields.start, t, pl.ds(at, PAIRS, stride=2), :] = even[:, here]
            lines[field - fields.start, t, pl.ds(at + 1, PAIRS, stride=2), :] = odd[:, here]

    for maker in range(z.makers):
        stage(2 * maker)

    def general(live_slots):
        def placed(pairs, column):
            turn = pltpu.roll(pairs, column, 1)
            other = pltpu.roll(turn, PATCH, 1)
            inside = (lane >= column) & (lane < column + PATCH)
            return jnp.where(inside, turn, 0.0), jnp.where(inside, other, 0.0)

        columns = [entry(i // 2, i % 2, 1) for i in live_slots]
        weights = [table[entry(i // 2, i % 2, 2)] for i in live_slots]
        even, odd = 0.0, 0.0
        for column, weight in zip(columns, weights):
            a, b = placed(weight, column)
            even, odd = even + a, odd + b
        even_inv, odd_inv = 1.0 / even, 1.0 / odd

        def one_field(field, carry):
            even, odd = 0.0, 0.0
            for i, column, weight in zip(live_slots, columns, weights):
                a, b = placed(pairs_of(i, field) * weight, column)
                even, odd = even + a, odd + b
            put(field, even * even_inv, odd * odd_inv)
            return carry

        lax.fori_loop(fields.start, fields.stop, one_field, 0)

    @pl.when(heavy)
    def _():
        for maker in range(z.makers):
            stage(2 * maker + 1)
        general(list(range(2 * z.makers)))

    @pl.when(jnp.logical_not(heavy))
    def _():
        if z.makers != 2:
            general([2 * maker for maker in range(z.makers)])
            return
        left_maker = (entry(0, 0, 1) != 0).astype(jnp.int32)
        left, right = 2 * left_maker, 2 - 2 * left_maker
        own, other = entry(0, 0, 2), entry(1, 0, 2)
        left_weight = table[jnp.where(left_maker == 0, own, other)]
        right_weight = table[jnp.where(left_maker == 0, other, own)]

        def merged(a, b):
            even = jnp.where(lane < PATCH, a, pltpu.roll(b, PATCH, 1))
            odd = jnp.where(lane < PATCH, pltpu.roll(a, PATCH, 1), b)
            return even, odd

        even_sum, odd_sum = merged(left_weight, right_weight)
        even_inv, odd_inv = 1.0 / even_sum, 1.0 / odd_sum

        def one_field(field, carry):
            even, odd = merged(
                pairs_of(left, field) * left_weight,
                pairs_of(right, field) * right_weight,
            )
            put(field, even * even_inv, odd * odd_inv)
            return carry

        lax.fori_loop(fields.start, fields.stop, one_field, 0)

    @pl.when((j == 0) & (chunk == 0))
    def _():
        turned_strength = jnp.transpose(smoothing[...] - MID)
        for dest in range(z.regions):
            for g in range(z.span // 8):
                top = z.width * dest + 8 * g
                rows = min(8, COLS - top)
                strength[dest, 0:rows, ROWS * g : ROWS * (g + 1)] = turned_strength[top : top + rows]

    @pl.when(lax.rem(j, quad) == quad - 1)
    def _():
        at = pl.multiple_of(lax.div(j, quad) * LANES, LANES)
        for f in range(PER_CHUNK):
            for t in range(TILES):
                turned[f, LANES * t : LANES * (t + 1), :] = jnp.transpose(lines[f, t])
        for k, out in enumerate(outs):
            dest = me ^ k
            first = dest * z.width
            if z.width % 8 == 0:
                first = pl.multiple_of(first, 8)
            block = [turned[f, pl.ds(first, z.span), :] for f in range(PER_CHUNK)]
            out[0 : z.main, pl.ds(at, LANES)] = jnp.concatenate(block, 0).astype(jnp.bfloat16)
            ends = (jnp.maximum(first - 1, 0), jnp.minimum(first + z.width, COLS - 1))
            edge = [turned[f, pl.ds(end, 1), :] for f in range(PER_CHUNK) for end in ends]
            edge.append(jnp.zeros((8 - len(edge), LANES), jnp.float32))
            if chunk == 0:
                edge.append(strength[dest, :, pl.ds(at, LANES)])
            edge = jnp.concatenate(edge, 0).astype(jnp.bfloat16)
            out[z.main : z.chunk_rows(chunk), pl.ds(at, LANES)] = edge


def blend(z, chunk, place, lists, tiles, received, table, smoothing, earlier):
    tile_block = (1, 1, FIELDS, FLAT)

    def first_region(place):
        return lax.rem(place[0], z.makers) * z.block

    def rank(j, place, own, *others):
        total = jnp.int32(0)
        first = first_region(place)
        for before in range(z.block):
            live = own[0, 1, first + before] >= 0
            total = total + jnp.where(live & (before < j), 1, 0)
        return z.block + jnp.minimum(total, z.heavy - 1)

    in_specs = [
        pl.BlockSpec(tile_block, lambda j, place, *lists: (first_region(place) + j, 0, 0, 0)),
        pl.BlockSpec(tile_block, lambda j, place, *lists: (first_region(place) + j, 1, 0, 0)),
    ]
    operands = [tiles, tiles]
    for item in received:
        in_specs += [
            pl.BlockSpec(tile_block, lambda j, *scalars: (0, j, 0, 0)),
            pl.BlockSpec(tile_block, lambda j, *scalars: (0, rank(j, *scalars), 0, 0)),
        ]
        operands += [item, item]
    in_specs += [
        pl.BlockSpec(table.shape, lambda j, *scalars: (0, 0, 0)),
        pl.BlockSpec(smoothing.shape, lambda j, *scalars: (0, 0)),
    ]
    in_specs += [pl.BlockSpec(memory_space=pl.ANY)] * len(earlier)
    shape = (z.chunk_rows(chunk), z.part)
    return pl.pallas_call(
        functools.partial(blend_kernel, z, chunk),
        out_shape=[jax.ShapeDtypeStruct(shape, jnp.bfloat16)] * z.regions,
        grid_spec=pltpu.PrefetchScalarGridSpec(
            num_scalar_prefetch=1 + z.makers,
            grid=(z.block,),
            in_specs=in_specs,
            out_specs=[pl.BlockSpec(shape, lambda j, *scalars: (0, 0))] * z.regions,
            scratch_shapes=[
                pltpu.VMEM((2 * z.makers, TILES, PAIRS * FIELDS, LANES), jnp.float32),
                pltpu.VMEM((PER_CHUNK, TILES, LANES, LANES), jnp.float32),
                pltpu.VMEM((PER_CHUNK, COLS + 8, LANES), jnp.float32),
                pltpu.VMEM((z.regions, 8, z.part), jnp.float32),
            ],
        ),
        compiler_params=pltpu.CompilerParams(vmem_limit_bytes=VMEM),
        cost_estimate=pl.CostEstimate(flops=50_000_000, bytes_accessed=4_000_000, transcendentals=0),
        name="blend",
    )(place, *lists, *operands, table, smoothing, *earlier)


SORT_STEPS = (
    ((0, 1), (2, 3), (4, 5), (6, 7)),
    ((0, 2), (1, 3), (4, 6), (5, 7)),
    ((1, 2), (5, 6)),
    ((0, 4), (1, 5), (2, 6), (3, 7)),
    ((2, 4), (3, 5)),
    ((1, 2), (3, 4), (5, 6)),
)


def score_kernel(z, chunk, place, *refs):
    blocks, refs = refs[: z.regions], refs[z.regions :]
    me = place[0]
    if chunk == 0:
        analysis, crps, spread, strength, padded, members, results = refs
        slot = lax.broadcasted_iota(jnp.int32, (8, LANES), 1) // ROWS
        quad = LANES // ROWS
        for first in range(0, z.regions, quad):
            pieces = []
            for k in range(first, first + quad):
                piece = blocks[k][z.main : z.main + 16, :].astype(jnp.float32)[8:16]
                turn = lax.rem(me ^ k, quad)
                pieces.append((pltpu.roll(piece, turn * ROWS, 1), turn))
            at = pl.multiple_of(lax.div(me ^ first, quad) * LANES, LANES)
            for g in range(z.span // 8):
                joined = jnp.full((8, LANES), MID)
                for piece, turn in pieces:
                    near = pltpu.roll(piece, (z.part - ROWS * g) % z.part, 1)[:, :LANES]
                    joined = jnp.where(slot == turn, near + MID, joined)
                strength[8 * g : 8 * (g + 1), pl.ds(at, LANES)] = joined
    else:
        strength, analysis = refs[:2]
        crps, spread, padded, members, results = refs[-5:]
    rows = z.rows
    lane = lax.broadcasted_iota(jnp.int32, (8, rows), 1)
    for f in range(PER_CHUNK):
        for sample in range(SAMPLES):
            for k in range(sample * z.makers, (sample + 1) * z.makers):
                block = blocks[k]
                lanes = pl.ds(pl.multiple_of(lax.rem(me ^ k, z.makers) * z.part, LANES), z.part)
                values = block[0 : z.main, :].astype(jnp.float32)
                padded[8 : 8 + z.span, lanes] = values[f * z.span : (f + 1) * z.span]
                edge = block[z.main : z.main + 8, :].astype(jnp.float32)
                padded[7:8, lanes] = edge[2 * f : 2 * f + 1]
                padded[8 + z.width : 9 + z.width, lanes] = edge[2 * f + 1 : 2 * f + 2]
            for g in range(z.span // 8):
                here = padded[8 + 8 * g : 16 + 8 * g, :]
                sides = padded[7 + 8 * g : 15 + 8 * g, :] + padded[9 + 8 * g : 17 + 8 * g, :]
                above = jnp.where(lane == 0, here, pltpu.roll(here, 1, 1))
                below = jnp.where(lane == rows - 1, here, pltpu.roll(here, rows - 1, 1))
                laplace = above + below + sides - 4.0 * here
                smooth = here + strength[8 * g : 8 * (g + 1), :] * laplace
                members[sample, 8 * g : 8 * (g + 1), :] = smooth.astype(jnp.bfloat16).astype(jnp.float32)
        target_field = analysis[f].astype(jnp.float32)
        for g in range(z.span // 8):
            here = slice(8 * g, min(8 * (g + 1), z.width))
            values = [members[sample, here, :] for sample in range(SAMPLES)]
            target = target_field[here]
            error = sum(jnp.abs(value - target) for value in values) * (1.0 / SAMPLES)
            average = sum(values) * (1.0 / SAMPLES)
            variance = sum((value - average) ** 2 for value in values) * (1.0 / (SAMPLES - 1.0))
            ranked = list(values)
            for step in SORT_STEPS:
                for low, high in step:
                    a, b = ranked[low], ranked[high]
                    ranked[low], ranked[high] = jnp.minimum(a, b), jnp.maximum(a, b)
            half = SAMPLES // 2
            pairs = sum(
                (2 * k - SAMPLES + 1.0) * (ranked[k] - ranked[SAMPLES - 1 - k]) for k in range(half, SAMPLES)
            )
            results[0, here, :] = error - pairs * (1.0 / (SAMPLES * SAMPLES))
            results[1, here, :] = variance
            results[2, here, :] = (average - target) ** 2
        crps[f] = results[0, 0 : z.width, :].astype(jnp.bfloat16)
        spread[0, f] = results[1, 0 : z.width, :].astype(jnp.bfloat16)
        spread[1, f] = results[2, 0 : z.width, :].astype(jnp.bfloat16)


def score(z, chunk, place, blocks, analysis, strength, earlier):
    width, rows = z.width, z.rows
    in_specs = [pl.BlockSpec(blocks[0].shape, lambda i, place: (0, 0))] * z.regions
    if chunk:
        in_specs.append(pl.BlockSpec(strength.shape, lambda i, place: (0, 0)))
    in_specs.append(pl.BlockSpec((PER_CHUNK, width, rows), lambda i, place: (chunk, 0, 0)))
    in_specs += [pl.BlockSpec(memory_space=pl.ANY)] * len(earlier)
    out_shape = [
        jax.ShapeDtypeStruct((FIELDS, width, rows), jnp.bfloat16),
        jax.ShapeDtypeStruct((2, FIELDS, width, rows), jnp.bfloat16),
    ]
    out_specs = [
        pl.BlockSpec((PER_CHUNK, width, rows), lambda i, place: (chunk, 0, 0)),
        pl.BlockSpec((2, PER_CHUNK, width, rows), lambda i, place: (0, chunk, 0, 0)),
    ]
    if chunk == 0:
        out_shape.append(jax.ShapeDtypeStruct((z.span, rows), jnp.float32))
        out_specs.append(pl.BlockSpec((z.span, rows), lambda i, place: (0, 0)))
    operands = [place, *blocks, *([strength] if chunk else []), analysis]
    return pl.pallas_call(
        functools.partial(score_kernel, z, chunk),
        out_shape=out_shape,
        grid_spec=pltpu.PrefetchScalarGridSpec(
            num_scalar_prefetch=1,
            grid=(1,),
            in_specs=in_specs,
            out_specs=out_specs,
            scratch_shapes=[
                pltpu.VMEM((z.span + 16, rows), jnp.float32),
                pltpu.VMEM((SAMPLES, z.span, rows), jnp.float32),
                pltpu.VMEM((3, z.span, rows), jnp.float32),
            ],
        ),
        input_output_aliases={len(operands) + i: i for i in range(len(earlier))},
        compiler_params=pltpu.CompilerParams(vmem_limit_bytes=VMEM),
        cost_estimate=pl.CostEstimate(flops=30_000_000, bytes_accessed=3_000_000, transcendentals=0),
        name="score",
    )(*operands, *earlier)


def swap_order(regions):
    far, near = list(range(regions // 2, regions)), list(range(regions // 2 - 1, 0, -1))
    order = []
    while far or near:
        taken = 1 if far else len(near)
        order += far[:2] + near[:taken]
        far, near = far[2:], near[taken:]
    return order


def shards(patch_tiles, slot_lists, blend_table, smoothing, analysis):
    z = Sizes(lax.axis_size("region"))
    place = lax.axis_index("region").reshape(1)
    turns = [
        [(i, i - i % z.makers + (i + k) % z.makers) for i in range(z.regions)] for k in range(1, z.makers)
    ]
    lists = jnp.transpose(slot_lists, (2, 1, 0))
    lists = [lists] + [lax.ppermute(lists, "region", turn) for turn in turns]
    packed = pack_tiles(z, lists[0], patch_tiles)
    received = [lax.ppermute(packed[k : k + 1], "region", turn) for k, turn in enumerate(turns)]
    table = blend_table.reshape(blend_table.shape[0], PAIRS, COLS)
    arrived = []
    for chunk in range(CHUNKS):
        earlier = [blocks[0] for blocks in arrived]
        blocks = list(blend(z, chunk, place, lists, patch_tiles, received, table, smoothing, earlier))
        for k in swap_order(z.regions):
            blocks[k] = lax.ppermute(blocks[k], "region", [(i, i ^ k) for i in range(z.regions)])
        arrived.append(blocks)
    analysis = jnp.swapaxes(analysis, 1, 2)
    strength, outs = None, ()
    for chunk in range(CHUNKS):
        outs = score(z, chunk, place, arrived[chunk], analysis, strength, outs)
        if chunk == 0:
            strength, outs = outs[2], outs[:2]
    return tuple(jnp.swapaxes(item, -1, -2) for item in outs)


def solution(mesh):
    return jax.shard_map(
        shards,
        mesh=mesh,
        in_specs=(
            P(("groups", "region"), None, None, None),
            P(("groups", "region"), None, None),
            P(),
            P("region", None),
            P(None, "groups", "region"),
        ),
        out_specs=(P(None, "groups", "region"), P(None, None, "groups", "region")),
        check_vma=False,
    )
```

```python
import functools

import jax
import jax.numpy as jnp
from jax import lax
from jax.experimental import pallas as pl
from jax.experimental.pallas import tpu as pltpu
from jax.sharding import PartitionSpec as P

SAMPLES = 8
FIELDS = 4
PATCH = 448
CAP = 2
ROWS = 32
COLS = 896
PAIRS = ROWS // 2
FLAT = ROWS * PATCH
LANES = 128
TILES = COLS // LANES
QUAD = LANES // ROWS
MID = 0.11
VMEM = 40 * 1024 * 1024


def round_up(value, step):
    return -(-value // step) * step


class Sizes:
    def __init__(self, regions):
        self.regions = regions
        self.makers = regions // SAMPLES
        self.block = regions // self.makers
        self.quads = self.block // QUAD
        self.width = COLS // regions
        self.span = round_up(self.width, 8)
        self.rows = regions * ROWS
        self.main = round_up(FIELDS * self.span, 16)
        self.sent = self.main + 16


def stage(staged, load):
    for k in range(PAIRS):
        for t in range(TILES):
            at = COLS * k + LANES * t
            staged[t, FIELDS * k : FIELDS * (k + 1), :] = load(at).astype(jnp.float32)


def staged_field(staged, field):
    return jnp.concatenate([staged[t, pl.ds(field, PAIRS, stride=FIELDS), :] for t in range(TILES)], 1)


def lane_index():
    return lax.broadcasted_iota(jnp.int32, (PAIRS, COLS), 1)


def place_side(pairs, column):
    left = (lane_index() < PATCH) & (column == 0)
    right = (lane_index() >= PATCH) & (column != 0)
    turned = pltpu.roll(pairs, PATCH, 1)
    even = jnp.where(left, pairs, jnp.where(right, turned, 0.0))
    odd = jnp.where(left, turned, jnp.where(right, pairs, 0.0))
    return even, odd


def place_any(pairs, column):
    inside = (lane_index() >= column) & (lane_index() < column + PATCH)
    turned = pltpu.roll(pairs, column, 1)
    return jnp.where(inside, turned, 0.0), jnp.where(inside, pltpu.roll(turned, PATCH, 1), 0.0)


def either_kind(z, heavy, body):
    @pl.when(heavy)
    def _():
        body(place_any, range(CAP))

    @pl.when(jnp.logical_not(heavy))
    def _():
        body(place_side if z.makers == 2 else place_any, range(1))


def own_kernel(z, place, *refs):
    lists, (tiles, table, half, inverse) = refs[: z.makers], refs[z.makers : z.makers + 4]
    landed, staged, weights, sems = refs[z.makers + 4 :]
    first = lax.rem(place[0], z.makers) * z.block

    def fetch(j):
        return pltpu.make_async_copy(tiles.at[first + j], landed.at[j], sems.at[j])

    for j in range(z.block):
        fetch(j).start()
    kinds = table.shape[0]
    for k in range(PAIRS):
        for t in range(TILES):
            at = COLS * k + LANES * t
            for low in range(0, kinds, 8):
                count = min(8, kinds - low)
                weights[t, pl.ds(PAIRS * low + k, count, stride=PAIRS), :] = table[
                    low : low + count, at : at + LANES
                ]

    def weight(kind):
        at = pl.multiple_of(kind * PAIRS, PAIRS)
        return jnp.concatenate([weights[t, pl.ds(at, PAIRS), :] for t in range(TILES)], 1)

    def region(j, carry):
        fetch(j).wait()

        def body(place_tile, slots):
            even, odd = 0.0, 0.0
            for maker in range(z.makers):
                for slot in slots:
                    column, kind = (lists[maker][field, slot, first + j] for field in (1, 2))
                    a, b = place_tile(weight(kind), column)
                    even, odd = even + a, odd + b
            inverse[j, 0] = 1.0 / even
            inverse[j, 1] = 1.0 / odd
            for slot in slots:
                stage(staged.at[slot], lambda at, slot=slot: landed[j, slot, :, at : at + LANES])

            def one_field(field, carry):
                even, odd = 0.0, 0.0
                for slot in slots:
                    column, kind = (lists[0][entry, slot, first + j] for entry in (1, 2))
                    a, b = place_tile(staged_field(staged.at[slot], field) * weight(kind), column)
                    even, odd = even + a, odd + b
                half[j, field, 0] = even * inverse[j, 0]
                half[j, field, 1] = odd * inverse[j, 1]
                return carry

            lax.fori_loop(0, FIELDS, one_field, 0)

        either_kind(z, lists[0][0, 1, first + j] >= 0, body)
        return carry

    lax.fori_loop(0, z.block, region, 0)


def own_share(z, place, lists, tiles, table):
    smem = pl.BlockSpec(memory_space=pltpu.SMEM)
    kinds = round_up(table.shape[0], 8)
    return pl.pallas_call(
        functools.partial(own_kernel, z),
        out_shape=[
            jax.ShapeDtypeStruct((z.block, FIELDS, 2, PAIRS, COLS), jnp.float32),
            jax.ShapeDtypeStruct((z.block, 2, PAIRS, COLS), jnp.float32),
        ],
        in_specs=[smem] * (1 + z.makers)
        + [pl.BlockSpec(memory_space=pltpu.HBM), pl.BlockSpec(memory_space=pltpu.VMEM)],
        out_specs=[pl.BlockSpec(memory_space=pltpu.VMEM)] * 2,
        scratch_shapes=[
            pltpu.VMEM((z.block, CAP, FIELDS, FLAT), jnp.bfloat16),
            pltpu.VMEM((CAP, TILES, PAIRS * FIELDS, LANES), jnp.float32),
            pltpu.VMEM((TILES, kinds * PAIRS, LANES), jnp.float32),
            pltpu.SemaphoreType.DMA((z.block,)),
        ],
        compiler_params=pltpu.CompilerParams(vmem_limit_bytes=VMEM),
        cost_estimate=pl.CostEstimate(flops=5_000_000, bytes_accessed=8_000_000, transcendentals=0),
        name="own_share",
    )(place, *lists, tiles, table)


def join_kernel(z, *refs):
    place, lists, refs = refs[0], refs[1 : 1 + z.makers], refs[1 + z.makers :]
    received, (half, inverse, table, smoothing, out) = refs[: z.makers - 1], refs[z.makers - 1 : z.makers + 4]
    staged, lines, turned, strength, blocks, sems = refs[z.makers + 4 :]
    first = lax.rem(place[0], z.makers) * z.block

    turned_strength = jnp.transpose(smoothing[...] - MID)
    for dest in range(z.regions):
        for g in range(z.span // 8):
            top = z.width * dest + 8 * g
            count, at = min(8, COLS - top), ROWS * (g % QUAD)
            strength[dest, g // QUAD, 0:count, at : at + ROWS] = turned_strength[top : top + count]

    def send(quad):
        return pltpu.make_async_copy(blocks.at[:, quad], out.at[:, quad], sems.at[quad])

    for quad in range(z.quads):

        def region(i, carry):
            j = quad * QUAD + i

            def body(place_tile, slots):
                entries = []
                for maker in range(1, z.makers):
                    for slot in slots:
                        index = (maker - 1) * CAP + slot
                        stage(
                            staged.at[index],
                            lambda at, maker=maker, slot=slot: received[maker - 1][j, slot, :, at : at + LANES],
                        )
                        column, kind = (lists[maker][field, slot, first + j] for field in (1, 2))
                        entries.append((index, column, kind))

                def one_field(field, carry):
                    even, odd = 0.0, 0.0
                    for index, column, kind in entries:
                        a, b = place_tile(staged_field(staged.at[index], field) * table[kind], column)
                        even, odd = even + a, odd + b
                    even = even * inverse[j, 0] + half[j, field, 0]
                    odd = odd * inverse[j, 1] + half[j, field, 1]
                    for t in range(TILES):
                        here = slice(LANES * t, LANES * (t + 1))
                        lines[field, t, pl.ds(ROWS * i, PAIRS, stride=2), :] = even[:, here]
                        lines[field, t, pl.ds(ROWS * i + 1, PAIRS, stride=2), :] = odd[:, here]
                    return carry

                lax.fori_loop(0, FIELDS, one_field, 0)

            either_kind(z, lists[0][0, 1, first + j] >= 0, body)
            return carry

        lax.fori_loop(0, QUAD, region, 0)
        for field in range(FIELDS):
            for t in range(TILES):
                turned[field, LANES * t : LANES * (t + 1), :] = jnp.transpose(lines[field, t])
        for dest in range(z.regions):
            top = z.width * dest
            for low in range(0, FIELDS, 2):
                block = [turned[field, top : top + z.span, :] for field in (low, low + 1)]
                blocks[dest, quad, low * z.span : (low + 2) * z.span, :] = jnp.concatenate(block, 0).astype(
                    jnp.bfloat16
                )
            ends = (max(top - 1, 0), min(top + z.width, COLS - 1))
            edge = [turned[field, end : end + 1, :] for field in range(FIELDS) for end in ends]
            edge.append(strength[dest, quad])
            blocks[dest, quad, z.main : z.sent, :] = jnp.concatenate(edge, 0).astype(jnp.bfloat16)
        send(quad).start()
    for quad in range(z.quads):
        send(quad).wait()


def join(z, place, lists, received, half, inverse, table, smoothing):
    smem = pl.BlockSpec(memory_space=pltpu.SMEM)
    vmem = pl.BlockSpec(memory_space=pltpu.VMEM)
    shape = (z.regions, z.quads, z.sent, LANES)
    return pl.pallas_call(
        functools.partial(join_kernel, z),
        out_shape=pltpu.HBM(shape, jnp.bfloat16),
        in_specs=[smem] * (1 + z.makers) + [vmem] * (z.makers + 3),
        out_specs=pl.BlockSpec(memory_space=pltpu.HBM),
        scratch_shapes=[
            pltpu.VMEM((CAP * (z.makers - 1), TILES, PAIRS * FIELDS, LANES), jnp.float32),
            pltpu.VMEM((FIELDS, TILES, LANES, LANES), jnp.float32),
            pltpu.VMEM((FIELDS, COLS + 8, LANES), jnp.float32),
            pltpu.VMEM((z.regions, z.quads, 8, LANES), jnp.float32),
            pltpu.VMEM(shape, jnp.bfloat16),
            pltpu.SemaphoreType.DMA((z.quads,)),
        ],
        compiler_params=pltpu.CompilerParams(vmem_limit_bytes=VMEM),
        cost_estimate=pl.CostEstimate(flops=5_000_000, bytes_accessed=8_000_000, transcendentals=0),
        name="join",
    )(place, *lists, *received, half, inverse, table, smoothing)


SORT_STEPS = (
    ((0, 1), (2, 3), (4, 5), (6, 7)),
    ((0, 2), (1, 3), (4, 6), (5, 7)),
    ((1, 2), (5, 6)),
    ((0, 4), (1, 5), (2, 6), (3, 7)),
    ((2, 4), (3, 5)),
    ((1, 2), (3, 4), (5, 6)),
)
STEP_FIELDS = 2


def score_kernel(z, blocks, analysis, crps, spread, strength, edges, padded):
    step = pl.program_id(0)
    rows = z.rows
    sources = [(source, quad) for source in range(z.regions) for quad in range(z.quads)]

    @pl.when(step == 0)
    def _():
        slot = lax.broadcasted_iota(jnp.int32, (8, LANES), 1) // ROWS
        for low in range(0, z.regions, QUAD):
            for quad in range(z.quads):
                tails = [
                    blocks[source, quad, z.main : z.sent, :].astype(jnp.float32)
                    for source in range(low, low + QUAD)
                ]
                for i, tail in enumerate(tails):
                    at = ((low + i) % z.makers * z.quads + quad) * LANES
                    edges[(low + i) // z.makers, :, at : at + LANES] = tail[0:8]
                for g in range(quad * QUAD, min((quad + 1) * QUAD, z.span // 8)):
                    joined = jnp.zeros((8, LANES), jnp.float32)
                    for i, tail in enumerate(tails):
                        near = pltpu.roll(tail[8:16], (i - g) % QUAD * ROWS, 1)
                        joined = jnp.where(slot == i, near, joined)
                    at = low // QUAD * LANES
                    strength[8 * g : 8 * (g + 1), at : at + LANES] = joined + MID

    top = pl.multiple_of(step * STEP_FIELDS * z.span, 16)
    for source, quad in sources:
        at = (source % z.makers * z.quads + quad) * LANES
        values = blocks[source, quad, pl.ds(top, STEP_FIELDS * z.span), :].astype(jnp.float32)
        for f in range(STEP_FIELDS):
            padded[source // z.makers, f, 8 : 8 + z.span, at : at + LANES] = values[f * z.span : (f + 1) * z.span]
    for sample in range(SAMPLES):
        for f in range(STEP_FIELDS):
            low = 2 * (step * STEP_FIELDS + f)
            padded[sample, f, 7:8, :] = edges[sample, pl.ds(low, 1), :]
            padded[sample, f, 8 + z.width : 9 + z.width, :] = edges[sample, pl.ds(low + 1, 1), :]
    for f in range(STEP_FIELDS):
        target_field = analysis[f].astype(jnp.float32)
        for low in range(0, z.width, 16):
            high = min(low + 16, z.width)
            shape = (high - low, rows)
            lane = lax.broadcasted_iota(jnp.int32, shape, 1)
            strong = strength[low:high, :]
            members = []
            for sample in range(SAMPLES):
                here = padded[sample, f, 8 + low : 8 + high, :]
                sides = padded[sample, f, 7 + low : 7 + high, :] + padded[sample, f, 9 + low : 9 + high, :]
                above = jnp.where(lane == 0, here, pltpu.roll(here, 1, 1))
                below = jnp.where(lane == rows - 1, here, pltpu.roll(here, rows - 1, 1))
                smooth = here + strong * (above + below + sides - 4.0 * here)
                members.append(smooth.astype(jnp.bfloat16))
            values = [member.astype(jnp.float32) for member in members]
            target = target_field[low:high]
            error = sum(jnp.abs(value - target) for value in values) * (1.0 / SAMPLES)
            average = sum(values) * (1.0 / SAMPLES)
            variance = sum((value - average) ** 2 for value in values) * (1.0 / (SAMPLES - 1.0))
            ranked = list(members)
            for pairs in SORT_STEPS:
                for a, b in pairs:
                    ranked[a], ranked[b] = jnp.minimum(ranked[a], ranked[b]), jnp.maximum(ranked[a], ranked[b])
            ranked = [member.astype(jnp.float32) for member in ranked]
            pairs = sum(
                (2 * k - SAMPLES + 1.0) * (ranked[k] - ranked[SAMPLES - 1 - k])
                for k in range(SAMPLES // 2, SAMPLES)
            )
            crps[f, low:high, :] = (error - pairs * (1.0 / (SAMPLES * SAMPLES))).astype(jnp.bfloat16)
            spread[0, f, low:high, :] = variance.astype(jnp.bfloat16)
            spread[1, f, low:high, :] = ((average - target) ** 2).astype(jnp.bfloat16)


def score(z, blocks, analysis):
    width, rows = z.width, z.rows
    return pl.pallas_call(
        functools.partial(score_kernel, z),
        out_shape=[
            jax.ShapeDtypeStruct((FIELDS, width, rows), jnp.bfloat16),
            jax.ShapeDtypeStruct((2, FIELDS, width, rows), jnp.bfloat16),
        ],
        grid=(FIELDS // STEP_FIELDS,),
        in_specs=[
            pl.BlockSpec(blocks.shape, lambda i: (0, 0, 0, 0)),
            pl.BlockSpec((STEP_FIELDS, width, rows), lambda i: (i, 0, 0)),
        ],
        out_specs=[
            pl.BlockSpec((STEP_FIELDS, width, rows), lambda i: (i, 0, 0)),
            pl.BlockSpec((2, STEP_FIELDS, width, rows), lambda i: (0, i, 0, 0)),
        ],
        scratch_shapes=[
            pltpu.VMEM((z.span, rows), jnp.float32),
            pltpu.VMEM((SAMPLES, 8, rows), jnp.float32),
            pltpu.VMEM((SAMPLES, STEP_FIELDS, z.span + 16, rows), jnp.float32),
        ],
        compiler_params=pltpu.CompilerParams(vmem_limit_bytes=VMEM),
        name="score",
    )(blocks, analysis)


def shards(patch_tiles, slot_lists, blend_table, smoothing, analysis):
    z = Sizes(lax.axis_size("region"))
    place = lax.axis_index("region")
    part = lax.rem(place, z.makers)
    place = place.reshape(1)
    turns = [
        [(i, i - i % z.makers + (i + k) % z.makers) for i in range(z.regions)] for k in range(1, z.makers)
    ]
    lists = jnp.transpose(slot_lists, (2, 1, 0))
    lists = [lists] + [lax.ppermute(lists, "region", turn) for turn in turns]
    received = []
    for k, turn in enumerate(turns, 1):
        first = lax.rem(part + k, z.makers) * z.block
        received.append(
            lax.ppermute(lax.dynamic_slice_in_dim(patch_tiles, first, z.block, 0), "region", turn)
        )
    half, inverse = own_share(z, place, lists, patch_tiles, blend_table)
    table = blend_table.reshape(blend_table.shape[0], PAIRS, COLS)
    blocks = join(z, place, lists, received, half, inverse, table, smoothing)
    moved = lax.all_to_all(blocks, "region", split_axis=0, concat_axis=0, tiled=True)
    outs = score(z, moved, jnp.swapaxes(analysis, 1, 2))
    return tuple(jnp.swapaxes(item, -1, -2) for item in outs)


def solution(mesh):
    return jax.shard_map(
        shards,
        mesh=mesh,
        in_specs=(
            P(("groups", "region"), None, None, None),
            P(("groups", "region"), None, None),
            P(),
            P("region", None),
            P(None, "groups", "region"),
        ),
        out_specs=(P(None, "groups", "region"), P(None, None, "groups", "region")),
        check_vma=False,
    )
```

```python
import functools

import jax
import jax.numpy as jnp
from jax import lax
from jax.experimental import pallas as pl
from jax.experimental.pallas import tpu as pltpu
from jax.sharding import PartitionSpec as P

SAMPLES = 8
FIELDS = 4
PATCH = 448
CAP = 2
ROWS = 32
COLS = 896
PAIRS = ROWS // 2
LINES = FIELDS * ROWS * PATCH // 128
LANES = 128
TILES = COLS // LANES
QUAD = LANES // ROWS
MID = 0.11
VMEM = 40 * 1024 * 1024
MOST_VMEM = 52 * 1024 * 1024


def round_up(value, step):
    return -(-value // step) * step


class Sizes:
    def __init__(self, regions):
        self.regions = regions
        self.makers = regions // SAMPLES
        self.block = regions // self.makers
        self.quads = self.block // QUAD
        self.width = COLS // regions
        self.span = round_up(self.width, 8)
        self.rows = regions * ROWS
        self.main = round_up(FIELDS * self.span, 16)
        self.sent = self.main + 16


def stage(staged, tile):
    staged[...] = tile.astype(jnp.float32)


def staged_field(staged, field):
    return jnp.concatenate(
        [staged[pl.ds(FIELDS * t + field, PAIRS, stride=FIELDS * TILES), :] for t in range(TILES)], 1
    )


def weight_of(weights, kind):
    at = pl.multiple_of(kind * PAIRS, PAIRS)
    return jnp.concatenate([weights[t, pl.ds(at, PAIRS), :] for t in range(TILES)], 1)


def lane_index():
    return lax.broadcasted_iota(jnp.int32, (PAIRS, COLS), 1)


def place_side(pairs, column):
    left = (lane_index() < PATCH) & (column == 0)
    right = (lane_index() >= PATCH) & (column != 0)
    turned = pltpu.roll(pairs, PATCH, 1)
    even = jnp.where(left, pairs, jnp.where(right, turned, 0.0))
    odd = jnp.where(left, turned, jnp.where(right, pairs, 0.0))
    return even, odd


def place_any(pairs, column):
    inside = (lane_index() >= column) & (lane_index() < column + PATCH)
    turned = pltpu.roll(pairs, column, 1)
    return jnp.where(inside, turned, 0.0), jnp.where(inside, pltpu.roll(turned, PATCH, 1), 0.0)


def either_kind(z, heavy, body):
    @pl.when(heavy)
    def _():
        body(place_any, range(CAP))

    @pl.when(jnp.logical_not(heavy))
    def _():
        body(place_side if z.makers == 2 else place_any, range(1))


def own_kernel(z, place, lists, tiles, table, half, total, weights, landed, staged, sems):
    first = lax.rem(place[0], z.makers) * z.block

    def fetch(j):
        return pltpu.make_async_copy(tiles.at[first + j], landed.at[j], sems.at[j])

    for j in range(z.block):
        fetch(j).start()
    kinds = table.shape[0]
    for k in range(PAIRS):
        for t in range(TILES):
            at = COLS * k + LANES * t
            for low in range(0, kinds, 8):
                count = min(8, kinds - low)
                weights[t, pl.ds(PAIRS * low + k, count, stride=PAIRS), :] = table[
                    low : low + count, at : at + LANES
                ]

    def region(j, carry):
        fetch(j).wait()

        def body(place_tile, slots):
            entries = []
            for slot in slots:
                stage(staged.at[slot], landed[j, slot])
                column, kind = (lists[field, slot, first + j] for field in (1, 2))
                entries.append((slot, column, weight_of(weights, kind)))
            even, odd = 0.0, 0.0
            for _, column, weight in entries:
                a, b = place_tile(weight, column)
                even, odd = even + a, odd + b
            total[j, 0], total[j, 1] = even, odd
            for field in range(FIELDS):
                even, odd = 0.0, 0.0
                for slot, column, weight in entries:
                    a, b = place_tile(staged_field(staged.at[slot], field) * weight, column)
                    even, odd = even + a, odd + b
                half[j, field, 0], half[j, field, 1] = even, odd

        either_kind(z, lists[0, 1, first + j] >= 0, body)
        return carry

    lax.fori_loop(0, z.block, region, 0)


def own_share(z, place, lists, tiles, table):
    smem = pl.BlockSpec(memory_space=pltpu.SMEM)
    vmem = pl.BlockSpec(memory_space=pltpu.VMEM)
    kinds = round_up(table.shape[0], 8)
    return pl.pallas_call(
        functools.partial(own_kernel, z),
        out_shape=[
            jax.ShapeDtypeStruct((z.block, FIELDS, 2, PAIRS, COLS), jnp.float32),
            jax.ShapeDtypeStruct((z.block, 2, PAIRS, COLS), jnp.float32),
            jax.ShapeDtypeStruct((TILES, kinds * PAIRS, LANES), jnp.float32),
        ],
        in_specs=[smem, smem, pl.BlockSpec(memory_space=pltpu.HBM), vmem],
        out_specs=[vmem] * 3,
        scratch_shapes=[
            pltpu.VMEM((z.block, CAP, LINES, LANES), jnp.bfloat16),
            pltpu.VMEM((CAP, LINES, LANES), jnp.float32),
            pltpu.SemaphoreType.DMA((z.block,)),
        ],
        compiler_params=pltpu.CompilerParams(vmem_limit_bytes=MOST_VMEM),
        cost_estimate=pl.CostEstimate(flops=5_000_000, bytes_accessed=8_000_000, transcendentals=0),
        name="own_share",
    )(place, lists, tiles, table)


def join_kernel(z, *refs):
    place, lists, refs = refs[0], refs[1 : 1 + z.makers], refs[1 + z.makers :]
    received, refs = refs[: z.makers - 1], refs[z.makers - 1 :]
    half, total, weights, smoothing, out, staged, lines, turned, strength, blocks, sems = refs
    first = lax.rem(place[0], z.makers) * z.block

    turned_strength = jnp.transpose(smoothing[...] - MID)
    for dest in range(z.regions):
        for g in range(z.span // 8):
            top = z.width * dest + 8 * g
            count, at = min(8, COLS - top), ROWS * (g % QUAD)
            strength[dest, g // QUAD, 0:count, at : at + ROWS] = turned_strength[top : top + count]

    def send(quad):
        return pltpu.make_async_copy(blocks.at[:, quad], out.at[:, quad], sems.at[quad])

    for quad in range(z.quads):

        def region(i, carry):
            j = quad * QUAD + i

            def body(place_tile, slots):
                entries = []
                for maker in range(1, z.makers):
                    for slot in slots:
                        index = (maker - 1) * CAP + slot
                        stage(staged.at[index], received[maker - 1][first + j, slot])
                        column, kind = (lists[maker][field, slot, first + j] for field in (1, 2))
                        entries.append((index, column, weight_of(weights, kind)))
                even, odd = total[j, 0], total[j, 1]
                for _, column, weight in entries:
                    a, b = place_tile(weight, column)
                    even, odd = even + a, odd + b
                even_inverse, odd_inverse = 1.0 / even, 1.0 / odd
                for field in range(FIELDS):
                    even, odd = half[j, field, 0], half[j, field, 1]
                    for index, column, weight in entries:
                        a, b = place_tile(staged_field(staged.at[index], field) * weight, column)
                        even, odd = even + a, odd + b
                    even, odd = even * even_inverse, odd * odd_inverse
                    for t in range(TILES):
                        here = slice(LANES * t, LANES * (t + 1))
                        lines[field, t, pl.ds(ROWS * i, PAIRS, stride=2), :] = even[:, here]
                        lines[field, t, pl.ds(ROWS * i + 1, PAIRS, stride=2), :] = odd[:, here]

            either_kind(z, lists[0][0, 1, first + j] >= 0, body)
            return carry

        lax.fori_loop(0, QUAD, region, 0)
        for field in range(FIELDS):
            for t in range(TILES):
                turned[field, LANES * t : LANES * (t + 1), :] = jnp.transpose(lines[field, t])
        for dest in range(z.regions):
            top = z.width * dest
            for low in range(0, FIELDS, 2):
                block = [turned[field, top : top + z.span, :] for field in (low, low + 1)]
                blocks[dest, quad, low * z.span : (low + 2) * z.span, :] = jnp.concatenate(block, 0).astype(
                    jnp.bfloat16
                )
            ends = (max(top - 1, 0), min(top + z.width, COLS - 1))
            edge = [turned[field, end : end + 1, :] for field in range(FIELDS) for end in ends]
            edge.append(strength[dest, quad])
            blocks[dest, quad, z.main : z.sent, :] = jnp.concatenate(edge, 0).astype(jnp.bfloat16)
        send(quad).start()
    for quad in range(z.quads):
        send(quad).wait()


def join(z, place, lists, received, half, total, weights, smoothing):
    smem = pl.BlockSpec(memory_space=pltpu.SMEM)
    vmem = pl.BlockSpec(memory_space=pltpu.VMEM)
    shape = (z.regions, z.quads, z.sent, LANES)
    return pl.pallas_call(
        functools.partial(join_kernel, z),
        out_shape=pltpu.HBM(shape, jnp.bfloat16),
        in_specs=[smem] * (1 + z.makers) + [vmem] * (z.makers + 3),
        out_specs=pl.BlockSpec(memory_space=pltpu.HBM),
        scratch_shapes=[
            pltpu.VMEM((CAP * (z.makers - 1), LINES, LANES), jnp.float32),
            pltpu.VMEM((FIELDS, TILES, LANES, LANES), jnp.float32),
            pltpu.VMEM((FIELDS, COLS + 8, LANES), jnp.float32),
            pltpu.VMEM((z.regions, z.quads, 8, LANES), jnp.float32),
            pltpu.VMEM(shape, jnp.bfloat16),
            pltpu.SemaphoreType.DMA((z.quads,)),
        ],
        compiler_params=pltpu.CompilerParams(vmem_limit_bytes=VMEM),
        cost_estimate=pl.CostEstimate(flops=5_000_000, bytes_accessed=8_000_000, transcendentals=0),
        name="join",
    )(place, *lists, *received, half, total, weights, smoothing)


SORT_STEPS = (
    ((0, 1), (2, 3), (4, 5), (6, 7)),
    ((0, 2), (1, 3), (4, 6), (5, 7)),
    ((1, 2), (5, 6)),
    ((0, 4), (1, 5), (2, 6), (3, 7)),
    ((2, 4), (3, 5)),
    ((1, 2), (3, 4), (5, 6)),
)
STEP_FIELDS = 2


def score_kernel(z, blocks, analysis, crps, spread, strength, edges, padded):
    step = pl.program_id(0)
    rows = z.rows
    sources = [(source, quad) for source in range(z.regions) for quad in range(z.quads)]

    @pl.when(step == 0)
    def _():
        slot = lax.broadcasted_iota(jnp.int32, (8, LANES), 1) // ROWS
        for low in range(0, z.regions, QUAD):
            for quad in range(z.quads):
                tails = [
                    blocks[source, quad, z.main : z.sent, :].astype(jnp.float32)
                    for source in range(low, low + QUAD)
                ]
                for i, tail in enumerate(tails):
                    at = ((low + i) % z.makers * z.quads + quad) * LANES
                    edges[(low + i) // z.makers, :, at : at + LANES] = tail[0:8]
                for g in range(quad * QUAD, min((quad + 1) * QUAD, z.span // 8)):
                    joined = jnp.zeros((8, LANES), jnp.float32)
                    for i, tail in enumerate(tails):
                        near = pltpu.roll(tail[8:16], (i - g) % QUAD * ROWS, 1)
                        joined = jnp.where(slot == i, near, joined)
                    at = low // QUAD * LANES
                    strength[8 * g : 8 * (g + 1), at : at + LANES] = joined + MID

    top = pl.multiple_of(step * STEP_FIELDS * z.span, 16)
    for source, quad in sources:
        at = (source % z.makers * z.quads + quad) * LANES
        values = blocks[source, quad, pl.ds(top, STEP_FIELDS * z.span), :].astype(jnp.float32)
        for f in range(STEP_FIELDS):
            padded[source // z.makers, f, 8 : 8 + z.span, at : at + LANES] = values[f * z.span : (f + 1) * z.span]
    for sample in range(SAMPLES):
        for f in range(STEP_FIELDS):
            low = 2 * (step * STEP_FIELDS + f)
            padded[sample, f, 7:8, :] = edges[sample, pl.ds(low, 1), :]
            padded[sample, f, 8 + z.width : 9 + z.width, :] = edges[sample, pl.ds(low + 1, 1), :]
    for f in range(STEP_FIELDS):
        target_field = analysis[f].astype(jnp.float32)
        for low in range(0, z.width, 16):
            high = min(low + 16, z.width)
            shape = (high - low, rows)
            lane = lax.broadcasted_iota(jnp.int32, shape, 1)
            strong = strength[low:high, :]
            members = []
            for sample in range(SAMPLES):
                here = padded[sample, f, 8 + low : 8 + high, :]
                sides = padded[sample, f, 7 + low : 7 + high, :] + padded[sample, f, 9 + low : 9 + high, :]
                above = jnp.where(lane == 0, here, pltpu.roll(here, 1, 1))
                below = jnp.where(lane == rows - 1, here, pltpu.roll(here, rows - 1, 1))
                smooth = here + strong * (above + below + sides - 4.0 * here)
                members.append(smooth.astype(jnp.bfloat16))
            values = [member.astype(jnp.float32) for member in members]
            target = target_field[low:high]
            error = sum(jnp.abs(value - target) for value in values) * (1.0 / SAMPLES)
            average = sum(values) * (1.0 / SAMPLES)
            variance = sum((value - average) ** 2 for value in values) * (1.0 / (SAMPLES - 1.0))
            ranked = list(members)
            for pairs in SORT_STEPS:
                for a, b in pairs:
                    ranked[a], ranked[b] = jnp.minimum(ranked[a], ranked[b]), jnp.maximum(ranked[a], ranked[b])
            ranked = [member.astype(jnp.float32) for member in ranked]
            pairs = sum(
                (2 * k - SAMPLES + 1.0) * (ranked[k] - ranked[SAMPLES - 1 - k])
                for k in range(SAMPLES // 2, SAMPLES)
            )
            crps[f, low:high, :] = (error - pairs * (1.0 / (SAMPLES * SAMPLES))).astype(jnp.bfloat16)
            spread[0, f, low:high, :] = variance.astype(jnp.bfloat16)
            spread[1, f, low:high, :] = ((average - target) ** 2).astype(jnp.bfloat16)


def score(z, blocks, analysis):
    width, rows = z.width, z.rows
    return pl.pallas_call(
        functools.partial(score_kernel, z),
        out_shape=[
            jax.ShapeDtypeStruct((FIELDS, width, rows), jnp.bfloat16),
            jax.ShapeDtypeStruct((2, FIELDS, width, rows), jnp.bfloat16),
        ],
        grid=(FIELDS // STEP_FIELDS,),
        in_specs=[
            pl.BlockSpec(blocks.shape, lambda i: (0, 0, 0, 0)),
            pl.BlockSpec((STEP_FIELDS, width, rows), lambda i: (i, 0, 0)),
        ],
        out_specs=[
            pl.BlockSpec((STEP_FIELDS, width, rows), lambda i: (i, 0, 0)),
            pl.BlockSpec((2, STEP_FIELDS, width, rows), lambda i: (0, i, 0, 0)),
        ],
        scratch_shapes=[
            pltpu.VMEM((z.span, rows), jnp.float32),
            pltpu.VMEM((SAMPLES, 8, rows), jnp.float32),
            pltpu.VMEM((SAMPLES, STEP_FIELDS, z.span + 16, rows), jnp.float32),
        ],
        compiler_params=pltpu.CompilerParams(vmem_limit_bytes=VMEM),
        name="score",
    )(blocks, analysis)


def shards(patch_tiles, slot_lists, blend_table, smoothing, analysis):
    z = Sizes(lax.axis_size("region"))
    place = lax.axis_index("region").reshape(1)
    turns = [
        [(i, i - i % z.makers + (i + k) % z.makers) for i in range(z.regions)] for k in range(1, z.makers)
    ]
    tiles = patch_tiles.reshape(z.regions, CAP, FIELDS, PAIRS * TILES, LANES)
    tiles = jnp.swapaxes(tiles, 2, 3).reshape(z.regions, CAP, LINES, LANES)
    lists = jnp.transpose(slot_lists, (2, 1, 0))
    received = [lax.ppermute(tiles, "region", turn) for turn in turns]
    lists = [lists] + [lax.ppermute(lists, "region", turn) for turn in turns]
    shares = own_share(z, place, lists[0], tiles, blend_table)
    blocks = join(z, place, lists, received, *shares, smoothing)
    moved = lax.all_to_all(blocks, "region", split_axis=0, concat_axis=0, tiled=True)
    outs = score(z, moved, jnp.swapaxes(analysis, 1, 2))
    return tuple(jnp.swapaxes(item, -1, -2) for item in outs)


def solution(mesh):
    return jax.shard_map(
        shards,
        mesh=mesh,
        in_specs=(
            P(("groups", "region"), None, None, None),
            P(("groups", "region"), None, None),
            P(),
            P("region", None),
            P(None, "groups", "region"),
        ),
        out_specs=(P(None, "groups", "region"), P(None, None, "groups", "region")),
        check_vma=False,
    )
```

```python
import functools

import jax
import jax.numpy as jnp
from jax import lax
from jax.experimental import pallas as pl
from jax.experimental.pallas import tpu as pltpu
from jax.sharding import PartitionSpec as P

SAMPLES = 8
FIELDS = 4
PATCH = 448
CAP = 2
ROWS = 32
COLS = 896
PAIRS = ROWS // 2
LINES = FIELDS * ROWS * PATCH // 128
LANES = 128
TILES = COLS // LANES
QUAD = LANES // ROWS
MID = 0.11
VMEM = 40 * 1024 * 1024
MOST_VMEM = 48 * 1024 * 1024


def round_up(value, step):
    return -(-value // step) * step


class Sizes:
    def __init__(self, regions):
        self.regions = regions
        self.makers = regions // SAMPLES
        self.block = regions // self.makers
        self.quads = self.block // QUAD
        self.width = COLS // regions
        self.span = round_up(self.width, 8)
        self.rows = regions * ROWS
        self.main = round_up(FIELDS * self.span, 16)
        self.sent = self.main + 16


def stage(staged, tile):
    staged[...] = tile.astype(jnp.float32)


def staged_field(staged, field):
    return jnp.concatenate(
        [staged[pl.ds(FIELDS * t + field, PAIRS, stride=FIELDS * TILES), :] for t in range(TILES)], 1
    )


def weight_of(weights, kind):
    at = pl.multiple_of(kind * PAIRS, PAIRS)
    return jnp.concatenate([weights[t, pl.ds(at, PAIRS), :] for t in range(TILES)], 1)


def lane_index():
    return lax.broadcasted_iota(jnp.int32, (PAIRS, COLS), 1)


def place_side(pairs, column):
    left = (lane_index() < PATCH) & (column == 0)
    right = (lane_index() >= PATCH) & (column != 0)
    turned = pltpu.roll(pairs, PATCH, 1)
    even = jnp.where(left, pairs, jnp.where(right, turned, 0.0))
    odd = jnp.where(left, turned, jnp.where(right, pairs, 0.0))
    return even, odd


def place_any(pairs, column):
    inside = (lane_index() >= column) & (lane_index() < column + PATCH)
    turned = pltpu.roll(pairs, column, 1)
    return jnp.where(inside, turned, 0.0), jnp.where(inside, pltpu.roll(turned, PATCH, 1), 0.0)


def either_kind(z, heavy, body):
    @pl.when(heavy)
    def _():
        body(place_any, range(CAP))

    @pl.when(jnp.logical_not(heavy))
    def _():
        body(place_side if z.makers == 2 else place_any, range(1))


def own_kernel(z, place, lists, tiles, table_hbm, smoothing, *refs):
    half, (total, weights, strength, landed, staged, table, sems) = refs[:FIELDS], refs[FIELDS:]
    first = lax.rem(place[0], z.makers) * z.block

    def fetch(j):
        return pltpu.make_async_copy(tiles.at[first + j], landed.at[j], sems.at[j])

    fetch_table = pltpu.make_async_copy(table_hbm, table, sems.at[z.block])
    fetch_table.start()
    for j in range(z.block):
        fetch(j).start()
    turned_strength = jnp.transpose(smoothing[...] - MID)
    for dest in range(z.regions):
        for g in range(z.span // 8):
            top = z.width * dest + 8 * g
            count, at = min(8, COLS - top), ROWS * (g % QUAD)
            strength[dest, g // QUAD, 0:count, at : at + ROWS] = turned_strength[top : top + count]
    fetch_table.wait()
    kinds = table.shape[0]
    for k in range(PAIRS):
        for t in range(TILES):
            at = COLS * k + LANES * t
            for low in range(0, kinds, 8):
                count = min(8, kinds - low)
                weights[t, pl.ds(PAIRS * low + k, count, stride=PAIRS), :] = table[
                    low : low + count, at : at + LANES
                ]

    def region(j, carry):
        fetch(j).wait()

        def body(place_tile, slots):
            entries = []
            for slot in slots:
                stage(staged.at[slot], landed[j, slot])
                column, kind = (lists[field, slot, first + j] for field in (1, 2))
                entries.append((slot, column, weight_of(weights, kind)))
            even, odd = 0.0, 0.0
            for _, column, weight in entries:
                a, b = place_tile(weight, column)
                even, odd = even + a, odd + b
            total[j, 0], total[j, 1] = even, odd
            for field in range(FIELDS):
                even, odd = 0.0, 0.0
                for slot, column, weight in entries:
                    a, b = place_tile(staged_field(staged.at[slot], field) * weight, column)
                    even, odd = even + a, odd + b
                half[field][j, 0], half[field][j, 1] = even, odd

        either_kind(z, lists[0, 1, first + j] >= 0, body)
        return carry

    lax.fori_loop(0, z.block, region, 0)


def own_share(z, place, lists, tiles, table, smoothing):
    smem = pl.BlockSpec(memory_space=pltpu.SMEM)
    vmem = pl.BlockSpec(memory_space=pltpu.VMEM)
    hbm = pl.BlockSpec(memory_space=pltpu.HBM)
    kinds = round_up(table.shape[0], 8)
    return pl.pallas_call(
        functools.partial(own_kernel, z),
        out_shape=[
            *[jax.ShapeDtypeStruct((z.block, 2, PAIRS, COLS), jnp.float32)] * (FIELDS + 1),
            jax.ShapeDtypeStruct((TILES, kinds * PAIRS, LANES), jnp.float32),
            jax.ShapeDtypeStruct((z.regions, z.quads, 8, LANES), jnp.float32),
        ],
        in_specs=[smem, smem, hbm, hbm, vmem],
        out_specs=[vmem] * (FIELDS + 3),
        scratch_shapes=[
            pltpu.VMEM((z.block, CAP, LINES, LANES), jnp.bfloat16),
            pltpu.VMEM((CAP, LINES, LANES), jnp.float32),
            pltpu.VMEM(table.shape, jnp.float32),
            pltpu.SemaphoreType.DMA((z.block + 1,)),
        ],
        compiler_params=pltpu.CompilerParams(vmem_limit_bytes=MOST_VMEM),
        cost_estimate=pl.CostEstimate(flops=5_000_000, bytes_accessed=8_000_000, transcendentals=0),
        name="own_share",
    )(place, lists, tiles, table, smoothing)


def join_kernel(z, *refs):
    place, lists, refs = refs[0], refs[1 : 1 + z.makers], refs[1 + z.makers :]
    received, refs = refs[: z.makers - 1], refs[z.makers - 1 :]
    half, (total, weights, strength, out, staged, lines, turned, blocks, sems) = refs[:FIELDS], refs[FIELDS:]
    first = lax.rem(place[0], z.makers) * z.block

    def send(quad):
        return pltpu.make_async_copy(blocks.at[:, quad], out.at[:, quad], sems.at[quad])

    for quad in range(z.quads):

        def region(i, carry):
            j = quad * QUAD + i

            def body(place_tile, slots):
                entries = []
                for maker in range(1, z.makers):
                    for slot in slots:
                        index = (maker - 1) * CAP + slot
                        stage(staged.at[index], received[maker - 1][first + j, slot])
                        column, kind = (lists[maker][field, slot, first + j] for field in (1, 2))
                        entries.append((index, column, weight_of(weights, kind)))
                even, odd = total[j, 0], total[j, 1]
                for _, column, weight in entries:
                    a, b = place_tile(weight, column)
                    even, odd = even + a, odd + b
                even_inverse, odd_inverse = 1.0 / even, 1.0 / odd
                for field in range(FIELDS):
                    even, odd = half[field][j, 0], half[field][j, 1]
                    for index, column, weight in entries:
                        a, b = place_tile(staged_field(staged.at[index], field) * weight, column)
                        even, odd = even + a, odd + b
                    even, odd = even * even_inverse, odd * odd_inverse
                    for t in range(TILES):
                        here = slice(LANES * t, LANES * (t + 1))
                        lines[field, t, pl.ds(ROWS * i, PAIRS, stride=2), :] = even[:, here]
                        lines[field, t, pl.ds(ROWS * i + 1, PAIRS, stride=2), :] = odd[:, here]

            either_kind(z, lists[0][0, 1, first + j] >= 0, body)
            return carry

        lax.fori_loop(0, QUAD, region, 0)
        for field in range(FIELDS):
            for t in range(TILES):
                turned[field, LANES * t : LANES * (t + 1), :] = jnp.transpose(lines[field, t])
        for dest in range(z.regions):
            top = z.width * dest
            for low in range(0, FIELDS, 2):
                block = [turned[field, top : top + z.span, :] for field in (low, low + 1)]
                blocks[dest, quad, low * z.span : (low + 2) * z.span, :] = jnp.concatenate(block, 0).astype(
                    jnp.bfloat16
                )
            ends = (max(top - 1, 0), min(top + z.width, COLS - 1))
            edge = [turned[field, end : end + 1, :] for field in range(FIELDS) for end in ends]
            edge.append(strength[dest, quad])
            blocks[dest, quad, z.main : z.sent, :] = jnp.concatenate(edge, 0).astype(jnp.bfloat16)
        send(quad).start()
    for quad in range(z.quads):
        send(quad).wait()


def join(z, place, lists, received, shares):
    smem = pl.BlockSpec(memory_space=pltpu.SMEM)
    vmem = pl.BlockSpec(memory_space=pltpu.VMEM)
    shape = (z.regions, z.quads, z.sent, LANES)
    return pl.pallas_call(
        functools.partial(join_kernel, z),
        out_shape=pltpu.HBM(shape, jnp.bfloat16),
        in_specs=[smem] * (1 + z.makers) + [vmem] * (z.makers - 1 + len(shares)),
        out_specs=pl.BlockSpec(memory_space=pltpu.HBM),
        scratch_shapes=[
            pltpu.VMEM((CAP * (z.makers - 1), LINES, LANES), jnp.float32),
            pltpu.VMEM((FIELDS, TILES, LANES, LANES), jnp.float32),
            pltpu.VMEM((FIELDS, COLS + 8, LANES), jnp.float32),
            pltpu.VMEM(shape, jnp.bfloat16),
            pltpu.SemaphoreType.DMA((z.quads,)),
        ],
        compiler_params=pltpu.CompilerParams(vmem_limit_bytes=VMEM),
        cost_estimate=pl.CostEstimate(flops=5_000_000, bytes_accessed=8_000_000, transcendentals=0),
        name="join",
    )(place, *lists, *received, *shares)


SORT_STEPS = (
    ((0, 1), (2, 3), (4, 5), (6, 7)),
    ((0, 2), (1, 3), (4, 6), (5, 7)),
    ((1, 2), (5, 6)),
    ((0, 4), (1, 5), (2, 6), (3, 7)),
    ((2, 4), (3, 5)),
    ((1, 2), (3, 4), (5, 6)),
)
STEP_FIELDS = 2


def score_kernel(z, blocks, analysis, crps, spread, strength, edges, padded):
    step = pl.program_id(0)
    rows = z.rows
    sources = [(source, quad) for source in range(z.regions) for quad in range(z.quads)]

    @pl.when(step == 0)
    def _():
        slot = lax.broadcasted_iota(jnp.int32, (8, LANES), 1) // ROWS
        for low in range(0, z.regions, QUAD):
            for quad in range(z.quads):
                tails = [
                    blocks[source, quad, z.main : z.sent, :].astype(jnp.float32)
                    for source in range(low, low + QUAD)
                ]
                for i, tail in enumerate(tails):
                    at = ((low + i) % z.makers * z.quads + quad) * LANES
                    edges[(low + i) // z.makers, :, at : at + LANES] = tail[0:8]
                for g in range(quad * QUAD, min((quad + 1) * QUAD, z.span // 8)):
                    joined = jnp.zeros((8, LANES), jnp.float32)
                    for i, tail in enumerate(tails):
                        near = pltpu.roll(tail[8:16], (i - g) % QUAD * ROWS, 1)
                        joined = jnp.where(slot == i, near, joined)
                    at = low // QUAD * LANES
                    strength[8 * g : 8 * (g + 1), at : at + LANES] = joined + MID

    top = pl.multiple_of(step * STEP_FIELDS * z.span, 16)
    for source, quad in sources:
        at = (source % z.makers * z.quads + quad) * LANES
        values = blocks[source, quad, pl.ds(top, STEP_FIELDS * z.span), :].astype(jnp.float32)
        for f in range(STEP_FIELDS):
            padded[source // z.makers, f, 8 : 8 + z.span, at : at + LANES] = values[f * z.span : (f + 1) * z.span]
    for sample in range(SAMPLES):
        for f in range(STEP_FIELDS):
            low = 2 * (step * STEP_FIELDS + f)
            padded[sample, f, 7:8, :] = edges[sample, pl.ds(low, 1), :]
            padded[sample, f, 8 + z.width : 9 + z.width, :] = edges[sample, pl.ds(low + 1, 1), :]
    for f in range(STEP_FIELDS):
        target_field = analysis[f].astype(jnp.float32)
        for low in range(0, z.width, 16):
            high = min(low + 16, z.width)
            shape = (high - low, rows)
            lane = lax.broadcasted_iota(jnp.int32, shape, 1)
            strong = strength[low:high, :]
            members = []
            for sample in range(SAMPLES):
                here = padded[sample, f, 8 + low : 8 + high, :]
                sides = padded[sample, f, 7 + low : 7 + high, :] + padded[sample, f, 9 + low : 9 + high, :]
                above = jnp.where(lane == 0, here, pltpu.roll(here, 1, 1))
                below = jnp.where(lane == rows - 1, here, pltpu.roll(here, rows - 1, 1))
                smooth = here + strong * (above + below + sides - 4.0 * here)
                members.append(smooth.astype(jnp.bfloat16))
            values = [member.astype(jnp.float32) for member in members]
            target = target_field[low:high]
            error = sum(jnp.abs(value - target) for value in values) * (1.0 / SAMPLES)
            average = sum(values) * (1.0 / SAMPLES)
            variance = sum((value - average) ** 2 for value in values) * (1.0 / (SAMPLES - 1.0))
            ranked = list(members)
            for pairs in SORT_STEPS:
                for a, b in pairs:
                    ranked[a], ranked[b] = jnp.minimum(ranked[a], ranked[b]), jnp.maximum(ranked[a], ranked[b])
            ranked = [member.astype(jnp.float32) for member in ranked]
            pairs = sum(
                (2 * k - SAMPLES + 1.0) * (ranked[k] - ranked[SAMPLES - 1 - k])
                for k in range(SAMPLES // 2, SAMPLES)
            )
            crps[f, low:high, :] = (error - pairs * (1.0 / (SAMPLES * SAMPLES))).astype(jnp.bfloat16)
            spread[0, f, low:high, :] = variance.astype(jnp.bfloat16)
            spread[1, f, low:high, :] = ((average - target) ** 2).astype(jnp.bfloat16)


def score(z, blocks, analysis):
    width, rows = z.width, z.rows
    return pl.pallas_call(
        functools.partial(score_kernel, z),
        out_shape=[
            jax.ShapeDtypeStruct((FIELDS, width, rows), jnp.bfloat16),
            jax.ShapeDtypeStruct((2, FIELDS, width, rows), jnp.bfloat16),
        ],
        grid=(FIELDS // STEP_FIELDS,),
        in_specs=[
            pl.BlockSpec(blocks.shape, lambda i: (0, 0, 0, 0)),
            pl.BlockSpec((STEP_FIELDS, width, rows), lambda i: (i, 0, 0)),
        ],
        out_specs=[
            pl.BlockSpec((STEP_FIELDS, width, rows), lambda i: (i, 0, 0)),
            pl.BlockSpec((2, STEP_FIELDS, width, rows), lambda i: (0, i, 0, 0)),
        ],
        scratch_shapes=[
            pltpu.VMEM((z.span, rows), jnp.float32),
            pltpu.VMEM((SAMPLES, 8, rows), jnp.float32),
            pltpu.VMEM((SAMPLES, STEP_FIELDS, z.span + 16, rows), jnp.float32),
        ],
        compiler_params=pltpu.CompilerParams(vmem_limit_bytes=VMEM),
        name="score",
    )(blocks, analysis)


def shards(patch_tiles, slot_lists, blend_table, smoothing, analysis):
    z = Sizes(lax.axis_size("region"))
    place = lax.axis_index("region").reshape(1)
    turns = [
        [(i, i - i % z.makers + (i + k) % z.makers) for i in range(z.regions)] for k in range(1, z.makers)
    ]
    tiles = patch_tiles.reshape(z.regions, CAP, FIELDS, PAIRS * TILES, LANES)
    tiles = jnp.swapaxes(tiles, 2, 3).reshape(z.regions, CAP, LINES, LANES)
    lists = jnp.transpose(slot_lists, (2, 1, 0))
    received = [lax.ppermute(tiles, "region", turn) for turn in turns]
    lists = [lists] + [lax.ppermute(lists, "region", turn) for turn in turns]
    shares = own_share(z, place, lists[0], tiles, blend_table, smoothing)
    blocks = join(z, place, lists, received, shares)
    moved = lax.all_to_all(blocks, "region", split_axis=0, concat_axis=0, tiled=True)
    outs = score(z, moved, jnp.swapaxes(analysis, 1, 2))
    return tuple(jnp.swapaxes(item, -1, -2) for item in outs)


def solution(mesh):
    return jax.shard_map(
        shards,
        mesh=mesh,
        in_specs=(
            P(("groups", "region"), None, None, None),
            P(("groups", "region"), None, None),
            P(),
            P("region", None),
            P(None, "groups", "region"),
        ),
        out_specs=(P(None, "groups", "region"), P(None, None, "groups", "region")),
        check_vma=False,
    )
```

```python
import functools

import jax
import jax.numpy as jnp
from jax import lax
from jax.experimental import pallas as pl
from jax.experimental.pallas import tpu as pltpu
from jax.sharding import PartitionSpec as P

SAMPLES = 8
FIELDS = 4
PATCH = 448
CAP = 2
ROWS = 32
COLS = 896
PAIRS = ROWS // 2
LINES = FIELDS * ROWS * PATCH // 128
LANES = 128
TILES = COLS // LANES
QUAD = LANES // ROWS
MID = 0.11
VMEM = 40 * 1024 * 1024
MOST_VMEM = 48 * 1024 * 1024


def round_up(value, step):
    return -(-value // step) * step


def swap_order(regions):
    far, near = list(range(regions // 2, regions)), list(range(1, regions // 2))
    near = near[regions // 4 - 1 :] + near[: regions // 4 - 1]
    return [0] + [item for pair in zip(far, near + [None]) for item in pair if item is not None]


class Sizes:
    def __init__(self, regions):
        self.regions = regions
        self.makers = regions // SAMPLES
        self.block = regions // self.makers
        self.quads = self.block // QUAD
        self.width = COLS // regions
        self.span = round_up(self.width, 8)
        self.rows = regions * ROWS
        self.main = round_up(FIELDS * self.span, 16)
        self.offsets = swap_order(regions)
        self.sent = self.main + 16


def stage(staged, tile):
    staged[...] = tile.astype(jnp.float32)


def staged_field(staged, field):
    return jnp.concatenate(
        [staged[pl.ds(FIELDS * t + field, PAIRS, stride=FIELDS * TILES), :] for t in range(TILES)], 1
    )


def weight_of(weights, kind):
    at = pl.multiple_of(kind * PAIRS, PAIRS)
    return jnp.concatenate([weights[t, pl.ds(at, PAIRS), :] for t in range(TILES)], 1)


def lane_index():
    return lax.broadcasted_iota(jnp.int32, (PAIRS, COLS), 1)


def place_side(pairs, column):
    left = (lane_index() < PATCH) & (column == 0)
    right = (lane_index() >= PATCH) & (column != 0)
    turned = pltpu.roll(pairs, PATCH, 1)
    even = jnp.where(left, pairs, jnp.where(right, turned, 0.0))
    odd = jnp.where(left, turned, jnp.where(right, pairs, 0.0))
    return even, odd


def place_any(pairs, column):
    inside = (lane_index() >= column) & (lane_index() < column + PATCH)
    turned = pltpu.roll(pairs, column, 1)
    return jnp.where(inside, turned, 0.0), jnp.where(inside, pltpu.roll(turned, PATCH, 1), 0.0)


def either_kind(z, heavy, body):
    @pl.when(heavy)
    def _():
        body(place_any, range(CAP))

    @pl.when(jnp.logical_not(heavy))
    def _():
        body(place_side if z.makers == 2 else place_any, range(1))


def own_kernel(z, place, lists, tiles, table_hbm, smoothing, *refs):
    half, (total, weights, strength, landed, staged, table, sems) = refs[:FIELDS], refs[FIELDS:]
    first = lax.rem(place[0], z.makers) * z.block

    def fetch(j):
        return pltpu.make_async_copy(tiles.at[first + j], landed.at[j], sems.at[j])

    fetch_table = pltpu.make_async_copy(table_hbm, table, sems.at[z.block])
    fetch_table.start()
    for j in range(z.block):
        fetch(j).start()
    turned_strength = jnp.transpose(smoothing[...] - MID)
    for dest in range(z.regions):
        for g in range(z.span // 8):
            top = z.width * dest + 8 * g
            count, at = min(8, COLS - top), ROWS * (g % QUAD)
            strength[dest, g // QUAD, 0:count, at : at + ROWS] = turned_strength[top : top + count]
    fetch_table.wait()
    kinds = table.shape[0]
    for k in range(PAIRS):
        for t in range(TILES):
            at = COLS * k + LANES * t
            for low in range(0, kinds, 8):
                count = min(8, kinds - low)
                weights[t, pl.ds(PAIRS * low + k, count, stride=PAIRS), :] = table[
                    low : low + count, at : at + LANES
                ]

    def region(j, carry):
        fetch(j).wait()

        def body(place_tile, slots):
            entries = []
            for slot in slots:
                stage(staged.at[slot], landed[j, slot])
                column, kind = (lists[field, slot, first + j] for field in (1, 2))
                entries.append((slot, column, weight_of(weights, kind)))
            even, odd = 0.0, 0.0
            for _, column, weight in entries:
                a, b = place_tile(weight, column)
                even, odd = even + a, odd + b
            total[j, 0], total[j, 1] = even, odd
            for field in range(FIELDS):
                even, odd = 0.0, 0.0
                for slot, column, weight in entries:
                    a, b = place_tile(staged_field(staged.at[slot], field) * weight, column)
                    even, odd = even + a, odd + b
                half[field][j, 0], half[field][j, 1] = even, odd

        either_kind(z, lists[0, 1, first + j] >= 0, body)
        return carry

    lax.fori_loop(0, z.block, region, 0)


def own_share(z, place, lists, tiles, table, smoothing):
    smem = pl.BlockSpec(memory_space=pltpu.SMEM)
    vmem = pl.BlockSpec(memory_space=pltpu.VMEM)
    hbm = pl.BlockSpec(memory_space=pltpu.HBM)
    kinds = round_up(table.shape[0], 8)
    return pl.pallas_call(
        functools.partial(own_kernel, z),
        out_shape=[
            *[jax.ShapeDtypeStruct((z.block, 2, PAIRS, COLS), jnp.float32)] * (FIELDS + 1),
            jax.ShapeDtypeStruct((TILES, kinds * PAIRS, LANES), jnp.float32),
            jax.ShapeDtypeStruct((z.regions, z.quads, 8, LANES), jnp.float32),
        ],
        in_specs=[smem, smem, hbm, hbm, vmem],
        out_specs=[vmem] * (FIELDS + 3),
        scratch_shapes=[
            pltpu.VMEM((z.block, CAP, LINES, LANES), jnp.bfloat16),
            pltpu.VMEM((CAP, LINES, LANES), jnp.float32),
            pltpu.VMEM(table.shape, jnp.float32),
            pltpu.SemaphoreType.DMA((z.block + 1,)),
        ],
        compiler_params=pltpu.CompilerParams(vmem_limit_bytes=MOST_VMEM),
        cost_estimate=pl.CostEstimate(flops=5_000_000, bytes_accessed=8_000_000, transcendentals=0),
        name="own_share",
    )(place, lists, tiles, table, smoothing)


def join_kernel(z, *refs):
    place, lists, refs = refs[0], refs[1 : 1 + z.makers], refs[1 + z.makers :]
    received, refs = refs[: z.makers - 1], refs[z.makers - 1 :]
    half, (total, weights, strength), outs = refs[:FIELDS], refs[FIELDS : FIELDS + 3], refs[FIELDS + 3 : -5]
    staged, lines, turned, blocks, sems = refs[-5:]
    me = place[0]
    first = lax.rem(me, z.makers) * z.block

    def send(i, quad):
        return pltpu.make_async_copy(blocks.at[i, quad], outs[i].at[quad], sems.at[i, quad])

    for quad in range(z.quads):

        def region(i, carry):
            j = quad * QUAD + i

            def body(place_tile, slots):
                entries = []
                for maker in range(1, z.makers):
                    for slot in slots:
                        index = (maker - 1) * CAP + slot
                        stage(staged.at[index], received[maker - 1][first + j, slot])
                        column, kind = (lists[maker][field, slot, first + j] for field in (1, 2))
                        entries.append((index, column, weight_of(weights, kind)))
                even, odd = total[j, 0], total[j, 1]
                for _, column, weight in entries:
                    a, b = place_tile(weight, column)
                    even, odd = even + a, odd + b
                even_inverse, odd_inverse = 1.0 / even, 1.0 / odd
                for field in range(FIELDS):
                    even, odd = half[field][j, 0], half[field][j, 1]
                    for index, column, weight in entries:
                        a, b = place_tile(staged_field(staged.at[index], field) * weight, column)
                        even, odd = even + a, odd + b
                    even, odd = even * even_inverse, odd * odd_inverse
                    for t in range(TILES):
                        here = slice(LANES * t, LANES * (t + 1))
                        lines[field, t, pl.ds(ROWS * i, PAIRS, stride=2), :] = even[:, here]
                        lines[field, t, pl.ds(ROWS * i + 1, PAIRS, stride=2), :] = odd[:, here]

            either_kind(z, lists[0][0, 1, first + j] >= 0, body)
            return carry

        lax.fori_loop(0, QUAD, region, 0)
        for field in range(FIELDS):
            for t in range(TILES):
                turned[field, LANES * t : LANES * (t + 1), :] = jnp.transpose(lines[field, t])
        for i, offset in enumerate(z.offsets):
            dest = me ^ offset
            top = dest * z.width
            if z.width % 8 == 0:
                top = pl.multiple_of(top, 8)
            for low in range(0, FIELDS, 2):
                block = [turned[field, pl.ds(top, z.span), :] for field in (low, low + 1)]
                blocks[i, quad, low * z.span : (low + 2) * z.span, :] = jnp.concatenate(block, 0).astype(
                    jnp.bfloat16
                )
            ends = (jnp.maximum(top - 1, 0), jnp.minimum(top + z.width, COLS - 1))
            edge = [turned[field, pl.ds(end, 1), :] for field in range(FIELDS) for end in ends]
            edge.append(strength[dest, quad])
            blocks[i, quad, z.main : z.sent, :] = jnp.concatenate(edge, 0).astype(jnp.bfloat16)
            send(i, quad).start()
    for quad in range(z.quads):
        for i in range(z.regions):
            send(i, quad).wait()


def join(z, place, lists, received, shares):
    smem = pl.BlockSpec(memory_space=pltpu.SMEM)
    vmem = pl.BlockSpec(memory_space=pltpu.VMEM)
    shape = (z.quads, z.sent, LANES)
    return pl.pallas_call(
        functools.partial(join_kernel, z),
        out_shape=[pltpu.HBM(shape, jnp.bfloat16)] * z.regions,
        in_specs=[smem] * (1 + z.makers) + [vmem] * (z.makers - 1 + len(shares)),
        out_specs=[pl.BlockSpec(memory_space=pltpu.HBM)] * z.regions,
        scratch_shapes=[
            pltpu.VMEM((CAP * (z.makers - 1), LINES, LANES), jnp.float32),
            pltpu.VMEM((FIELDS, TILES, LANES, LANES), jnp.float32),
            pltpu.VMEM((FIELDS, COLS + 8, LANES), jnp.float32),
            pltpu.VMEM((z.regions, *shape), jnp.bfloat16),
            pltpu.SemaphoreType.DMA((z.regions, z.quads)),
        ],
        compiler_params=pltpu.CompilerParams(vmem_limit_bytes=VMEM),
        cost_estimate=pl.CostEstimate(flops=5_000_000, bytes_accessed=8_000_000, transcendentals=0),
        name="join",
    )(place, *lists, *received, *shares)


SORT_STEPS = (
    ((0, 1), (2, 3), (4, 5), (6, 7)),
    ((0, 2), (1, 3), (4, 6), (5, 7)),
    ((1, 2), (5, 6)),
    ((0, 4), (1, 5), (2, 6), (3, 7)),
    ((2, 4), (3, 5)),
    ((1, 2), (3, 4), (5, 6)),
)
STEP_FIELDS = 2


def score_kernel(z, place, *refs):
    blocks = dict(zip(z.offsets, refs))
    analysis, crps, spread, strength, edges, padded = refs[z.regions :]
    me = place[0]
    step = pl.program_id(0)
    rows = z.rows

    def lanes_of(offset, quad):
        at = (lax.rem(me ^ offset, z.makers) * z.quads + quad) * LANES
        return pl.ds(pl.multiple_of(at, LANES), LANES)

    @pl.when(step == 0)
    def _():
        slot = lax.broadcasted_iota(jnp.int32, (8, LANES), 1) // ROWS
        for low in range(0, z.regions, QUAD):
            offsets = range(low, low + QUAD)
            slots = [lax.rem(me ^ offset, QUAD) for offset in offsets]
            at = pl.multiple_of(lax.div(me ^ low, QUAD) * LANES, LANES)
            for quad in range(z.quads):
                tails = [blocks[offset][quad, z.main : z.sent, :].astype(jnp.float32) for offset in offsets]
                for offset, tail in zip(offsets, tails):
                    edges[offset // z.makers, :, lanes_of(offset, quad)] = tail[0:8]
                for g in range(quad * QUAD, min((quad + 1) * QUAD, z.span // 8)):
                    joined = jnp.zeros((8, LANES), jnp.float32)
                    for i, tail in zip(slots, tails):
                        near = pltpu.roll(tail[8:16], lax.rem(i + QUAD - g % QUAD, QUAD) * ROWS, 1)
                        joined = jnp.where(slot == i, near, joined)
                    strength[8 * g : 8 * (g + 1), pl.ds(at, LANES)] = joined + MID

    top = pl.multiple_of(step * STEP_FIELDS * z.span, 16)
    for offset in range(z.regions):
        for quad in range(z.quads):
            values = blocks[offset][quad, pl.ds(top, STEP_FIELDS * z.span), :].astype(jnp.float32)
            for f in range(STEP_FIELDS):
                padded[offset // z.makers, f, 8 : 8 + z.span, lanes_of(offset, quad)] = values[
                    f * z.span : (f + 1) * z.span
                ]
    for sample in range(SAMPLES):
        for f in range(STEP_FIELDS):
            low = 2 * (step * STEP_FIELDS + f)
            padded[sample, f, 7:8, :] = edges[sample, pl.ds(low, 1), :]
            padded[sample, f, 8 + z.width : 9 + z.width, :] = edges[sample, pl.ds(low + 1, 1), :]
    for f in range(STEP_FIELDS):
        target_field = analysis[f].astype(jnp.float32)
        for low in range(0, z.width, 16):
            high = min(low + 16, z.width)
            shape = (high - low, rows)
            lane = lax.broadcasted_iota(jnp.int32, shape, 1)
            strong = strength[low:high, :]
            members = []
            for sample in range(SAMPLES):
                here = padded[sample, f, 8 + low : 8 + high, :]
                sides = padded[sample, f, 7 + low : 7 + high, :] + padded[sample, f, 9 + low : 9 + high, :]
                above = jnp.where(lane == 0, here, pltpu.roll(here, 1, 1))
                below = jnp.where(lane == rows - 1, here, pltpu.roll(here, rows - 1, 1))
                smooth = here + strong * (above + below + sides - 4.0 * here)
                members.append(smooth.astype(jnp.bfloat16))
            values = [member.astype(jnp.float32) for member in members]
            target = target_field[low:high]
            error = sum(jnp.abs(value - target) for value in values) * (1.0 / SAMPLES)
            average = sum(values) * (1.0 / SAMPLES)
            variance = sum((value - average) ** 2 for value in values) * (1.0 / (SAMPLES - 1.0))
            ranked = list(members)
            for pairs in SORT_STEPS:
                for a, b in pairs:
                    ranked[a], ranked[b] = jnp.minimum(ranked[a], ranked[b]), jnp.maximum(ranked[a], ranked[b])
            ranked = [member.astype(jnp.float32) for member in ranked]
            pairs = sum(
                (2 * k - SAMPLES + 1.0) * (ranked[k] - ranked[SAMPLES - 1 - k])
                for k in range(SAMPLES // 2, SAMPLES)
            )
            crps[f, low:high, :] = (error - pairs * (1.0 / (SAMPLES * SAMPLES))).astype(jnp.bfloat16)
            spread[0, f, low:high, :] = variance.astype(jnp.bfloat16)
            spread[1, f, low:high, :] = ((average - target) ** 2).astype(jnp.bfloat16)


def score(z, place, blocks, analysis):
    width, rows = z.width, z.rows
    return pl.pallas_call(
        functools.partial(score_kernel, z),
        out_shape=[
            jax.ShapeDtypeStruct((FIELDS, width, rows), jnp.bfloat16),
            jax.ShapeDtypeStruct((2, FIELDS, width, rows), jnp.bfloat16),
        ],
        grid=(FIELDS // STEP_FIELDS,),
        in_specs=[pl.BlockSpec(memory_space=pltpu.SMEM)]
        + [pl.BlockSpec(blocks[0].shape, lambda i: (0, 0, 0))] * z.regions
        + [pl.BlockSpec((STEP_FIELDS, width, rows), lambda i: (i, 0, 0))],
        out_specs=[
            pl.BlockSpec((STEP_FIELDS, width, rows), lambda i: (i, 0, 0)),
            pl.BlockSpec((2, STEP_FIELDS, width, rows), lambda i: (0, i, 0, 0)),
        ],
        scratch_shapes=[
            pltpu.VMEM((z.span, rows), jnp.float32),
            pltpu.VMEM((SAMPLES, 8, rows), jnp.float32),
            pltpu.VMEM((SAMPLES, STEP_FIELDS, z.span + 16, rows), jnp.float32),
        ],
        compiler_params=pltpu.CompilerParams(vmem_limit_bytes=VMEM),
        name="score",
    )(place, *blocks, analysis)


def shards(patch_tiles, slot_lists, blend_table, smoothing, analysis):
    z = Sizes(lax.axis_size("region"))
    place = lax.axis_index("region").reshape(1)
    turns = [
        [(i, i - i % z.makers + (i + k) % z.makers) for i in range(z.regions)] for k in range(1, z.makers)
    ]
    tiles = patch_tiles.reshape(z.regions, CAP, FIELDS, PAIRS * TILES, LANES)
    tiles = jnp.swapaxes(tiles, 2, 3).reshape(z.regions, CAP, LINES, LANES)
    lists = jnp.transpose(slot_lists, (2, 1, 0))
    received = [lax.ppermute(tiles, "region", turn) for turn in turns]
    lists = [lists] + [lax.ppermute(lists, "region", turn) for turn in turns]
    shares = own_share(z, place, lists[0], tiles, blend_table, smoothing)
    blocks = join(z, place, lists, received, shares)
    moved = [blocks[0]] + [
        lax.ppermute(block, "region", [(i, i ^ offset) for i in range(z.regions)])
        for block, offset in zip(blocks[1:], z.offsets[1:])
    ]
    outs = score(z, place, moved, jnp.swapaxes(analysis, 1, 2))
    return tuple(jnp.swapaxes(item, -1, -2) for item in outs)


def solution(mesh):
    return jax.shard_map(
        shards,
        mesh=mesh,
        in_specs=(
            P(("groups", "region"), None, None, None),
            P(("groups", "region"), None, None),
            P(),
            P("region", None),
            P(None, "groups", "region"),
        ),
        out_specs=(P(None, "groups", "region"), P(None, None, "groups", "region")),
        check_vma=False,
    )
```

```python
import functools

import jax
import jax.numpy as jnp
from jax import lax
from jax.experimental import pallas as pl
from jax.experimental.pallas import tpu as pltpu
from jax.sharding import PartitionSpec as P

SAMPLES = 8
FIELDS = 4
PATCH = 448
CAP = 2
ROWS = 32
COLS = 896
PAIRS = ROWS // 2
LINES = FIELDS * ROWS * PATCH // 128
LANES = 128
TILES = COLS // LANES
QUAD = LANES // ROWS
MID = 0.11
VMEM = 40 * 1024 * 1024
MOST_VMEM = 50 * 1024 * 1024


def round_up(value, step):
    return -(-value // step) * step


def swap_order(regions):
    far, near = list(range(regions // 2, regions)), list(range(1, regions // 2))
    near = near[regions // 4 - 1 :] + near[: regions // 4 - 1]
    return [0] + [item for pair in zip(far, near + [None]) for item in pair if item is not None]


class Sizes:
    def __init__(self, regions):
        self.regions = regions
        self.makers = regions // SAMPLES
        self.block = regions // self.makers
        self.quads = self.block // QUAD
        self.width = COLS // regions
        self.span = round_up(self.width, 8)
        self.rows = regions * ROWS
        self.main = round_up(FIELDS * self.span, 16)
        self.offsets = swap_order(regions)
        self.strong = 8 * -(-self.span // (8 * QUAD))

    def sent(self, quad):
        return self.main + 8 + (self.strong if quad == self.quads - 1 else 0)


def stage(staged, tile):
    staged[...] = tile.astype(jnp.float32)


def staged_field(staged, field):
    return jnp.concatenate(
        [staged[pl.ds(FIELDS * t + field, PAIRS, stride=FIELDS * TILES), :] for t in range(TILES)], 1
    )


def weight_of(weights, kind):
    at = pl.multiple_of(kind * PAIRS, PAIRS)
    return jnp.concatenate([weights[t, pl.ds(at, PAIRS), :] for t in range(TILES)], 1)


def lane_index():
    return lax.broadcasted_iota(jnp.int32, (PAIRS, COLS), 1)


def place_side(pairs, column):
    left = (lane_index() < PATCH) & (column == 0)
    right = (lane_index() >= PATCH) & (column != 0)
    turned = pltpu.roll(pairs, PATCH, 1)
    even = jnp.where(left, pairs, jnp.where(right, turned, 0.0))
    odd = jnp.where(left, turned, jnp.where(right, pairs, 0.0))
    return even, odd


def place_any(pairs, column):
    inside = (lane_index() >= column) & (lane_index() < column + PATCH)
    turned = pltpu.roll(pairs, column, 1)
    return jnp.where(inside, turned, 0.0), jnp.where(inside, pltpu.roll(turned, PATCH, 1), 0.0)


def either_kind(z, heavy, body):
    @pl.when(heavy)
    def _():
        body(place_any, range(CAP))

    @pl.when(jnp.logical_not(heavy))
    def _():
        body(place_side if z.makers == 2 else place_any, range(1))


def fetch_regions(tiles, first, landed, sems):
    return [pltpu.make_async_copy(tiles.at[first + i], landed.at[i], sems.at[i]) for i in range(QUAD)]


def first_kernel(z, place, lists, tiles, table_hbm, *refs):
    half, (total, weights, later, landed, staged, table, sems, later_sems) = refs[:FIELDS], refs[FIELDS:]
    first = lax.rem(place[0], z.makers) * z.block
    fetches = fetch_regions(tiles, first, landed, sems)
    later_fetches = fetch_regions(tiles, first + QUAD, later, later_sems)
    fetch_table = pltpu.make_async_copy(table_hbm, table, sems.at[QUAD])
    fetch_table.start()
    for fetch in fetches + later_fetches:
        fetch.start()
    fetch_table.wait()
    kinds = table.shape[0]
    for k in range(PAIRS):
        for t in range(TILES):
            at = COLS * k + LANES * t
            for low in range(0, kinds, 8):
                count = min(8, kinds - low)
                weights[t, pl.ds(PAIRS * low + k, count, stride=PAIRS), :] = table[
                    low : low + count, at : at + LANES
                ]
    for fetch in fetches:
        fetch.wait()

    def region(j, carry):
        def body(place_tile, slots):
            entries = []
            for slot in slots:
                stage(staged.at[slot], landed[j, slot])
                column, kind = (lists[field, slot, first + j] for field in (1, 2))
                entries.append((slot, column, weight_of(weights, kind)))
            even, odd = 0.0, 0.0
            for _, column, weight in entries:
                a, b = place_tile(weight, column)
                even, odd = even + a, odd + b
            total[j, 0], total[j, 1] = even, odd
            for field in range(FIELDS):
                even, odd = 0.0, 0.0
                for slot, column, weight in entries:
                    a, b = place_tile(staged_field(staged.at[slot], field) * weight, column)
                    even, odd = even + a, odd + b
                half[field][j, 0], half[field][j, 1] = even, odd

        either_kind(z, lists[0, 1, first + j] >= 0, body)
        return carry

    lax.fori_loop(0, QUAD, region, 0)
    for fetch in later_fetches:
        fetch.wait()


def first_share(z, place, lists, tiles, table):
    smem = pl.BlockSpec(memory_space=pltpu.SMEM)
    vmem = pl.BlockSpec(memory_space=pltpu.VMEM)
    hbm = pl.BlockSpec(memory_space=pltpu.HBM)
    kinds = round_up(table.shape[0], 8)
    return pl.pallas_call(
        functools.partial(first_kernel, z),
        out_shape=[
            *[jax.ShapeDtypeStruct((QUAD, 2, PAIRS, COLS), jnp.float32)] * (FIELDS + 1),
            jax.ShapeDtypeStruct((TILES, kinds * PAIRS, LANES), jnp.float32),
            jax.ShapeDtypeStruct((QUAD, CAP, LINES, LANES), jnp.bfloat16),
        ],
        in_specs=[smem, smem, hbm, hbm],
        out_specs=[vmem] * (FIELDS + 3),
        scratch_shapes=[
            pltpu.VMEM((QUAD, CAP, LINES, LANES), jnp.bfloat16),
            pltpu.VMEM((CAP, LINES, LANES), jnp.float32),
            pltpu.VMEM(table.shape, jnp.float32),
            pltpu.SemaphoreType.DMA((QUAD + 1,)),
            pltpu.SemaphoreType.DMA((QUAD,)),
        ],
        compiler_params=pltpu.CompilerParams(vmem_limit_bytes=MOST_VMEM),
        cost_estimate=pl.CostEstimate(flops=5_000_000, bytes_accessed=8_000_000, transcendentals=0),
        name="first_share",
    )(place, lists, tiles, table)


def blend_kernel(z, quad, *refs):
    place, lists, refs = refs[0], refs[1 : 1 + z.makers], refs[1 + z.makers :]
    received, weights, refs = refs[: z.makers - 1], refs[z.makers - 1], refs[z.makers :]
    staged, lines, turned, strength, blocks, sems = refs[-6:]
    if quad == 0:
        half, total, outs = refs[:FIELDS], refs[FIELDS], refs[-6 - z.regions : -6]
    else:
        (own, smoothing, analysis_hbm), outs, analysis = refs[:3], refs[-7 - z.regions : -7], refs[-7]
        fetch_analysis = pltpu.make_async_copy(analysis_hbm, analysis, sems.at[z.regions])
        fetch_analysis.start()
        turned_strength = jnp.transpose(smoothing[...] - MID)
        for dest in range(z.regions):
            for g in range(z.span // 8):
                top, low = z.width * dest + 8 * g, 8 * (g // QUAD)
                count, at = min(8, COLS - top), ROWS * (g % QUAD)
                strength[dest, low : low + count, at : at + ROWS] = turned_strength[top : top + count]
    me = place[0]
    first = lax.rem(me, z.makers) * z.block + quad * QUAD

    def region(j, carry):
        def body(place_tile, slots):
            entries = []
            for maker in range(0 if quad else 1, z.makers):
                for slot in slots:
                    index = maker * CAP + slot
                    tile = received[maker - 1][first + j, slot] if maker else own[j, slot]
                    stage(staged.at[index], tile)
                    column, kind = (lists[maker][field, slot, first + j] for field in (1, 2))
                    entries.append((index, column, weight_of(weights, kind)))
            even, odd = (0.0, 0.0) if quad else (total[j, 0], total[j, 1])
            for _, column, weight in entries:
                a, b = place_tile(weight, column)
                even, odd = even + a, odd + b
            even_inverse, odd_inverse = 1.0 / even, 1.0 / odd
            for field in range(FIELDS):
                even, odd = (0.0, 0.0) if quad else (half[field][j, 0], half[field][j, 1])
                for index, column, weight in entries:
                    a, b = place_tile(staged_field(staged.at[index], field) * weight, column)
                    even, odd = even + a, odd + b
                even, odd = even * even_inverse, odd * odd_inverse
                for t in range(TILES):
                    here = slice(LANES * t, LANES * (t + 1))
                    lines[field, t, pl.ds(ROWS * j, PAIRS, stride=2), :] = even[:, here]
                    lines[field, t, pl.ds(ROWS * j + 1, PAIRS, stride=2), :] = odd[:, here]

        either_kind(z, lists[0][0, 1, first + j] >= 0, body)
        return carry

    lax.fori_loop(0, QUAD, region, 0)
    for field in range(FIELDS):
        for t in range(TILES):
            turned[field, LANES * t : LANES * (t + 1), :] = jnp.transpose(lines[field, t])

    def send(i):
        return pltpu.make_async_copy(blocks.at[i], outs[i], sems.at[i])

    for i, offset in enumerate(z.offsets):
        dest = me ^ offset
        top = dest * z.width
        if z.width % 8 == 0:
            top = pl.multiple_of(top, 8)
        for low in range(0, FIELDS, 2):
            block = [turned[field, pl.ds(top, z.span), :] for field in (low, low + 1)]
            blocks[i, low * z.span : (low + 2) * z.span, :] = jnp.concatenate(block, 0).astype(jnp.bfloat16)
        ends = (jnp.maximum(top - 1, 0), jnp.minimum(top + z.width, COLS - 1))
        edge = [turned[field, pl.ds(end, 1), :] for field in range(FIELDS) for end in ends]
        if quad == z.quads - 1:
            edge.append(strength[dest])
        blocks[i, z.main : z.sent(quad), :] = jnp.concatenate(edge, 0).astype(jnp.bfloat16)
        send(i).start()
    for i in range(z.regions):
        send(i).wait()
    if quad:
        fetch_analysis.wait()


def blend(z, quad, place, lists, received, weights, shares, before=()):
    smem = pl.BlockSpec(memory_space=pltpu.SMEM)
    vmem = pl.BlockSpec(memory_space=pltpu.VMEM)
    hbm = pl.BlockSpec(memory_space=pltpu.HBM)
    shape = (z.sent(quad), LANES)
    out_shape = [pltpu.HBM(shape, jnp.bfloat16)] * z.regions
    if quad:
        out_shape.append(jax.ShapeDtypeStruct(shares[-1].shape, shares[-1].dtype))
    share_specs = [vmem, vmem, hbm] if quad else [vmem] * len(shares)
    return pl.pallas_call(
        functools.partial(blend_kernel, z, quad),
        out_shape=out_shape,
        in_specs=[smem] * (1 + z.makers)
        + [vmem] * z.makers
        + share_specs
        + [pl.BlockSpec(memory_space=pl.ANY)] * len(before),
        out_specs=[hbm] * z.regions + [vmem] * (len(out_shape) - z.regions),
        scratch_shapes=[
            pltpu.VMEM((CAP * z.makers, LINES, LANES), jnp.float32),
            pltpu.VMEM((FIELDS, TILES, LANES, LANES), jnp.float32),
            pltpu.VMEM((FIELDS, COLS + 8, LANES), jnp.float32),
            pltpu.VMEM((z.regions, z.strong, LANES), jnp.float32),
            pltpu.VMEM((z.regions, *shape), jnp.bfloat16),
            pltpu.SemaphoreType.DMA((z.regions + 1,)),
        ],
        compiler_params=pltpu.CompilerParams(vmem_limit_bytes=VMEM),
        cost_estimate=pl.CostEstimate(flops=5_000_000, bytes_accessed=8_000_000, transcendentals=0),
        name="blend",
    )(place, *lists, *received, weights, *shares, *before)


SORT_STEPS = (
    ((0, 1), (2, 3), (4, 5), (6, 7)),
    ((0, 2), (1, 3), (4, 6), (5, 7)),
    ((1, 2), (5, 6)),
    ((0, 4), (1, 5), (2, 6), (3, 7)),
    ((2, 4), (3, 5)),
    ((1, 2), (3, 4), (5, 6)),
)
STEP_FIELDS = 2


def score_kernel(z, place, *refs):
    count = z.regions * z.quads
    blocks = {
        (offset, quad): refs[quad * z.regions + i] for i, offset in enumerate(z.offsets) for quad in range(z.quads)
    }
    analysis, crps, spread, strength, edges, padded = refs[count:]
    me = place[0]
    step = pl.program_id(0)
    rows = z.rows

    def lanes_of(offset, quad):
        at = (lax.rem(me ^ offset, z.makers) * z.quads + quad) * LANES
        return pl.ds(pl.multiple_of(at, LANES), LANES)

    @pl.when(step == 0)
    def _():
        slot = lax.broadcasted_iota(jnp.int32, (8, LANES), 1) // ROWS
        for low in range(0, z.regions, QUAD):
            offsets = range(low, low + QUAD)
            slots = [lax.rem(me ^ offset, QUAD) for offset in offsets]
            at = pl.multiple_of(lax.div(me ^ low, QUAD) * LANES, LANES)
            for quad in range(z.quads):
                tails = [blocks[offset, quad][z.main : z.sent(quad), :].astype(jnp.float32) for offset in offsets]
                for offset, tail in zip(offsets, tails):
                    edges[offset // z.makers, :, lanes_of(offset, quad)] = tail[0:8]
            for g in range(z.span // 8):
                joined = jnp.zeros((8, LANES), jnp.float32)
                for i, tail in zip(slots, tails):
                    rows_of_g = tail[8 * (g // QUAD + 1) : 8 * (g // QUAD + 2)]
                    near = pltpu.roll(rows_of_g, lax.rem(i + QUAD - g % QUAD, QUAD) * ROWS, 1)
                    joined = jnp.where(slot == i, near, joined)
                strength[8 * g : 8 * (g + 1), pl.ds(at, LANES)] = joined + MID

    top = pl.multiple_of(step * STEP_FIELDS * z.span, 16)
    for offset in range(z.regions):
        for quad in range(z.quads):
            values = blocks[offset, quad][pl.ds(top, STEP_FIELDS * z.span), :].astype(jnp.float32)
            for f in range(STEP_FIELDS):
                padded[offset // z.makers, f, 8 : 8 + z.span, lanes_of(offset, quad)] = values[
                    f * z.span : (f + 1) * z.span
                ]
    for sample in range(SAMPLES):
        for f in range(STEP_FIELDS):
            low = 2 * (step * STEP_FIELDS + f)
            padded[sample, f, 7:8, :] = edges[sample, pl.ds(low, 1), :]
            padded[sample, f, 8 + z.width : 9 + z.width, :] = edges[sample, pl.ds(low + 1, 1), :]
    for f in range(STEP_FIELDS):
        target_field = analysis[step * STEP_FIELDS + f].astype(jnp.float32)
        for low in range(0, z.width, 16):
            high = min(low + 16, z.width)
            shape = (high - low, rows)
            lane = lax.broadcasted_iota(jnp.int32, shape, 1)
            strong = strength[low:high, :]
            members = []
            for sample in range(SAMPLES):
                here = padded[sample, f, 8 + low : 8 + high, :]
                sides = padded[sample, f, 7 + low : 7 + high, :] + padded[sample, f, 9 + low : 9 + high, :]
                above = jnp.where(lane == 0, here, pltpu.roll(here, 1, 1))
                below = jnp.where(lane == rows - 1, here, pltpu.roll(here, rows - 1, 1))
                smooth = here + strong * (above + below + sides - 4.0 * here)
                members.append(smooth.astype(jnp.bfloat16))
            values = [member.astype(jnp.float32) for member in members]
            target = target_field[low:high]
            error = sum(jnp.abs(value - target) for value in values) * (1.0 / SAMPLES)
            average = sum(values) * (1.0 / SAMPLES)
            variance = sum((value - average) ** 2 for value in values) * (1.0 / (SAMPLES - 1.0))
            ranked = list(members)
            for pairs in SORT_STEPS:
                for a, b in pairs:
                    ranked[a], ranked[b] = jnp.minimum(ranked[a], ranked[b]), jnp.maximum(ranked[a], ranked[b])
            ranked = [member.astype(jnp.float32) for member in ranked]
            pairs = sum(
                (2 * k - SAMPLES + 1.0) * (ranked[k] - ranked[SAMPLES - 1 - k])
                for k in range(SAMPLES // 2, SAMPLES)
            )
            crps[f, low:high, :] = (error - pairs * (1.0 / (SAMPLES * SAMPLES))).astype(jnp.bfloat16)
            spread[0, f, low:high, :] = variance.astype(jnp.bfloat16)
            spread[1, f, low:high, :] = ((average - target) ** 2).astype(jnp.bfloat16)


def score(z, place, blocks, analysis):
    width, rows = z.width, z.rows
    return pl.pallas_call(
        functools.partial(score_kernel, z),
        out_shape=[
            jax.ShapeDtypeStruct((FIELDS, width, rows), jnp.bfloat16),
            jax.ShapeDtypeStruct((2, FIELDS, width, rows), jnp.bfloat16),
        ],
        grid=(FIELDS // STEP_FIELDS,),
        in_specs=[pl.BlockSpec(memory_space=pltpu.SMEM)]
        + [pl.BlockSpec(memory_space=pltpu.VMEM)] * (len(blocks) + 1),
        out_specs=[
            pl.BlockSpec((STEP_FIELDS, width, rows), lambda i: (i, 0, 0)),
            pl.BlockSpec((2, STEP_FIELDS, width, rows), lambda i: (0, i, 0, 0)),
        ],
        scratch_shapes=[
            pltpu.VMEM((z.span, rows), jnp.float32),
            pltpu.VMEM((SAMPLES, 8, rows), jnp.float32),
            pltpu.VMEM((SAMPLES, STEP_FIELDS, z.span + 16, rows), jnp.float32),
        ],
        compiler_params=pltpu.CompilerParams(vmem_limit_bytes=VMEM),
        name="score",
    )(place, *blocks, analysis)


def shards(patch_tiles, slot_lists, blend_table, smoothing, analysis):
    z = Sizes(lax.axis_size("region"))
    place = lax.axis_index("region").reshape(1)
    turns = [
        [(i, i - i % z.makers + (i + k) % z.makers) for i in range(z.regions)] for k in range(1, z.makers)
    ]
    tiles = patch_tiles.reshape(z.regions, CAP, FIELDS, PAIRS * TILES, LANES)
    tiles = jnp.swapaxes(tiles, 2, 3).reshape(z.regions, CAP, LINES, LANES)
    lists = jnp.transpose(slot_lists, (2, 1, 0))
    received = [lax.ppermute(tiles, "region", turn) for turn in turns]
    lists = [lists] + [lax.ppermute(lists, "region", turn) for turn in turns]
    *shares, weights, own = first_share(z, place, lists[0], tiles, blend_table)
    analysis = jnp.swapaxes(analysis, 1, 2)
    moved, before = [], []
    for quad in range(z.quads):
        blocks = blend(z, quad, place, lists, received, weights, shares, before)
        moved += [blocks[0]] + [
            lax.ppermute(block, "region", [(i, i ^ offset) for i in range(z.regions)])
            for block, offset in zip(blocks[1 : z.regions], z.offsets[1:])
        ]
        shares, before = [own, smoothing, analysis], moved[2:3]
    analysis = blocks[z.regions]
    outs = score(z, place, moved, analysis)
    return tuple(jnp.swapaxes(item, -1, -2) for item in outs)


def solution(mesh):
    return jax.shard_map(
        shards,
        mesh=mesh,
        in_specs=(
            P(("groups", "region"), None, None, None),
            P(("groups", "region"), None, None),
            P(),
            P("region", None),
            P(None, "groups", "region"),
        ),
        out_specs=(P(None, "groups", "region"), P(None, None, "groups", "region")),
        check_vma=False,
    )
```

```python
import functools

import jax
import jax.numpy as jnp
from jax import lax
from jax.experimental import pallas as pl
from jax.experimental.pallas import tpu as pltpu
from jax.sharding import PartitionSpec as P

SAMPLES = 8
FIELDS = 4
PATCH = 448
CAP = 2
ROWS = 32
COLS = 896
PAIRS = ROWS // 2
LINES = FIELDS * ROWS * PATCH // 128
LANES = 128
TILES = COLS // LANES
QUAD = LANES // ROWS
MID = 0.11
VMEM = 40 * 1024 * 1024
MOST_VMEM = 46 * 1024 * 1024


def round_up(value, step):
    return -(-value // step) * step


def swap_order(regions):
    far, near = list(range(regions // 2, regions)), list(range(1, regions // 2))
    near = near[regions // 4 - 1 :] + near[: regions // 4 - 1]
    return [0] + [item for pair in zip(far, near + [None]) for item in pair if item is not None]


class Sizes:
    def __init__(self, regions):
        self.regions = regions
        self.makers = regions // SAMPLES
        self.block = regions // self.makers
        self.quads = self.block // QUAD
        self.width = COLS // regions
        self.span = round_up(self.width, 8)
        self.rows = regions * ROWS
        self.main = round_up(FIELDS * self.span, 16)
        self.offsets = swap_order(regions)
        self.sent = self.main + 16


def stage(staged, tile):
    staged[...] = tile.astype(jnp.float32)


def staged_tile(staged, field, t):
    return staged[pl.ds(FIELDS * t + field, PAIRS, stride=FIELDS * TILES), :]


def weight_tile(weights, kind, t):
    return weights[t, pl.ds(pl.multiple_of(kind * PAIRS, PAIRS), PAIRS), :]


SLOTS = TILES + 2


def zero(sums):
    for parity in range(2):
        for t in range(SLOTS):
            sums[parity, t] = jnp.zeros((PAIRS, LANES), jnp.float32)


def add_side(sums, tile, column, fresh):
    pairs = jnp.concatenate([tile(t) for t in range(TILES)], 1)
    turned = pltpu.roll(pairs, PATCH, 1)
    lane = lax.broadcasted_iota(jnp.int32, pairs.shape, 1)
    left = (lane < PATCH) & (column == 0)
    right = (lane >= PATCH) & (column != 0)
    placed = (
        jnp.where(left, pairs, jnp.where(right, turned, 0.0)),
        jnp.where(left, turned, jnp.where(right, pairs, 0.0)),
    )
    for parity in range(2):
        for t in range(TILES):
            piece = placed[parity][:, LANES * t : LANES * (t + 1)]
            sums[parity, t + 1] = piece if fresh else sums[parity, t + 1] + piece


def add_any(sums, tile, column, fresh):
    if fresh:
        zero(sums)
    lane = lax.broadcasted_iota(jnp.int32, (PAIRS, LANES), 1)
    middle = PATCH // LANES
    split = PATCH % LANES
    for parity in range(2):
        first = middle * parity
        start = column if parity == 0 else column + COLS - PATCH
        shift = lax.rem(start, LANES)
        at = lax.div(start, LANES) + first + 1 - (TILES if parity else 0)
        turned = []
        for t in range(first, first + middle + 1):
            piece = tile(t)
            if t == middle:
                piece = jnp.where((lane >= split) if parity else (lane < split), piece, 0.0)
            turned.append(pltpu.roll(piece, shift, 1))
        none = jnp.zeros((PAIRS, LANES), jnp.float32)
        for v in range(middle + 2):
            low = turned[v - 1] if v else none
            high = turned[v] if v <= middle else none
            sums[parity, at + v] = sums[parity, at + v] + jnp.where(lane < shift, low, high)


def either_kind(z, heavy, body):
    @pl.when(heavy)
    def _():
        body(add_any, range(CAP))

    @pl.when(jnp.logical_not(heavy))
    def _():
        body(add_side if z.makers == 2 else add_any, range(1))


def own_kernel(z, place, lists, tiles, table_hbm, *refs):
    half, (total, weights, landed, staged, table, sems) = refs[:FIELDS], refs[FIELDS:]
    first = lax.rem(place[0], z.makers) * z.block

    def fetch(j):
        return pltpu.make_async_copy(tiles.at[first + j], landed.at[j], sems.at[j])

    fetch_table = pltpu.make_async_copy(table_hbm, table, sems.at[z.block])
    fetch_table.start()
    for j in range(z.block):
        fetch(j).start()
    fetch_table.wait()
    kinds = table.shape[0]
    for k in range(PAIRS):
        for t in range(TILES):
            at = COLS * k + LANES * t
            for low in range(0, kinds, 8):
                count = min(8, kinds - low)
                weights[t, pl.ds(PAIRS * low + k, count, stride=PAIRS), :] = table[
                    low : low + count, at : at + LANES
                ]

    def region(j, carry):
        fetch(j).wait()

        def body(add, slots):
            for slot in slots:
                stage(staged.at[slot], landed[j, slot])
            entries = [(slot, *(lists[entry, slot, first + j] for entry in (1, 2))) for slot in slots]
            for i, (_, column, kind) in enumerate(entries):
                add(total.at[j], functools.partial(weight_tile, weights, kind), column, i == 0)
            for field in range(FIELDS):
                for i, (slot, column, kind) in enumerate(entries):

                    def tile(t):
                        return staged_tile(staged.at[slot], field, t) * weight_tile(weights, kind, t)

                    add(half[field].at[j], tile, column, i == 0)

        either_kind(z, lists[0, 1, first + j] >= 0, body)
        return carry

    lax.fori_loop(0, z.block, region, 0)


def own_share(z, place, lists, tiles, table):
    smem = pl.BlockSpec(memory_space=pltpu.SMEM)
    vmem = pl.BlockSpec(memory_space=pltpu.VMEM)
    hbm = pl.BlockSpec(memory_space=pltpu.HBM)
    kinds = round_up(table.shape[0], 8)
    return pl.pallas_call(
        functools.partial(own_kernel, z),
        out_shape=[
            *[jax.ShapeDtypeStruct((z.block, 2, SLOTS, PAIRS, LANES), jnp.float32)] * (FIELDS + 1),
            jax.ShapeDtypeStruct((TILES, kinds * PAIRS, LANES), jnp.float32),
        ],
        in_specs=[smem, smem, hbm, hbm],
        out_specs=[vmem] * (FIELDS + 2),
        scratch_shapes=[
            pltpu.VMEM((z.block, CAP, LINES, LANES), jnp.bfloat16),
            pltpu.VMEM((CAP, LINES, LANES), jnp.float32),
            pltpu.VMEM(table.shape, jnp.float32),
            pltpu.SemaphoreType.DMA((z.block + 1,)),
        ],
        compiler_params=pltpu.CompilerParams(vmem_limit_bytes=MOST_VMEM),
        cost_estimate=pl.CostEstimate(flops=5_000_000, bytes_accessed=8_000_000, transcendentals=0),
        name="own_share",
    )(place, lists, tiles, table)


def strength_kernel(z, smoothing, _, strength):
    turned_strength = jnp.transpose(smoothing[...] - MID)
    for dest in range(z.regions):
        for g in range(z.span // 8):
            top = z.width * dest + 8 * g
            count, at = min(8, COLS - top), ROWS * (g % QUAD)
            strength[dest, g // QUAD, 0:count, at : at + ROWS] = turned_strength[top : top + count]


def strength_blocks(z, smoothing, before):
    return pl.pallas_call(
        functools.partial(strength_kernel, z),
        out_shape=jax.ShapeDtypeStruct((z.regions, z.quads, 8, LANES), jnp.float32),
        in_specs=[pl.BlockSpec(memory_space=pltpu.VMEM), pl.BlockSpec(memory_space=pl.ANY)],
        out_specs=pl.BlockSpec(memory_space=pltpu.VMEM),
        compiler_params=pltpu.CompilerParams(vmem_limit_bytes=VMEM),
        name="strength_blocks",
    )(smoothing, before)


def join_kernel(z, *refs):
    place, lists, refs = refs[0], refs[1 : 1 + z.makers], refs[1 + z.makers :]
    received, refs = refs[: z.makers - 1], refs[z.makers - 1 :]
    half, (total, weights, strength), outs = refs[:FIELDS], refs[FIELDS : FIELDS + 3], refs[FIELDS + 3 : -6]
    staged, sums, lines, turned, blocks, sems = refs[-6:]
    me = place[0]
    first = lax.rem(me, z.makers) * z.block
    row, column = (lax.broadcasted_iota(jnp.int32, (LANES, LANES), axis) for axis in (0, 1))
    identity = (row == column).astype(jnp.bfloat16)

    def send(i, quad):
        return pltpu.make_async_copy(blocks.at[i, quad], outs[i].at[quad], sems.at[i, quad])

    for quad in range(z.quads):

        def region(i, carry):
            j = quad * QUAD + i

            def body(add, slots):
                entries = []
                for maker in range(1, z.makers):
                    for slot in slots:
                        index = (maker - 1) * CAP + slot
                        stage(staged.at[index], received[maker - 1][first + j, slot])
                        entries.append((index, *(lists[maker][entry, slot, first + j] for entry in (1, 2))))

                def begin(index, own):
                    for parity in range(2):
                        for t in range(SLOTS):
                            sums[index, parity, t] = own[j, parity, t]

                begin(FIELDS, total)
                for _, column, kind in entries:
                    add(sums.at[FIELDS], functools.partial(weight_tile, weights, kind), column, False)
                inverse = [[1.0 / sums[FIELDS, parity, t + 1] for t in range(TILES)] for parity in range(2)]
                for field in range(FIELDS):
                    begin(field, half[field])
                    for index, column, kind in entries:

                        def tile(t):
                            return staged_tile(staged.at[index], field, t) * weight_tile(weights, kind, t)

                        add(sums.at[field], tile, column, False)
                    for parity in range(2):
                        for t in range(TILES):
                            lines[field, t, pl.ds(ROWS * i + parity, PAIRS, stride=2), :] = (
                                sums[field, parity, t + 1] * inverse[parity][t]
                            )

            either_kind(z, lists[0][0, 1, first + j] >= 0, body)
            return carry

        lax.fori_loop(0, QUAD, region, 0)
        for field in range(FIELDS):
            for t in range(TILES):
                turned[field, LANES * t : LANES * (t + 1), :] = lax.dot_general(
                    identity,
                    lines[field, t].astype(jnp.bfloat16),
                    (((1,), (1,)), ((), ())),
                    preferred_element_type=jnp.float32,
                )
        for i, offset in enumerate(z.offsets):
            target = blocks.at[i, quad] if i else outs[0].at[quad]
            dest = me ^ offset
            top = dest * z.width
            if z.width % 8 == 0:
                top = pl.multiple_of(top, 8)
            for low in range(0, FIELDS, 2):
                block = [turned[field, pl.ds(top, z.span), :] for field in (low, low + 1)]
                target[low * z.span : (low + 2) * z.span, :] = jnp.concatenate(block, 0).astype(jnp.bfloat16)
            ends = (jnp.maximum(top - 1, 0), jnp.minimum(top + z.width, COLS - 1))
            edge = [turned[field, pl.ds(end, 1), :] for field in range(FIELDS) for end in ends]
            edge.append(strength[dest, quad])
            target[z.main : z.sent, :] = jnp.concatenate(edge, 0).astype(jnp.bfloat16)
            if i:
                send(i, quad).start()
    for quad in range(z.quads):
        for i in range(1, z.regions):
            send(i, quad).wait()


def join(z, place, lists, received, shares):
    smem = pl.BlockSpec(memory_space=pltpu.SMEM)
    vmem = pl.BlockSpec(memory_space=pltpu.VMEM)
    hbm = pl.BlockSpec(memory_space=pltpu.HBM)
    shape = (z.quads, z.sent, LANES)
    return pl.pallas_call(
        functools.partial(join_kernel, z),
        out_shape=[jax.ShapeDtypeStruct(shape, jnp.bfloat16)]
        + [pltpu.HBM(shape, jnp.bfloat16)] * (z.regions - 1),
        in_specs=[smem] * (1 + z.makers) + [vmem] * (z.makers - 1 + len(shares)),
        out_specs=[vmem] + [hbm] * (z.regions - 1),
        scratch_shapes=[
            pltpu.VMEM((CAP * (z.makers - 1), LINES, LANES), jnp.float32),
            pltpu.VMEM((FIELDS + 1, 2, SLOTS, PAIRS, LANES), jnp.float32),
            pltpu.VMEM((FIELDS, TILES, LANES, LANES), jnp.float32),
            pltpu.VMEM((FIELDS, COLS + 8, LANES), jnp.float32),
            pltpu.VMEM((z.regions, *shape), jnp.bfloat16),
            pltpu.SemaphoreType.DMA((z.regions, z.quads)),
        ],
        compiler_params=pltpu.CompilerParams(vmem_limit_bytes=VMEM),
        cost_estimate=pl.CostEstimate(flops=5_000_000, bytes_accessed=8_000_000, transcendentals=0),
        name="join",
    )(place, *lists, *received, *shares)


SORT_STEPS = (
    ((0, 1), (2, 3), (4, 5), (6, 7)),
    ((0, 2), (1, 3), (4, 6), (5, 7)),
    ((1, 2), (5, 6)),
    ((0, 4), (1, 5), (2, 6), (3, 7)),
    ((2, 4), (3, 5)),
    ((1, 2), (3, 4), (5, 6)),
)
STEP_FIELDS = 2


def score_kernel(z, place, *refs):
    blocks = dict(zip(z.offsets, refs))
    analysis, crps, spread, strength, edges, padded = refs[z.regions :]
    me = place[0]
    step = pl.program_id(0)
    rows = z.rows

    def lanes_of(offset, quad):
        at = (lax.rem(me ^ offset, z.makers) * z.quads + quad) * LANES
        return pl.ds(pl.multiple_of(at, LANES), LANES)

    @pl.when(step == 0)
    def _():
        slot = lax.broadcasted_iota(jnp.int32, (8, LANES), 1) // ROWS
        for low in range(0, z.regions, QUAD):
            offsets = range(low, low + QUAD)
            slots = [lax.rem(me ^ offset, QUAD) for offset in offsets]
            at = pl.multiple_of(lax.div(me ^ low, QUAD) * LANES, LANES)
            for quad in range(z.quads):
                tails = [blocks[offset][quad, z.main : z.sent, :].astype(jnp.float32) for offset in offsets]
                for offset, tail in zip(offsets, tails):
                    edges[offset // z.makers, :, lanes_of(offset, quad)] = tail[0:8]
                for g in range(quad * QUAD, min((quad + 1) * QUAD, z.span // 8)):
                    joined = jnp.zeros((8, LANES), jnp.float32)
                    for i, tail in zip(slots, tails):
                        near = pltpu.roll(tail[8:16], lax.rem(i + QUAD - g % QUAD, QUAD) * ROWS, 1)
                        joined = jnp.where(slot == i, near, joined)
                    strength[8 * g : 8 * (g + 1), pl.ds(at, LANES)] = joined + MID

    top = pl.multiple_of(step * STEP_FIELDS * z.span, 16)
    for offset in range(z.regions):
        for quad in range(z.quads):
            values = blocks[offset][quad, pl.ds(top, STEP_FIELDS * z.span), :].astype(jnp.float32)
            for f in range(STEP_FIELDS):
                padded[offset // z.makers, f, 8 : 8 + z.span, lanes_of(offset, quad)] = values[
                    f * z.span : (f + 1) * z.span
                ]
    for sample in range(SAMPLES):
        for f in range(STEP_FIELDS):
            low = 2 * (step * STEP_FIELDS + f)
            padded[sample, f, 7:8, :] = edges[sample, pl.ds(low, 1), :]
            padded[sample, f, 8 + z.width : 9 + z.width, :] = edges[sample, pl.ds(low + 1, 1), :]
    for f in range(STEP_FIELDS):
        target_field = analysis[f].astype(jnp.float32)
        for low in range(0, z.width, 16):
            high = min(low + 16, z.width)
            lane = lax.broadcasted_iota(jnp.int32, (high - low, LANES), 1)
            strong = strength[low:high, :]
            members = []
            for sample in range(SAMPLES):
                here = padded[sample, f, 8 + low : 8 + high, :]
                sides = padded[sample, f, 7 + low : 7 + high, :] + padded[sample, f, 9 + low : 9 + high, :]
                pieces = [here[:, at : at + LANES] for at in range(0, rows, LANES)]
                later = [pltpu.roll(piece, 1, 1) for piece in pieces]
                sooner = [pltpu.roll(piece, LANES - 1, 1) for piece in pieces]
                above = [jnp.where(lane == 0, a, b) for a, b in zip([pieces[0]] + later[:-1], later)]
                below = [jnp.where(lane == LANES - 1, a, b) for a, b in zip(sooner[1:] + [pieces[-1]], sooner)]
                along = jnp.concatenate([a + b for a, b in zip(above, below)], 1)
                smooth = here + strong * (along + sides - 4.0 * here)
                members.append(smooth.astype(jnp.bfloat16))
            values = [member.astype(jnp.float32) for member in members]
            target = target_field[low:high]
            error = sum(jnp.abs(value - target) for value in values) * (1.0 / SAMPLES)
            average = sum(values) * (1.0 / SAMPLES)
            variance = sum((value - average) ** 2 for value in values) * (1.0 / (SAMPLES - 1.0))
            ranked = list(members)
            for pairs in SORT_STEPS:
                for a, b in pairs:
                    ranked[a], ranked[b] = jnp.minimum(ranked[a], ranked[b]), jnp.maximum(ranked[a], ranked[b])
            ranked = [member.astype(jnp.float32) for member in ranked]
            pairs = sum(
                (2 * k - SAMPLES + 1.0) * (ranked[k] - ranked[SAMPLES - 1 - k])
                for k in range(SAMPLES // 2, SAMPLES)
            )
            crps[f, low:high, :] = (error - pairs * (1.0 / (SAMPLES * SAMPLES))).astype(jnp.bfloat16)
            spread[0, f, low:high, :] = variance.astype(jnp.bfloat16)
            spread[1, f, low:high, :] = ((average - target) ** 2).astype(jnp.bfloat16)


def score(z, place, blocks, analysis):
    width, rows = z.width, z.rows
    return pl.pallas_call(
        functools.partial(score_kernel, z),
        out_shape=[
            jax.ShapeDtypeStruct((FIELDS, width, rows), jnp.bfloat16),
            jax.ShapeDtypeStruct((2, FIELDS, width, rows), jnp.bfloat16),
        ],
        grid=(FIELDS // STEP_FIELDS,),
        in_specs=[pl.BlockSpec(memory_space=pltpu.SMEM)]
        + [pl.BlockSpec(memory_space=pltpu.VMEM)] * z.regions
        + [pl.BlockSpec((STEP_FIELDS, width, rows), lambda i: (i, 0, 0))],
        out_specs=[
            pl.BlockSpec((STEP_FIELDS, width, rows), lambda i: (i, 0, 0)),
            pl.BlockSpec((2, STEP_FIELDS, width, rows), lambda i: (0, i, 0, 0)),
        ],
        scratch_shapes=[
            pltpu.VMEM((z.span, rows), jnp.float32),
            pltpu.VMEM((SAMPLES, 8, rows), jnp.float32),
            pltpu.VMEM((SAMPLES, STEP_FIELDS, z.span + 16, rows), jnp.float32),
        ],
        compiler_params=pltpu.CompilerParams(vmem_limit_bytes=VMEM),
        name="score",
    )(place, *blocks, analysis)


def shards(patch_tiles, slot_lists, blend_table, smoothing, analysis):
    z = Sizes(lax.axis_size("region"))
    place = lax.axis_index("region").reshape(1)
    turns = [
        [(i, i - i % z.makers + (i + k) % z.makers) for i in range(z.regions)] for k in range(1, z.makers)
    ]
    tiles = patch_tiles.reshape(z.regions, CAP, FIELDS, PAIRS * TILES, LANES)
    tiles = jnp.swapaxes(tiles, 2, 3).reshape(z.regions, CAP, LINES, LANES)
    lists = jnp.transpose(slot_lists, (2, 1, 0))
    received = [lax.ppermute(tiles, "region", turn) for turn in turns]
    lists = [lists] + [lax.ppermute(lists, "region", turn) for turn in turns]
    shares = own_share(z, place, lists[0], tiles, blend_table)
    shares = [*shares, strength_blocks(z, smoothing, shares[-1])]
    blocks = join(z, place, lists, received, shares)
    moved = [blocks[0]] + [
        lax.ppermute(block, "region", [(i, i ^ offset) for i in range(z.regions)])
        for block, offset in zip(blocks[1:], z.offsets[1:])
    ]
    outs = score(z, place, moved, jnp.swapaxes(analysis, 1, 2))
    return tuple(jnp.swapaxes(item, -1, -2) for item in outs)


def solution(mesh):
    return jax.shard_map(
        shards,
        mesh=mesh,
        in_specs=(
            P(("groups", "region"), None, None, None),
            P(("groups", "region"), None, None),
            P(),
            P("region", None),
            P(None, "groups", "region"),
        ),
        out_specs=(P(None, "groups", "region"), P(None, None, "groups", "region")),
        check_vma=False,
    )
```

```python
import functools

import jax
import jax.numpy as jnp
from jax import lax
from jax.experimental import pallas as pl
from jax.experimental.pallas import tpu as pltpu
from jax.sharding import PartitionSpec as P

SAMPLES = 8
FIELDS = 4
PATCH = 448
CAP = 2
ROWS = 32
COLS = 896
PAIRS = ROWS // 2
LINES = FIELDS * ROWS * PATCH // 128
LANES = 128
TILES = COLS // LANES
QUAD = LANES // ROWS
MID = 0.11
VMEM = 40 * 1024 * 1024
MOST_VMEM = 46 * 1024 * 1024


def round_up(value, step):
    return -(-value // step) * step


def swap_order(regions):
    far, near = list(range(regions // 2, regions)), list(range(1, regions // 2))
    near = near[regions // 4 - 1 :] + near[: regions // 4 - 1]
    return [0] + [item for pair in zip(far, near + [None]) for item in pair if item is not None]


class Sizes:
    def __init__(self, regions):
        self.regions = regions
        self.makers = regions // SAMPLES
        self.block = regions // self.makers
        self.quads = self.block // QUAD
        self.width = COLS // regions
        self.span = round_up(self.width, 8)
        self.rows = regions * ROWS
        self.main = round_up(FIELDS * self.span, 16)
        self.offsets = swap_order(regions)
        self.sent = self.main + 8


def stage(staged, tile):
    staged[...] = tile.astype(jnp.float32)


def staged_tile(staged, field, t):
    return staged[pl.ds(FIELDS * t + field, PAIRS, stride=FIELDS * TILES), :]


def weight_tile(weights, kind, t):
    return weights[t, pl.ds(pl.multiple_of(kind * PAIRS, PAIRS), PAIRS), :]


SLOTS = TILES + 2


def zero(sums):
    for parity in range(2):
        for t in range(SLOTS):
            sums[parity, t] = jnp.zeros((PAIRS, LANES), jnp.float32)


def add_side(sums, tile, column, fresh):
    for parity, placed in enumerate(place_side(tile, column)):
        for t, piece in enumerate(placed):
            sums[parity, t + 1] = piece if fresh else sums[parity, t + 1] + piece


def place_side(tile, column):
    pairs = jnp.concatenate([tile(t) for t in range(TILES)], 1)
    turned = pltpu.roll(pairs, PATCH, 1)
    lane = lax.broadcasted_iota(jnp.int32, pairs.shape, 1)
    left = (lane < PATCH) & (column == 0)
    right = (lane >= PATCH) & (column != 0)
    even = jnp.where(left, pairs, jnp.where(right, turned, 0.0))
    odd = jnp.where(left, turned, jnp.where(right, pairs, 0.0))
    return [[rows[:, LANES * t : LANES * (t + 1)] for t in range(TILES)] for rows in (even, odd)]


def add_any(sums, tile, column, fresh):
    if fresh:
        zero(sums)
    lane = lax.broadcasted_iota(jnp.int32, (PAIRS, LANES), 1)
    middle = PATCH // LANES
    split = PATCH % LANES
    for parity in range(2):
        first = middle * parity
        start = column if parity == 0 else column + COLS - PATCH
        shift = lax.rem(start, LANES)
        at = lax.div(start, LANES) + first + 1 - (TILES if parity else 0)
        turned = []
        for t in range(first, first + middle + 1):
            piece = tile(t)
            if t == middle:
                piece = jnp.where((lane >= split) if parity else (lane < split), piece, 0.0)
            turned.append(pltpu.roll(piece, shift, 1))
        none = jnp.zeros((PAIRS, LANES), jnp.float32)
        for v in range(middle + 2):
            low = turned[v - 1] if v else none
            high = turned[v] if v <= middle else none
            sums[parity, at + v] = sums[parity, at + v] + jnp.where(lane < shift, low, high)


def either_kind(z, heavy, body):
    @pl.when(heavy)
    def _():
        body(add_any, range(CAP))

    @pl.when(jnp.logical_not(heavy))
    def _():
        body(add_side if z.makers == 2 else add_any, range(1))


def own_kernel(z, place, lists, tiles, table_hbm, *refs):
    half, (total, weights, landed, staged, table, sems) = refs[:FIELDS], refs[FIELDS:]
    first = lax.rem(place[0], z.makers) * z.block

    def fetch(j):
        return pltpu.make_async_copy(tiles.at[first + j], landed.at[j], sems.at[j])

    fetch_table = pltpu.make_async_copy(table_hbm, table, sems.at[z.block])
    fetch_table.start()
    for j in range(z.block):
        fetch(j).start()
    fetch_table.wait()
    kinds = table.shape[0]
    for k in range(PAIRS):
        for t in range(TILES):
            at = COLS * k + LANES * t
            for low in range(0, kinds, 8):
                count = min(8, kinds - low)
                weights[t, pl.ds(PAIRS * low + k, count, stride=PAIRS), :] = table[
                    low : low + count, at : at + LANES
                ]

    def region(j, carry):
        fetch(j).wait()

        def body(add, slots):
            for slot in slots:
                stage(staged.at[slot], landed[j, slot])
            entries = [(slot, *(lists[entry, slot, first + j] for entry in (1, 2))) for slot in slots]
            for i, (_, column, kind) in enumerate(entries):
                add(total.at[j], functools.partial(weight_tile, weights, kind), column, i == 0)
            for field in range(FIELDS):
                for i, (slot, column, kind) in enumerate(entries):

                    def tile(t):
                        return staged_tile(staged.at[slot], field, t) * weight_tile(weights, kind, t)

                    add(half[field].at[j], tile, column, i == 0)

        either_kind(z, lists[0, 1, first + j] >= 0, body)
        return carry

    lax.fori_loop(0, z.block, region, 0)


def own_share(z, place, lists, tiles, table):
    smem = pl.BlockSpec(memory_space=pltpu.SMEM)
    vmem = pl.BlockSpec(memory_space=pltpu.VMEM)
    hbm = pl.BlockSpec(memory_space=pltpu.HBM)
    kinds = round_up(table.shape[0], 8)
    return pl.pallas_call(
        functools.partial(own_kernel, z),
        out_shape=[
            *[jax.ShapeDtypeStruct((z.block, 2, SLOTS, PAIRS, LANES), jnp.float32)] * (FIELDS + 1),
            jax.ShapeDtypeStruct((TILES, kinds * PAIRS, LANES), jnp.float32),
        ],
        in_specs=[smem, smem, hbm, hbm],
        out_specs=[vmem] * (FIELDS + 2),
        scratch_shapes=[
            pltpu.VMEM((z.block, CAP, LINES, LANES), jnp.bfloat16),
            pltpu.VMEM((CAP, LINES, LANES), jnp.float32),
            pltpu.VMEM(table.shape, jnp.float32),
            pltpu.SemaphoreType.DMA((z.block + 1,)),
        ],
        compiler_params=pltpu.CompilerParams(vmem_limit_bytes=MOST_VMEM),
        cost_estimate=pl.CostEstimate(flops=5_000_000, bytes_accessed=8_000_000, transcendentals=0),
        name="own_share",
    )(place, lists, tiles, table)


def strength_kernel(z, place, gathered, strength):
    start = place[0] * z.width
    tile, shift = lax.div(start, LANES), lax.rem(start, LANES)
    lane = lax.broadcasted_iota(jnp.int32, (z.rows, LANES), 1)
    low, high = (
        pltpu.roll(
            gathered[:, pl.ds(pl.multiple_of(t * LANES, LANES), LANES)].astype(jnp.float32), LANES - shift, 1
        )
        for t in (tile, jnp.minimum(tile + 1, TILES - 1))
    )
    strength[...] = jnp.transpose(jnp.where(lane < LANES - shift, low, high))[0 : z.span] + MID


def own_strength(z, place, gathered):
    return pl.pallas_call(
        functools.partial(strength_kernel, z),
        out_shape=jax.ShapeDtypeStruct((z.span, z.rows), jnp.float32),
        in_specs=[pl.BlockSpec(memory_space=pltpu.SMEM), pl.BlockSpec(memory_space=pltpu.VMEM)],
        out_specs=pl.BlockSpec(memory_space=pltpu.VMEM),
        compiler_params=pltpu.CompilerParams(vmem_limit_bytes=VMEM),
        cost_estimate=pl.CostEstimate(flops=1_000_000, bytes_accessed=1_000_000, transcendentals=0),
        name="own_strength",
    )(place, gathered)


def join_kernel(z, *refs):
    place, lists, refs = refs[0], refs[1 : 1 + z.makers], refs[1 + z.makers :]
    received, refs = refs[: z.makers - 1], refs[z.makers - 1 :]
    half, (total, weights), outs = refs[:FIELDS], refs[FIELDS : FIELDS + 2], refs[FIELDS + 2 : -6]
    staged, sums, lines, turned, blocks, sems = refs[-6:]
    me = place[0]
    first = lax.rem(me, z.makers) * z.block
    row, column = (lax.broadcasted_iota(jnp.int32, (LANES, LANES), axis) for axis in (0, 1))
    identity = (row == column).astype(jnp.bfloat16)

    def send(i, quad):
        return pltpu.make_async_copy(blocks.at[i, quad], outs[i].at[quad], sems.at[i, quad])

    for quad in range(z.quads):

        def region(i, carry):
            j = quad * QUAD + i

            def body(add, slots):
                entries = []
                for maker in range(1, z.makers):
                    for slot in slots:
                        index = (maker - 1) * CAP + slot
                        stage(staged.at[index], received[maker - 1][first + j, slot])
                        entries.append((index, *(lists[maker][entry, slot, first + j] for entry in (1, 2))))

                def joined(own, index, tile_of):
                    if add is add_side:
                        ((_, column, _),) = entries
                        placed = place_side(tile_of(entries[0]), column)
                        return [
                            [own[j, parity, t + 1] + piece for t, piece in enumerate(placed[parity])]
                            for parity in range(2)
                        ]
                    for parity in range(2):
                        for t in range(SLOTS):
                            sums[index, parity, t] = own[j, parity, t]
                    for entry in entries:
                        add(sums.at[index], tile_of(entry), entry[1], False)
                    return [[sums[index, parity, t + 1] for t in range(TILES)] for parity in range(2)]

                def weight_of(entry):
                    return functools.partial(weight_tile, weights, entry[2])

                def field_of(field, entry):
                    return lambda t: staged_tile(staged.at[entry[0]], field, t) * weight_tile(weights, entry[2], t)

                inverse = [[1.0 / piece for piece in rows] for rows in joined(total, FIELDS, weight_of)]
                for field in range(FIELDS):
                    pieces = joined(half[field], field, functools.partial(field_of, field))
                    for parity in range(2):
                        for t in range(TILES):
                            lines[field, t, pl.ds(ROWS * i + parity, PAIRS, stride=2), :] = (
                                pieces[parity][t] * inverse[parity][t]
                            )

            either_kind(z, lists[0][0, 1, first + j] >= 0, body)
            return carry

        lax.fori_loop(0, QUAD, region, 0)
        for field in range(FIELDS):
            for t in range(TILES):
                turned[field, LANES * t : LANES * (t + 1), :] = lax.dot_general(
                    identity,
                    lines[field, t].astype(jnp.bfloat16),
                    (((1,), (1,)), ((), ())),
                    preferred_element_type=jnp.float32,
                )
        for i, offset in enumerate(z.offsets):
            target = blocks.at[i, quad] if i else outs[0].at[quad]
            dest = me ^ offset
            top = dest * z.width
            if z.width % 8 == 0:
                top = pl.multiple_of(top, 8)
            for low in range(0, FIELDS, 2):
                block = [turned[field, pl.ds(top, z.span), :] for field in (low, low + 1)]
                target[low * z.span : (low + 2) * z.span, :] = jnp.concatenate(block, 0).astype(jnp.bfloat16)
            ends = (jnp.maximum(top - 1, 0), jnp.minimum(top + z.width, COLS - 1))
            edge = [turned[field, pl.ds(end, 1), :] for field in range(FIELDS) for end in ends]
            target[z.main : z.sent, :] = jnp.concatenate(edge, 0).astype(jnp.bfloat16)
            if i:
                send(i, quad).start()
    for quad in range(z.quads):
        for i in range(1, z.regions):
            send(i, quad).wait()


def join(z, place, lists, received, shares):
    smem = pl.BlockSpec(memory_space=pltpu.SMEM)
    vmem = pl.BlockSpec(memory_space=pltpu.VMEM)
    hbm = pl.BlockSpec(memory_space=pltpu.HBM)
    shape = (z.quads, z.sent, LANES)
    return pl.pallas_call(
        functools.partial(join_kernel, z),
        out_shape=[jax.ShapeDtypeStruct(shape, jnp.bfloat16)]
        + [pltpu.HBM(shape, jnp.bfloat16)] * (z.regions - 1),
        in_specs=[smem] * (1 + z.makers) + [vmem] * (z.makers - 1 + len(shares)),
        out_specs=[vmem] + [hbm] * (z.regions - 1),
        scratch_shapes=[
            pltpu.VMEM((CAP * (z.makers - 1), LINES, LANES), jnp.float32),
            pltpu.VMEM((FIELDS + 1, 2, SLOTS, PAIRS, LANES), jnp.float32),
            pltpu.VMEM((FIELDS, TILES, LANES, LANES), jnp.float32),
            pltpu.VMEM((FIELDS, COLS + 8, LANES), jnp.float32),
            pltpu.VMEM((z.regions, *shape), jnp.bfloat16),
            pltpu.SemaphoreType.DMA((z.regions, z.quads)),
        ],
        compiler_params=pltpu.CompilerParams(vmem_limit_bytes=VMEM),
        cost_estimate=pl.CostEstimate(flops=5_000_000, bytes_accessed=8_000_000, transcendentals=0),
        name="join",
    )(place, *lists, *received, *shares)


SORT_STEPS = (
    ((0, 1), (2, 3), (4, 5), (6, 7)),
    ((0, 2), (1, 3), (4, 6), (5, 7)),
    ((1, 2), (5, 6)),
    ((0, 4), (1, 5), (2, 6), (3, 7)),
    ((2, 4), (3, 5)),
    ((1, 2), (3, 4), (5, 6)),
)
STEP_FIELDS = 2


def score_kernel(z, place, *refs):
    blocks = dict(zip(z.offsets, refs))
    strength, analysis, crps, spread, edges, padded = refs[z.regions :]
    me = place[0]
    step = pl.program_id(0)
    rows = z.rows

    def lanes_of(offset, quad):
        at = (lax.rem(me ^ offset, z.makers) * z.quads + quad) * LANES
        return pl.ds(pl.multiple_of(at, LANES), LANES)

    @pl.when(step == 0)
    def _():
        for offset in range(z.regions):
            for quad in range(z.quads):
                edges[offset // z.makers, :, lanes_of(offset, quad)] = blocks[offset][
                    quad, z.main : z.sent, :
                ].astype(jnp.float32)

    top = pl.multiple_of(step * STEP_FIELDS * z.span, 16)
    for offset in range(z.regions):
        for quad in range(z.quads):
            values = blocks[offset][quad, pl.ds(top, STEP_FIELDS * z.span), :].astype(jnp.float32)
            for f in range(STEP_FIELDS):
                padded[offset // z.makers, f, 8 : 8 + z.span, lanes_of(offset, quad)] = values[
                    f * z.span : (f + 1) * z.span
                ]
    for sample in range(SAMPLES):
        for f in range(STEP_FIELDS):
            low = 2 * (step * STEP_FIELDS + f)
            padded[sample, f, 7:8, :] = edges[sample, pl.ds(low, 1), :]
            padded[sample, f, 8 + z.width : 9 + z.width, :] = edges[sample, pl.ds(low + 1, 1), :]
    for f in range(STEP_FIELDS):
        target_field = analysis[f].astype(jnp.float32)
        for low in range(0, z.width, 16):
            high = min(low + 16, z.width)
            lane = lax.broadcasted_iota(jnp.int32, (high - low, LANES), 1)
            strong = strength[low:high, :]
            members = []
            for sample in range(SAMPLES):
                here = padded[sample, f, 8 + low : 8 + high, :]
                sides = padded[sample, f, 7 + low : 7 + high, :] + padded[sample, f, 9 + low : 9 + high, :]
                pieces = [here[:, at : at + LANES] for at in range(0, rows, LANES)]
                later = [pltpu.roll(piece, 1, 1) for piece in pieces]
                sooner = [pltpu.roll(piece, LANES - 1, 1) for piece in pieces]
                above = [jnp.where(lane == 0, a, b) for a, b in zip([pieces[0]] + later[:-1], later)]
                below = [jnp.where(lane == LANES - 1, a, b) for a, b in zip(sooner[1:] + [pieces[-1]], sooner)]
                along = jnp.concatenate([a + b for a, b in zip(above, below)], 1)
                smooth = here + strong * (along + sides - 4.0 * here)
                members.append(smooth.astype(jnp.bfloat16))
            values = [member.astype(jnp.float32) for member in members]
            target = target_field[low:high]
            error = sum(jnp.abs(value - target) for value in values) * (1.0 / SAMPLES)
            average = sum(values) * (1.0 / SAMPLES)
            variance = sum((value - average) ** 2 for value in values) * (1.0 / (SAMPLES - 1.0))
            ranked = list(members)
            for pairs in SORT_STEPS:
                for a, b in pairs:
                    ranked[a], ranked[b] = jnp.minimum(ranked[a], ranked[b]), jnp.maximum(ranked[a], ranked[b])
            ranked = [member.astype(jnp.float32) for member in ranked]
            pairs = sum(
                (2 * k - SAMPLES + 1.0) * (ranked[k] - ranked[SAMPLES - 1 - k])
                for k in range(SAMPLES // 2, SAMPLES)
            )
            crps[f, low:high, :] = (error - pairs * (1.0 / (SAMPLES * SAMPLES))).astype(jnp.bfloat16)
            spread[0, f, low:high, :] = variance.astype(jnp.bfloat16)
            spread[1, f, low:high, :] = ((average - target) ** 2).astype(jnp.bfloat16)


def score(z, place, blocks, strength, analysis):
    width, rows = z.width, z.rows
    return pl.pallas_call(
        functools.partial(score_kernel, z),
        out_shape=[
            jax.ShapeDtypeStruct((FIELDS, width, rows), jnp.bfloat16),
            jax.ShapeDtypeStruct((2, FIELDS, width, rows), jnp.bfloat16),
        ],
        grid=(FIELDS // STEP_FIELDS,),
        in_specs=[pl.BlockSpec(memory_space=pltpu.SMEM)]
        + [pl.BlockSpec(memory_space=pltpu.VMEM)] * (z.regions + 1)
        + [pl.BlockSpec((STEP_FIELDS, width, rows), lambda i: (i, 0, 0))],
        out_specs=[
            pl.BlockSpec((STEP_FIELDS, width, rows), lambda i: (i, 0, 0)),
            pl.BlockSpec((2, STEP_FIELDS, width, rows), lambda i: (0, i, 0, 0)),
        ],
        scratch_shapes=[
            pltpu.VMEM((SAMPLES, 8, rows), jnp.float32),
            pltpu.VMEM((SAMPLES, STEP_FIELDS, z.span + 16, rows), jnp.float32),
        ],
        compiler_params=pltpu.CompilerParams(vmem_limit_bytes=VMEM),
        name="score",
    )(place, *blocks, strength, analysis)


def shards(patch_tiles, slot_lists, blend_table, smoothing, analysis):
    z = Sizes(lax.axis_size("region"))
    place = lax.axis_index("region").reshape(1)
    turns = [
        [(i, i - i % z.makers + (i + k) % z.makers) for i in range(z.regions)] for k in range(1, z.makers)
    ]
    gathered = lax.all_gather((smoothing - MID).astype(jnp.bfloat16), "region", tiled=True)
    tiles = patch_tiles.reshape(z.regions, CAP, FIELDS, PAIRS * TILES, LANES)
    tiles = jnp.swapaxes(tiles, 2, 3).reshape(z.regions, CAP, LINES, LANES)
    lists = jnp.transpose(slot_lists, (2, 1, 0))
    received = [lax.ppermute(tiles, "region", turn) for turn in turns]
    lists = [lists] + [lax.ppermute(lists, "region", turn) for turn in turns]
    shares = own_share(z, place, lists[0], tiles, blend_table)
    blocks = join(z, place, lists, received, shares)
    moved = [blocks[0]] + [
        lax.ppermute(block, "region", [(i, i ^ offset) for i in range(z.regions)])
        for block, offset in zip(blocks[1:], z.offsets[1:])
    ]
    strength = own_strength(z, place, gathered)
    outs = score(z, place, moved, strength, jnp.swapaxes(analysis, 1, 2))
    return tuple(jnp.swapaxes(item, -1, -2) for item in outs)


def solution(mesh):
    return jax.shard_map(
        shards,
        mesh=mesh,
        in_specs=(
            P(("groups", "region"), None, None, None),
            P(("groups", "region"), None, None),
            P(),
            P("region", None),
            P(None, "groups", "region"),
        ),
        out_specs=(P(None, "groups", "region"), P(None, None, "groups", "region")),
        check_vma=False,
    )
```

```python
import functools

import jax
import jax.numpy as jnp
from jax import lax
from jax.experimental import pallas as pl
from jax.experimental.pallas import tpu as pltpu
from jax.sharding import PartitionSpec as P

SAMPLES = 8
FIELDS = 4
PATCH = 448
CAP = 2
ROWS = 32
COLS = 896
PAIRS = ROWS // 2
LINES = FIELDS * ROWS * PATCH // 128
LANES = 128
TILES = COLS // LANES
QUAD = LANES // ROWS
MID = 0.11
VMEM = 40 * 1024 * 1024
MOST_VMEM = 48 * 1024 * 1024


def round_up(value, step):
    return -(-value // step) * step


def swap_order(regions):
    far, near = list(range(regions // 2, regions)), list(range(1, regions // 2))
    near = near[regions // 4 - 1 :] + near[: regions // 4 - 1]
    return [0] + [item for pair in zip(far, near + [None]) for item in pair if item is not None]


class Sizes:
    def __init__(self, regions):
        self.regions = regions
        self.makers = regions // SAMPLES
        self.block = regions // self.makers
        self.quads = self.block // QUAD
        self.width = COLS // regions
        self.span = round_up(self.width, 8)
        self.rows = regions * ROWS
        self.main = round_up(FIELDS * self.span, 16)
        self.offsets = swap_order(regions)
        self.sent = self.main + 16


def stage(staged, tile):
    staged[...] = tile.astype(jnp.float32)


def staged_tile(staged, field, t):
    return staged[pl.ds(FIELDS * t + field, PAIRS, stride=FIELDS * TILES), :]


def weight_tile(weights, kind, t):
    return weights[t, pl.ds(pl.multiple_of(kind * PAIRS, PAIRS), PAIRS), :]


SLOTS = TILES + 2


def place_side(tile, column):
    pairs = jnp.concatenate([tile(t) for t in range(TILES)], 1)
    turned = pltpu.roll(pairs, PATCH, 1)
    lane = lax.broadcasted_iota(jnp.int32, pairs.shape, 1)
    left = (lane < PATCH) & (column == 0)
    right = (lane >= PATCH) & (column != 0)
    even = jnp.where(left, pairs, jnp.where(right, turned, 0.0))
    odd = jnp.where(left, turned, jnp.where(right, pairs, 0.0))
    return [[rows[:, LANES * t : LANES * (t + 1)] for t in range(TILES)] for rows in (even, odd)]


def add_any(sums, tile, column):
    lane = lax.broadcasted_iota(jnp.int32, (PAIRS, LANES), 1)
    middle = PATCH // LANES
    split = PATCH % LANES
    for parity in range(2):
        first = middle * parity
        start = column if parity == 0 else column + COLS - PATCH
        shift = lax.rem(start, LANES)
        at = lax.div(start, LANES) + first + 1 - (TILES if parity else 0)
        turned = []
        for t in range(first, first + middle + 1):
            piece = tile(t)
            if t == middle:
                piece = jnp.where((lane >= split) if parity else (lane < split), piece, 0.0)
            turned.append(pltpu.roll(piece, shift, 1))
        none = jnp.zeros((PAIRS, LANES), jnp.float32)
        for v in range(middle + 2):
            low = turned[v - 1] if v else none
            high = turned[v] if v <= middle else none
            sums[parity, at + v] = sums[parity, at + v] + jnp.where(lane < shift, low, high)


def place_all(side, sums, items):
    if side:
        placed = [place_side(*item) for item in items]
        return [[sum(item[parity][t] for item in placed) for t in range(TILES)] for parity in range(2)]
    for parity in range(2):
        for t in range(SLOTS):
            sums[parity, t] = jnp.zeros((PAIRS, LANES), jnp.float32)
    for item in items:
        add_any(sums, *item)
    return [[sums[parity, t + 1] for t in range(TILES)] for parity in range(2)]


def either_kind(z, heavy, body):
    @pl.when(heavy)
    def _():
        body(False, range(CAP))

    @pl.when(jnp.logical_not(heavy))
    def _():
        body(z.makers == 2, range(1))


def own_kernel(z, place, *refs):
    lists, (tiles, table_hbm), refs = refs[: z.makers], refs[z.makers : z.makers + 2], refs[z.makers + 2 :]
    half, (inverse, weights, landed, staged, sums, table, sems) = refs[:FIELDS], refs[FIELDS:]
    first = lax.rem(place[0], z.makers) * z.block

    def fetch(j):
        return pltpu.make_async_copy(tiles.at[first + j], landed.at[j], sems.at[j])

    fetch_table = pltpu.make_async_copy(table_hbm, table, sems.at[z.block])
    fetch_table.start()
    for j in range(z.block):
        fetch(j).start()
    fetch_table.wait()
    kinds = table.shape[0]
    for k in range(PAIRS):
        for t in range(TILES):
            at = COLS * k + LANES * t
            for low in range(0, kinds, 8):
                count = min(8, kinds - low)
                weights[t, pl.ds(PAIRS * low + k, count, stride=PAIRS), :] = table[
                    low : low + count, at : at + LANES
                ]

    def region(j, carry):
        fetch(j).wait()

        def body(side, slots):
            def weight_item(maker, slot):
                column, kind = (lists[maker][entry, slot, first + j] for entry in (1, 2))
                return functools.partial(weight_tile, weights, kind), column

            def field_item(field, slot):
                weight, column = weight_item(0, slot)
                return lambda t: staged_tile(staged.at[slot], field, t) * weight(t), column

            for slot in slots:
                stage(staged.at[slot], landed[j, slot])
            items = [weight_item(maker, slot) for maker in range(z.makers) for slot in slots]
            inverses = [[1.0 / piece for piece in rows] for rows in place_all(side, sums.at[FIELDS], items)]
            for parity in range(2):
                for t in range(TILES):
                    inverse[j, parity, t] = inverses[parity][t]
            for field in range(FIELDS):
                pieces = place_all(side, sums.at[field], [field_item(field, slot) for slot in slots])
                for parity in range(2):
                    for t in range(TILES):
                        half[field][j, parity, t] = pieces[parity][t] * inverses[parity][t]

        either_kind(z, lists[0][0, 1, first + j] >= 0, body)
        return carry

    lax.fori_loop(0, z.block, region, 0)


def own_share(z, place, lists, tiles, table):
    smem = pl.BlockSpec(memory_space=pltpu.SMEM)
    vmem = pl.BlockSpec(memory_space=pltpu.VMEM)
    hbm = pl.BlockSpec(memory_space=pltpu.HBM)
    kinds = round_up(table.shape[0], 8)
    return pl.pallas_call(
        functools.partial(own_kernel, z),
        out_shape=[
            *[jax.ShapeDtypeStruct((z.block, 2, TILES, PAIRS, LANES), jnp.float32)] * (FIELDS + 1),
            jax.ShapeDtypeStruct((TILES, kinds * PAIRS, LANES), jnp.float32),
        ],
        in_specs=[smem] * (1 + z.makers) + [hbm, hbm],
        out_specs=[vmem] * (FIELDS + 2),
        scratch_shapes=[
            pltpu.VMEM((z.block, CAP, LINES, LANES), jnp.bfloat16),
            pltpu.VMEM((CAP, LINES, LANES), jnp.float32),
            pltpu.VMEM((FIELDS + 1, 2, SLOTS, PAIRS, LANES), jnp.float32),
            pltpu.VMEM(table.shape, jnp.float32),
            pltpu.SemaphoreType.DMA((z.block + 1,)),
        ],
        compiler_params=pltpu.CompilerParams(vmem_limit_bytes=MOST_VMEM),
        cost_estimate=pl.CostEstimate(flops=5_000_000, bytes_accessed=8_000_000, transcendentals=0),
        name="own_share",
    )(place, *lists, tiles, table)


def strength_kernel(z, smoothing, _, strength):
    turned_strength = jnp.transpose(smoothing[...] - MID)
    for dest in range(z.regions):
        for g in range(z.span // 8):
            top = z.width * dest + 8 * g
            count, at = min(8, COLS - top), ROWS * (g % QUAD)
            strength[dest, g // QUAD, 0:count, at : at + ROWS] = turned_strength[top : top + count]


def strength_blocks(z, smoothing, before):
    return pl.pallas_call(
        functools.partial(strength_kernel, z),
        out_shape=jax.ShapeDtypeStruct((z.regions, z.quads, 8, LANES), jnp.float32),
        in_specs=[pl.BlockSpec(memory_space=pltpu.VMEM), pl.BlockSpec(memory_space=pl.ANY)],
        out_specs=pl.BlockSpec(memory_space=pltpu.VMEM),
        compiler_params=pltpu.CompilerParams(vmem_limit_bytes=VMEM),
        name="strength_blocks",
    )(smoothing, before)


def join_kernel(z, *refs):
    place, lists, refs = refs[0], refs[1 : 1 + z.makers], refs[1 + z.makers :]
    received, refs = refs[: z.makers - 1], refs[z.makers - 1 :]
    half, (inverse, weights, strength), outs = refs[:FIELDS], refs[FIELDS : FIELDS + 3], refs[FIELDS + 3 : -6]
    staged, sums, lines, turned, blocks, sems = refs[-6:]
    me = place[0]
    first = lax.rem(me, z.makers) * z.block
    row, column = (lax.broadcasted_iota(jnp.int32, (LANES, LANES), axis) for axis in (0, 1))
    identity = (row == column).astype(jnp.bfloat16)

    def send(i, quad):
        return pltpu.make_async_copy(blocks.at[i, quad], outs[i].at[quad], sems.at[i, quad])

    for quad in range(z.quads):

        def region(i, carry):
            j = quad * QUAD + i

            def body(side, slots):
                sources = [(maker, slot) for maker in range(1, z.makers) for slot in slots]

                def field_item(field, maker, slot):
                    column, kind = (lists[maker][entry, slot, first + j] for entry in (1, 2))
                    own = staged.at[(maker - 1) * CAP + slot]
                    return lambda t: staged_tile(own, field, t) * weight_tile(weights, kind, t), column

                for maker, slot in sources:
                    stage(staged.at[(maker - 1) * CAP + slot], received[maker - 1][first + j, slot])
                for field in range(FIELDS):
                    pieces = place_all(side, sums.at[field], [field_item(field, *source) for source in sources])
                    for parity in range(2):
                        for t in range(TILES):
                            lines[field, t, pl.ds(ROWS * i + parity, PAIRS, stride=2), :] = (
                                half[field][j, parity, t] + pieces[parity][t] * inverse[j, parity, t]
                            )

            either_kind(z, lists[0][0, 1, first + j] >= 0, body)
            return carry

        lax.fori_loop(0, QUAD, region, 0)
        for field in range(FIELDS):
            for t in range(TILES):
                turned[field, LANES * t : LANES * (t + 1), :] = lax.dot_general(
                    identity,
                    lines[field, t].astype(jnp.bfloat16),
                    (((1,), (1,)), ((), ())),
                    preferred_element_type=jnp.float32,
                )
        for i, offset in enumerate(z.offsets):
            target = blocks.at[i, quad] if i else outs[0].at[quad]
            dest = me ^ offset
            top = dest * z.width
            if z.width % 8 == 0:
                top = pl.multiple_of(top, 8)
            for low in range(0, FIELDS, 2):
                block = [turned[field, pl.ds(top, z.span), :] for field in (low, low + 1)]
                target[low * z.span : (low + 2) * z.span, :] = jnp.concatenate(block, 0).astype(jnp.bfloat16)
            ends = (jnp.maximum(top - 1, 0), jnp.minimum(top + z.width, COLS - 1))
            edge = [turned[field, pl.ds(end, 1), :] for field in range(FIELDS) for end in ends]
            edge.append(strength[dest, quad])
            target[z.main : z.sent, :] = jnp.concatenate(edge, 0).astype(jnp.bfloat16)
            if i:
                send(i, quad).start()
    for quad in range(z.quads):
        for i in range(1, z.regions):
            send(i, quad).wait()


def join(z, place, lists, received, shares):
    smem = pl.BlockSpec(memory_space=pltpu.SMEM)
    vmem = pl.BlockSpec(memory_space=pltpu.VMEM)
    hbm = pl.BlockSpec(memory_space=pltpu.HBM)
    shape = (z.quads, z.sent, LANES)
    return pl.pallas_call(
        functools.partial(join_kernel, z),
        out_shape=[jax.ShapeDtypeStruct(shape, jnp.bfloat16)]
        + [pltpu.HBM(shape, jnp.bfloat16)] * (z.regions - 1),
        in_specs=[smem] * (1 + z.makers) + [vmem] * (z.makers - 1 + len(shares)),
        out_specs=[vmem] + [hbm] * (z.regions - 1),
        scratch_shapes=[
            pltpu.VMEM((CAP * (z.makers - 1), LINES, LANES), jnp.float32),
            pltpu.VMEM((FIELDS, 2, SLOTS, PAIRS, LANES), jnp.float32),
            pltpu.VMEM((FIELDS, TILES, LANES, LANES), jnp.float32),
            pltpu.VMEM((FIELDS, COLS + 8, LANES), jnp.float32),
            pltpu.VMEM((z.regions, *shape), jnp.bfloat16),
            pltpu.SemaphoreType.DMA((z.regions, z.quads)),
        ],
        compiler_params=pltpu.CompilerParams(vmem_limit_bytes=VMEM),
        cost_estimate=pl.CostEstimate(flops=5_000_000, bytes_accessed=8_000_000, transcendentals=0),
        name="join",
    )(place, *lists, *received, *shares)


SORT_STEPS = (
    ((0, 1), (2, 3), (4, 5), (6, 7)),
    ((0, 2), (1, 3), (4, 6), (5, 7)),
    ((1, 2), (5, 6)),
    ((0, 4), (1, 5), (2, 6), (3, 7)),
    ((2, 4), (3, 5)),
    ((1, 2), (3, 4), (5, 6)),
)
STEP_FIELDS = 2


def score_kernel(z, place, *refs):
    blocks = dict(zip(z.offsets, refs))
    analysis, crps, spread, strength, edges, padded = refs[z.regions :]
    me = place[0]
    step = pl.program_id(0)
    rows = z.rows

    def tile_of(offset, quad):
        return lax.rem(me ^ offset, z.makers) * z.quads + quad

    @pl.when(step == 0)
    def _():
        slot = lax.broadcasted_iota(jnp.int32, (8, LANES), 1) // ROWS
        for low in range(0, z.regions, QUAD):
            offsets = range(low, low + QUAD)
            slots = [lax.rem(me ^ offset, QUAD) for offset in offsets]
            at = lax.div(me ^ low, QUAD)
            for quad in range(z.quads):
                tails = [blocks[offset][quad, z.main : z.sent, :].astype(jnp.float32) for offset in offsets]
                for offset, tail in zip(offsets, tails):
                    edges[offset // z.makers, tile_of(offset, quad)] = tail[0:8]
                for g in range(quad * QUAD, min((quad + 1) * QUAD, z.span // 8)):
                    joined = jnp.zeros((8, LANES), jnp.float32)
                    for i, tail in zip(slots, tails):
                        near = pltpu.roll(tail[8:16], lax.rem(i + QUAD - g % QUAD, QUAD) * ROWS, 1)
                        joined = jnp.where(slot == i, near, joined)
                    strength[at, 8 * g : 8 * (g + 1), :] = joined + MID

    top = pl.multiple_of(step * STEP_FIELDS * z.span, 16)
    for offset in range(z.regions):
        for quad in range(z.quads):
            values = blocks[offset][quad, pl.ds(top, STEP_FIELDS * z.span), :].astype(jnp.float32)
            for f in range(STEP_FIELDS):
                padded[offset // z.makers, f, tile_of(offset, quad), 8 : 8 + z.span, :] = values[
                    f * z.span : (f + 1) * z.span
                ]
    tiles = rows // LANES
    for sample in range(SAMPLES):
        for f in range(STEP_FIELDS):
            low = 2 * (step * STEP_FIELDS + f)
            for t in range(tiles):
                padded[sample, f, t, 7:8, :] = edges[sample, t, pl.ds(low, 1), :]
                padded[sample, f, t, 8 + z.width : 9 + z.width, :] = edges[sample, t, pl.ds(low + 1, 1), :]
    for f, low in ((f, low) for f in range(STEP_FIELDS) for low in range(0, z.width, 16)):
        high = min(low + 16, z.width)
        lane = lax.broadcasted_iota(jnp.int32, (high - low, LANES), 1)
        smoothed = [[] for _ in range(tiles)]
        for sample in range(SAMPLES):
            field = padded.at[sample, f]
            pieces = [field[t, 8 + low : 8 + high, :] for t in range(tiles)]
            later = [pltpu.roll(piece, 1, 1) for piece in pieces]
            sooner = [pltpu.roll(piece, LANES - 1, 1) for piece in pieces]
            for t, here in enumerate(pieces):
                above = jnp.where(lane == 0, later[t - 1] if t else here, later[t])
                below = jnp.where(lane == LANES - 1, sooner[t + 1] if t + 1 < tiles else here, sooner[t])
                sides = field[t, 7 + low : 7 + high, :] + field[t, 9 + low : 9 + high, :]
                smooth = here + strength[t, low:high, :] * (above + below + sides - 4.0 * here)
                smoothed[t].append(smooth.astype(jnp.bfloat16))
        for t, members in enumerate(smoothed):
            lanes = slice(LANES * t, LANES * (t + 1))
            values = [member.astype(jnp.float32) for member in members]
            target = analysis[f, low:high, lanes].astype(jnp.float32)
            error = sum(jnp.abs(value - target) for value in values) * (1.0 / SAMPLES)
            average = sum(values) * (1.0 / SAMPLES)
            variance = sum((value - average) ** 2 for value in values) * (1.0 / (SAMPLES - 1.0))
            ranked = list(members)
            for pairs in SORT_STEPS:
                for a, b in pairs:
                    ranked[a], ranked[b] = jnp.minimum(ranked[a], ranked[b]), jnp.maximum(ranked[a], ranked[b])
            ranked = [member.astype(jnp.float32) for member in ranked]
            pairs = sum(
                (2 * k - SAMPLES + 1.0) * (ranked[k] - ranked[SAMPLES - 1 - k])
                for k in range(SAMPLES // 2, SAMPLES)
            )
            crps[f, low:high, lanes] = (error - pairs * (1.0 / (SAMPLES * SAMPLES))).astype(jnp.bfloat16)
            spread[0, f, low:high, lanes] = variance.astype(jnp.bfloat16)
            spread[1, f, low:high, lanes] = ((average - target) ** 2).astype(jnp.bfloat16)


def score(z, place, blocks, analysis):
    width, rows = z.width, z.rows
    return pl.pallas_call(
        functools.partial(score_kernel, z),
        out_shape=[
            jax.ShapeDtypeStruct((FIELDS, width, rows), jnp.bfloat16),
            jax.ShapeDtypeStruct((2, FIELDS, width, rows), jnp.bfloat16),
        ],
        grid=(FIELDS // STEP_FIELDS,),
        in_specs=[pl.BlockSpec(memory_space=pltpu.SMEM)]
        + [pl.BlockSpec(memory_space=pltpu.VMEM)] * z.regions
        + [pl.BlockSpec((STEP_FIELDS, width, rows), lambda i: (i, 0, 0))],
        out_specs=[
            pl.BlockSpec((STEP_FIELDS, width, rows), lambda i: (i, 0, 0)),
            pl.BlockSpec((2, STEP_FIELDS, width, rows), lambda i: (0, i, 0, 0)),
        ],
        scratch_shapes=[
            pltpu.VMEM((rows // LANES, z.span, LANES), jnp.float32),
            pltpu.VMEM((SAMPLES, rows // LANES, 8, LANES), jnp.float32),
            pltpu.VMEM((SAMPLES, STEP_FIELDS, rows // LANES, z.span + 16, LANES), jnp.float32),
        ],
        compiler_params=pltpu.CompilerParams(vmem_limit_bytes=VMEM),
        name="score",
    )(place, *blocks, analysis)


def shards(patch_tiles, slot_lists, blend_table, smoothing, analysis):
    z = Sizes(lax.axis_size("region"))
    place = lax.axis_index("region").reshape(1)
    turns = [
        [(i, i - i % z.makers + (i + k) % z.makers) for i in range(z.regions)] for k in range(1, z.makers)
    ]
    tiles = patch_tiles.reshape(z.regions, CAP, FIELDS, PAIRS * TILES, LANES)
    tiles = jnp.swapaxes(tiles, 2, 3).reshape(z.regions, CAP, LINES, LANES)
    lists = jnp.transpose(slot_lists, (2, 1, 0))
    received = [lax.ppermute(tiles, "region", turn) for turn in turns]
    lists = [lists] + [lax.ppermute(lists, "region", turn) for turn in turns]
    shares = own_share(z, place, lists, tiles, blend_table)
    shares = [*shares, strength_blocks(z, smoothing, shares[-1])]
    blocks = join(z, place, lists, received, shares)
    moved = [blocks[0]] + [
        lax.ppermute(block, "region", [(i, i ^ offset) for i in range(z.regions)])
        for block, offset in zip(blocks[1:], z.offsets[1:])
    ]
    outs = score(z, place, moved, jnp.swapaxes(analysis, 1, 2))
    return tuple(jnp.swapaxes(item, -1, -2) for item in outs)


def solution(mesh):
    return jax.shard_map(
        shards,
        mesh=mesh,
        in_specs=(
            P(("groups", "region"), None, None, None),
            P(("groups", "region"), None, None),
            P(),
            P("region", None),
            P(None, "groups", "region"),
        ),
        out_specs=(P(None, "groups", "region"), P(None, None, "groups", "region")),
        check_vma=False,
    )
```

```python
import functools

import jax
import jax.numpy as jnp
from jax import lax
from jax.experimental import pallas as pl
from jax.experimental.pallas import tpu as pltpu
from jax.sharding import PartitionSpec as P

SAMPLES = 8
FIELDS = 4
PATCH = 448
CAP = 2
ROWS = 32
COLS = 896
PAIRS = ROWS // 2
LINES = FIELDS * ROWS * PATCH // 128
LANES = 128
TILES = COLS // LANES
QUAD = LANES // ROWS
MID = 0.11
VMEM = 40 * 1024 * 1024
MOST_VMEM = 48 * 1024 * 1024


def round_up(value, step):
    return -(-value // step) * step


def swap_order(regions):
    half, quarter = regions // 2, regions // 4
    far = [offset for i in range(quarter) for offset in (half + quarter + i, half + i)]
    near = list(range(quarter, half)) + list(range(1, quarter))
    return [0] + [item for pair in zip(far, near + [None]) for item in pair if item is not None]


class Sizes:
    def __init__(self, regions):
        self.regions = regions
        self.makers = regions // SAMPLES
        self.block = regions // self.makers
        self.quads = self.block // QUAD
        self.width = COLS // regions
        self.span = round_up(self.width, 8)
        self.rows = regions * ROWS
        self.main = round_up(FIELDS * self.span, 16)
        self.offsets = swap_order(regions)
        self.sent = self.main + 16


def stage(staged, tile):
    staged[...] = tile.astype(jnp.float32)


def staged_tile(staged, field, t):
    return staged[pl.ds(FIELDS * t + field, PAIRS, stride=FIELDS * TILES), :]


def weight_tile(weights, kind, t):
    return weights[t, pl.ds(pl.multiple_of(kind * PAIRS, PAIRS), PAIRS), :]


SLOTS = TILES + 2


def place_side(tile, column):
    pairs = jnp.concatenate([tile(t) for t in range(TILES)], 1)
    turned = pltpu.roll(pairs, PATCH, 1)
    lane = lax.broadcasted_iota(jnp.int32, pairs.shape, 1)
    left = (lane < PATCH) & (column == 0)
    right = (lane >= PATCH) & (column != 0)
    even = jnp.where(left, pairs, jnp.where(right, turned, 0.0))
    odd = jnp.where(left, turned, jnp.where(right, pairs, 0.0))
    return [[rows[:, LANES * t : LANES * (t + 1)] for t in range(TILES)] for rows in (even, odd)]


def add_any(sums, tile, column):
    lane = lax.broadcasted_iota(jnp.int32, (PAIRS, LANES), 1)
    middle = PATCH // LANES
    split = PATCH % LANES
    for parity in range(2):
        first = middle * parity
        start = column if parity == 0 else column + COLS - PATCH
        shift = lax.rem(start, LANES)
        at = lax.div(start, LANES) + first + 1 - (TILES if parity else 0)
        turned = []
        for t in range(first, first + middle + 1):
            piece = tile(t)
            if t == middle:
                piece = jnp.where((lane >= split) if parity else (lane < split), piece, 0.0)
            turned.append(pltpu.roll(piece, shift, 1))
        none = jnp.zeros((PAIRS, LANES), jnp.float32)
        for v in range(middle + 2):
            low = turned[v - 1] if v else none
            high = turned[v] if v <= middle else none
            sums[parity, at + v] = sums[parity, at + v] + jnp.where(lane < shift, low, high)


def place_all(side, sums, items):
    if side:
        placed = [place_side(*item) for item in items]
        return [[sum(item[parity][t] for item in placed) for t in range(TILES)] for parity in range(2)]
    for parity in range(2):
        for t in range(SLOTS):
            sums[parity, t] = jnp.zeros((PAIRS, LANES), jnp.float32)
    for item in items:
        add_any(sums, *item)
    return [[sums[parity, t + 1] for t in range(TILES)] for parity in range(2)]


def either_kind(z, heavy, body):
    @pl.when(heavy)
    def _():
        body(False, range(CAP))

    @pl.when(jnp.logical_not(heavy))
    def _():
        body(z.makers == 2, range(1))


def own_kernel(z, place, lists, tiles, table_hbm, *refs):
    half, (total, weights, landed, staged, sums, table, sems) = refs[:FIELDS], refs[FIELDS:]
    first = lax.rem(place[0], z.makers) * z.block

    def fetch(j):
        return pltpu.make_async_copy(tiles.at[first + j], landed.at[j], sems.at[j])

    fetch_table = pltpu.make_async_copy(table_hbm, table, sems.at[z.block])
    fetch_table.start()
    for j in range(z.block):
        fetch(j).start()
    fetch_table.wait()
    kinds = table.shape[0]
    for k in range(PAIRS):
        for t in range(TILES):
            at = COLS * k + LANES * t
            for low in range(0, kinds, 8):
                count = min(8, kinds - low)
                weights[t, pl.ds(PAIRS * low + k, count, stride=PAIRS), :] = table[
                    low : low + count, at : at + LANES
                ]

    def region(j, carry):
        fetch(j).wait()

        def body(side, slots):
            def weight_item(slot):
                column, kind = (lists[entry, slot, first + j] for entry in (1, 2))
                return functools.partial(weight_tile, weights, kind), column

            def field_item(field, slot):
                weight, column = weight_item(slot)
                return lambda t: staged_tile(staged.at[slot], field, t) * weight(t), column

            for slot in slots:
                stage(staged.at[slot], landed[j, slot])
            for index in range(FIELDS + 1):
                items = [field_item(index, slot) if index < FIELDS else weight_item(slot) for slot in slots]
                pieces = place_all(side, sums.at[index], items)
                target = half[index] if index < FIELDS else total
                for parity in range(2):
                    for t in range(TILES):
                        target[j, parity, t] = pieces[parity][t]

        either_kind(z, lists[0, 1, first + j] >= 0, body)
        return carry

    lax.fori_loop(0, z.block, region, 0)


def own_share(z, place, lists, tiles, table):
    smem = pl.BlockSpec(memory_space=pltpu.SMEM)
    vmem = pl.BlockSpec(memory_space=pltpu.VMEM)
    hbm = pl.BlockSpec(memory_space=pltpu.HBM)
    kinds = round_up(table.shape[0], 8)
    return pl.pallas_call(
        functools.partial(own_kernel, z),
        out_shape=[
            *[jax.ShapeDtypeStruct((z.block, 2, TILES, PAIRS, LANES), jnp.float32)] * (FIELDS + 1),
            jax.ShapeDtypeStruct((TILES, kinds * PAIRS, LANES), jnp.float32),
        ],
        in_specs=[smem, smem, hbm, hbm],
        out_specs=[vmem] * (FIELDS + 2),
        scratch_shapes=[
            pltpu.VMEM((z.block, CAP, LINES, LANES), jnp.bfloat16),
            pltpu.VMEM((CAP, LINES, LANES), jnp.float32),
            pltpu.VMEM((FIELDS + 1, 2, SLOTS, PAIRS, LANES), jnp.float32),
            pltpu.VMEM(table.shape, jnp.float32),
            pltpu.SemaphoreType.DMA((z.block + 1,)),
        ],
        compiler_params=pltpu.CompilerParams(vmem_limit_bytes=MOST_VMEM),
        cost_estimate=pl.CostEstimate(flops=5_000_000, bytes_accessed=8_000_000, transcendentals=0),
        name="own_share",
    )(place, lists, tiles, table)


def strength_kernel(z, smoothing, _, strength):
    turned_strength = jnp.transpose(smoothing[...] - MID)
    for dest in range(z.regions):
        for g in range(z.span // 8):
            top = z.width * dest + 8 * g
            count, at = min(8, COLS - top), ROWS * (g % QUAD)
            strength[dest, g // QUAD, 0:count, at : at + ROWS] = turned_strength[top : top + count]


def strength_blocks(z, smoothing, before):
    return pl.pallas_call(
        functools.partial(strength_kernel, z),
        out_shape=jax.ShapeDtypeStruct((z.regions, z.quads, 8, LANES), jnp.float32),
        in_specs=[pl.BlockSpec(memory_space=pltpu.VMEM), pl.BlockSpec(memory_space=pl.ANY)],
        out_specs=pl.BlockSpec(memory_space=pltpu.VMEM),
        compiler_params=pltpu.CompilerParams(vmem_limit_bytes=VMEM),
        name="strength_blocks",
    )(smoothing, before)


def join_kernel(z, *refs):
    place, lists, refs = refs[0], refs[1 : 1 + z.makers], refs[1 + z.makers :]
    received, refs = refs[: z.makers - 1], refs[z.makers - 1 :]
    half, (total, weights, strength), outs = refs[:FIELDS], refs[FIELDS : FIELDS + 3], refs[FIELDS + 3 : -6]
    staged, sums, lines, turned, blocks, sems = refs[-6:]
    me = place[0]
    first = lax.rem(me, z.makers) * z.block
    row, column = (lax.broadcasted_iota(jnp.int32, (LANES, LANES), axis) for axis in (0, 1))
    identity = (row == column).astype(jnp.bfloat16)

    def send(i, quad):
        return pltpu.make_async_copy(blocks.at[z.offsets[i], quad], outs[i].at[quad], sems.at[i, quad])

    def one_quad(quad, carry):
        def region(i, carry):
            j = quad * QUAD + i

            def body(side, slots):
                sources = [(maker, slot) for maker in range(1, z.makers) for slot in slots]

                def weight_item(maker, slot):
                    column, kind = (lists[maker][entry, slot, first + j] for entry in (1, 2))
                    return functools.partial(weight_tile, weights, kind), column

                def field_item(field, maker, slot):
                    weight, column = weight_item(maker, slot)
                    return lambda t: staged_tile(staged.at[(maker - 1) * CAP + slot], field, t) * weight(t), column

                for maker, slot in sources:
                    stage(staged.at[(maker - 1) * CAP + slot], received[maker - 1][first + j, slot])
                others = place_all(side, sums.at[FIELDS], [weight_item(*source) for source in sources])
                inverse = [[1.0 / (total[j, parity, t] + others[parity][t]) for t in range(TILES)] for parity in range(2)]
                for field in range(FIELDS):
                    pieces = place_all(side, sums.at[field], [field_item(field, *source) for source in sources])
                    for parity in range(2):
                        for t in range(TILES):
                            lines[field, t, pl.ds(ROWS * i + parity, PAIRS, stride=2), :] = (
                                half[field][j, parity, t] + pieces[parity][t]
                            ) * inverse[parity][t]

            either_kind(z, lists[0][0, 1, first + j] >= 0, body)
            return carry

        lax.fori_loop(0, QUAD, region, 0)

        def transpose(t, carry):
            for field in range(FIELDS):
                turned[field, pl.ds(pl.multiple_of(LANES * t, LANES), LANES), :] = lax.dot_general(
                    identity,
                    lines[field, t].astype(jnp.bfloat16),
                    (((1,), (1,)), ((), ())),
                    preferred_element_type=jnp.float32,
                )
            return carry

        lax.fori_loop(0, TILES, transpose, 0)

        def emit(dest, carry):
            target = blocks.at[me ^ dest, quad]
            top = dest * z.width
            if z.width % 8 == 0:
                top = pl.multiple_of(top, 8)
            for low in range(0, FIELDS, 2):
                block = [turned[field, pl.ds(top, z.span), :] for field in (low, low + 1)]
                target[low * z.span : (low + 2) * z.span, :] = jnp.concatenate(block, 0).astype(jnp.bfloat16)
            ends = (jnp.maximum(top - 1, 0), jnp.minimum(top + z.width, COLS - 1))
            edge = [turned[field, pl.ds(end, 1), :] for field in range(FIELDS) for end in ends]
            edge.append(strength[dest, quad])
            target[z.main : z.sent, :] = jnp.concatenate(edge, 0).astype(jnp.bfloat16)
            return carry

        lax.fori_loop(0, z.regions, emit, 0)
        for i in range(z.regions):
            send(i, quad).start()
        return carry

    lax.fori_loop(0, z.quads, one_quad, 0)
    for quad in range(z.quads):
        for i in range(z.regions):
            send(i, quad).wait()


def join(z, place, lists, received, shares):
    smem = pl.BlockSpec(memory_space=pltpu.SMEM)
    vmem = pl.BlockSpec(memory_space=pltpu.VMEM)
    hbm = pl.BlockSpec(memory_space=pltpu.HBM)
    shape = (z.quads, z.sent, LANES)
    return pl.pallas_call(
        functools.partial(join_kernel, z),
        out_shape=[jax.ShapeDtypeStruct(shape, jnp.bfloat16)]
        + [pltpu.HBM(shape, jnp.bfloat16)] * (z.regions - 1),
        in_specs=[smem] * (1 + z.makers) + [vmem] * (z.makers - 1 + len(shares)),
        out_specs=[vmem] + [hbm] * (z.regions - 1),
        scratch_shapes=[
            pltpu.VMEM((CAP * (z.makers - 1), LINES, LANES), jnp.float32),
            pltpu.VMEM((FIELDS + 1, 2, SLOTS, PAIRS, LANES), jnp.float32),
            pltpu.VMEM((FIELDS, TILES, LANES, LANES), jnp.float32),
            pltpu.VMEM((FIELDS, COLS + 8, LANES), jnp.float32),
            pltpu.VMEM((z.regions, *shape), jnp.bfloat16),
            pltpu.SemaphoreType.DMA((z.regions, z.quads)),
        ],
        compiler_params=pltpu.CompilerParams(vmem_limit_bytes=VMEM),
        cost_estimate=pl.CostEstimate(flops=5_000_000, bytes_accessed=8_000_000, transcendentals=0),
        name="join",
    )(place, *lists, *received, *shares)


SORT_STEPS = (
    ((0, 1), (2, 3), (4, 5), (6, 7)),
    ((0, 2), (1, 3), (4, 6), (5, 7)),
    ((1, 2), (5, 6)),
    ((0, 4), (1, 5), (2, 6), (3, 7)),
    ((2, 4), (3, 5)),
    ((1, 2), (3, 4), (5, 6)),
)
STEP_FIELDS = 2


def score_kernel(z, place, *refs):
    blocks = dict(zip(z.offsets, refs))
    analysis, crps, spread, strength, edges, padded = refs[z.regions :]
    me = place[0]
    step = pl.program_id(0)
    rows = z.rows

    def tile_of(offset, quad):
        return lax.rem(me ^ offset, z.makers) * z.quads + quad

    @pl.when(step == 0)
    def _():
        slot = lax.broadcasted_iota(jnp.int32, (8, LANES), 1) // ROWS
        for low in range(0, z.regions, QUAD):
            offsets = range(low, low + QUAD)
            slots = [lax.rem(me ^ offset, QUAD) for offset in offsets]
            at = lax.div(me ^ low, QUAD)
            for quad in range(z.quads):
                tails = [blocks[offset][quad, z.main : z.sent, :].astype(jnp.float32) for offset in offsets]
                for offset, tail in zip(offsets, tails):
                    edges[offset // z.makers, tile_of(offset, quad)] = tail[0:8]
                for g in range(quad * QUAD, min((quad + 1) * QUAD, z.span // 8)):
                    joined = jnp.zeros((8, LANES), jnp.float32)
                    for i, tail in zip(slots, tails):
                        near = pltpu.roll(tail[8:16], lax.rem(i + QUAD - g % QUAD, QUAD) * ROWS, 1)
                        joined = jnp.where(slot == i, near, joined)
                    strength[at, 8 * g : 8 * (g + 1), :] = joined + MID

    top = pl.multiple_of(step * STEP_FIELDS * z.span, 16)
    for offset in range(z.regions):
        for quad in range(z.quads):
            values = blocks[offset][quad, pl.ds(top, STEP_FIELDS * z.span), :].astype(jnp.float32)
            for f in range(STEP_FIELDS):
                padded[offset // z.makers, f, tile_of(offset, quad), 8 : 8 + z.span, :] = values[
                    f * z.span : (f + 1) * z.span
                ]
    tiles = rows // LANES
    for sample in range(SAMPLES):
        for f in range(STEP_FIELDS):
            low = 2 * (step * STEP_FIELDS + f)
            for t in range(tiles):
                padded[sample, f, t, 7:8, :] = edges[sample, t, pl.ds(low, 1), :]
                padded[sample, f, t, 8 + z.width : 9 + z.width, :] = edges[sample, t, pl.ds(low + 1, 1), :]
    def score_rows(f, low, count):
        lane = lax.broadcasted_iota(jnp.int32, (count, LANES), 1)
        here_rows = pl.ds(low, count)
        smoothed = [[] for _ in range(tiles)]
        for sample in range(SAMPLES):
            field = padded.at[sample, f]
            pieces = [field[t, pl.ds(8 + low, count), :] for t in range(tiles)]
            later = [pltpu.roll(piece, 1, 1) for piece in pieces]
            sooner = [pltpu.roll(piece, LANES - 1, 1) for piece in pieces]
            for t, here in enumerate(pieces):
                above = jnp.where(lane == 0, later[t - 1] if t else here, later[t])
                below = jnp.where(lane == LANES - 1, sooner[t + 1] if t + 1 < tiles else here, sooner[t])
                sides = field[t, pl.ds(7 + low, count), :] + field[t, pl.ds(9 + low, count), :]
                smooth = here + strength[t, here_rows, :] * (above + below + sides - 4.0 * here)
                smoothed[t].append(smooth.astype(jnp.bfloat16))
        for t, members in enumerate(smoothed):
            lanes = slice(LANES * t, LANES * (t + 1))
            values = [member.astype(jnp.float32) for member in members]
            target = analysis[f, here_rows, lanes].astype(jnp.float32)
            error = sum(jnp.abs(value - target) for value in values) * (1.0 / SAMPLES)
            average = sum(values) * (1.0 / SAMPLES)
            variance = sum((value - average) ** 2 for value in values) * (1.0 / (SAMPLES - 1.0))
            ranked = list(members)
            for pairs in SORT_STEPS:
                for a, b in pairs:
                    ranked[a], ranked[b] = jnp.minimum(ranked[a], ranked[b]), jnp.maximum(ranked[a], ranked[b])
            ranked = [member.astype(jnp.float32) for member in ranked]
            pairs = sum(
                (2 * k - SAMPLES + 1.0) * (ranked[k] - ranked[SAMPLES - 1 - k])
                for k in range(SAMPLES // 2, SAMPLES)
            )
            crps[f, here_rows, lanes] = (error - pairs * (1.0 / (SAMPLES * SAMPLES))).astype(jnp.bfloat16)
            spread[0, f, here_rows, lanes] = variance.astype(jnp.bfloat16)
            spread[1, f, here_rows, lanes] = ((average - target) ** 2).astype(jnp.bfloat16)

    def score_field(f, carry):
        groups = z.width // 16

        def group(g, carry):
            score_rows(f, pl.multiple_of(16 * g, 16), 16)
            return carry

        lax.fori_loop(0, groups, group, 0)
        if z.width % 16:
            score_rows(f, 16 * groups, z.width % 16)
        return carry

    lax.fori_loop(0, STEP_FIELDS, score_field, 0)


def score(z, place, blocks, analysis):
    width, rows = z.width, z.rows
    return pl.pallas_call(
        functools.partial(score_kernel, z),
        out_shape=[
            jax.ShapeDtypeStruct((FIELDS, width, rows), jnp.bfloat16),
            jax.ShapeDtypeStruct((2, FIELDS, width, rows), jnp.bfloat16),
        ],
        grid=(FIELDS // STEP_FIELDS,),
        in_specs=[pl.BlockSpec(memory_space=pltpu.SMEM)]
        + [pl.BlockSpec(memory_space=pltpu.VMEM)] * z.regions
        + [pl.BlockSpec((STEP_FIELDS, width, rows), lambda i: (i, 0, 0))],
        out_specs=[
            pl.BlockSpec((STEP_FIELDS, width, rows), lambda i: (i, 0, 0)),
            pl.BlockSpec((2, STEP_FIELDS, width, rows), lambda i: (0, i, 0, 0)),
        ],
        scratch_shapes=[
            pltpu.VMEM((rows // LANES, z.span, LANES), jnp.float32),
            pltpu.VMEM((SAMPLES, rows // LANES, 8, LANES), jnp.float32),
            pltpu.VMEM((SAMPLES, STEP_FIELDS, rows // LANES, z.span + 16, LANES), jnp.float32),
        ],
        compiler_params=pltpu.CompilerParams(vmem_limit_bytes=VMEM),
        name="score",
    )(place, *blocks, analysis)


def shards(patch_tiles, slot_lists, blend_table, smoothing, analysis):
    z = Sizes(lax.axis_size("region"))
    place = lax.axis_index("region").reshape(1)
    turns = [
        [(i, i - i % z.makers + (i + k) % z.makers) for i in range(z.regions)] for k in range(1, z.makers)
    ]
    tiles = patch_tiles.reshape(z.regions, CAP, FIELDS, PAIRS * TILES, LANES)
    tiles = jnp.swapaxes(tiles, 2, 3).reshape(z.regions, CAP, LINES, LANES)
    lists = jnp.transpose(slot_lists, (2, 1, 0))
    received = [lax.ppermute(tiles, "region", turn) for turn in turns]
    lists = [lists] + [lax.ppermute(lists, "region", turn) for turn in turns]
    shares = own_share(z, place, lists[0], tiles, blend_table)
    shares = [*shares, strength_blocks(z, smoothing, shares[-1])]
    blocks = join(z, place, lists, received, shares)
    moved = [blocks[0]] + [
        lax.ppermute(block, "region", [(i, i ^ offset) for i in range(z.regions)])
        for block, offset in zip(blocks[1:], z.offsets[1:])
    ]
    outs = score(z, place, moved, jnp.swapaxes(analysis, 1, 2))
    return tuple(jnp.swapaxes(item, -1, -2) for item in outs)


def solution(mesh):
    return jax.shard_map(
        shards,
        mesh=mesh,
        in_specs=(
            P(("groups", "region"), None, None, None),
            P(("groups", "region"), None, None),
            P(),
            P("region", None),
            P(None, "groups", "region"),
        ),
        out_specs=(P(None, "groups", "region"), P(None, None, "groups", "region")),
        check_vma=False,
    )
```

```python
import functools

import jax
import jax.numpy as jnp
from jax import lax
from jax.experimental import pallas as pl
from jax.experimental.pallas import tpu as pltpu
from jax.sharding import PartitionSpec as P

SAMPLES = 8
FIELDS = 4
PATCH = 448
CAP = 2
ROWS = 32
COLS = 896
PAIRS = ROWS // 2
LINES = FIELDS * ROWS * PATCH // 128
LANES = 128
TILES = COLS // LANES
QUAD = LANES // ROWS
MID = 0.11
VMEM = 40 * 1024 * 1024
MOST_VMEM = 48 * 1024 * 1024


def round_up(value, step):
    return -(-value // step) * step


def swap_order(regions):
    half, quarter = regions // 2, regions // 4
    far = [offset for i in range(quarter) for offset in (half + quarter + i, half + i)]
    near = list(range(quarter, half)) + list(range(1, quarter))
    return [0] + [item for pair in zip(far, near + [None]) for item in pair if item is not None]


class Sizes:
    def __init__(self, regions):
        self.regions = regions
        self.makers = regions // SAMPLES
        self.block = regions // self.makers
        self.quads = self.block // QUAD
        self.width = COLS // regions
        self.span = round_up(self.width, 8)
        self.rows = regions * ROWS
        self.main = round_up(FIELDS * self.span, 16)
        self.offsets = swap_order(regions)
        self.sent = self.main + 16


def stage(staged, tile):
    staged[...] = tile.astype(jnp.float32)


def staged_tile(staged, field, t):
    return staged[pl.ds(FIELDS * t + field, PAIRS, stride=FIELDS * TILES), :]


def weight_tile(weights, kind, t):
    return weights[t, pl.ds(pl.multiple_of(kind * PAIRS, PAIRS), PAIRS), :]


SLOTS = TILES + 2


def place_side(tile, column):
    pairs = jnp.concatenate([tile(t) for t in range(TILES)], 1)
    turned = pltpu.roll(pairs, PATCH, 1)
    lane = lax.broadcasted_iota(jnp.int32, pairs.shape, 1)
    left = (lane < PATCH) & (column == 0)
    right = (lane >= PATCH) & (column != 0)
    even = jnp.where(left, pairs, jnp.where(right, turned, 0.0))
    odd = jnp.where(left, turned, jnp.where(right, pairs, 0.0))
    return [[rows[:, LANES * t : LANES * (t + 1)] for t in range(TILES)] for rows in (even, odd)]


def add_any(sums, tile, column):
    lane = lax.broadcasted_iota(jnp.int32, (PAIRS, LANES), 1)
    middle = PATCH // LANES
    split = PATCH % LANES
    for parity in range(2):
        first = middle * parity
        start = column if parity == 0 else column + COLS - PATCH
        shift = lax.rem(start, LANES)
        at = lax.div(start, LANES) + first + 1 - (TILES if parity else 0)
        turned = []
        for t in range(first, first + middle + 1):
            piece = tile(t)
            if t == middle:
                piece = jnp.where((lane >= split) if parity else (lane < split), piece, 0.0)
            turned.append(pltpu.roll(piece, shift, 1))
        none = jnp.zeros((PAIRS, LANES), jnp.float32)
        for v in range(middle + 2):
            low = turned[v - 1] if v else none
            high = turned[v] if v <= middle else none
            sums[parity, at + v] = sums[parity, at + v] + jnp.where(lane < shift, low, high)


def place_all(side, sums, items):
    if side:
        placed = [place_side(*item) for item in items]
        return [[sum(item[parity][t] for item in placed) for t in range(TILES)] for parity in range(2)]
    for parity in range(2):
        for t in range(SLOTS):
            sums[parity, t] = jnp.zeros((PAIRS, LANES), jnp.float32)
    for item in items:
        add_any(sums, *item)
    return [[sums[parity, t + 1] for t in range(TILES)] for parity in range(2)]


def either_kind(z, heavy, body):
    @pl.when(heavy)
    def _():
        body(False, range(CAP))

    @pl.when(jnp.logical_not(heavy))
    def _():
        body(z.makers == 2, range(1))


def own_kernel(z, place, lists, tiles, table_hbm, *refs):
    half, (total, weights, landed, staged, sums, table, sems) = refs[:FIELDS], refs[FIELDS:]
    first = lax.rem(place[0], z.makers) * z.block

    def fetch(j):
        return pltpu.make_async_copy(tiles.at[first + j], landed.at[j], sems.at[j])

    fetch_table = pltpu.make_async_copy(table_hbm, table, sems.at[z.block])
    fetch_table.start()
    for j in range(z.block):
        fetch(j).start()
    fetch_table.wait()
    kinds = table.shape[0]
    for k in range(PAIRS):
        for t in range(TILES):
            at = COLS * k + LANES * t
            for low in range(0, kinds, 8):
                count = min(8, kinds - low)
                weights[t, pl.ds(PAIRS * low + k, count, stride=PAIRS), :] = table[
                    low : low + count, at : at + LANES
                ]

    def region(j, carry):
        fetch(j).wait()

        def body(side, slots):
            def weight_item(slot):
                column, kind = (lists[entry, slot, first + j] for entry in (1, 2))
                return functools.partial(weight_tile, weights, kind), column

            def field_item(field, slot):
                weight, column = weight_item(slot)
                return lambda t: staged_tile(staged.at[slot], field, t) * weight(t), column

            for slot in slots:
                stage(staged.at[slot], landed[j, slot])
            for index in range(FIELDS + 1):
                items = [field_item(index, slot) if index < FIELDS else weight_item(slot) for slot in slots]
                pieces = place_all(side, sums.at[index], items)
                target = half[index] if index < FIELDS else total
                for parity in range(2):
                    for t in range(TILES):
                        target[j, parity, t] = pieces[parity][t]

        either_kind(z, lists[0, 1, first + j] >= 0, body)
        return carry

    lax.fori_loop(0, z.block, region, 0)


def own_share(z, place, lists, tiles, table):
    smem = pl.BlockSpec(memory_space=pltpu.SMEM)
    vmem = pl.BlockSpec(memory_space=pltpu.VMEM)
    hbm = pl.BlockSpec(memory_space=pltpu.HBM)
    kinds = round_up(table.shape[0], 8)
    return pl.pallas_call(
        functools.partial(own_kernel, z),
        out_shape=[
            *[jax.ShapeDtypeStruct((z.block, 2, TILES, PAIRS, LANES), jnp.float32)] * (FIELDS + 1),
            jax.ShapeDtypeStruct((TILES, kinds * PAIRS, LANES), jnp.float32),
        ],
        in_specs=[smem, smem, hbm, hbm],
        out_specs=[vmem] * (FIELDS + 2),
        scratch_shapes=[
            pltpu.VMEM((z.block, CAP, LINES, LANES), jnp.bfloat16),
            pltpu.VMEM((CAP, LINES, LANES), jnp.float32),
            pltpu.VMEM((FIELDS + 1, 2, SLOTS, PAIRS, LANES), jnp.float32),
            pltpu.VMEM(table.shape, jnp.float32),
            pltpu.SemaphoreType.DMA((z.block + 1,)),
        ],
        compiler_params=pltpu.CompilerParams(vmem_limit_bytes=MOST_VMEM),
        cost_estimate=pl.CostEstimate(flops=5_000_000, bytes_accessed=8_000_000, transcendentals=0),
        name="own_share",
    )(place, lists, tiles, table)


def strength_kernel(z, smoothing, _, strength):
    turned_strength = jnp.transpose(smoothing[...] - MID)
    for dest in range(z.regions):
        for g in range(z.span // 8):
            top = z.width * dest + 8 * g
            count, at = min(8, COLS - top), ROWS * (g % QUAD)
            strength[dest, g // QUAD, 0:count, at : at + ROWS] = turned_strength[top : top + count]


def strength_blocks(z, smoothing, before):
    return pl.pallas_call(
        functools.partial(strength_kernel, z),
        out_shape=jax.ShapeDtypeStruct((z.regions, z.quads, 8, LANES), jnp.float32),
        in_specs=[pl.BlockSpec(memory_space=pltpu.VMEM), pl.BlockSpec(memory_space=pl.ANY)],
        out_specs=pl.BlockSpec(memory_space=pltpu.VMEM),
        compiler_params=pltpu.CompilerParams(vmem_limit_bytes=VMEM),
        name="strength_blocks",
    )(smoothing, before)


def join_kernel(z, *refs):
    place, lists, refs = refs[0], refs[1 : 1 + z.makers], refs[1 + z.makers :]
    received, refs = refs[: z.makers - 1], refs[z.makers - 1 :]
    half, (total, weights, strength), outs = refs[:FIELDS], refs[FIELDS : FIELDS + 3], refs[FIELDS + 3 : -4]
    staged, sums, lines, turned = refs[-4:]
    me = place[0]
    first = lax.rem(me, z.makers) * z.block
    row, column = (lax.broadcasted_iota(jnp.int32, (LANES, LANES), axis) for axis in (0, 1))
    identity = (row == column).astype(jnp.bfloat16)

    for quad in range(z.quads):

        def region(i, carry):
            j = quad * QUAD + i

            def body(side, slots):
                sources = [(maker, slot) for maker in range(1, z.makers) for slot in slots]

                def weight_item(maker, slot):
                    column, kind = (lists[maker][entry, slot, first + j] for entry in (1, 2))
                    return functools.partial(weight_tile, weights, kind), column

                def field_item(field, maker, slot):
                    weight, column = weight_item(maker, slot)
                    return lambda t: staged_tile(staged.at[(maker - 1) * CAP + slot], field, t) * weight(t), column

                for maker, slot in sources:
                    stage(staged.at[(maker - 1) * CAP + slot], received[maker - 1][first + j, slot])
                others = place_all(side, sums.at[FIELDS], [weight_item(*source) for source in sources])
                inverse = [[1.0 / (total[j, parity, t] + others[parity][t]) for t in range(TILES)] for parity in range(2)]
                for field in range(FIELDS):
                    pieces = place_all(side, sums.at[field], [field_item(field, *source) for source in sources])
                    for parity in range(2):
                        for t in range(TILES):
                            lines[field, t, pl.ds(ROWS * i + parity, PAIRS, stride=2), :] = (
                                half[field][j, parity, t] + pieces[parity][t]
                            ) * inverse[parity][t]

            either_kind(z, lists[0][0, 1, first + j] >= 0, body)
            return carry

        lax.fori_loop(0, QUAD, region, 0)

        for field in range(FIELDS):
            for t in range(TILES):
                turned[field, LANES * t : LANES * (t + 1), :] = lax.dot_general(
                    identity,
                    lines[field, t].astype(jnp.bfloat16),
                    (((1,), (1,)), ((), ())),
                    preferred_element_type=jnp.float32,
                )
        for out, offset in zip(outs, z.offsets):
            dest = me ^ offset
            top = dest * z.width
            if z.width % 8 == 0:
                top = pl.multiple_of(top, 8)
            for low in range(0, FIELDS, 2):
                block = [turned[field, pl.ds(top, z.span), :] for field in (low, low + 1)]
                out[quad, low * z.span : (low + 2) * z.span, :] = jnp.concatenate(block, 0).astype(jnp.bfloat16)
            ends = (jnp.maximum(top - 1, 0), jnp.minimum(top + z.width, COLS - 1))
            edge = [turned[field, pl.ds(end, 1), :] for field in range(FIELDS) for end in ends]
            edge.append(strength[dest, quad])
            out[quad, z.main : z.sent, :] = jnp.concatenate(edge, 0).astype(jnp.bfloat16)


def join(z, place, lists, received, shares):
    smem = pl.BlockSpec(memory_space=pltpu.SMEM)
    vmem = pl.BlockSpec(memory_space=pltpu.VMEM)
    shape = (z.quads, z.sent, LANES)
    return pl.pallas_call(
        functools.partial(join_kernel, z),
        out_shape=[jax.ShapeDtypeStruct(shape, jnp.bfloat16)] * z.regions,
        in_specs=[smem] * (1 + z.makers) + [vmem] * (z.makers - 1 + len(shares)),
        out_specs=[vmem] * z.regions,
        scratch_shapes=[
            pltpu.VMEM((CAP * (z.makers - 1), LINES, LANES), jnp.float32),
            pltpu.VMEM((FIELDS + 1, 2, SLOTS, PAIRS, LANES), jnp.float32),
            pltpu.VMEM((FIELDS, TILES, LANES, LANES), jnp.float32),
            pltpu.VMEM((FIELDS, COLS + 8, LANES), jnp.float32),
        ],
        compiler_params=pltpu.CompilerParams(vmem_limit_bytes=VMEM),
        cost_estimate=pl.CostEstimate(flops=5_000_000, bytes_accessed=8_000_000, transcendentals=0),
        name="join",
    )(place, *lists, *received, *shares)


SORT_STEPS = (
    ((0, 1), (2, 3), (4, 5), (6, 7)),
    ((0, 2), (1, 3), (4, 6), (5, 7)),
    ((1, 2), (5, 6)),
    ((0, 4), (1, 5), (2, 6), (3, 7)),
    ((2, 4), (3, 5)),
    ((1, 2), (3, 4), (5, 6)),
)
STEP_FIELDS = 2


def score_kernel(z, place, *refs):
    blocks = dict(zip(z.offsets, refs))
    analysis, crps, spread, strength, edges, padded = refs[z.regions :]
    me = place[0]
    step = pl.program_id(0)
    rows = z.rows

    def tile_of(offset, quad):
        return lax.rem(me ^ offset, z.makers) * z.quads + quad

    @pl.when(step == 0)
    def _():
        slot = lax.broadcasted_iota(jnp.int32, (8, LANES), 1) // ROWS
        for low in range(0, z.regions, QUAD):
            offsets = range(low, low + QUAD)
            slots = [lax.rem(me ^ offset, QUAD) for offset in offsets]
            at = lax.div(me ^ low, QUAD)
            for quad in range(z.quads):
                tails = [blocks[offset][quad, z.main : z.sent, :].astype(jnp.float32) for offset in offsets]
                for offset, tail in zip(offsets, tails):
                    edges[offset // z.makers, tile_of(offset, quad)] = tail[0:8]
                for g in range(quad * QUAD, min((quad + 1) * QUAD, z.span // 8)):
                    joined = jnp.zeros((8, LANES), jnp.float32)
                    for i, tail in zip(slots, tails):
                        near = pltpu.roll(tail[8:16], lax.rem(i + QUAD - g % QUAD, QUAD) * ROWS, 1)
                        joined = jnp.where(slot == i, near, joined)
                    strength[at, 8 * g : 8 * (g + 1), :] = joined + MID

    top = pl.multiple_of(step * STEP_FIELDS * z.span, 16)
    for offset in range(z.regions):
        for quad in range(z.quads):
            values = blocks[offset][quad, pl.ds(top, STEP_FIELDS * z.span), :].astype(jnp.float32)
            for f in range(STEP_FIELDS):
                padded[offset // z.makers, f, tile_of(offset, quad), 8 : 8 + z.span, :] = values[
                    f * z.span : (f + 1) * z.span
                ]
    tiles = rows // LANES
    for sample in range(SAMPLES):
        for f in range(STEP_FIELDS):
            low = 2 * (step * STEP_FIELDS + f)
            for t in range(tiles):
                padded[sample, f, t, 7:8, :] = edges[sample, t, pl.ds(low, 1), :]
                padded[sample, f, t, 8 + z.width : 9 + z.width, :] = edges[sample, t, pl.ds(low + 1, 1), :]
    for f, low in ((f, low) for f in range(STEP_FIELDS) for low in range(0, z.width, 16)):
        high = min(low + 16, z.width)
        lane = lax.broadcasted_iota(jnp.int32, (high - low, LANES), 1)
        smoothed = [[] for _ in range(tiles)]
        for sample in range(SAMPLES):
            field = padded.at[sample, f]
            pieces = [field[t, 8 + low : 8 + high, :] for t in range(tiles)]
            later = [pltpu.roll(piece, 1, 1) for piece in pieces]
            sooner = [pltpu.roll(piece, LANES - 1, 1) for piece in pieces]
            for t, here in enumerate(pieces):
                above = jnp.where(lane == 0, later[t - 1] if t else here, later[t])
                below = jnp.where(lane == LANES - 1, sooner[t + 1] if t + 1 < tiles else here, sooner[t])
                sides = field[t, 7 + low : 7 + high, :] + field[t, 9 + low : 9 + high, :]
                smooth = here + strength[t, low:high, :] * (above + below + sides - 4.0 * here)
                smoothed[t].append(smooth.astype(jnp.bfloat16))
        for t, members in enumerate(smoothed):
            lanes = slice(LANES * t, LANES * (t + 1))
            values = [member.astype(jnp.float32) for member in members]
            target = analysis[f, low:high, lanes].astype(jnp.float32)
            error = sum(jnp.abs(value - target) for value in values) * (1.0 / SAMPLES)
            average = sum(values) * (1.0 / SAMPLES)
            variance = sum((value - average) ** 2 for value in values) * (1.0 / (SAMPLES - 1.0))
            ranked = list(members)
            for pairs in SORT_STEPS:
                for a, b in pairs:
                    ranked[a], ranked[b] = jnp.minimum(ranked[a], ranked[b]), jnp.maximum(ranked[a], ranked[b])
            ranked = [member.astype(jnp.float32) for member in ranked]
            pairs = sum(
                (2 * k - SAMPLES + 1.0) * (ranked[k] - ranked[SAMPLES - 1 - k])
                for k in range(SAMPLES // 2, SAMPLES)
            )
            crps[f, low:high, lanes] = (error - pairs * (1.0 / (SAMPLES * SAMPLES))).astype(jnp.bfloat16)
            spread[0, f, low:high, lanes] = variance.astype(jnp.bfloat16)
            spread[1, f, low:high, lanes] = ((average - target) ** 2).astype(jnp.bfloat16)


def score(z, place, blocks, analysis):
    width, rows = z.width, z.rows
    return pl.pallas_call(
        functools.partial(score_kernel, z),
        out_shape=[
            jax.ShapeDtypeStruct((FIELDS, width, rows), jnp.bfloat16),
            jax.ShapeDtypeStruct((2, FIELDS, width, rows), jnp.bfloat16),
        ],
        grid=(FIELDS // STEP_FIELDS,),
        in_specs=[pl.BlockSpec(memory_space=pltpu.SMEM)]
        + [pl.BlockSpec(memory_space=pltpu.VMEM)] * z.regions
        + [pl.BlockSpec((STEP_FIELDS, width, rows), lambda i: (i, 0, 0))],
        out_specs=[
            pl.BlockSpec((STEP_FIELDS, width, rows), lambda i: (i, 0, 0)),
            pl.BlockSpec((2, STEP_FIELDS, width, rows), lambda i: (0, i, 0, 0)),
        ],
        scratch_shapes=[
            pltpu.VMEM((rows // LANES, z.span, LANES), jnp.float32),
            pltpu.VMEM((SAMPLES, rows // LANES, 8, LANES), jnp.float32),
            pltpu.VMEM((SAMPLES, STEP_FIELDS, rows // LANES, z.span + 16, LANES), jnp.float32),
        ],
        compiler_params=pltpu.CompilerParams(vmem_limit_bytes=VMEM),
        name="score",
    )(place, *blocks, analysis)


def shards(patch_tiles, slot_lists, blend_table, smoothing, analysis):
    z = Sizes(lax.axis_size("region"))
    place = lax.axis_index("region").reshape(1)
    turns = [
        [(i, i - i % z.makers + (i + k) % z.makers) for i in range(z.regions)] for k in range(1, z.makers)
    ]
    tiles = patch_tiles.reshape(z.regions, CAP, FIELDS, PAIRS * TILES, LANES)
    tiles = jnp.swapaxes(tiles, 2, 3).reshape(z.regions, CAP, LINES, LANES)
    lists = jnp.transpose(slot_lists, (2, 1, 0))
    received = [lax.ppermute(tiles, "region", turn) for turn in turns]
    lists = [lists] + [lax.ppermute(lists, "region", turn) for turn in turns]
    shares = own_share(z, place, lists[0], tiles, blend_table)
    shares = [*shares, strength_blocks(z, smoothing, shares[-1])]
    blocks = join(z, place, lists, received, shares)
    moved = [blocks[0]] + [
        lax.ppermute(block, "region", [(i, i ^ offset) for i in range(z.regions)])
        for block, offset in zip(blocks[1:], z.offsets[1:])
    ]
    outs = score(z, place, moved, jnp.swapaxes(analysis, 1, 2))
    return tuple(jnp.swapaxes(item, -1, -2) for item in outs)


def solution(mesh):
    return jax.shard_map(
        shards,
        mesh=mesh,
        in_specs=(
            P(("groups", "region"), None, None, None),
            P(("groups", "region"), None, None),
            P(),
            P("region", None),
            P(None, "groups", "region"),
        ),
        out_specs=(P(None, "groups", "region"), P(None, None, "groups", "region")),
        check_vma=False,
    )
```

```python
import functools

import jax
import jax.numpy as jnp
from jax import lax
from jax.experimental import pallas as pl
from jax.experimental.pallas import tpu as pltpu
from jax.sharding import PartitionSpec as P

SAMPLES = 8
FIELDS = 4
PATCH = 448
CAP = 2
ROWS = 32
COLS = 896
PAIRS = ROWS // 2
LINES = FIELDS * ROWS * PATCH // 128
LANES = 128
TILES = COLS // LANES
QUAD = LANES // ROWS
MID = 0.11
VMEM = 40 * 1024 * 1024
MOST_VMEM = 48 * 1024 * 1024


def round_up(value, step):
    return -(-value // step) * step


def swap_order(regions):
    half, quarter = regions // 2, regions // 4
    far = [offset for i in range(quarter) for offset in (half + quarter + i, half + i)]
    near = list(range(quarter, half)) + list(range(1, quarter))
    return [0] + [item for pair in zip(far, near + [None]) for item in pair if item is not None]


class Sizes:
    def __init__(self, regions):
        self.regions = regions
        self.makers = regions // SAMPLES
        self.block = regions // self.makers
        self.quads = self.block // QUAD
        self.width = COLS // regions
        self.span = round_up(self.width, 8)
        self.rows = regions * ROWS
        self.main = round_up(FIELDS * self.span, 16)
        self.offsets = swap_order(regions)
        self.sent = self.main + 16


def stage(staged, tile):
    staged[...] = tile.astype(jnp.float32)


def staged_tile(staged, field, t):
    return staged[pl.ds(FIELDS * t + field, PAIRS, stride=FIELDS * TILES), :]


def weight_tile(weights, kind, t):
    return weights[t, pl.ds(pl.multiple_of(kind * PAIRS, PAIRS), PAIRS), :]


SLOTS = TILES + 2


def place_side(tile, column):
    pairs = jnp.concatenate([tile(t) for t in range(TILES)], 1)
    turned = pltpu.roll(pairs, PATCH, 1)
    lane = lax.broadcasted_iota(jnp.int32, pairs.shape, 1)
    left = (lane < PATCH) & (column == 0)
    right = (lane >= PATCH) & (column != 0)
    even = jnp.where(left, pairs, jnp.where(right, turned, 0.0))
    odd = jnp.where(left, turned, jnp.where(right, pairs, 0.0))
    return [[rows[:, LANES * t : LANES * (t + 1)] for t in range(TILES)] for rows in (even, odd)]


def add_any(sums, tile, column):
    lane = lax.broadcasted_iota(jnp.int32, (PAIRS, LANES), 1)
    middle = PATCH // LANES
    split = PATCH % LANES
    for parity in range(2):
        first = middle * parity
        start = column if parity == 0 else column + COLS - PATCH
        shift = lax.rem(start, LANES)
        at = lax.div(start, LANES) + first + 1 - (TILES if parity else 0)
        turned = []
        for t in range(first, first + middle + 1):
            piece = tile(t)
            if t == middle:
                piece = jnp.where((lane >= split) if parity else (lane < split), piece, 0.0)
            turned.append(pltpu.roll(piece, shift, 1))
        none = jnp.zeros((PAIRS, LANES), jnp.float32)
        for v in range(middle + 2):
            low = turned[v - 1] if v else none
            high = turned[v] if v <= middle else none
            sums[parity, at + v] = sums[parity, at + v] + jnp.where(lane < shift, low, high)


def place_all(side, sums, items):
    if side:
        placed = [place_side(*item) for item in items]
        return [[sum(item[parity][t] for item in placed) for t in range(TILES)] for parity in range(2)]
    for parity in range(2):
        for t in range(SLOTS):
            sums[parity, t] = jnp.zeros((PAIRS, LANES), jnp.float32)
    for item in items:
        add_any(sums, *item)
    return [[sums[parity, t + 1] for t in range(TILES)] for parity in range(2)]


def each_region(z, heavy, body):
    for i in range(QUAD):
        if z.makers == 2:
            body(i, True, range(1))
        else:
            pl.when(jnp.logical_not(heavy(i)))(functools.partial(body, i, False, range(1)))

    def again(i, carry):
        pl.when(heavy(i))(functools.partial(body, i, False, range(CAP)))
        return carry

    lax.fori_loop(0, QUAD, again, 0)


def staged_index(i, side, maker, slot, others):
    return i * others + maker if side else QUAD * others + maker * CAP + slot


def own_kernel(z, place, lists, tiles, table_hbm, *refs):
    half, (total, weights, landed, staged, sums, table, sems) = refs[:FIELDS], refs[FIELDS:]
    first = lax.rem(place[0], z.makers) * z.block

    def fetch(j):
        return pltpu.make_async_copy(tiles.at[first + j], landed.at[j], sems.at[j])

    fetch_table = pltpu.make_async_copy(table_hbm, table, sems.at[z.block])
    fetch_table.start()
    for j in range(z.block):
        fetch(j).start()
    fetch_table.wait()
    kinds = table.shape[0]
    for k in range(PAIRS):
        for t in range(TILES):
            at = COLS * k + LANES * t
            for low in range(0, kinds, 8):
                count = min(8, kinds - low)
                weights[t, pl.ds(PAIRS * low + k, count, stride=PAIRS), :] = table[
                    low : low + count, at : at + LANES
                ]

    def group(quad, carry):
        for i in range(QUAD):
            fetch(quad * QUAD + i).wait()

        def body(i, side, slots):
            j = quad * QUAD + i

            def weight_item(slot):
                column, kind = (lists[entry, slot, first + j] for entry in (1, 2))
                return functools.partial(weight_tile, weights, kind), column

            def field_item(field, slot):
                weight, column = weight_item(slot)
                own = staged.at[staged_index(i, side, 0, slot, 1)]
                return lambda t: staged_tile(own, field, t) * weight(t), column

            for slot in slots:
                stage(staged.at[staged_index(i, side, 0, slot, 1)], landed[j, slot])
            for index in range(FIELDS + 1):
                items = [field_item(index, slot) if index < FIELDS else weight_item(slot) for slot in slots]
                pieces = place_all(side, sums.at[index], items)
                target = half[index] if index < FIELDS else total
                for parity in range(2):
                    for t in range(TILES):
                        target[j, parity, t] = pieces[parity][t]

        each_region(z, lambda i: lists[0, 1, first + quad * QUAD + i] >= 0, body)
        return carry

    lax.fori_loop(0, z.quads, group, 0)


def own_share(z, place, lists, tiles, table):
    smem = pl.BlockSpec(memory_space=pltpu.SMEM)
    vmem = pl.BlockSpec(memory_space=pltpu.VMEM)
    hbm = pl.BlockSpec(memory_space=pltpu.HBM)
    kinds = round_up(table.shape[0], 8)
    return pl.pallas_call(
        functools.partial(own_kernel, z),
        out_shape=[
            *[jax.ShapeDtypeStruct((z.block, 2, TILES, PAIRS, LANES), jnp.float32)] * (FIELDS + 1),
            jax.ShapeDtypeStruct((TILES, kinds * PAIRS, LANES), jnp.float32),
        ],
        in_specs=[smem, smem, hbm, hbm],
        out_specs=[vmem] * (FIELDS + 2),
        scratch_shapes=[
            pltpu.VMEM((z.block, CAP, LINES, LANES), jnp.bfloat16),
            pltpu.VMEM((QUAD + CAP, LINES, LANES), jnp.float32),
            pltpu.VMEM((FIELDS + 1, 2, SLOTS, PAIRS, LANES), jnp.float32),
            pltpu.VMEM(table.shape, jnp.float32),
            pltpu.SemaphoreType.DMA((z.block + 1,)),
        ],
        compiler_params=pltpu.CompilerParams(vmem_limit_bytes=MOST_VMEM),
        cost_estimate=pl.CostEstimate(flops=5_000_000, bytes_accessed=8_000_000, transcendentals=0),
        name="own_share",
    )(place, lists, tiles, table)


def strength_kernel(z, smoothing, _, strength):
    turned_strength = jnp.transpose(smoothing[...] - MID)
    for dest in range(z.regions):
        for g in range(z.span // 8):
            top = z.width * dest + 8 * g
            count, at = min(8, COLS - top), ROWS * (g % QUAD)
            strength[dest, g // QUAD, 0:count, at : at + ROWS] = turned_strength[top : top + count]


def strength_blocks(z, smoothing, before):
    return pl.pallas_call(
        functools.partial(strength_kernel, z),
        out_shape=jax.ShapeDtypeStruct((z.regions, z.quads, 8, LANES), jnp.float32),
        in_specs=[pl.BlockSpec(memory_space=pltpu.VMEM), pl.BlockSpec(memory_space=pl.ANY)],
        out_specs=pl.BlockSpec(memory_space=pltpu.VMEM),
        compiler_params=pltpu.CompilerParams(vmem_limit_bytes=VMEM),
        name="strength_blocks",
    )(smoothing, before)


def join_kernel(z, *refs):
    place, lists, refs = refs[0], refs[1 : 1 + z.makers], refs[1 + z.makers :]
    received, refs = refs[: z.makers - 1], refs[z.makers - 1 :]
    half, (total, weights, strength), outs = refs[:FIELDS], refs[FIELDS : FIELDS + 3], refs[FIELDS + 3 : -4]
    staged, sums, lines, turned = refs[-4:]
    me = place[0]
    first = lax.rem(me, z.makers) * z.block
    row, column = (lax.broadcasted_iota(jnp.int32, (LANES, LANES), axis) for axis in (0, 1))
    identity = (row == column).astype(jnp.bfloat16)

    for quad in range(z.quads):

        def body(i, side, slots):
            j = quad * QUAD + i
            sources = [(maker, slot) for maker in range(1, z.makers) for slot in slots]

            def staged_of(maker, slot):
                return staged.at[staged_index(i, side, maker - 1, slot, z.makers - 1)]

            def weight_item(maker, slot):
                column, kind = (lists[maker][entry, slot, first + j] for entry in (1, 2))
                return functools.partial(weight_tile, weights, kind), column

            def field_item(field, maker, slot):
                weight, column = weight_item(maker, slot)
                return lambda t: staged_tile(staged_of(maker, slot), field, t) * weight(t), column

            for maker, slot in sources:
                stage(staged_of(maker, slot), received[maker - 1][first + j, slot])
            others = place_all(side, sums.at[FIELDS], [weight_item(*source) for source in sources])
            inverse = [[1.0 / (total[j, parity, t] + others[parity][t]) for t in range(TILES)] for parity in range(2)]
            for field in range(FIELDS):
                pieces = place_all(side, sums.at[field], [field_item(field, *source) for source in sources])
                for parity in range(2):
                    for t in range(TILES):
                        lines[field, t, pl.ds(ROWS * i + parity, PAIRS, stride=2), :] = (
                            half[field][j, parity, t] + pieces[parity][t]
                        ) * inverse[parity][t]

        each_region(z, lambda i: lists[0][0, 1, first + quad * QUAD + i] >= 0, body)
        for field in range(FIELDS):
            for t in range(TILES):
                turned[field, LANES * t : LANES * (t + 1), :] = lax.dot_general(
                    identity,
                    lines[field, t].astype(jnp.bfloat16),
                    (((1,), (1,)), ((), ())),
                    preferred_element_type=jnp.float32,
                )
        for out, offset in zip(outs, z.offsets):
            dest = me ^ offset
            top = dest * z.width
            if z.width % 8 == 0:
                top = pl.multiple_of(top, 8)
            for low in range(0, FIELDS, 2):
                block = [turned[field, pl.ds(top, z.span), :] for field in (low, low + 1)]
                out[quad, low * z.span : (low + 2) * z.span, :] = jnp.concatenate(block, 0).astype(jnp.bfloat16)
            ends = (jnp.maximum(top - 1, 0), jnp.minimum(top + z.width, COLS - 1))
            edge = [turned[field, pl.ds(end, 1), :] for field in range(FIELDS) for end in ends]
            edge.append(strength[dest, quad])
            out[quad, z.main : z.sent, :] = jnp.concatenate(edge, 0).astype(jnp.bfloat16)


def join(z, place, lists, received, shares):
    smem = pl.BlockSpec(memory_space=pltpu.SMEM)
    vmem = pl.BlockSpec(memory_space=pltpu.VMEM)
    shape = (z.quads, z.sent, LANES)
    return pl.pallas_call(
        functools.partial(join_kernel, z),
        out_shape=[jax.ShapeDtypeStruct(shape, jnp.bfloat16)] * z.regions,
        in_specs=[smem] * (1 + z.makers) + [vmem] * (z.makers - 1 + len(shares)),
        out_specs=[vmem] * z.regions,
        scratch_shapes=[
            pltpu.VMEM(((QUAD + CAP) * (z.makers - 1), LINES, LANES), jnp.float32),
            pltpu.VMEM((FIELDS + 1, 2, SLOTS, PAIRS, LANES), jnp.float32),
            pltpu.VMEM((FIELDS, TILES, LANES, LANES), jnp.float32),
            pltpu.VMEM((FIELDS, COLS + 8, LANES), jnp.float32),
        ],
        compiler_params=pltpu.CompilerParams(vmem_limit_bytes=VMEM),
        cost_estimate=pl.CostEstimate(flops=5_000_000, bytes_accessed=8_000_000, transcendentals=0),
        name="join",
    )(place, *lists, *received, *shares)


SORT_STEPS = (
    ((0, 1), (2, 3), (4, 5), (6, 7)),
    ((0, 2), (1, 3), (4, 6), (5, 7)),
    ((1, 2), (5, 6)),
    ((0, 4), (1, 5), (2, 6), (3, 7)),
    ((2, 4), (3, 5)),
    ((1, 2), (3, 4), (5, 6)),
)
STEP_FIELDS = 2


def score_kernel(z, place, *refs):
    blocks = dict(zip(z.offsets, refs))
    analysis, crps, spread, strength, edges, padded = refs[z.regions :]
    me = place[0]
    step = pl.program_id(0)
    rows = z.rows

    def tile_of(offset, quad):
        return lax.rem(me ^ offset, z.makers) * z.quads + quad

    @pl.when(step == 0)
    def _():
        slot = lax.broadcasted_iota(jnp.int32, (8, LANES), 1) // ROWS
        for low in range(0, z.regions, QUAD):
            offsets = range(low, low + QUAD)
            slots = [lax.rem(me ^ offset, QUAD) for offset in offsets]
            at = lax.div(me ^ low, QUAD)
            for quad in range(z.quads):
                tails = [blocks[offset][quad, z.main : z.sent, :].astype(jnp.float32) for offset in offsets]
                for offset, tail in zip(offsets, tails):
                    edges[offset // z.makers, tile_of(offset, quad)] = tail[0:8]
                for g in range(quad * QUAD, min((quad + 1) * QUAD, z.span // 8)):
                    joined = jnp.zeros((8, LANES), jnp.float32)
                    for i, tail in zip(slots, tails):
                        near = pltpu.roll(tail[8:16], lax.rem(i + QUAD - g % QUAD, QUAD) * ROWS, 1)
                        joined = jnp.where(slot == i, near, joined)
                    strength[at, 8 * g : 8 * (g + 1), :] = joined + MID

    top = pl.multiple_of(step * STEP_FIELDS * z.span, 16)
    for offset in range(z.regions):
        for quad in range(z.quads):
            values = blocks[offset][quad, pl.ds(top, STEP_FIELDS * z.span), :].astype(jnp.float32)
            for f in range(STEP_FIELDS):
                padded[offset // z.makers, f, tile_of(offset, quad), 8 : 8 + z.span, :] = values[
                    f * z.span : (f + 1) * z.span
                ]
    tiles = rows // LANES
    for sample in range(SAMPLES):
        for f in range(STEP_FIELDS):
            low = 2 * (step * STEP_FIELDS + f)
            for t in range(tiles):
                padded[sample, f, t, 7:8, :] = edges[sample, t, pl.ds(low, 1), :]
                padded[sample, f, t, 8 + z.width : 9 + z.width, :] = edges[sample, t, pl.ds(low + 1, 1), :]
    for f, low in ((f, low) for f in range(STEP_FIELDS) for low in range(0, z.width, 16)):
        high = min(low + 16, z.width)
        lane = lax.broadcasted_iota(jnp.int32, (high - low, LANES), 1)
        smoothed = [[] for _ in range(tiles)]
        for sample in range(SAMPLES):
            field = padded.at[sample, f]
            pieces = [field[t, 8 + low : 8 + high, :] for t in range(tiles)]
            later = [pltpu.roll(piece, 1, 1) for piece in pieces]
            sooner = [pltpu.roll(piece, LANES - 1, 1) for piece in pieces]
            for t, here in enumerate(pieces):
                above = jnp.where(lane == 0, later[t - 1] if t else here, later[t])
                below = jnp.where(lane == LANES - 1, sooner[t + 1] if t + 1 < tiles else here, sooner[t])
                sides = field[t, 7 + low : 7 + high, :] + field[t, 9 + low : 9 + high, :]
                smooth = here + strength[t, low:high, :] * (above + below + sides - 4.0 * here)
                smoothed[t].append(smooth.astype(jnp.bfloat16))
        for t, members in enumerate(smoothed):
            lanes = slice(LANES * t, LANES * (t + 1))
            values = [member.astype(jnp.float32) for member in members]
            target = analysis[f, low:high, lanes].astype(jnp.float32)
            error = sum(jnp.abs(value - target) for value in values) * (1.0 / SAMPLES)
            average = sum(values) * (1.0 / SAMPLES)
            variance = sum((value - average) ** 2 for value in values) * (1.0 / (SAMPLES - 1.0))
            ranked = list(members)
            for pairs in SORT_STEPS:
                for a, b in pairs:
                    ranked[a], ranked[b] = jnp.minimum(ranked[a], ranked[b]), jnp.maximum(ranked[a], ranked[b])
            ranked = [member.astype(jnp.float32) for member in ranked]
            pairs = sum(
                (2 * k - SAMPLES + 1.0) * (ranked[k] - ranked[SAMPLES - 1 - k])
                for k in range(SAMPLES // 2, SAMPLES)
            )
            crps[f, low:high, lanes] = (error - pairs * (1.0 / (SAMPLES * SAMPLES))).astype(jnp.bfloat16)
            spread[0, f, low:high, lanes] = variance.astype(jnp.bfloat16)
            spread[1, f, low:high, lanes] = ((average - target) ** 2).astype(jnp.bfloat16)


def score(z, place, blocks, analysis):
    width, rows = z.width, z.rows
    return pl.pallas_call(
        functools.partial(score_kernel, z),
        out_shape=[
            jax.ShapeDtypeStruct((FIELDS, width, rows), jnp.bfloat16),
            jax.ShapeDtypeStruct((2, FIELDS, width, rows), jnp.bfloat16),
        ],
        grid=(FIELDS // STEP_FIELDS,),
        in_specs=[pl.BlockSpec(memory_space=pltpu.SMEM)]
        + [pl.BlockSpec(memory_space=pltpu.VMEM)] * z.regions
        + [pl.BlockSpec((STEP_FIELDS, width, rows), lambda i: (i, 0, 0))],
        out_specs=[
            pl.BlockSpec((STEP_FIELDS, width, rows), lambda i: (i, 0, 0)),
            pl.BlockSpec((2, STEP_FIELDS, width, rows), lambda i: (0, i, 0, 0)),
        ],
        scratch_shapes=[
            pltpu.VMEM((rows // LANES, z.span, LANES), jnp.float32),
            pltpu.VMEM((SAMPLES, rows // LANES, 8, LANES), jnp.float32),
            pltpu.VMEM((SAMPLES, STEP_FIELDS, rows // LANES, z.span + 16, LANES), jnp.float32),
        ],
        compiler_params=pltpu.CompilerParams(vmem_limit_bytes=VMEM),
        name="score",
    )(place, *blocks, analysis)


def shards(patch_tiles, slot_lists, blend_table, smoothing, analysis):
    z = Sizes(lax.axis_size("region"))
    place = lax.axis_index("region").reshape(1)
    turns = [
        [(i, i - i % z.makers + (i + k) % z.makers) for i in range(z.regions)] for k in range(1, z.makers)
    ]
    tiles = patch_tiles.reshape(z.regions, CAP, FIELDS, PAIRS * TILES, LANES)
    tiles = jnp.swapaxes(tiles, 2, 3).reshape(z.regions, CAP, LINES, LANES)
    lists = jnp.transpose(slot_lists, (2, 1, 0))
    received = [lax.ppermute(tiles, "region", turn) for turn in turns]
    lists = [lists] + [lax.ppermute(lists, "region", turn) for turn in turns]
    shares = own_share(z, place, lists[0], tiles, blend_table)
    shares = [*shares, strength_blocks(z, smoothing, shares[-1])]
    blocks = join(z, place, lists, received, shares)
    moved = [blocks[0]] + [
        lax.ppermute(block, "region", [(i, i ^ offset) for i in range(z.regions)])
        for block, offset in zip(blocks[1:], z.offsets[1:])
    ]
    outs = score(z, place, moved, jnp.swapaxes(analysis, 1, 2))
    return tuple(jnp.swapaxes(item, -1, -2) for item in outs)


def solution(mesh):
    return jax.shard_map(
        shards,
        mesh=mesh,
        in_specs=(
            P(("groups", "region"), None, None, None),
            P(("groups", "region"), None, None),
            P(),
            P("region", None),
            P(None, "groups", "region"),
        ),
        out_specs=(P(None, "groups", "region"), P(None, None, "groups", "region")),
        check_vma=False,
    )
```

```python
import functools

import jax
import jax.numpy as jnp
from jax import lax
from jax.experimental import pallas as pl
from jax.experimental.pallas import tpu as pltpu
from jax.sharding import PartitionSpec as P

SAMPLES = 8
FIELDS = 4
PATCH = 448
CAP = 2
ROWS = 32
COLS = 896
PAIRS = ROWS // 2
LINES = FIELDS * ROWS * PATCH // 128
LANES = 128
TILES = COLS // LANES
QUAD = LANES // ROWS
MID = 0.11
VMEM = 40 * 1024 * 1024
MOST_VMEM = 48 * 1024 * 1024


def round_up(value, step):
    return -(-value // step) * step


def swap_order(regions):
    half, quarter = regions // 2, regions // 4
    far = [offset for i in range(quarter) for offset in (half + quarter + i, half + i)]
    near = list(range(quarter, half)) + list(range(1, quarter))
    return [0] + [item for pair in zip(far, near + [None]) for item in pair if item is not None]


class Sizes:
    def __init__(self, regions):
        self.regions = regions
        self.makers = regions // SAMPLES
        self.block = regions // self.makers
        self.quads = self.block // QUAD
        self.width = COLS // regions
        self.span = round_up(self.width, 8)
        self.rows = regions * ROWS
        self.main = round_up(FIELDS * self.span, 16)
        self.offsets = swap_order(regions)
        self.sent = self.main + 16


def stage(staged, tile):
    staged[...] = tile.astype(jnp.float32)


def staged_tile(staged, field, t):
    return staged[pl.ds(FIELDS * t + field, PAIRS, stride=FIELDS * TILES), :]


def weight_tile(weights, kind, t):
    return weights[t, pl.ds(pl.multiple_of(kind * PAIRS, PAIRS), PAIRS), :]


SLOTS = TILES + 2


def place_side(tile, column):
    pairs = jnp.concatenate([tile(t) for t in range(TILES)], 1)
    turned = pltpu.roll(pairs, PATCH, 1)
    lane = lax.broadcasted_iota(jnp.int32, pairs.shape, 1)
    left = (lane < PATCH) & (column == 0)
    right = (lane >= PATCH) & (column != 0)
    even = jnp.where(left, pairs, jnp.where(right, turned, 0.0))
    odd = jnp.where(left, turned, jnp.where(right, pairs, 0.0))
    return [[rows[:, LANES * t : LANES * (t + 1)] for t in range(TILES)] for rows in (even, odd)]


def add_any(sums, tile, column):
    lane = lax.broadcasted_iota(jnp.int32, (PAIRS, LANES), 1)
    middle = PATCH // LANES
    split = PATCH % LANES
    for parity in range(2):
        first = middle * parity
        start = column if parity == 0 else column + COLS - PATCH
        shift = lax.rem(start, LANES)
        at = lax.div(start, LANES) + first + 1 - (TILES if parity else 0)
        turned = []
        for t in range(first, first + middle + 1):
            piece = tile(t)
            if t == middle:
                piece = jnp.where((lane >= split) if parity else (lane < split), piece, 0.0)
            turned.append(pltpu.roll(piece, shift, 1))
        none = jnp.zeros((PAIRS, LANES), jnp.float32)
        for v in range(middle + 2):
            low = turned[v - 1] if v else none
            high = turned[v] if v <= middle else none
            sums[parity, at + v] = sums[parity, at + v] + jnp.where(lane < shift, low, high)


def place_all(side, sums, items):
    if side:
        placed = [place_side(*item) for item in items]
        return [[sum(item[parity][t] for item in placed) for t in range(TILES)] for parity in range(2)]
    for parity in range(2):
        for t in range(SLOTS):
            sums[parity, t] = jnp.zeros((PAIRS, LANES), jnp.float32)
    for item in items:
        add_any(sums, *item)
    return [[sums[parity, t + 1] for t in range(TILES)] for parity in range(2)]


def each_region(z, heavy, body):
    for i in range(QUAD):
        if z.makers == 2:
            body(i, True, range(1))
        else:
            pl.when(jnp.logical_not(heavy(i)))(functools.partial(body, i, False, range(1)))

    def again(i, carry):
        pl.when(heavy(i))(functools.partial(body, i, False, range(CAP)))
        return carry

    lax.fori_loop(0, QUAD, again, 0)


def staged_index(i, side, maker, slot, others):
    return i * others + maker if side else QUAD * others + maker * CAP + slot


def own_kernel(z, place, lists, tiles, table_hbm, *refs):
    half, (total, weights, landed, staged, sums, table, sems) = refs[:FIELDS], refs[FIELDS:]
    first = lax.rem(place[0], z.makers) * z.block

    def fetch(j):
        return pltpu.make_async_copy(tiles.at[first + j], landed.at[j], sems.at[j])

    fetch_table = pltpu.make_async_copy(table_hbm, table, sems.at[z.block])
    fetch_table.start()
    for j in range(z.block):
        fetch(j).start()
    fetch_table.wait()
    kinds = table.shape[0]
    for k in range(PAIRS):
        for t in range(TILES):
            at = COLS * k + LANES * t
            for low in range(0, kinds, 8):
                count = min(8, kinds - low)
                weights[t, pl.ds(PAIRS * low + k, count, stride=PAIRS), :] = table[
                    low : low + count, at : at + LANES
                ]

    def group(quad, carry):
        for i in range(QUAD):
            fetch(quad * QUAD + i).wait()

        def body(i, side, slots):
            j = quad * QUAD + i

            def weight_item(slot):
                column, kind = (lists[entry, slot, first + j] for entry in (1, 2))
                return functools.partial(weight_tile, weights, kind), column

            def field_item(field, slot):
                weight, column = weight_item(slot)
                own = staged.at[staged_index(i, side, 0, slot, 1)]
                return lambda t: staged_tile(own, field, t) * weight(t), column

            for slot in slots:
                stage(staged.at[staged_index(i, side, 0, slot, 1)], landed[j, slot])
            for index in range(FIELDS + 1):
                items = [field_item(index, slot) if index < FIELDS else weight_item(slot) for slot in slots]
                pieces = place_all(side, sums.at[index], items)
                target = half[index] if index < FIELDS else total
                for parity in range(2):
                    for t in range(TILES):
                        target[j, parity, t] = pieces[parity][t]

        each_region(z, lambda i: lists[0, 1, first + quad * QUAD + i] >= 0, body)
        return carry

    lax.fori_loop(0, z.quads, group, 0)


def own_share(z, place, lists, tiles, table):
    smem = pl.BlockSpec(memory_space=pltpu.SMEM)
    vmem = pl.BlockSpec(memory_space=pltpu.VMEM)
    hbm = pl.BlockSpec(memory_space=pltpu.HBM)
    kinds = round_up(table.shape[0], 8)
    return pl.pallas_call(
        functools.partial(own_kernel, z),
        out_shape=[
            *[jax.ShapeDtypeStruct((z.block, 2, TILES, PAIRS, LANES), jnp.float32)] * (FIELDS + 1),
            jax.ShapeDtypeStruct((TILES, kinds * PAIRS, LANES), jnp.float32),
        ],
        in_specs=[smem, smem, hbm, hbm],
        out_specs=[vmem] * (FIELDS + 2),
        scratch_shapes=[
            pltpu.VMEM((z.block, CAP, LINES, LANES), jnp.bfloat16),
            pltpu.VMEM((QUAD + CAP, LINES, LANES), jnp.float32),
            pltpu.VMEM((FIELDS + 1, 2, SLOTS, PAIRS, LANES), jnp.float32),
            pltpu.VMEM(table.shape, jnp.float32),
            pltpu.SemaphoreType.DMA((z.block + 1,)),
        ],
        compiler_params=pltpu.CompilerParams(vmem_limit_bytes=MOST_VMEM),
        cost_estimate=pl.CostEstimate(flops=5_000_000, bytes_accessed=8_000_000, transcendentals=0),
        name="own_share",
    )(place, lists, tiles, table)


def strength_kernel(z, smoothing, _, strength):
    turned_strength = jnp.transpose(smoothing[...] - MID)
    for dest in range(z.regions):
        for g in range(z.span // 8):
            top = z.width * dest + 8 * g
            count, at = min(8, COLS - top), ROWS * (g % QUAD)
            strength[dest, g // QUAD, 0:count, at : at + ROWS] = turned_strength[top : top + count]


def strength_blocks(z, smoothing, before):
    return pl.pallas_call(
        functools.partial(strength_kernel, z),
        out_shape=jax.ShapeDtypeStruct((z.regions, z.quads, 8, LANES), jnp.float32),
        in_specs=[pl.BlockSpec(memory_space=pltpu.VMEM), pl.BlockSpec(memory_space=pl.ANY)],
        out_specs=pl.BlockSpec(memory_space=pltpu.VMEM),
        compiler_params=pltpu.CompilerParams(vmem_limit_bytes=VMEM),
        name="strength_blocks",
    )(smoothing, before)


def join_kernel(z, *refs):
    place, lists, refs = refs[0], refs[1 : 1 + z.makers], refs[1 + z.makers :]
    received, refs = refs[: z.makers - 1], refs[z.makers - 1 :]
    half, (total, weights, strength), outs = refs[:FIELDS], refs[FIELDS : FIELDS + 3], refs[FIELDS + 3 : -5]
    staged, sums, lines, turned, edges = refs[-5:]
    me = place[0]
    first = lax.rem(me, z.makers) * z.block
    row, column = (lax.broadcasted_iota(jnp.int32, (LANES, LANES), axis) for axis in (0, 1))
    identity = (row == column).astype(jnp.bfloat16)

    for quad in range(z.quads):

        def body(i, side, slots):
            j = quad * QUAD + i
            sources = [(maker, slot) for maker in range(1, z.makers) for slot in slots]

            def staged_of(maker, slot):
                return staged.at[staged_index(i, side, maker - 1, slot, z.makers - 1)]

            def weight_item(maker, slot):
                column, kind = (lists[maker][entry, slot, first + j] for entry in (1, 2))
                return functools.partial(weight_tile, weights, kind), column

            def field_item(field, maker, slot):
                weight, column = weight_item(maker, slot)
                return lambda t: staged_tile(staged_of(maker, slot), field, t) * weight(t), column

            for maker, slot in sources:
                stage(staged_of(maker, slot), received[maker - 1][first + j, slot])
            others = place_all(side, sums.at[FIELDS], [weight_item(*source) for source in sources])
            inverse = [[1.0 / (total[j, parity, t] + others[parity][t]) for t in range(TILES)] for parity in range(2)]
            for field in range(FIELDS):
                pieces = place_all(side, sums.at[field], [field_item(field, *source) for source in sources])
                for parity in range(2):
                    for t in range(TILES):
                        lines[field, t, pl.ds(ROWS * i + parity, PAIRS, stride=2), :] = (
                            half[field][j, parity, t] + pieces[parity][t]
                        ) * inverse[parity][t]

        each_region(z, lambda i: lists[0][0, 1, first + quad * QUAD + i] >= 0, body)
        for t in range(TILES):
            for field in range(FIELDS):
                here = slice(LANES * t, LANES * (t + 1))
                if field % 2:
                    turned[field, here, :] = jnp.transpose(lines[field, t])
                else:
                    turned[field, here, :] = lax.dot_general(
                        identity,
                        lines[field, t].astype(jnp.bfloat16),
                        (((1,), (1,)), ((), ())),
                        preferred_element_type=jnp.float32,
                    )
        for i, (out, offset) in enumerate(zip(outs, z.offsets)):
            dest = me ^ offset
            top = dest * z.width
            if z.width % 8 == 0:
                top = pl.multiple_of(top, 8)
            ends = (jnp.maximum(top - 1, 0), jnp.minimum(top + z.width, COLS - 1))
            for field in range(FIELDS):
                for side, end in enumerate(ends):
                    edges[i, 2 * field + side : 2 * field + side + 1, :] = turned[field, pl.ds(end, 1), :]
            for low in range(0, FIELDS, 2):
                block = [turned[field, pl.ds(top, z.span), :] for field in (low, low + 1)]
                out[quad, low * z.span : (low + 2) * z.span, :] = jnp.concatenate(block, 0).astype(jnp.bfloat16)
            tail = jnp.concatenate([edges[i], strength[dest, quad]], 0)
            out[quad, z.main : z.sent, :] = tail.astype(jnp.bfloat16)


def join(z, place, lists, received, shares):
    smem = pl.BlockSpec(memory_space=pltpu.SMEM)
    vmem = pl.BlockSpec(memory_space=pltpu.VMEM)
    shape = (z.quads, z.sent, LANES)
    return pl.pallas_call(
        functools.partial(join_kernel, z),
        out_shape=[jax.ShapeDtypeStruct(shape, jnp.bfloat16)] * z.regions,
        in_specs=[smem] * (1 + z.makers) + [vmem] * (z.makers - 1 + len(shares)),
        out_specs=[vmem] * z.regions,
        scratch_shapes=[
            pltpu.VMEM(((QUAD + CAP) * (z.makers - 1), LINES, LANES), jnp.float32),
            pltpu.VMEM((FIELDS + 1, 2, SLOTS, PAIRS, LANES), jnp.float32),
            pltpu.VMEM((FIELDS, TILES, LANES, LANES), jnp.float32),
            pltpu.VMEM((FIELDS, COLS + 8, LANES), jnp.float32),
            pltpu.VMEM((z.regions, 8, LANES), jnp.float32),
        ],
        compiler_params=pltpu.CompilerParams(vmem_limit_bytes=VMEM),
        cost_estimate=pl.CostEstimate(flops=5_000_000, bytes_accessed=8_000_000, transcendentals=0),
        name="join",
    )(place, *lists, *received, *shares)


SORT_STEPS = (
    ((0, 1), (2, 3), (4, 5), (6, 7)),
    ((0, 2), (1, 3), (4, 6), (5, 7)),
    ((1, 2), (5, 6)),
    ((0, 4), (1, 5), (2, 6), (3, 7)),
    ((2, 4), (3, 5)),
    ((1, 2), (3, 4), (5, 6)),
)
STEP_FIELDS = 2


def score_kernel(z, place, *refs):
    blocks = dict(zip(z.offsets, refs))
    analysis, crps, spread, strength, edges, padded = refs[z.regions :]
    me = place[0]
    step = pl.program_id(0)
    rows = z.rows

    def tile_of(offset, quad):
        return lax.rem(me ^ offset, z.makers) * z.quads + quad

    @pl.when(step == 0)
    def _():
        slot = lax.broadcasted_iota(jnp.int32, (8, LANES), 1) // ROWS
        for low in range(0, z.regions, QUAD):
            offsets = range(low, low + QUAD)
            slots = [lax.rem(me ^ offset, QUAD) for offset in offsets]
            at = lax.div(me ^ low, QUAD)
            for quad in range(z.quads):
                tails = [blocks[offset][quad, z.main : z.sent, :].astype(jnp.float32) for offset in offsets]
                for offset, tail in zip(offsets, tails):
                    edges[offset // z.makers, tile_of(offset, quad)] = tail[0:8]
                for g in range(quad * QUAD, min((quad + 1) * QUAD, z.span // 8)):
                    joined = jnp.zeros((8, LANES), jnp.float32)
                    for i, tail in zip(slots, tails):
                        near = pltpu.roll(tail[8:16], lax.rem(i + QUAD - g % QUAD, QUAD) * ROWS, 1)
                        joined = jnp.where(slot == i, near, joined)
                    strength[at, 8 * g : 8 * (g + 1), :] = joined + MID

    top = pl.multiple_of(step * STEP_FIELDS * z.span, 16)
    for offset in range(z.regions):
        for quad in range(z.quads):
            values = blocks[offset][quad, pl.ds(top, STEP_FIELDS * z.span), :].astype(jnp.float32)
            for f in range(STEP_FIELDS):
                padded[offset // z.makers, f, tile_of(offset, quad), 8 : 8 + z.span, :] = values[
                    f * z.span : (f + 1) * z.span
                ]
    tiles = rows // LANES
    for sample in range(SAMPLES):
        for f in range(STEP_FIELDS):
            low = 2 * (step * STEP_FIELDS + f)
            for t in range(tiles):
                padded[sample, f, t, 7:8, :] = edges[sample, t, pl.ds(low, 1), :]
                padded[sample, f, t, 8 + z.width : 9 + z.width, :] = edges[sample, t, pl.ds(low + 1, 1), :]
    for f, low in ((f, low) for f in range(STEP_FIELDS) for low in range(0, z.width, 16)):
        high = min(low + 16, z.width)
        lane = lax.broadcasted_iota(jnp.int32, (high - low, LANES), 1)
        smoothed = [[] for _ in range(tiles)]
        for sample in range(SAMPLES):
            field = padded.at[sample, f]
            pieces = [field[t, 8 + low : 8 + high, :] for t in range(tiles)]
            later = [pltpu.roll(piece, 1, 1) for piece in pieces]
            sooner = [pltpu.roll(piece, LANES - 1, 1) for piece in pieces]
            for t, here in enumerate(pieces):
                above = jnp.where(lane == 0, later[t - 1] if t else here, later[t])
                below = jnp.where(lane == LANES - 1, sooner[t + 1] if t + 1 < tiles else here, sooner[t])
                sides = field[t, 7 + low : 7 + high, :] + field[t, 9 + low : 9 + high, :]
                smooth = here + strength[t, low:high, :] * (above + below + sides - 4.0 * here)
                smoothed[t].append(smooth.astype(jnp.bfloat16))
        for t, members in enumerate(smoothed):
            lanes = slice(LANES * t, LANES * (t + 1))
            values = [member.astype(jnp.float32) for member in members]
            target = analysis[f, low:high, lanes].astype(jnp.float32)
            error = sum(jnp.abs(value - target) for value in values) * (1.0 / SAMPLES)
            average = sum(values) * (1.0 / SAMPLES)
            variance = sum((value - average) ** 2 for value in values) * (1.0 / (SAMPLES - 1.0))
            ranked = list(members)
            for pairs in SORT_STEPS:
                for a, b in pairs:
                    ranked[a], ranked[b] = jnp.minimum(ranked[a], ranked[b]), jnp.maximum(ranked[a], ranked[b])
            ranked = [member.astype(jnp.float32) for member in ranked]
            pairs = sum(
                (2 * k - SAMPLES + 1.0) * (ranked[k] - ranked[SAMPLES - 1 - k])
                for k in range(SAMPLES // 2, SAMPLES)
            )
            crps[f, low:high, lanes] = (error - pairs * (1.0 / (SAMPLES * SAMPLES))).astype(jnp.bfloat16)
            spread[0, f, low:high, lanes] = variance.astype(jnp.bfloat16)
            spread[1, f, low:high, lanes] = ((average - target) ** 2).astype(jnp.bfloat16)


def score(z, place, blocks, analysis):
    width, rows = z.width, z.rows
    return pl.pallas_call(
        functools.partial(score_kernel, z),
        out_shape=[
            jax.ShapeDtypeStruct((FIELDS, width, rows), jnp.bfloat16),
            jax.ShapeDtypeStruct((2, FIELDS, width, rows), jnp.bfloat16),
        ],
        grid=(FIELDS // STEP_FIELDS,),
        in_specs=[pl.BlockSpec(memory_space=pltpu.SMEM)]
        + [pl.BlockSpec(memory_space=pltpu.VMEM)] * z.regions
        + [pl.BlockSpec((STEP_FIELDS, width, rows), lambda i: (i, 0, 0))],
        out_specs=[
            pl.BlockSpec((STEP_FIELDS, width, rows), lambda i: (i, 0, 0)),
            pl.BlockSpec((2, STEP_FIELDS, width, rows), lambda i: (0, i, 0, 0)),
        ],
        scratch_shapes=[
            pltpu.VMEM((rows // LANES, z.span, LANES), jnp.float32),
            pltpu.VMEM((SAMPLES, rows // LANES, 8, LANES), jnp.float32),
            pltpu.VMEM((SAMPLES, STEP_FIELDS, rows // LANES, z.span + 16, LANES), jnp.float32),
        ],
        compiler_params=pltpu.CompilerParams(vmem_limit_bytes=VMEM),
        name="score",
    )(place, *blocks, analysis)


def shards(patch_tiles, slot_lists, blend_table, smoothing, analysis):
    z = Sizes(lax.axis_size("region"))
    place = lax.axis_index("region").reshape(1)
    turns = [
        [(i, i - i % z.makers + (i + k) % z.makers) for i in range(z.regions)] for k in range(1, z.makers)
    ]
    tiles = patch_tiles.reshape(z.regions, CAP, FIELDS, PAIRS * TILES, LANES)
    tiles = jnp.swapaxes(tiles, 2, 3).reshape(z.regions, CAP, LINES, LANES)
    lists = jnp.transpose(slot_lists, (2, 1, 0))
    received = [lax.ppermute(tiles, "region", turn) for turn in turns]
    lists = [lists] + [lax.ppermute(lists, "region", turn) for turn in turns]
    shares = own_share(z, place, lists[0], tiles, blend_table)
    shares = [*shares, strength_blocks(z, smoothing, shares[-1])]
    blocks = join(z, place, lists, received, shares)
    moved = [blocks[0]] + [
        lax.ppermute(block, "region", [(i, i ^ offset) for i in range(z.regions)])
        for block, offset in zip(blocks[1:], z.offsets[1:])
    ]
    outs = score(z, place, moved, jnp.swapaxes(analysis, 1, 2))
    return tuple(jnp.swapaxes(item, -1, -2) for item in outs)


def solution(mesh):
    return jax.shard_map(
        shards,
        mesh=mesh,
        in_specs=(
            P(("groups", "region"), None, None, None),
            P(("groups", "region"), None, None),
            P(),
            P("region", None),
            P(None, "groups", "region"),
        ),
        out_specs=(P(None, "groups", "region"), P(None, None, "groups", "region")),
        check_vma=False,
    )
```

```python
import functools

import jax
import jax.numpy as jnp
from jax import lax
from jax.experimental import pallas as pl
from jax.experimental.pallas import tpu as pltpu
from jax.sharding import PartitionSpec as P

SAMPLES = 8
FIELDS = 4
PATCH = 448
CAP = 2
ROWS = 32
COLS = 896
PAIRS = ROWS // 2
LINES = FIELDS * ROWS * PATCH // 128
LANES = 128
TILES = COLS // LANES
QUAD = LANES // ROWS
MID = 0.11
VMEM = 40 * 1024 * 1024
MOST_VMEM = 48 * 1024 * 1024


def round_up(value, step):
    return -(-value // step) * step


def swap_order(regions):
    half, quarter = regions // 2, regions // 4
    far = [offset for i in range(quarter) for offset in (half + quarter + i, half + i)]
    near = list(range(quarter, half)) + list(range(1, quarter))
    return [0] + [item for pair in zip(far, near + [None]) for item in pair if item is not None]


class Sizes:
    def __init__(self, regions):
        self.regions = regions
        self.makers = regions // SAMPLES
        self.block = regions // self.makers
        self.quads = self.block // QUAD
        self.width = COLS // regions
        self.span = round_up(self.width, 8)
        self.rows = regions * ROWS
        self.main = round_up(FIELDS * self.span, 16)
        self.offsets = swap_order(regions)
        arrived = self.offsets[: regions - 5]
        groups = [range(sample * self.makers, (sample + 1) * self.makers) for sample in range(SAMPLES)]
        self.early = [sample for sample, group in enumerate(groups) if all(k in arrived for k in group)]
        self.sent = self.main + 16


def stage(staged, tile):
    staged[...] = tile.astype(jnp.float32)


def staged_tile(staged, field, t):
    return staged[pl.ds(FIELDS * t + field, PAIRS, stride=FIELDS * TILES), :]


def weight_tile(weights, kind, t):
    return weights[t, pl.ds(pl.multiple_of(kind * PAIRS, PAIRS), PAIRS), :]


SLOTS = TILES + 2


def place_side(tile, column):
    pairs = jnp.concatenate([tile(t) for t in range(TILES)], 1)
    turned = pltpu.roll(pairs, PATCH, 1)
    lane = lax.broadcasted_iota(jnp.int32, pairs.shape, 1)
    left = (lane < PATCH) & (column == 0)
    right = (lane >= PATCH) & (column != 0)
    even = jnp.where(left, pairs, jnp.where(right, turned, 0.0))
    odd = jnp.where(left, turned, jnp.where(right, pairs, 0.0))
    return [[rows[:, LANES * t : LANES * (t + 1)] for t in range(TILES)] for rows in (even, odd)]


def add_any(sums, tile, column):
    lane = lax.broadcasted_iota(jnp.int32, (PAIRS, LANES), 1)
    middle = PATCH // LANES
    split = PATCH % LANES
    for parity in range(2):
        first = middle * parity
        start = column if parity == 0 else column + COLS - PATCH
        shift = lax.rem(start, LANES)
        at = lax.div(start, LANES) + first + 1 - (TILES if parity else 0)
        turned = []
        for t in range(first, first + middle + 1):
            piece = tile(t)
            if t == middle:
                piece = jnp.where((lane >= split) if parity else (lane < split), piece, 0.0)
            turned.append(pltpu.roll(piece, shift, 1))
        none = jnp.zeros((PAIRS, LANES), jnp.float32)
        for v in range(middle + 2):
            low = turned[v - 1] if v else none
            high = turned[v] if v <= middle else none
            sums[parity, at + v] = sums[parity, at + v] + jnp.where(lane < shift, low, high)


def place_all(side, sums, items):
    if side:
        placed = [place_side(*item) for item in items]
        return [[sum(item[parity][t] for item in placed) for t in range(TILES)] for parity in range(2)]
    for parity in range(2):
        for t in range(SLOTS):
            sums[parity, t] = jnp.zeros((PAIRS, LANES), jnp.float32)
    for item in items:
        add_any(sums, *item)
    return [[sums[parity, t + 1] for t in range(TILES)] for parity in range(2)]


def each_region(z, heavy, body):
    for i in range(QUAD):
        if z.makers == 2:
            body(i, True, range(1))
        else:
            pl.when(jnp.logical_not(heavy(i)))(functools.partial(body, i, False, range(1)))

    def again(i, carry):
        pl.when(heavy(i))(functools.partial(body, i, False, range(CAP)))
        return carry

    lax.fori_loop(0, QUAD, again, 0)


def staged_index(i, side, maker, slot, others):
    return i * others + maker if side else QUAD * others + maker * CAP + slot


def own_kernel(z, place, lists, tiles, table_hbm, *refs):
    half, (total, weights, landed, staged, sums, table, sems) = refs[:FIELDS], refs[FIELDS:]
    first = lax.rem(place[0], z.makers) * z.block

    def fetch(j):
        return pltpu.make_async_copy(tiles.at[first + j], landed.at[j], sems.at[j])

    fetch_table = pltpu.make_async_copy(table_hbm, table, sems.at[z.block])
    fetch_table.start()
    for j in range(z.block):
        fetch(j).start()
    fetch_table.wait()
    kinds = table.shape[0]
    for k in range(PAIRS):
        for t in range(TILES):
            at = COLS * k + LANES * t
            for low in range(0, kinds, 8):
                count = min(8, kinds - low)
                weights[t, pl.ds(PAIRS * low + k, count, stride=PAIRS), :] = table[
                    low : low + count, at : at + LANES
                ]

    def group(quad, carry):
        for i in range(QUAD):
            fetch(quad * QUAD + i).wait()

        def body(i, side, slots):
            j = quad * QUAD + i

            def weight_item(slot):
                column, kind = (lists[entry, slot, first + j] for entry in (1, 2))
                return functools.partial(weight_tile, weights, kind), column

            def field_item(field, slot):
                weight, column = weight_item(slot)
                own = staged.at[staged_index(i, side, 0, slot, 1)]
                return lambda t: staged_tile(own, field, t) * weight(t), column

            for slot in slots:
                stage(staged.at[staged_index(i, side, 0, slot, 1)], landed[j, slot])
            for index in range(FIELDS + 1):
                items = [field_item(index, slot) if index < FIELDS else weight_item(slot) for slot in slots]
                pieces = place_all(side, sums.at[index], items)
                target = half[index] if index < FIELDS else total
                for parity in range(2):
                    for t in range(TILES):
                        target[j, parity, t] = pieces[parity][t]

        each_region(z, lambda i: lists[0, 1, first + quad * QUAD + i] >= 0, body)
        return carry

    lax.fori_loop(0, z.quads, group, 0)


def own_share(z, place, lists, tiles, table):
    smem = pl.BlockSpec(memory_space=pltpu.SMEM)
    vmem = pl.BlockSpec(memory_space=pltpu.VMEM)
    hbm = pl.BlockSpec(memory_space=pltpu.HBM)
    kinds = round_up(table.shape[0], 8)
    return pl.pallas_call(
        functools.partial(own_kernel, z),
        out_shape=[
            *[jax.ShapeDtypeStruct((z.block, 2, TILES, PAIRS, LANES), jnp.float32)] * (FIELDS + 1),
            jax.ShapeDtypeStruct((TILES, kinds * PAIRS, LANES), jnp.float32),
        ],
        in_specs=[smem, smem, hbm, hbm],
        out_specs=[vmem] * (FIELDS + 2),
        scratch_shapes=[
            pltpu.VMEM((z.block, CAP, LINES, LANES), jnp.bfloat16),
            pltpu.VMEM((QUAD + CAP, LINES, LANES), jnp.float32),
            pltpu.VMEM((FIELDS + 1, 2, SLOTS, PAIRS, LANES), jnp.float32),
            pltpu.VMEM(table.shape, jnp.float32),
            pltpu.SemaphoreType.DMA((z.block + 1,)),
        ],
        compiler_params=pltpu.CompilerParams(vmem_limit_bytes=MOST_VMEM),
        cost_estimate=pl.CostEstimate(flops=5_000_000, bytes_accessed=8_000_000, transcendentals=0),
        name="own_share",
    )(place, lists, tiles, table)


def strength_kernel(z, smoothing, _, strength):
    turned_strength = jnp.transpose(smoothing[...] - MID)
    for dest in range(z.regions):
        for g in range(z.span // 8):
            top = z.width * dest + 8 * g
            count, at = min(8, COLS - top), ROWS * (g % QUAD)
            strength[dest, g // QUAD, 0:count, at : at + ROWS] = turned_strength[top : top + count]


def strength_blocks(z, smoothing, before):
    return pl.pallas_call(
        functools.partial(strength_kernel, z),
        out_shape=jax.ShapeDtypeStruct((z.regions, z.quads, 8, LANES), jnp.float32),
        in_specs=[pl.BlockSpec(memory_space=pltpu.VMEM), pl.BlockSpec(memory_space=pl.ANY)],
        out_specs=pl.BlockSpec(memory_space=pltpu.VMEM),
        compiler_params=pltpu.CompilerParams(vmem_limit_bytes=VMEM),
        name="strength_blocks",
    )(smoothing, before)


def join_kernel(z, *refs):
    place, lists, refs = refs[0], refs[1 : 1 + z.makers], refs[1 + z.makers :]
    received, refs = refs[: z.makers - 1], refs[z.makers - 1 :]
    half, (total, weights, strength), outs = refs[:FIELDS], refs[FIELDS : FIELDS + 3], refs[FIELDS + 3 : -5]
    staged, sums, lines, turned, edges = refs[-5:]
    me = place[0]
    first = lax.rem(me, z.makers) * z.block
    row, column = (lax.broadcasted_iota(jnp.int32, (LANES, LANES), axis) for axis in (0, 1))
    identity = (row == column).astype(jnp.bfloat16)

    for quad in range(z.quads):

        def body(i, side, slots):
            j = quad * QUAD + i
            sources = [(maker, slot) for maker in range(1, z.makers) for slot in slots]

            def staged_of(maker, slot):
                return staged.at[staged_index(i, side, maker - 1, slot, z.makers - 1)]

            def weight_item(maker, slot):
                column, kind = (lists[maker][entry, slot, first + j] for entry in (1, 2))
                return functools.partial(weight_tile, weights, kind), column

            def field_item(field, maker, slot):
                weight, column = weight_item(maker, slot)
                return lambda t: staged_tile(staged_of(maker, slot), field, t) * weight(t), column

            for maker, slot in sources:
                stage(staged_of(maker, slot), received[maker - 1][first + j, slot])
            others = place_all(side, sums.at[FIELDS], [weight_item(*source) for source in sources])
            inverse = [[1.0 / (total[j, parity, t] + others[parity][t]) for t in range(TILES)] for parity in range(2)]
            for field in range(FIELDS):
                pieces = place_all(side, sums.at[field], [field_item(field, *source) for source in sources])
                for parity in range(2):
                    for t in range(TILES):
                        lines[field, t, pl.ds(ROWS * i + parity, PAIRS, stride=2), :] = (
                            half[field][j, parity, t] + pieces[parity][t]
                        ) * inverse[parity][t]

        each_region(z, lambda i: lists[0][0, 1, first + quad * QUAD + i] >= 0, body)
        for t in range(TILES):
            for field in range(FIELDS):
                here = slice(LANES * t, LANES * (t + 1))
                if field % 2:
                    turned[field, here, :] = jnp.transpose(lines[field, t])
                else:
                    turned[field, here, :] = lax.dot_general(
                        identity,
                        lines[field, t].astype(jnp.bfloat16),
                        (((1,), (1,)), ((), ())),
                        preferred_element_type=jnp.float32,
                    )
        for i, (out, offset) in enumerate(zip(outs, z.offsets)):
            dest = me ^ offset
            top = dest * z.width
            if z.width % 8 == 0:
                top = pl.multiple_of(top, 8)
            ends = (jnp.maximum(top - 1, 0), jnp.minimum(top + z.width, COLS - 1))
            for field in range(FIELDS):
                for side, end in enumerate(ends):
                    edges[i, 2 * field + side : 2 * field + side + 1, :] = turned[field, pl.ds(end, 1), :]
            for low in range(0, FIELDS, 2):
                block = [turned[field, pl.ds(top, z.span), :] for field in (low, low + 1)]
                out[quad, low * z.span : (low + 2) * z.span, :] = jnp.concatenate(block, 0).astype(jnp.bfloat16)
            tail = jnp.concatenate([edges[i], strength[dest, quad]], 0)
            out[quad, z.main : z.sent, :] = tail.astype(jnp.bfloat16)


def join(z, place, lists, received, shares):
    smem = pl.BlockSpec(memory_space=pltpu.SMEM)
    vmem = pl.BlockSpec(memory_space=pltpu.VMEM)
    shape = (z.quads, z.sent, LANES)
    return pl.pallas_call(
        functools.partial(join_kernel, z),
        out_shape=[jax.ShapeDtypeStruct(shape, jnp.bfloat16)] * z.regions,
        in_specs=[smem] * (1 + z.makers) + [vmem] * (z.makers - 1 + len(shares)),
        out_specs=[vmem] * z.regions,
        scratch_shapes=[
            pltpu.VMEM(((QUAD + CAP) * (z.makers - 1), LINES, LANES), jnp.float32),
            pltpu.VMEM((FIELDS + 1, 2, SLOTS, PAIRS, LANES), jnp.float32),
            pltpu.VMEM((FIELDS, TILES, LANES, LANES), jnp.float32),
            pltpu.VMEM((FIELDS, COLS + 8, LANES), jnp.float32),
            pltpu.VMEM((z.regions, 8, LANES), jnp.float32),
        ],
        compiler_params=pltpu.CompilerParams(vmem_limit_bytes=VMEM),
        cost_estimate=pl.CostEstimate(flops=5_000_000, bytes_accessed=8_000_000, transcendentals=0),
        name="join",
    )(place, *lists, *received, *shares)


SORT_STEPS = (
    ((0, 1), (2, 3), (4, 5), (6, 7)),
    ((0, 2), (1, 3), (4, 6), (5, 7)),
    ((1, 2), (5, 6)),
    ((0, 4), (1, 5), (2, 6), (3, 7)),
    ((2, 4), (3, 5)),
    ((1, 2), (3, 4), (5, 6)),
)
STEP_FIELDS = 2


def differences(field, low, count, tiles):
    lane = lax.broadcasted_iota(jnp.int32, (count, LANES), 1)
    pieces = [field[t, 8 + low : 8 + low + count, :] for t in range(tiles)]
    later = [pltpu.roll(piece, 1, 1) for piece in pieces]
    sooner = [pltpu.roll(piece, LANES - 1, 1) for piece in pieces]
    results = []
    for t, here in enumerate(pieces):
        above = jnp.where(lane == 0, later[t - 1] if t else here, later[t])
        below = jnp.where(lane == LANES - 1, sooner[t + 1] if t + 1 < tiles else here, sooner[t])
        sides = field[t, 7 + low : 7 + low + count, :] + field[t, 9 + low : 9 + low + count, :]
        results.append((here, above + below + sides - 4.0 * here))
    return results


def early_kernel(z, place, *refs):
    offsets = [sample * z.makers + part for sample in z.early for part in range(z.makers)]
    blocks = dict(zip(offsets, refs))
    results, edges, padded = refs[-3:]
    me = place[0]
    tiles = z.rows // LANES
    for offset in offsets:
        index = z.early.index(offset // z.makers)
        for quad in range(z.quads):
            tile = lax.rem(me ^ offset, z.makers) * z.quads + quad
            values = blocks[offset][quad, 0 : z.main, :].astype(jnp.float32)
            tail = blocks[offset][quad, z.main : z.sent, :].astype(jnp.float32)
            for field in range(FIELDS):
                target = padded.at[index, field, tile]
                target[8 : 8 + z.span, :] = values[field * z.span : (field + 1) * z.span]
            edges[index, tile] = tail[0:8]

    def one_field(field, carry):
        for index in range(len(z.early)):
            for t in range(tiles):
                padded[index, field, t, 7:8, :] = edges[index, t, pl.ds(2 * field, 1), :]
                padded[index, field, t, 8 + z.width : 9 + z.width, :] = edges[index, t, pl.ds(2 * field + 1, 1), :]
            for low in range(0, z.width, 8):
                count = min(8, z.width - low)
                found = differences(padded.at[index, field], low, count, tiles)
                for t, pair in enumerate(found):
                    for kind, rows in enumerate(pair):
                        results[kind, index, field, t, low : low + count, :] = rows
        return carry

    lax.fori_loop(0, FIELDS, one_field, 0)


def early_differences(z, place, blocks, last):
    tiles = z.rows // LANES
    vmem, anywhere = pl.BlockSpec(memory_space=pltpu.VMEM), pl.BlockSpec(memory_space=pl.ANY)
    shape = (2, len(z.early), FIELDS, tiles, z.span, LANES)
    return pl.pallas_call(
        functools.partial(early_kernel, z),
        out_shape=[jax.ShapeDtypeStruct(last.shape, last.dtype), jax.ShapeDtypeStruct(shape, jnp.float32)],
        in_specs=[pl.BlockSpec(memory_space=pltpu.SMEM)] + [vmem] * len(blocks) + [anywhere],
        out_specs=[anywhere, vmem],
        scratch_shapes=[
            pltpu.VMEM((len(z.early), tiles, 8, LANES), jnp.float32),
            pltpu.VMEM((len(z.early), FIELDS, tiles, z.span + 16, LANES), jnp.float32),
        ],
        input_output_aliases={1 + len(blocks): 0},
        compiler_params=pltpu.CompilerParams(vmem_limit_bytes=VMEM),
        cost_estimate=pl.CostEstimate(flops=5_000_000, bytes_accessed=4_000_000, transcendentals=0),
        name="early_differences",
    )(place, *blocks, last)


def score_kernel(z, place, *refs):
    blocks = dict(zip(z.offsets, refs))
    early, analysis, crps, spread, strength, edges, padded = refs[z.regions :]
    me = place[0]
    step = pl.program_id(0)
    rows = z.rows

    def tile_of(offset, quad):
        return lax.rem(me ^ offset, z.makers) * z.quads + quad

    @pl.when(step == 0)
    def _():
        slot = lax.broadcasted_iota(jnp.int32, (8, LANES), 1) // ROWS
        for low in range(0, z.regions, QUAD):
            offsets = range(low, low + QUAD)
            slots = [lax.rem(me ^ offset, QUAD) for offset in offsets]
            at = lax.div(me ^ low, QUAD)
            for quad in range(z.quads):
                tails = [blocks[offset][quad, z.main : z.sent, :].astype(jnp.float32) for offset in offsets]
                for offset, tail in zip(offsets, tails):
                    edges[offset // z.makers, tile_of(offset, quad)] = tail[0:8]
                for g in range(quad * QUAD, min((quad + 1) * QUAD, z.span // 8)):
                    joined = jnp.zeros((8, LANES), jnp.float32)
                    for i, tail in zip(slots, tails):
                        near = pltpu.roll(tail[8:16], lax.rem(i + QUAD - g % QUAD, QUAD) * ROWS, 1)
                        joined = jnp.where(slot == i, near, joined)
                    strength[at, 8 * g : 8 * (g + 1), :] = joined + MID

    top = pl.multiple_of(step * STEP_FIELDS * z.span, 16)
    for offset in range(z.regions):
        if offset // z.makers in z.early:
            continue
        for quad in range(z.quads):
            values = blocks[offset][quad, pl.ds(top, STEP_FIELDS * z.span), :].astype(jnp.float32)
            for f in range(STEP_FIELDS):
                padded[offset // z.makers, f, tile_of(offset, quad), 8 : 8 + z.span, :] = values[
                    f * z.span : (f + 1) * z.span
                ]
    tiles = rows // LANES
    for sample in range(SAMPLES):
        if sample in z.early:
            continue
        for f in range(STEP_FIELDS):
            low = 2 * (step * STEP_FIELDS + f)
            for t in range(tiles):
                padded[sample, f, t, 7:8, :] = edges[sample, t, pl.ds(low, 1), :]
                padded[sample, f, t, 8 + z.width : 9 + z.width, :] = edges[sample, t, pl.ds(low + 1, 1), :]
    for f, low in ((f, low) for f in range(STEP_FIELDS) for low in range(0, z.width, 16)):
        high = min(low + 16, z.width)
        smoothed = [[] for _ in range(tiles)]
        for sample in range(SAMPLES):
            if sample in z.early:
                own = (z.early.index(sample), step * STEP_FIELDS + f)
                found = [[early[kind, *own, t, low:high, :] for kind in range(2)] for t in range(tiles)]
            else:
                found = differences(padded.at[sample, f], low, high - low, tiles)
            for t, (here, difference) in enumerate(found):
                smooth = here + strength[t, low:high, :] * difference
                smoothed[t].append(smooth.astype(jnp.bfloat16))
        for t, members in enumerate(smoothed):
            lanes = slice(LANES * t, LANES * (t + 1))
            values = [member.astype(jnp.float32) for member in members]
            target = analysis[f, low:high, lanes].astype(jnp.float32)
            error = sum(jnp.abs(value - target) for value in values) * (1.0 / SAMPLES)
            average = sum(values) * (1.0 / SAMPLES)
            variance = sum((value - average) ** 2 for value in values) * (1.0 / (SAMPLES - 1.0))
            ranked = list(members)
            for pairs in SORT_STEPS:
                for a, b in pairs:
                    ranked[a], ranked[b] = jnp.minimum(ranked[a], ranked[b]), jnp.maximum(ranked[a], ranked[b])
            ranked = [member.astype(jnp.float32) for member in ranked]
            pairs = sum(
                (2 * k - SAMPLES + 1.0) * (ranked[k] - ranked[SAMPLES - 1 - k])
                for k in range(SAMPLES // 2, SAMPLES)
            )
            crps[f, low:high, lanes] = (error - pairs * (1.0 / (SAMPLES * SAMPLES))).astype(jnp.bfloat16)
            spread[0, f, low:high, lanes] = variance.astype(jnp.bfloat16)
            spread[1, f, low:high, lanes] = ((average - target) ** 2).astype(jnp.bfloat16)


def score(z, place, blocks, early, analysis):
    width, rows = z.width, z.rows
    return pl.pallas_call(
        functools.partial(score_kernel, z),
        out_shape=[
            jax.ShapeDtypeStruct((FIELDS, width, rows), jnp.bfloat16),
            jax.ShapeDtypeStruct((2, FIELDS, width, rows), jnp.bfloat16),
        ],
        grid=(FIELDS // STEP_FIELDS,),
        in_specs=[pl.BlockSpec(memory_space=pltpu.SMEM)]
        + [pl.BlockSpec(memory_space=pltpu.VMEM)] * (z.regions + 1)
        + [pl.BlockSpec((STEP_FIELDS, width, rows), lambda i: (i, 0, 0))],
        out_specs=[
            pl.BlockSpec((STEP_FIELDS, width, rows), lambda i: (i, 0, 0)),
            pl.BlockSpec((2, STEP_FIELDS, width, rows), lambda i: (0, i, 0, 0)),
        ],
        scratch_shapes=[
            pltpu.VMEM((rows // LANES, z.span, LANES), jnp.float32),
            pltpu.VMEM((SAMPLES, rows // LANES, 8, LANES), jnp.float32),
            pltpu.VMEM((SAMPLES, STEP_FIELDS, rows // LANES, z.span + 16, LANES), jnp.float32),
        ],
        compiler_params=pltpu.CompilerParams(vmem_limit_bytes=VMEM),
        name="score",
    )(place, *blocks, early, analysis)


def shards(patch_tiles, slot_lists, blend_table, smoothing, analysis):
    z = Sizes(lax.axis_size("region"))
    place = lax.axis_index("region").reshape(1)
    turns = [
        [(i, i - i % z.makers + (i + k) % z.makers) for i in range(z.regions)] for k in range(1, z.makers)
    ]
    tiles = patch_tiles.reshape(z.regions, CAP, FIELDS, PAIRS * TILES, LANES)
    tiles = jnp.swapaxes(tiles, 2, 3).reshape(z.regions, CAP, LINES, LANES)
    lists = jnp.transpose(slot_lists, (2, 1, 0))
    received = [lax.ppermute(tiles, "region", turn) for turn in turns]
    lists = [lists] + [lax.ppermute(lists, "region", turn) for turn in turns]
    shares = own_share(z, place, lists[0], tiles, blend_table)
    shares = [*shares, strength_blocks(z, smoothing, shares[-1])]
    blocks = join(z, place, lists, received, shares)
    def swapped(block, offset):
        return lax.ppermute(block, "region", [(i, i ^ offset) for i in range(z.regions)])

    moved = [blocks[0]] + [swapped(block, offset) for block, offset in zip(blocks[1:-1], z.offsets[1:-1])]
    needed = [
        moved[z.offsets.index(sample * z.makers + part)] for sample in z.early for part in range(z.makers)
    ]
    last, early = early_differences(z, place, needed, blocks[-1])
    moved.append(swapped(last, z.offsets[-1]))
    outs = score(z, place, moved, early, jnp.swapaxes(analysis, 1, 2))
    return tuple(jnp.swapaxes(item, -1, -2) for item in outs)


def solution(mesh):
    return jax.shard_map(
        shards,
        mesh=mesh,
        in_specs=(
            P(("groups", "region"), None, None, None),
            P(("groups", "region"), None, None),
            P(),
            P("region", None),
            P(None, "groups", "region"),
        ),
        out_specs=(P(None, "groups", "region"), P(None, None, "groups", "region")),
        check_vma=False,
    )
```

```python
import functools

import jax
import jax.numpy as jnp
from jax import lax
from jax.experimental import pallas as pl
from jax.experimental.pallas import tpu as pltpu
from jax.sharding import PartitionSpec as P

SAMPLES = 8
FIELDS = 4
PATCH = 448
CAP = 2
ROWS = 32
COLS = 896
PAIRS = ROWS // 2
LINES = FIELDS * ROWS * PATCH // 128
LANES = 128
TILES = COLS // LANES
QUAD = LANES // ROWS
MID = 0.11
VMEM = 40 * 1024 * 1024
PACK_VMEM = 52 * 1024 * 1024
MOST_VMEM = 48 * 1024 * 1024


def round_up(value, step):
    return -(-value // step) * step


def swap_order(regions):
    half, quarter = regions // 2, regions // 4
    far = [offset for i in range(quarter) for offset in (half + quarter + i, half + i)]
    near = list(range(quarter, half)) + list(range(1, quarter))
    return [0] + [item for pair in zip(far, near + [None]) for item in pair if item is not None]


class Sizes:
    def __init__(self, regions):
        self.regions = regions
        self.makers = regions // SAMPLES
        self.block = regions // self.makers
        self.quads = self.block // QUAD
        self.width = COLS // regions
        self.span = round_up(self.width, 8)
        self.rows = regions * ROWS
        self.main = round_up(FIELDS * self.span, 16)
        self.offsets = swap_order(regions)
        arrived = self.offsets[: regions - 5]
        groups = [range(sample * self.makers, (sample + 1) * self.makers) for sample in range(SAMPLES)]
        self.early = [sample for sample, group in enumerate(groups) if all(k in arrived for k in group)]
        self.later = [
            sample
            for sample, group in enumerate(groups)
            if sample not in self.early and self.offsets[-1] not in group
        ]
        self.sent = self.main + 16


def stage(staged, tile):
    staged[...] = tile.astype(jnp.float32)


def staged_tile(staged, field, t):
    return staged[pl.ds(FIELDS * t + field, PAIRS, stride=FIELDS * TILES), :]


def weight_tile(weights, kind, t):
    return weights[t, pl.ds(pl.multiple_of(kind * PAIRS, PAIRS), PAIRS), :]


SLOTS = TILES + 2


def place_side(tile, column):
    pairs = jnp.concatenate([tile(t) for t in range(TILES)], 1)
    turned = pltpu.roll(pairs, PATCH, 1)
    lane = lax.broadcasted_iota(jnp.int32, pairs.shape, 1)
    left = (lane < PATCH) & (column == 0)
    right = (lane >= PATCH) & (column != 0)
    even = jnp.where(left, pairs, jnp.where(right, turned, 0.0))
    odd = jnp.where(left, turned, jnp.where(right, pairs, 0.0))
    return [[rows[:, LANES * t : LANES * (t + 1)] for t in range(TILES)] for rows in (even, odd)]


def add_any(sums, tile, column):
    lane = lax.broadcasted_iota(jnp.int32, (PAIRS, LANES), 1)
    middle = PATCH // LANES
    split = PATCH % LANES
    for parity in range(2):
        first = middle * parity
        start = column if parity == 0 else column + COLS - PATCH
        shift = lax.rem(start, LANES)
        at = lax.div(start, LANES) + first + 1 - (TILES if parity else 0)
        turned = []
        for t in range(first, first + middle + 1):
            piece = tile(t)
            if t == middle:
                piece = jnp.where((lane >= split) if parity else (lane < split), piece, 0.0)
            turned.append(pltpu.roll(piece, shift, 1))
        none = jnp.zeros((PAIRS, LANES), jnp.float32)
        for v in range(middle + 2):
            low = turned[v - 1] if v else none
            high = turned[v] if v <= middle else none
            sums[parity, at + v] = sums[parity, at + v] + jnp.where(lane < shift, low, high)


def place_all(side, sums, items):
    if side:
        placed = [place_side(*item) for item in items]
        return [[sum(item[parity][t] for item in placed) for t in range(TILES)] for parity in range(2)]
    for parity in range(2):
        for t in range(SLOTS):
            sums[parity, t] = jnp.zeros((PAIRS, LANES), jnp.float32)
    for item in items:
        add_any(sums, *item)
    return [[sums[parity, t + 1] for t in range(TILES)] for parity in range(2)]


def each_region(z, heavy, body):
    for i in range(QUAD):
        if z.makers == 2:
            body(i, True, range(1))
        else:
            pl.when(jnp.logical_not(heavy(i)))(functools.partial(body, i, False, range(1)))

    def again(i, carry):
        pl.when(heavy(i))(functools.partial(body, i, False, range(CAP)))
        return carry

    lax.fori_loop(0, QUAD, again, 0)


def staged_index(i, side, maker, slot, others):
    return i * others + maker if side else QUAD * others + maker * CAP + slot


def pack_kernel(z, place, tiles, *refs):
    packed, sems = refs[:-1], refs[-1]
    part = lax.rem(place[0], z.makers)
    copies = []
    for k, target in enumerate(packed):
        first = lax.rem(part + k + 1, z.makers) * z.block
        for j in range(z.block):
            copies.append(pltpu.make_async_copy(tiles.at[first + j], target.at[j], sems.at[k, j]))
    for copy in copies:
        copy.start()
    for copy in copies:
        copy.wait()


def pack(z, place, tiles):
    shape = jax.ShapeDtypeStruct((z.block, *tiles.shape[1:]), tiles.dtype)
    return pl.pallas_call(
        functools.partial(pack_kernel, z),
        out_shape=[shape] * (z.makers - 1),
        in_specs=[pl.BlockSpec(memory_space=pltpu.SMEM), pl.BlockSpec(memory_space=pltpu.HBM)],
        out_specs=[pl.BlockSpec(memory_space=pltpu.VMEM)] * (z.makers - 1),
        scratch_shapes=[pltpu.SemaphoreType.DMA((z.makers - 1, z.block))],
        compiler_params=pltpu.CompilerParams(vmem_limit_bytes=PACK_VMEM),
        name="pack",
    )(place, tiles)


def own_kernel(z, place, lists, tiles, table_hbm, *refs):
    half, (total, weights, landed, staged, sums, table, sems) = refs[:FIELDS], refs[FIELDS:]
    first = lax.rem(place[0], z.makers) * z.block

    def fetch(j):
        return pltpu.make_async_copy(tiles.at[first + j], landed.at[j], sems.at[j])

    fetch_table = pltpu.make_async_copy(table_hbm, table, sems.at[z.block])
    fetch_table.start()
    for j in range(z.block):
        fetch(j).start()
    fetch_table.wait()
    kinds = table.shape[0]
    for k in range(PAIRS):
        for t in range(TILES):
            at = COLS * k + LANES * t
            for low in range(0, kinds, 8):
                count = min(8, kinds - low)
                weights[t, pl.ds(PAIRS * low + k, count, stride=PAIRS), :] = table[
                    low : low + count, at : at + LANES
                ]

    def group(quad, carry):
        for i in range(QUAD):
            fetch(quad * QUAD + i).wait()

        def body(i, side, slots):
            j = quad * QUAD + i

            def weight_item(slot):
                column, kind = (lists[entry, slot, first + j] for entry in (1, 2))
                return functools.partial(weight_tile, weights, kind), column

            def field_item(field, slot):
                weight, column = weight_item(slot)
                own = staged.at[staged_index(i, side, 0, slot, 1)]
                return lambda t: staged_tile(own, field, t) * weight(t), column

            for slot in slots:
                stage(staged.at[staged_index(i, side, 0, slot, 1)], landed[j, slot])
            for index in range(FIELDS + 1):
                items = [field_item(index, slot) if index < FIELDS else weight_item(slot) for slot in slots]
                pieces = place_all(side, sums.at[index], items)
                target = half[index] if index < FIELDS else total
                for parity in range(2):
                    for t in range(TILES):
                        target[j, parity, t] = pieces[parity][t]

        each_region(z, lambda i: lists[0, 1, first + quad * QUAD + i] >= 0, body)
        return carry

    lax.fori_loop(0, z.quads, group, 0)


def own_share(z, place, lists, tiles, table):
    smem = pl.BlockSpec(memory_space=pltpu.SMEM)
    vmem = pl.BlockSpec(memory_space=pltpu.VMEM)
    hbm = pl.BlockSpec(memory_space=pltpu.HBM)
    kinds = round_up(table.shape[0], 8)
    return pl.pallas_call(
        functools.partial(own_kernel, z),
        out_shape=[
            *[jax.ShapeDtypeStruct((z.block, 2, TILES, PAIRS, LANES), jnp.float32)] * (FIELDS + 1),
            jax.ShapeDtypeStruct((TILES, kinds * PAIRS, LANES), jnp.float32),
        ],
        in_specs=[smem, smem, hbm, hbm],
        out_specs=[vmem] * (FIELDS + 2),
        scratch_shapes=[
            pltpu.VMEM((z.block, CAP, LINES, LANES), jnp.bfloat16),
            pltpu.VMEM((QUAD + CAP, LINES, LANES), jnp.float32),
            pltpu.VMEM((FIELDS + 1, 2, SLOTS, PAIRS, LANES), jnp.float32),
            pltpu.VMEM(table.shape, jnp.float32),
            pltpu.SemaphoreType.DMA((z.block + 1,)),
        ],
        compiler_params=pltpu.CompilerParams(vmem_limit_bytes=MOST_VMEM),
        cost_estimate=pl.CostEstimate(flops=5_000_000, bytes_accessed=8_000_000, transcendentals=0),
        name="own_share",
    )(place, lists, tiles, table)


def strength_kernel(z, smoothing, _, strength):
    turned_strength = jnp.transpose(smoothing[...] - MID)
    for dest in range(z.regions):
        for g in range(z.span // 8):
            top = z.width * dest + 8 * g
            count, at = min(8, COLS - top), ROWS * (g % QUAD)
            strength[dest, g // QUAD, 0:count, at : at + ROWS] = turned_strength[top : top + count]


def strength_blocks(z, smoothing, before):
    return pl.pallas_call(
        functools.partial(strength_kernel, z),
        out_shape=jax.ShapeDtypeStruct((z.regions, z.quads, 8, LANES), jnp.float32),
        in_specs=[pl.BlockSpec(memory_space=pltpu.VMEM), pl.BlockSpec(memory_space=pl.ANY)],
        out_specs=pl.BlockSpec(memory_space=pltpu.VMEM),
        compiler_params=pltpu.CompilerParams(vmem_limit_bytes=VMEM),
        name="strength_blocks",
    )(smoothing, before)


def join_kernel(z, *refs):
    place, lists, refs = refs[0], refs[1 : 1 + z.makers], refs[1 + z.makers :]
    received, refs = refs[: z.makers - 1], refs[z.makers - 1 :]
    half, (total, weights, strength), outs = refs[:FIELDS], refs[FIELDS : FIELDS + 3], refs[FIELDS + 3 : -5]
    staged, sums, lines, turned, edges = refs[-5:]
    me = place[0]
    first = lax.rem(me, z.makers) * z.block
    row, column = (lax.broadcasted_iota(jnp.int32, (LANES, LANES), axis) for axis in (0, 1))
    identity = (row == column).astype(jnp.bfloat16)

    for quad in range(z.quads):

        def body(i, side, slots):
            j = quad * QUAD + i
            sources = [(maker, slot) for maker in range(1, z.makers) for slot in slots]

            def staged_of(maker, slot):
                return staged.at[staged_index(i, side, maker - 1, slot, z.makers - 1)]

            def weight_item(maker, slot):
                column, kind = (lists[maker][entry, slot, first + j] for entry in (1, 2))
                return functools.partial(weight_tile, weights, kind), column

            def field_item(field, maker, slot):
                weight, column = weight_item(maker, slot)
                return lambda t: staged_tile(staged_of(maker, slot), field, t) * weight(t), column

            for maker, slot in sources:
                stage(staged_of(maker, slot), received[maker - 1][j, slot])
            others = place_all(side, sums.at[FIELDS], [weight_item(*source) for source in sources])
            inverse = [[1.0 / (total[j, parity, t] + others[parity][t]) for t in range(TILES)] for parity in range(2)]
            for field in range(FIELDS):
                pieces = place_all(side, sums.at[field], [field_item(field, *source) for source in sources])
                for parity in range(2):
                    for t in range(TILES):
                        lines[field, t, pl.ds(ROWS * i + parity, PAIRS, stride=2), :] = (
                            half[field][j, parity, t] + pieces[parity][t]
                        ) * inverse[parity][t]

        each_region(z, lambda i: lists[0][0, 1, first + quad * QUAD + i] >= 0, body)
        for t in range(TILES):
            for field in range(FIELDS):
                here = slice(LANES * t, LANES * (t + 1))
                if field % 2:
                    turned[field, here, :] = jnp.transpose(lines[field, t])
                else:
                    turned[field, here, :] = lax.dot_general(
                        identity,
                        lines[field, t].astype(jnp.bfloat16),
                        (((1,), (1,)), ((), ())),
                        preferred_element_type=jnp.float32,
                    )
        for i, (out, offset) in enumerate(zip(outs, z.offsets)):
            dest = me ^ offset
            top = dest * z.width
            if z.width % 8 == 0:
                top = pl.multiple_of(top, 8)
            ends = (jnp.maximum(top - 1, 0), jnp.minimum(top + z.width, COLS - 1))
            for field in range(FIELDS):
                for side, end in enumerate(ends):
                    edges[i, 2 * field + side : 2 * field + side + 1, :] = turned[field, pl.ds(end, 1), :]
            for low in range(0, FIELDS, 2):
                block = [turned[field, pl.ds(top, z.span), :] for field in (low, low + 1)]
                out[quad, low * z.span : (low + 2) * z.span, :] = jnp.concatenate(block, 0).astype(jnp.bfloat16)
            tail = jnp.concatenate([edges[i], strength[dest, quad]], 0)
            out[quad, z.main : z.sent, :] = tail.astype(jnp.bfloat16)


def join(z, place, lists, received, shares):
    smem = pl.BlockSpec(memory_space=pltpu.SMEM)
    vmem = pl.BlockSpec(memory_space=pltpu.VMEM)
    shape = (z.quads, z.sent, LANES)
    return pl.pallas_call(
        functools.partial(join_kernel, z),
        out_shape=[jax.ShapeDtypeStruct(shape, jnp.bfloat16)] * z.regions,
        in_specs=[smem] * (1 + z.makers) + [vmem] * (z.makers - 1 + len(shares)),
        out_specs=[vmem] * z.regions,
        scratch_shapes=[
            pltpu.VMEM(((QUAD + CAP) * (z.makers - 1), LINES, LANES), jnp.float32),
            pltpu.VMEM((FIELDS + 1, 2, SLOTS, PAIRS, LANES), jnp.float32),
            pltpu.VMEM((FIELDS, TILES, LANES, LANES), jnp.float32),
            pltpu.VMEM((FIELDS, COLS + 8, LANES), jnp.float32),
            pltpu.VMEM((z.regions, 8, LANES), jnp.float32),
        ],
        compiler_params=pltpu.CompilerParams(vmem_limit_bytes=VMEM),
        cost_estimate=pl.CostEstimate(flops=5_000_000, bytes_accessed=8_000_000, transcendentals=0),
        name="join",
    )(place, *lists, *received, *shares)


SORT_STEPS = (
    ((0, 1), (2, 3), (4, 5), (6, 7)),
    ((0, 2), (1, 3), (4, 6), (5, 7)),
    ((1, 2), (5, 6)),
    ((0, 4), (1, 5), (2, 6), (3, 7)),
    ((2, 4), (3, 5)),
    ((1, 2), (3, 4), (5, 6)),
)
STEP_FIELDS = 2


def differences(field, low, count, tiles):
    lane = lax.broadcasted_iota(jnp.int32, (count, LANES), 1)
    pieces = [field[t, 8 + low : 8 + low + count, :] for t in range(tiles)]
    later = [pltpu.roll(piece, 1, 1) for piece in pieces]
    sooner = [pltpu.roll(piece, LANES - 1, 1) for piece in pieces]
    results = []
    for t, here in enumerate(pieces):
        above = jnp.where(lane == 0, later[t - 1] if t else here, later[t])
        below = jnp.where(lane == LANES - 1, sooner[t + 1] if t + 1 < tiles else here, sooner[t])
        sides = field[t, 7 + low : 7 + low + count, :] + field[t, 9 + low : 9 + low + count, :]
        results.append((here, above + below + sides - 4.0 * here))
    return results


def early_kernel(z, samples, place, *refs):
    offsets = [sample * z.makers + part for sample in samples for part in range(z.makers)]
    blocks = dict(zip(offsets, refs))
    results, edges, padded = refs[-3:]
    me = place[0]
    tiles = z.rows // LANES
    for offset in offsets:
        index = samples.index(offset // z.makers)
        for quad in range(z.quads):
            tile = lax.rem(me ^ offset, z.makers) * z.quads + quad
            values = blocks[offset][quad, 0 : z.main, :].astype(jnp.float32)
            tail = blocks[offset][quad, z.main : z.sent, :].astype(jnp.float32)
            for field in range(FIELDS):
                target = padded.at[index, field, tile]
                target[8 : 8 + z.span, :] = values[field * z.span : (field + 1) * z.span]
            edges[index, tile] = tail[0:8]

    def one_field(field, carry):
        for index in range(len(samples)):
            for t in range(tiles):
                padded[index, field, t, 7:8, :] = edges[index, t, pl.ds(2 * field, 1), :]
                padded[index, field, t, 8 + z.width : 9 + z.width, :] = edges[index, t, pl.ds(2 * field + 1, 1), :]
            for low in range(0, z.width, 8):
                count = min(8, z.width - low)
                found = differences(padded.at[index, field], low, count, tiles)
                for t, pair in enumerate(found):
                    for kind, rows in enumerate(pair):
                        results[kind, index, field, t, low : low + count, :] = rows
        return carry

    lax.fori_loop(0, FIELDS, one_field, 0)


def early_differences(z, samples, place, blocks, last=()):
    tiles = z.rows // LANES
    vmem, anywhere = pl.BlockSpec(memory_space=pltpu.VMEM), pl.BlockSpec(memory_space=pl.ANY)
    shape = (2, len(samples), FIELDS, tiles, z.span, LANES)
    return pl.pallas_call(
        functools.partial(early_kernel, z, samples),
        out_shape=[jax.ShapeDtypeStruct(item.shape, item.dtype) for item in last]
        + [jax.ShapeDtypeStruct(shape, jnp.float32)],
        in_specs=[pl.BlockSpec(memory_space=pltpu.SMEM)] + [vmem] * len(blocks) + [anywhere] * len(last),
        out_specs=[anywhere] * len(last) + [vmem],
        scratch_shapes=[
            pltpu.VMEM((len(samples), tiles, 8, LANES), jnp.float32),
            pltpu.VMEM((len(samples), FIELDS, tiles, z.span + 16, LANES), jnp.float32),
        ],
        input_output_aliases={1 + len(blocks) + i: i for i in range(len(last))},
        compiler_params=pltpu.CompilerParams(vmem_limit_bytes=VMEM),
        cost_estimate=pl.CostEstimate(flops=5_000_000, bytes_accessed=4_000_000, transcendentals=0),
        name="early_differences",
    )(place, *blocks, *last)


def score_kernel(z, place, *refs):
    blocks = dict(zip(z.offsets, refs))
    early, later, analysis, crps, spread, strength, edges, padded = refs[z.regions :]
    me = place[0]
    step = pl.program_id(0)
    rows = z.rows

    def tile_of(offset, quad):
        return lax.rem(me ^ offset, z.makers) * z.quads + quad

    @pl.when(step == 0)
    def _():
        slot = lax.broadcasted_iota(jnp.int32, (8, LANES), 1) // ROWS
        for low in range(0, z.regions, QUAD):
            offsets = range(low, low + QUAD)
            slots = [lax.rem(me ^ offset, QUAD) for offset in offsets]
            at = lax.div(me ^ low, QUAD)
            for quad in range(z.quads):
                tails = [blocks[offset][quad, z.main : z.sent, :].astype(jnp.float32) for offset in offsets]
                for offset, tail in zip(offsets, tails):
                    edges[offset // z.makers, tile_of(offset, quad)] = tail[0:8]
                for g in range(quad * QUAD, min((quad + 1) * QUAD, z.span // 8)):
                    joined = jnp.zeros((8, LANES), jnp.float32)
                    for i, tail in zip(slots, tails):
                        near = pltpu.roll(tail[8:16], lax.rem(i + QUAD - g % QUAD, QUAD) * ROWS, 1)
                        joined = jnp.where(slot == i, near, joined)
                    strength[at, 8 * g : 8 * (g + 1), :] = joined + MID

    top = pl.multiple_of(step * STEP_FIELDS * z.span, 16)
    for offset in range(z.regions):
        if offset // z.makers in z.early + z.later:
            continue
        for quad in range(z.quads):
            values = blocks[offset][quad, pl.ds(top, STEP_FIELDS * z.span), :].astype(jnp.float32)
            for f in range(STEP_FIELDS):
                padded[offset // z.makers, f, tile_of(offset, quad), 8 : 8 + z.span, :] = values[
                    f * z.span : (f + 1) * z.span
                ]
    tiles = rows // LANES
    for sample in range(SAMPLES):
        if sample in z.early + z.later:
            continue
        for f in range(STEP_FIELDS):
            low = 2 * (step * STEP_FIELDS + f)
            for t in range(tiles):
                padded[sample, f, t, 7:8, :] = edges[sample, t, pl.ds(low, 1), :]
                padded[sample, f, t, 8 + z.width : 9 + z.width, :] = edges[sample, t, pl.ds(low + 1, 1), :]
    for f, low in ((f, low) for f in range(STEP_FIELDS) for low in range(0, z.width, 16)):
        high = min(low + 16, z.width)
        smoothed = [[] for _ in range(tiles)]
        for sample in range(SAMPLES):
            if sample in z.early + z.later:
                samples, ready = (z.early, early) if sample in z.early else (z.later, later)
                own = (samples.index(sample), step * STEP_FIELDS + f)
                found = [[ready[kind, *own, t, low:high, :] for kind in range(2)] for t in range(tiles)]
            else:
                found = differences(padded.at[sample, f], low, high - low, tiles)
            for t, (here, difference) in enumerate(found):
                smooth = here + strength[t, low:high, :] * difference
                smoothed[t].append(smooth.astype(jnp.bfloat16))
        for t, members in enumerate(smoothed):
            lanes = slice(LANES * t, LANES * (t + 1))
            values = [member.astype(jnp.float32) for member in members]
            target = analysis[f, low:high, lanes].astype(jnp.float32)
            error = sum(jnp.abs(value - target) for value in values) * (1.0 / SAMPLES)
            average = sum(values) * (1.0 / SAMPLES)
            variance = sum((value - average) ** 2 for value in values) * (1.0 / (SAMPLES - 1.0))
            ranked = list(members)
            for pairs in SORT_STEPS:
                for a, b in pairs:
                    ranked[a], ranked[b] = jnp.minimum(ranked[a], ranked[b]), jnp.maximum(ranked[a], ranked[b])
            ranked = [member.astype(jnp.float32) for member in ranked]
            pairs = sum(
                (2 * k - SAMPLES + 1.0) * (ranked[k] - ranked[SAMPLES - 1 - k])
                for k in range(SAMPLES // 2, SAMPLES)
            )
            crps[f, low:high, lanes] = (error - pairs * (1.0 / (SAMPLES * SAMPLES))).astype(jnp.bfloat16)
            spread[0, f, low:high, lanes] = variance.astype(jnp.bfloat16)
            spread[1, f, low:high, lanes] = ((average - target) ** 2).astype(jnp.bfloat16)


def score(z, place, blocks, early, later, analysis):
    width, rows = z.width, z.rows
    return pl.pallas_call(
        functools.partial(score_kernel, z),
        out_shape=[
            jax.ShapeDtypeStruct((FIELDS, width, rows), jnp.bfloat16),
            jax.ShapeDtypeStruct((2, FIELDS, width, rows), jnp.bfloat16),
        ],
        grid=(FIELDS // STEP_FIELDS,),
        in_specs=[pl.BlockSpec(memory_space=pltpu.SMEM)]
        + [pl.BlockSpec(memory_space=pltpu.VMEM)] * (z.regions + 2)
        + [pl.BlockSpec((STEP_FIELDS, width, rows), lambda i: (i, 0, 0))],
        out_specs=[
            pl.BlockSpec((STEP_FIELDS, width, rows), lambda i: (i, 0, 0)),
            pl.BlockSpec((2, STEP_FIELDS, width, rows), lambda i: (0, i, 0, 0)),
        ],
        scratch_shapes=[
            pltpu.VMEM((rows // LANES, z.span, LANES), jnp.float32),
            pltpu.VMEM((SAMPLES, rows // LANES, 8, LANES), jnp.float32),
            pltpu.VMEM((SAMPLES, STEP_FIELDS, rows // LANES, z.span + 16, LANES), jnp.float32),
        ],
        compiler_params=pltpu.CompilerParams(vmem_limit_bytes=VMEM),
        name="score",
    )(place, *blocks, early, later, analysis)


def shards(patch_tiles, slot_lists, blend_table, smoothing, analysis):
    z = Sizes(lax.axis_size("region"))
    place = lax.axis_index("region").reshape(1)
    turns = [
        [(i, i - i % z.makers + (i + k) % z.makers) for i in range(z.regions)] for k in range(1, z.makers)
    ]
    tiles = patch_tiles.reshape(z.regions, CAP, FIELDS, PAIRS * TILES, LANES)
    tiles = jnp.swapaxes(tiles, 2, 3).reshape(z.regions, CAP, LINES, LANES)
    lists = jnp.transpose(slot_lists, (2, 1, 0))
    received = [lax.ppermute(item, "region", turn) for item, turn in zip(pack(z, place, tiles), turns)]
    lists = [lists] + [lax.ppermute(lists, "region", turn) for turn in turns]
    shares = own_share(z, place, lists[0], tiles, blend_table)
    shares = [*shares, strength_blocks(z, smoothing, shares[-1])]
    blocks = join(z, place, lists, received, shares)
    def swapped(block, offset):
        return lax.ppermute(block, "region", [(i, i ^ offset) for i in range(z.regions)])

    moved = [blocks[0]] + [swapped(block, offset) for block, offset in zip(blocks[1:-1], z.offsets[1:-1])]
    def blocks_of(samples):
        return [moved[z.offsets.index(sample * z.makers + part)] for sample in samples for part in range(z.makers)]

    last, early = early_differences(z, z.early, place, blocks_of(z.early), [blocks[-1]])
    (later,) = early_differences(z, z.later, place, blocks_of(z.later))
    moved.append(swapped(last, z.offsets[-1]))
    outs = score(z, place, moved, early, later, jnp.swapaxes(analysis, 1, 2))
    return tuple(jnp.swapaxes(item, -1, -2) for item in outs)


def solution(mesh):
    return jax.shard_map(
        shards,
        mesh=mesh,
        in_specs=(
            P(("groups", "region"), None, None, None),
            P(("groups", "region"), None, None),
            P(),
            P("region", None),
            P(None, "groups", "region"),
        ),
        out_specs=(P(None, "groups", "region"), P(None, None, "groups", "region")),
        check_vma=False,
    )
```

```python
import functools

import jax
import jax.numpy as jnp
from jax import lax
from jax.experimental import pallas as pl
from jax.experimental.pallas import tpu as pltpu
from jax.sharding import PartitionSpec as P

SAMPLES = 8
FIELDS = 4
PATCH = 448
CAP = 2
ROWS = 32
COLS = 896
PAIRS = ROWS // 2
LINES = FIELDS * ROWS * PATCH // 128
LANES = 128
TILES = COLS // LANES
QUAD = LANES // ROWS
MID = 0.11
VMEM = 40 * 1024 * 1024
PACK_VMEM = 52 * 1024 * 1024
MOST_VMEM = 48 * 1024 * 1024


def round_up(value, step):
    return -(-value // step) * step


def swap_order(regions):
    half, quarter = regions // 2, regions // 4
    far = [offset for i in range(quarter) for offset in (half + quarter + i, half + i)]
    near = list(range(quarter, half)) + list(range(1, quarter))
    return [0] + [item for pair in zip(far, near + [None]) for item in pair if item is not None]


class Sizes:
    def __init__(self, regions):
        self.regions = regions
        self.makers = regions // SAMPLES
        self.block = regions // self.makers
        self.quads = self.block // QUAD
        self.width = COLS // regions
        self.span = round_up(self.width, 8)
        self.rows = regions * ROWS
        self.main = round_up(FIELDS * self.span, 16)
        self.offsets = swap_order(regions)
        arrived = self.offsets[: regions - 5]
        groups = [range(sample * self.makers, (sample + 1) * self.makers) for sample in range(SAMPLES)]
        self.early = [sample for sample, group in enumerate(groups) if all(k in arrived for k in group)]
        self.later = [
            sample
            for sample, group in enumerate(groups)
            if sample not in self.early and self.offsets[-1] not in group
        ]
        self.sent = self.main + 16


def stage(staged, tile):
    staged[...] = tile.astype(jnp.float32)


def staged_tile(staged, field, t):
    return staged[pl.ds(FIELDS * t + field, PAIRS, stride=FIELDS * TILES), :]


def weight_tile(weights, kind, t):
    return weights[t, pl.ds(pl.multiple_of(kind * PAIRS, PAIRS), PAIRS), :]


SLOTS = TILES + 2


def place_side(tile, column):
    pairs = jnp.concatenate([tile(t) for t in range(TILES)], 1)
    turned = pltpu.roll(pairs, PATCH, 1)
    lane = lax.broadcasted_iota(jnp.int32, pairs.shape, 1)
    left = (lane < PATCH) & (column == 0)
    right = (lane >= PATCH) & (column != 0)
    even = jnp.where(left, pairs, jnp.where(right, turned, 0.0))
    odd = jnp.where(left, turned, jnp.where(right, pairs, 0.0))
    return [[rows[:, LANES * t : LANES * (t + 1)] for t in range(TILES)] for rows in (even, odd)]


def add_any(sums, tile, column):
    lane = lax.broadcasted_iota(jnp.int32, (PAIRS, LANES), 1)
    middle = PATCH // LANES
    split = PATCH % LANES
    for parity in range(2):
        first = middle * parity
        start = column if parity == 0 else column + COLS - PATCH
        shift = lax.rem(start, LANES)
        at = lax.div(start, LANES) + first + 1 - (TILES if parity else 0)
        turned = []
        for t in range(first, first + middle + 1):
            piece = tile(t)
            if t == middle:
                piece = jnp.where((lane >= split) if parity else (lane < split), piece, 0.0)
            turned.append(pltpu.roll(piece, shift, 1))
        none = jnp.zeros((PAIRS, LANES), jnp.float32)
        for v in range(middle + 2):
            low = turned[v - 1] if v else none
            high = turned[v] if v <= middle else none
            sums[parity, at + v] = sums[parity, at + v] + jnp.where(lane < shift, low, high)


def place_all(side, sums, items):
    if side:
        placed = [place_side(*item) for item in items]
        return [[sum(item[parity][t] for item in placed) for t in range(TILES)] for parity in range(2)]
    for parity in range(2):
        for t in range(SLOTS):
            sums[parity, t] = jnp.zeros((PAIRS, LANES), jnp.float32)
    for item in items:
        add_any(sums, *item)
    return [[sums[parity, t + 1] for t in range(TILES)] for parity in range(2)]


def each_region(z, heavy, body):
    for i in range(QUAD):
        if z.makers == 2:
            body(i, True, range(1))
        else:
            pl.when(jnp.logical_not(heavy(i)))(functools.partial(body, i, False, range(1)))

    def again(i, carry):
        pl.when(heavy(i))(functools.partial(body, i, False, range(CAP)))
        return carry

    lax.fori_loop(0, QUAD, again, 0)


def staged_index(i, side, maker, slot, others):
    return i * others + maker if side else QUAD * others + maker * CAP + slot


def pack_kernel(z, place, tiles, *refs):
    packed, sems = refs[:-1], refs[-1]
    part = lax.rem(place[0], z.makers)
    copies = []
    for k, target in enumerate(packed):
        first = lax.rem(part + k + 1, z.makers) * z.block
        for j in range(z.block):
            copies.append(pltpu.make_async_copy(tiles.at[first + j], target.at[j], sems.at[k, j]))
    for copy in copies:
        copy.start()
    for copy in copies:
        copy.wait()


def pack(z, place, tiles):
    shape = jax.ShapeDtypeStruct((z.block, *tiles.shape[1:]), tiles.dtype)
    return pl.pallas_call(
        functools.partial(pack_kernel, z),
        out_shape=[shape] * (z.makers - 1),
        in_specs=[pl.BlockSpec(memory_space=pltpu.SMEM), pl.BlockSpec(memory_space=pltpu.HBM)],
        out_specs=[pl.BlockSpec(memory_space=pltpu.VMEM)] * (z.makers - 1),
        scratch_shapes=[pltpu.SemaphoreType.DMA((z.makers - 1, z.block))],
        compiler_params=pltpu.CompilerParams(vmem_limit_bytes=PACK_VMEM),
        name="pack",
    )(place, tiles)


def own_kernel(z, place, lists, tiles, table_hbm, *refs):
    half, (total, weights, landed, staged, sums, table, sems, table_sem) = refs[:FIELDS], refs[FIELDS:]
    first = lax.rem(place[0], z.makers) * z.block

    def fetch(j, slot):
        return pltpu.make_async_copy(tiles.at[first + j, slot], landed.at[j, slot], sems.at[j, slot])

    def heavy(j):
        return lists[0, 1, first + j] >= 0

    fetch_table = pltpu.make_async_copy(table_hbm, table, table_sem.at[0])
    fetch_table.start()
    for j in range(z.block):
        fetch(j, 0).start()
    for j in range(z.block):
        pl.when(heavy(j))(fetch(j, 1).start)
    fetch_table.wait()
    kinds = table.shape[0]
    for k in range(PAIRS):
        for t in range(TILES):
            at = COLS * k + LANES * t
            for low in range(0, kinds, 8):
                count = min(8, kinds - low)
                weights[t, pl.ds(PAIRS * low + k, count, stride=PAIRS), :] = table[
                    low : low + count, at : at + LANES
                ]

    def group(quad, carry):
        for i in range(QUAD):
            fetch(quad * QUAD + i, 0).wait()

        def body(i, side, slots):
            j = quad * QUAD + i
            if len(slots) > 1:
                fetch(j, 1).wait()

            def weight_item(slot):
                column, kind = (lists[entry, slot, first + j] for entry in (1, 2))
                return functools.partial(weight_tile, weights, kind), column

            def field_item(field, slot):
                weight, column = weight_item(slot)
                own = staged.at[staged_index(i, side, 0, slot, 1)]
                return lambda t: staged_tile(own, field, t) * weight(t), column

            for slot in slots:
                stage(staged.at[staged_index(i, side, 0, slot, 1)], landed[j, slot])
            for index in range(FIELDS + 1):
                items = [field_item(index, slot) if index < FIELDS else weight_item(slot) for slot in slots]
                pieces = place_all(side, sums.at[index], items)
                target = half[index] if index < FIELDS else total
                for parity in range(2):
                    for t in range(TILES):
                        target[j, parity, t] = pieces[parity][t]

        each_region(z, lambda i: heavy(quad * QUAD + i), body)
        return carry

    lax.fori_loop(0, z.quads, group, 0)


def own_share(z, place, lists, tiles, table):
    smem = pl.BlockSpec(memory_space=pltpu.SMEM)
    vmem = pl.BlockSpec(memory_space=pltpu.VMEM)
    hbm = pl.BlockSpec(memory_space=pltpu.HBM)
    kinds = round_up(table.shape[0], 8)
    return pl.pallas_call(
        functools.partial(own_kernel, z),
        out_shape=[
            *[jax.ShapeDtypeStruct((z.block, 2, TILES, PAIRS, LANES), jnp.float32)] * (FIELDS + 1),
            jax.ShapeDtypeStruct((TILES, kinds * PAIRS, LANES), jnp.float32),
        ],
        in_specs=[smem, smem, hbm, hbm],
        out_specs=[vmem] * (FIELDS + 2),
        scratch_shapes=[
            pltpu.VMEM((z.block, CAP, LINES, LANES), jnp.bfloat16),
            pltpu.VMEM((QUAD + CAP, LINES, LANES), jnp.float32),
            pltpu.VMEM((FIELDS + 1, 2, SLOTS, PAIRS, LANES), jnp.float32),
            pltpu.VMEM(table.shape, jnp.float32),
            pltpu.SemaphoreType.DMA((z.block, CAP)),
            pltpu.SemaphoreType.DMA((1,)),
        ],
        compiler_params=pltpu.CompilerParams(vmem_limit_bytes=MOST_VMEM),
        cost_estimate=pl.CostEstimate(flops=5_000_000, bytes_accessed=8_000_000, transcendentals=0),
        name="own_share",
    )(place, lists, tiles, table)


def strength_kernel(z, smoothing, _, strength):
    turned_strength = jnp.transpose(smoothing[...] - MID)
    for dest in range(z.regions):
        for g in range(z.span // 8):
            top = z.width * dest + 8 * g
            count, at = min(8, COLS - top), ROWS * (g % QUAD)
            strength[dest, g // QUAD, 0:count, at : at + ROWS] = turned_strength[top : top + count]


def strength_blocks(z, smoothing, before):
    return pl.pallas_call(
        functools.partial(strength_kernel, z),
        out_shape=jax.ShapeDtypeStruct((z.regions, z.quads, 8, LANES), jnp.float32),
        in_specs=[pl.BlockSpec(memory_space=pltpu.VMEM), pl.BlockSpec(memory_space=pl.ANY)],
        out_specs=pl.BlockSpec(memory_space=pltpu.VMEM),
        compiler_params=pltpu.CompilerParams(vmem_limit_bytes=VMEM),
        name="strength_blocks",
    )(smoothing, before)


def join_kernel(z, *refs):
    place, lists, refs = refs[0], refs[1 : 1 + z.makers], refs[1 + z.makers :]
    received, refs = refs[: z.makers - 1], refs[z.makers - 1 :]
    half, (total, weights, strength), outs = refs[:FIELDS], refs[FIELDS : FIELDS + 3], refs[FIELDS + 3 : -5]
    staged, sums, lines, turned, edges = refs[-5:]
    me = place[0]
    first = lax.rem(me, z.makers) * z.block
    row, column = (lax.broadcasted_iota(jnp.int32, (LANES, LANES), axis) for axis in (0, 1))
    identity = (row == column).astype(jnp.bfloat16)

    for quad in range(z.quads):

        def body(i, side, slots):
            j = quad * QUAD + i
            sources = [(maker, slot) for maker in range(1, z.makers) for slot in slots]

            def staged_of(maker, slot):
                return staged.at[staged_index(i, side, maker - 1, slot, z.makers - 1)]

            def weight_item(maker, slot):
                column, kind = (lists[maker][entry, slot, first + j] for entry in (1, 2))
                return functools.partial(weight_tile, weights, kind), column

            def field_item(field, maker, slot):
                weight, column = weight_item(maker, slot)
                return lambda t: staged_tile(staged_of(maker, slot), field, t) * weight(t), column

            for maker, slot in sources:
                stage(staged_of(maker, slot), received[maker - 1][j, slot])
            others = place_all(side, sums.at[FIELDS], [weight_item(*source) for source in sources])
            inverse = [[1.0 / (total[j, parity, t] + others[parity][t]) for t in range(TILES)] for parity in range(2)]
            for field in range(FIELDS):
                pieces = place_all(side, sums.at[field], [field_item(field, *source) for source in sources])
                for parity in range(2):
                    for t in range(TILES):
                        lines[field, t, pl.ds(ROWS * i + parity, PAIRS, stride=2), :] = (
                            half[field][j, parity, t] + pieces[parity][t]
                        ) * inverse[parity][t]

        each_region(z, lambda i: lists[0][0, 1, first + quad * QUAD + i] >= 0, body)
        for t in range(TILES):
            for field in range(FIELDS):
                here = slice(LANES * t, LANES * (t + 1))
                if field % 2:
                    turned[field, here, :] = jnp.transpose(lines[field, t])
                else:
                    turned[field, here, :] = lax.dot_general(
                        identity,
                        lines[field, t].astype(jnp.bfloat16),
                        (((1,), (1,)), ((), ())),
                        preferred_element_type=jnp.float32,
                    )
        for i, (out, offset) in enumerate(zip(outs, z.offsets)):
            dest = me ^ offset
            top = dest * z.width
            if z.width % 8 == 0:
                top = pl.multiple_of(top, 8)
            ends = (jnp.maximum(top - 1, 0), jnp.minimum(top + z.width, COLS - 1))
            for field in range(FIELDS):
                for side, end in enumerate(ends):
                    edges[i, 2 * field + side : 2 * field + side + 1, :] = turned[field, pl.ds(end, 1), :]
            for low in range(0, FIELDS, 2):
                block = [turned[field, pl.ds(top, z.span), :] for field in (low, low + 1)]
                out[quad, low * z.span : (low + 2) * z.span, :] = jnp.concatenate(block, 0).astype(jnp.bfloat16)
            tail = jnp.concatenate([edges[i], strength[dest, quad]], 0)
            out[quad, z.main : z.sent, :] = tail.astype(jnp.bfloat16)


def join(z, place, lists, received, shares):
    smem = pl.BlockSpec(memory_space=pltpu.SMEM)
    vmem = pl.BlockSpec(memory_space=pltpu.VMEM)
    shape = (z.quads, z.sent, LANES)
    return pl.pallas_call(
        functools.partial(join_kernel, z),
        out_shape=[jax.ShapeDtypeStruct(shape, jnp.bfloat16)] * z.regions,
        in_specs=[smem] * (1 + z.makers) + [vmem] * (z.makers - 1 + len(shares)),
        out_specs=[vmem] * z.regions,
        scratch_shapes=[
            pltpu.VMEM(((QUAD + CAP) * (z.makers - 1), LINES, LANES), jnp.float32),
            pltpu.VMEM((FIELDS + 1, 2, SLOTS, PAIRS, LANES), jnp.float32),
            pltpu.VMEM((FIELDS, TILES, LANES, LANES), jnp.float32),
            pltpu.VMEM((FIELDS, COLS + 8, LANES), jnp.float32),
            pltpu.VMEM((z.regions, 8, LANES), jnp.float32),
        ],
        compiler_params=pltpu.CompilerParams(vmem_limit_bytes=VMEM),
        cost_estimate=pl.CostEstimate(flops=5_000_000, bytes_accessed=8_000_000, transcendentals=0),
        name="join",
    )(place, *lists, *received, *shares)


SORT_STEPS = (
    ((0, 1), (2, 3), (4, 5), (6, 7)),
    ((0, 2), (1, 3), (4, 6), (5, 7)),
    ((1, 2), (5, 6)),
    ((0, 4), (1, 5), (2, 6), (3, 7)),
    ((2, 4), (3, 5)),
    ((1, 2), (3, 4), (5, 6)),
)
STEP_FIELDS = 2


def differences(field, low, count, tiles):
    lane = lax.broadcasted_iota(jnp.int32, (count, LANES), 1)
    pieces = [field[t, 8 + low : 8 + low + count, :] for t in range(tiles)]
    later = [pltpu.roll(piece, 1, 1) for piece in pieces]
    sooner = [pltpu.roll(piece, LANES - 1, 1) for piece in pieces]
    results = []
    for t, here in enumerate(pieces):
        above = jnp.where(lane == 0, later[t - 1] if t else here, later[t])
        below = jnp.where(lane == LANES - 1, sooner[t + 1] if t + 1 < tiles else here, sooner[t])
        sides = field[t, 7 + low : 7 + low + count, :] + field[t, 9 + low : 9 + low + count, :]
        results.append((here, above + below + sides - 4.0 * here))
    return results


def early_kernel(z, samples, place, *refs):
    offsets = [sample * z.makers + part for sample in samples for part in range(z.makers)]
    blocks = dict(zip(offsets, refs))
    results, edges, padded = refs[-3:]
    me = place[0]
    tiles = z.rows // LANES
    for offset in offsets:
        index = samples.index(offset // z.makers)
        for quad in range(z.quads):
            tile = lax.rem(me ^ offset, z.makers) * z.quads + quad
            values = blocks[offset][quad, 0 : z.main, :].astype(jnp.float32)
            tail = blocks[offset][quad, z.main : z.sent, :].astype(jnp.float32)
            for field in range(FIELDS):
                target = padded.at[index, field, tile]
                target[8 : 8 + z.span, :] = values[field * z.span : (field + 1) * z.span]
            edges[index, tile] = tail[0:8]

    def one_field(field, carry):
        for index in range(len(samples)):
            for t in range(tiles):
                padded[index, field, t, 7:8, :] = edges[index, t, pl.ds(2 * field, 1), :]
                padded[index, field, t, 8 + z.width : 9 + z.width, :] = edges[index, t, pl.ds(2 * field + 1, 1), :]
            for low in range(0, z.width, 8):
                count = min(8, z.width - low)
                found = differences(padded.at[index, field], low, count, tiles)
                for t, pair in enumerate(found):
                    for kind, rows in enumerate(pair):
                        results[kind, index, field, t, low : low + count, :] = rows
        return carry

    lax.fori_loop(0, FIELDS, one_field, 0)


def early_differences(z, samples, place, blocks, last=()):
    tiles = z.rows // LANES
    vmem, anywhere = pl.BlockSpec(memory_space=pltpu.VMEM), pl.BlockSpec(memory_space=pl.ANY)
    shape = (2, len(samples), FIELDS, tiles, z.span, LANES)
    return pl.pallas_call(
        functools.partial(early_kernel, z, samples),
        out_shape=[jax.ShapeDtypeStruct(item.shape, item.dtype) for item in last]
        + [jax.ShapeDtypeStruct(shape, jnp.float32)],
        in_specs=[pl.BlockSpec(memory_space=pltpu.SMEM)] + [vmem] * len(blocks) + [anywhere] * len(last),
        out_specs=[anywhere] * len(last) + [vmem],
        scratch_shapes=[
            pltpu.VMEM((len(samples), tiles, 8, LANES), jnp.float32),
            pltpu.VMEM((len(samples), FIELDS, tiles, z.span + 16, LANES), jnp.float32),
        ],
        input_output_aliases={1 + len(blocks) + i: i for i in range(len(last))},
        compiler_params=pltpu.CompilerParams(vmem_limit_bytes=VMEM),
        cost_estimate=pl.CostEstimate(flops=5_000_000, bytes_accessed=4_000_000, transcendentals=0),
        name="early_differences",
    )(place, *blocks, *last)


def score_kernel(z, place, *refs):
    blocks = dict(zip(z.offsets, refs))
    early, later, analysis, crps, spread, strength, edges, padded = refs[z.regions :]
    me = place[0]
    step = pl.program_id(0)
    rows = z.rows

    def tile_of(offset, quad):
        return lax.rem(me ^ offset, z.makers) * z.quads + quad

    @pl.when(step == 0)
    def _():
        slot = lax.broadcasted_iota(jnp.int32, (8, LANES), 1) // ROWS
        for low in range(0, z.regions, QUAD):
            offsets = range(low, low + QUAD)
            slots = [lax.rem(me ^ offset, QUAD) for offset in offsets]
            at = lax.div(me ^ low, QUAD)
            for quad in range(z.quads):
                tails = [blocks[offset][quad, z.main : z.sent, :].astype(jnp.float32) for offset in offsets]
                for offset, tail in zip(offsets, tails):
                    edges[offset // z.makers, tile_of(offset, quad)] = tail[0:8]
                for g in range(quad * QUAD, min((quad + 1) * QUAD, z.span // 8)):
                    joined = jnp.zeros((8, LANES), jnp.float32)
                    for i, tail in zip(slots, tails):
                        near = pltpu.roll(tail[8:16], lax.rem(i + QUAD - g % QUAD, QUAD) * ROWS, 1)
                        joined = jnp.where(slot == i, near, joined)
                    strength[at, 8 * g : 8 * (g + 1), :] = joined + MID

    top = pl.multiple_of(step * STEP_FIELDS * z.span, 16)
    for offset in range(z.regions):
        if offset // z.makers in z.early + z.later:
            continue
        for quad in range(z.quads):
            values = blocks[offset][quad, pl.ds(top, STEP_FIELDS * z.span), :].astype(jnp.float32)
            for f in range(STEP_FIELDS):
                padded[offset // z.makers, f, tile_of(offset, quad), 8 : 8 + z.span, :] = values[
                    f * z.span : (f + 1) * z.span
                ]
    tiles = rows // LANES
    for sample in range(SAMPLES):
        if sample in z.early + z.later:
            continue
        for f in range(STEP_FIELDS):
            low = 2 * (step * STEP_FIELDS + f)
            for t in range(tiles):
                padded[sample, f, t, 7:8, :] = edges[sample, t, pl.ds(low, 1), :]
                padded[sample, f, t, 8 + z.width : 9 + z.width, :] = edges[sample, t, pl.ds(low + 1, 1), :]
    for f, low in ((f, low) for f in range(STEP_FIELDS) for low in range(0, z.width, 16)):
        high = min(low + 16, z.width)
        smoothed = [[] for _ in range(tiles)]
        for sample in range(SAMPLES):
            if sample in z.early + z.later:
                samples, ready = (z.early, early) if sample in z.early else (z.later, later)
                own = (samples.index(sample), step * STEP_FIELDS + f)
                found = [[ready[kind, *own, t, low:high, :] for kind in range(2)] for t in range(tiles)]
            else:
                found = differences(padded.at[sample, f], low, high - low, tiles)
            for t, (here, difference) in enumerate(found):
                smooth = here + strength[t, low:high, :] * difference
                smoothed[t].append(smooth.astype(jnp.bfloat16))
        for t, members in enumerate(smoothed):
            lanes = slice(LANES * t, LANES * (t + 1))
            values = [member.astype(jnp.float32) for member in members]
            target = analysis[f, low:high, lanes].astype(jnp.float32)
            error = sum(jnp.abs(value - target) for value in values) * (1.0 / SAMPLES)
            average = sum(values) * (1.0 / SAMPLES)
            variance = sum((value - average) ** 2 for value in values) * (1.0 / (SAMPLES - 1.0))
            ranked = list(members)
            for pairs in SORT_STEPS:
                for a, b in pairs:
                    ranked[a], ranked[b] = jnp.minimum(ranked[a], ranked[b]), jnp.maximum(ranked[a], ranked[b])
            ranked = [member.astype(jnp.float32) for member in ranked]
            pairs = sum(
                (2 * k - SAMPLES + 1.0) * (ranked[k] - ranked[SAMPLES - 1 - k])
                for k in range(SAMPLES // 2, SAMPLES)
            )
            crps[f, low:high, lanes] = (error - pairs * (1.0 / (SAMPLES * SAMPLES))).astype(jnp.bfloat16)
            spread[0, f, low:high, lanes] = variance.astype(jnp.bfloat16)
            spread[1, f, low:high, lanes] = ((average - target) ** 2).astype(jnp.bfloat16)


def score(z, place, blocks, early, later, analysis):
    width, rows = z.width, z.rows
    return pl.pallas_call(
        functools.partial(score_kernel, z),
        out_shape=[
            jax.ShapeDtypeStruct((FIELDS, width, rows), jnp.bfloat16),
            jax.ShapeDtypeStruct((2, FIELDS, width, rows), jnp.bfloat16),
        ],
        grid=(FIELDS // STEP_FIELDS,),
        in_specs=[pl.BlockSpec(memory_space=pltpu.SMEM)]
        + [pl.BlockSpec(memory_space=pltpu.VMEM)] * (z.regions + 2)
        + [pl.BlockSpec((STEP_FIELDS, width, rows), lambda i: (i, 0, 0))],
        out_specs=[
            pl.BlockSpec((STEP_FIELDS, width, rows), lambda i: (i, 0, 0)),
            pl.BlockSpec((2, STEP_FIELDS, width, rows), lambda i: (0, i, 0, 0)),
        ],
        scratch_shapes=[
            pltpu.VMEM((rows // LANES, z.span, LANES), jnp.float32),
            pltpu.VMEM((SAMPLES, rows // LANES, 8, LANES), jnp.float32),
            pltpu.VMEM((SAMPLES, STEP_FIELDS, rows // LANES, z.span + 16, LANES), jnp.float32),
        ],
        compiler_params=pltpu.CompilerParams(vmem_limit_bytes=VMEM),
        name="score",
    )(place, *blocks, early, later, analysis)


def shards(patch_tiles, slot_lists, blend_table, smoothing, analysis):
    z = Sizes(lax.axis_size("region"))
    place = lax.axis_index("region").reshape(1)
    turns = [
        [(i, i - i % z.makers + (i + k) % z.makers) for i in range(z.regions)] for k in range(1, z.makers)
    ]
    tiles = patch_tiles.reshape(z.regions, CAP, FIELDS, PAIRS * TILES, LANES)
    tiles = jnp.swapaxes(tiles, 2, 3).reshape(z.regions, CAP, LINES, LANES)
    lists = jnp.transpose(slot_lists, (2, 1, 0))
    received = [lax.ppermute(item, "region", turn) for item, turn in zip(pack(z, place, tiles), turns)]
    lists = [lists] + [lax.ppermute(lists, "region", turn) for turn in turns]
    shares = own_share(z, place, lists[0], tiles, blend_table)
    shares = [*shares, strength_blocks(z, smoothing, shares[-1])]
    blocks = join(z, place, lists, received, shares)
    def swapped(block, offset):
        return lax.ppermute(block, "region", [(i, i ^ offset) for i in range(z.regions)])

    moved = [blocks[0]] + [swapped(block, offset) for block, offset in zip(blocks[1:-1], z.offsets[1:-1])]
    def blocks_of(samples):
        return [moved[z.offsets.index(sample * z.makers + part)] for sample in samples for part in range(z.makers)]

    last, early = early_differences(z, z.early, place, blocks_of(z.early), [blocks[-1]])
    (later,) = early_differences(z, z.later, place, blocks_of(z.later))
    moved.append(swapped(last, z.offsets[-1]))
    outs = score(z, place, moved, early, later, jnp.swapaxes(analysis, 1, 2))
    return tuple(jnp.swapaxes(item, -1, -2) for item in outs)


def solution(mesh):
    return jax.shard_map(
        shards,
        mesh=mesh,
        in_specs=(
            P(("groups", "region"), None, None, None),
            P(("groups", "region"), None, None),
            P(),
            P("region", None),
            P(None, "groups", "region"),
        ),
        out_specs=(P(None, "groups", "region"), P(None, None, "groups", "region")),
        check_vma=False,
    )
```

```python
import functools

import jax
import jax.numpy as jnp
from jax import lax
from jax.experimental import pallas as pl
from jax.experimental.pallas import tpu as pltpu
from jax.sharding import PartitionSpec as P

SAMPLES = 8
FIELDS = 4
PATCH = 448
CAP = 2
ROWS = 32
COLS = 896
PAIRS = ROWS // 2
PITCH = PAIRS + 1
LINES = FIELDS * ROWS * PATCH // 128
LANES = 128
TILES = COLS // LANES
QUAD = LANES // ROWS
MID = 0.11
VMEM = 40 * 1024 * 1024
PACK_VMEM = 52 * 1024 * 1024
MOST_VMEM = 47 * 1024 * 1024


def round_up(value, step):
    return -(-value // step) * step


def swap_order(regions):
    half, quarter = regions // 2, regions // 4
    far = [offset for i in range(quarter) for offset in (half + quarter + i, half + i)]
    near = list(range(quarter, half)) + list(range(1, quarter))
    return [0] + [item for pair in zip(far, near + [None]) for item in pair if item is not None]


class Sizes:
    def __init__(self, regions):
        self.regions = regions
        self.makers = regions // SAMPLES
        self.block = regions // self.makers
        self.quads = self.block // QUAD
        self.width = COLS // regions
        self.span = round_up(self.width, 8)
        self.rows = regions * ROWS
        self.main = round_up(FIELDS * self.span, 16)
        self.offsets = swap_order(regions)
        arrived = self.offsets[: regions - 5]
        groups = [range(sample * self.makers, (sample + 1) * self.makers) for sample in range(SAMPLES)]
        self.early = [sample for sample, group in enumerate(groups) if all(k in arrived for k in group)]
        self.later = [
            sample
            for sample, group in enumerate(groups)
            if sample not in self.early and self.offsets[-1] not in group
        ]
        self.sent = self.main + 16


def stage(staged, tile):
    staged[...] = tile.astype(jnp.float32)


def staged_tile(staged, field, t):
    return staged[pl.ds(FIELDS * t + field, PAIRS, stride=FIELDS * TILES), :]


def weight_tile(weights, kind, t):
    return weights[t, pl.ds(kind * PITCH, PAIRS), :]


SLOTS = TILES + 2


def place_side(tile, column):
    pairs = jnp.concatenate([tile(t) for t in range(TILES)], 1)
    turned = pltpu.roll(pairs, PATCH, 1)
    lane = lax.broadcasted_iota(jnp.int32, pairs.shape, 1)
    left = (lane < PATCH) & (column == 0)
    right = (lane >= PATCH) & (column != 0)
    even = jnp.where(left, pairs, jnp.where(right, turned, 0.0))
    odd = jnp.where(left, turned, jnp.where(right, pairs, 0.0))
    return [[rows[:, LANES * t : LANES * (t + 1)] for t in range(TILES)] for rows in (even, odd)]


def add_any(sums, tile, column):
    lane = lax.broadcasted_iota(jnp.int32, (PAIRS, LANES), 1)
    middle = PATCH // LANES
    split = PATCH % LANES
    for parity in range(2):
        first = middle * parity
        start = column if parity == 0 else column + COLS - PATCH
        shift = lax.rem(start, LANES)
        at = lax.div(start, LANES) + first + 1 - (TILES if parity else 0)
        turned = []
        for t in range(first, first + middle + 1):
            piece = tile(t)
            if t == middle:
                piece = jnp.where((lane >= split) if parity else (lane < split), piece, 0.0)
            turned.append(pltpu.roll(piece, shift, 1))
        none = jnp.zeros((PAIRS, LANES), jnp.float32)
        for v in range(middle + 2):
            low = turned[v - 1] if v else none
            high = turned[v] if v <= middle else none
            sums[parity, at + v] = sums[parity, at + v] + jnp.where(lane < shift, low, high)


def place_all(side, sums, items):
    if side:
        placed = [place_side(*item) for item in items]
        return [[sum(item[parity][t] for item in placed) for t in range(TILES)] for parity in range(2)]
    for parity in range(2):
        for t in range(SLOTS):
            sums[parity, t] = jnp.zeros((PAIRS, LANES), jnp.float32)
    for item in items:
        add_any(sums, *item)
    return [[sums[parity, t + 1] for t in range(TILES)] for parity in range(2)]


def each_region(z, heavy, body):
    for i in range(QUAD):
        if z.makers == 2:
            body(i, True, range(1))
        else:
            pl.when(jnp.logical_not(heavy(i)))(functools.partial(body, i, False, range(1)))

    def again(i, carry):
        pl.when(heavy(i))(functools.partial(body, i, False, range(CAP)))
        return carry

    lax.fori_loop(0, QUAD, again, 0)


def staged_index(i, side, maker, slot, others):
    return i * others + maker if side else QUAD * others + maker * CAP + slot


def pack_kernel(z, place, tiles, *refs):
    packed, sems = refs[:-1], refs[-1]
    part = lax.rem(place[0], z.makers)
    copies = []
    for k, target in enumerate(packed):
        first = lax.rem(part + k + 1, z.makers) * z.block
        for j in range(z.block):
            copies.append(pltpu.make_async_copy(tiles.at[first + j], target.at[j], sems.at[k, j]))
    for copy in copies:
        copy.start()
    for copy in copies:
        copy.wait()


def pack(z, place, tiles):
    shape = jax.ShapeDtypeStruct((z.block, *tiles.shape[1:]), tiles.dtype)
    return pl.pallas_call(
        functools.partial(pack_kernel, z),
        out_shape=[shape] * (z.makers - 1),
        in_specs=[pl.BlockSpec(memory_space=pltpu.SMEM), pl.BlockSpec(memory_space=pltpu.HBM)],
        out_specs=[pl.BlockSpec(memory_space=pltpu.VMEM)] * (z.makers - 1),
        scratch_shapes=[pltpu.SemaphoreType.DMA((z.makers - 1, z.block))],
        compiler_params=pltpu.CompilerParams(vmem_limit_bytes=PACK_VMEM),
        name="pack",
    )(place, tiles)


def own_kernel(z, place, lists, tiles, table_hbm, *refs):
    half, (total, weights, landed, staged, sums, table, sems) = refs[:FIELDS], refs[FIELDS:]
    first = lax.rem(place[0], z.makers) * z.block

    def fetch(j):
        return pltpu.make_async_copy(tiles.at[first + j], landed.at[j], sems.at[j])

    fetch_table = pltpu.make_async_copy(table_hbm, table, sems.at[z.block])
    fetch_table.start()
    for j in range(z.block):
        fetch(j).start()
    fetch_table.wait()
    kinds = table.shape[0]
    for k in range(PAIRS):
        for t in range(TILES):
            at = COLS * k + LANES * t
            for low in range(0, kinds, 8):
                count = min(8, kinds - low)
                weights[t, pl.ds(PITCH * low + k, count, stride=PITCH), :] = table[
                    low : low + count, at : at + LANES
                ]

    def group(quad, carry):
        for i in range(QUAD):
            fetch(quad * QUAD + i).wait()

        def body(i, side, slots):
            j = quad * QUAD + i

            def weight_item(slot):
                column, kind = (lists[entry, slot, first + j] for entry in (1, 2))
                return functools.partial(weight_tile, weights, kind), column

            def field_item(field, slot):
                weight, column = weight_item(slot)
                own = staged.at[staged_index(i, side, 0, slot, 1)]
                return lambda t: staged_tile(own, field, t) * weight(t), column

            for slot in slots:
                stage(staged.at[staged_index(i, side, 0, slot, 1)], landed[j, slot])
            for index in range(FIELDS + 1):
                items = [field_item(index, slot) if index < FIELDS else weight_item(slot) for slot in slots]
                pieces = place_all(side, sums.at[index], items)
                target = half[index] if index < FIELDS else total
                for parity in range(2):
                    for t in range(TILES):
                        target[j, parity, t] = pieces[parity][t]

        each_region(z, lambda i: lists[0, 1, first + quad * QUAD + i] >= 0, body)
        return carry

    lax.fori_loop(0, z.quads, group, 0)


def own_share(z, place, lists, tiles, table):
    smem = pl.BlockSpec(memory_space=pltpu.SMEM)
    vmem = pl.BlockSpec(memory_space=pltpu.VMEM)
    hbm = pl.BlockSpec(memory_space=pltpu.HBM)
    kinds = round_up(table.shape[0], 8)
    return pl.pallas_call(
        functools.partial(own_kernel, z),
        out_shape=[
            *[jax.ShapeDtypeStruct((z.block, 2, TILES, PAIRS, LANES), jnp.float32)] * (FIELDS + 1),
            jax.ShapeDtypeStruct((TILES, kinds * PITCH, LANES), jnp.float32),
        ],
        in_specs=[smem, smem, hbm, hbm],
        out_specs=[vmem] * (FIELDS + 2),
        scratch_shapes=[
            pltpu.VMEM((z.block, CAP, LINES, LANES), jnp.bfloat16),
            pltpu.VMEM((QUAD + CAP, LINES, LANES), jnp.float32),
            pltpu.VMEM((FIELDS + 1, 2, SLOTS, PAIRS, LANES), jnp.float32),
            pltpu.VMEM(table.shape, jnp.float32),
            pltpu.SemaphoreType.DMA((z.block + 1,)),
        ],
        compiler_params=pltpu.CompilerParams(vmem_limit_bytes=MOST_VMEM),
        cost_estimate=pl.CostEstimate(flops=5_000_000, bytes_accessed=8_000_000, transcendentals=0),
        name="own_share",
    )(place, lists, tiles, table)


def strength_kernel(z, smoothing, _, strength):
    turned_strength = jnp.transpose(smoothing[...] - MID)
    for dest in range(z.regions):
        for g in range(z.span // 8):
            top = z.width * dest + 8 * g
            count, at = min(8, COLS - top), ROWS * (g % QUAD)
            strength[dest, g // QUAD, 0:count, at : at + ROWS] = turned_strength[top : top + count]


def strength_blocks(z, smoothing, before):
    return pl.pallas_call(
        functools.partial(strength_kernel, z),
        out_shape=jax.ShapeDtypeStruct((z.regions, z.quads, 8, LANES), jnp.float32),
        in_specs=[pl.BlockSpec(memory_space=pltpu.VMEM), pl.BlockSpec(memory_space=pl.ANY)],
        out_specs=pl.BlockSpec(memory_space=pltpu.VMEM),
        compiler_params=pltpu.CompilerParams(vmem_limit_bytes=VMEM),
        name="strength_blocks",
    )(smoothing, before)


def join_kernel(z, *refs):
    place, lists, refs = refs[0], refs[1 : 1 + z.makers], refs[1 + z.makers :]
    received, refs = refs[: z.makers - 1], refs[z.makers - 1 :]
    half, (total, weights, strength), outs = refs[:FIELDS], refs[FIELDS : FIELDS + 3], refs[FIELDS + 3 : -5]
    staged, sums, lines, turned, edges = refs[-5:]
    me = place[0]
    first = lax.rem(me, z.makers) * z.block
    row, column = (lax.broadcasted_iota(jnp.int32, (LANES, LANES), axis) for axis in (0, 1))
    identity = (row == column).astype(jnp.bfloat16)

    for quad in range(z.quads):

        def body(i, side, slots):
            j = quad * QUAD + i
            sources = [(maker, slot) for maker in range(1, z.makers) for slot in slots]

            def staged_of(maker, slot):
                return staged.at[staged_index(i, side, maker - 1, slot, z.makers - 1)]

            def weight_item(maker, slot):
                column, kind = (lists[maker][entry, slot, first + j] for entry in (1, 2))
                return functools.partial(weight_tile, weights, kind), column

            def field_item(field, maker, slot):
                weight, column = weight_item(maker, slot)
                return lambda t: staged_tile(staged_of(maker, slot), field, t) * weight(t), column

            for maker, slot in sources:
                stage(staged_of(maker, slot), received[maker - 1][j, slot])
            others = place_all(side, sums.at[FIELDS], [weight_item(*source) for source in sources])
            inverse = [[1.0 / (total[j, parity, t] + others[parity][t]) for t in range(TILES)] for parity in range(2)]
            for field in range(FIELDS):
                pieces = place_all(side, sums.at[field], [field_item(field, *source) for source in sources])
                for parity in range(2):
                    for t in range(TILES):
                        lines[field, t, pl.ds(ROWS * i + parity, PAIRS, stride=2), :] = (
                            half[field][j, parity, t] + pieces[parity][t]
                        ) * inverse[parity][t]

        each_region(z, lambda i: lists[0][0, 1, first + quad * QUAD + i] >= 0, body)
        for t in range(TILES):
            for field in range(FIELDS):
                here = slice(LANES * t, LANES * (t + 1))
                if field % 2:
                    turned[field, here, :] = jnp.transpose(lines[field, t])
                else:
                    turned[field, here, :] = lax.dot_general(
                        identity,
                        lines[field, t].astype(jnp.bfloat16),
                        (((1,), (1,)), ((), ())),
                        preferred_element_type=jnp.float32,
                    )
        for i, (out, offset) in enumerate(zip(outs, z.offsets)):
            dest = me ^ offset
            top = dest * z.width
            if z.width % 8 == 0:
                top = pl.multiple_of(top, 8)
            ends = (jnp.maximum(top - 1, 0), jnp.minimum(top + z.width, COLS - 1))
            for field in range(FIELDS):
                for side, end in enumerate(ends):
                    edges[i, 2 * field + side : 2 * field + side + 1, :] = turned[field, pl.ds(end, 1), :]
            for low in range(0, FIELDS, 2):
                block = [turned[field, pl.ds(top, z.span), :] for field in (low, low + 1)]
                out[quad, low * z.span : (low + 2) * z.span, :] = jnp.concatenate(block, 0).astype(jnp.bfloat16)
            tail = jnp.concatenate([edges[i], strength[dest, quad]], 0)
            out[quad, z.main : z.sent, :] = tail.astype(jnp.bfloat16)


def join(z, place, lists, received, shares):
    smem = pl.BlockSpec(memory_space=pltpu.SMEM)
    vmem = pl.BlockSpec(memory_space=pltpu.VMEM)
    shape = (z.quads, z.sent, LANES)
    return pl.pallas_call(
        functools.partial(join_kernel, z),
        out_shape=[jax.ShapeDtypeStruct(shape, jnp.bfloat16)] * z.regions,
        in_specs=[smem] * (1 + z.makers) + [vmem] * (z.makers - 1 + len(shares)),
        out_specs=[vmem] * z.regions,
        scratch_shapes=[
            pltpu.VMEM(((QUAD + CAP) * (z.makers - 1), LINES, LANES), jnp.float32),
            pltpu.VMEM((FIELDS + 1, 2, SLOTS, PAIRS, LANES), jnp.float32),
            pltpu.VMEM((FIELDS, TILES, LANES, LANES), jnp.float32),
            pltpu.VMEM((FIELDS, COLS + 8, LANES), jnp.float32),
            pltpu.VMEM((z.regions, 8, LANES), jnp.float32),
        ],
        compiler_params=pltpu.CompilerParams(vmem_limit_bytes=VMEM),
        cost_estimate=pl.CostEstimate(flops=5_000_000, bytes_accessed=8_000_000, transcendentals=0),
        name="join",
    )(place, *lists, *received, *shares)


SORT_STEPS = (
    ((0, 1), (2, 3), (4, 5), (6, 7)),
    ((0, 2), (1, 3), (4, 6), (5, 7)),
    ((1, 2), (5, 6)),
    ((0, 4), (1, 5), (2, 6), (3, 7)),
    ((2, 4), (3, 5)),
    ((1, 2), (3, 4), (5, 6)),
)
STEP_FIELDS = 2


def differences(field, low, count, tiles):
    lane = lax.broadcasted_iota(jnp.int32, (count, LANES), 1)
    pieces = [field[t, 8 + low : 8 + low + count, :] for t in range(tiles)]
    later = [pltpu.roll(piece, 1, 1) for piece in pieces]
    sooner = [pltpu.roll(piece, LANES - 1, 1) for piece in pieces]
    results = []
    for t, here in enumerate(pieces):
        above = jnp.where(lane == 0, later[t - 1] if t else here, later[t])
        below = jnp.where(lane == LANES - 1, sooner[t + 1] if t + 1 < tiles else here, sooner[t])
        sides = field[t, 7 + low : 7 + low + count, :] + field[t, 9 + low : 9 + low + count, :]
        results.append((here, above + below + sides - 4.0 * here))
    return results


def early_kernel(z, samples, place, *refs):
    offsets = [sample * z.makers + part for sample in samples for part in range(z.makers)]
    blocks = dict(zip(offsets, refs))
    results, edges, padded = refs[-3:]
    me = place[0]
    tiles = z.rows // LANES
    for offset in offsets:
        index = samples.index(offset // z.makers)
        for quad in range(z.quads):
            tile = lax.rem(me ^ offset, z.makers) * z.quads + quad
            values = blocks[offset][quad, 0 : z.main, :].astype(jnp.float32)
            tail = blocks[offset][quad, z.main : z.sent, :].astype(jnp.float32)
            for field in range(FIELDS):
                target = padded.at[index, field, tile]
                target[8 : 8 + z.span, :] = values[field * z.span : (field + 1) * z.span]
            edges[index, tile] = tail[0:8]

    def one_field(field, carry):
        for index in range(len(samples)):
            for t in range(tiles):
                padded[index, field, t, 7:8, :] = edges[index, t, pl.ds(2 * field, 1), :]
                padded[index, field, t, 8 + z.width : 9 + z.width, :] = edges[index, t, pl.ds(2 * field + 1, 1), :]
            for low in range(0, z.width, 8):
                count = min(8, z.width - low)
                found = differences(padded.at[index, field], low, count, tiles)
                for t, pair in enumerate(found):
                    for kind, rows in enumerate(pair):
                        results[kind, index, field, t, low : low + count, :] = rows
        return carry

    lax.fori_loop(0, FIELDS, one_field, 0)


def early_differences(z, samples, place, blocks, last=()):
    tiles = z.rows // LANES
    vmem, anywhere = pl.BlockSpec(memory_space=pltpu.VMEM), pl.BlockSpec(memory_space=pl.ANY)
    shape = (2, len(samples), FIELDS, tiles, z.span, LANES)
    return pl.pallas_call(
        functools.partial(early_kernel, z, samples),
        out_shape=[jax.ShapeDtypeStruct(item.shape, item.dtype) for item in last]
        + [jax.ShapeDtypeStruct(shape, jnp.float32)],
        in_specs=[pl.BlockSpec(memory_space=pltpu.SMEM)] + [vmem] * len(blocks) + [anywhere] * len(last),
        out_specs=[anywhere] * len(last) + [vmem],
        scratch_shapes=[
            pltpu.VMEM((len(samples), tiles, 8, LANES), jnp.float32),
            pltpu.VMEM((len(samples), FIELDS, tiles, z.span + 16, LANES), jnp.float32),
        ],
        input_output_aliases={1 + len(blocks) + i: i for i in range(len(last))},
        compiler_params=pltpu.CompilerParams(vmem_limit_bytes=VMEM),
        cost_estimate=pl.CostEstimate(flops=5_000_000, bytes_accessed=4_000_000, transcendentals=0),
        name="early_differences",
    )(place, *blocks, *last)


def score_kernel(z, place, *refs):
    blocks = dict(zip(z.offsets, refs))
    early, later, analysis, crps, spread, strength, edges, padded = refs[z.regions :]
    me = place[0]
    step = pl.program_id(0)
    rows = z.rows

    def tile_of(offset, quad):
        return lax.rem(me ^ offset, z.makers) * z.quads + quad

    @pl.when(step == 0)
    def _():
        slot = lax.broadcasted_iota(jnp.int32, (8, LANES), 1) // ROWS
        for low in range(0, z.regions, QUAD):
            offsets = range(low, low + QUAD)
            slots = [lax.rem(me ^ offset, QUAD) for offset in offsets]
            at = lax.div(me ^ low, QUAD)
            for quad in range(z.quads):
                tails = [blocks[offset][quad, z.main : z.sent, :].astype(jnp.float32) for offset in offsets]
                for offset, tail in zip(offsets, tails):
                    edges[offset // z.makers, tile_of(offset, quad)] = tail[0:8]
                for g in range(quad * QUAD, min((quad + 1) * QUAD, z.span // 8)):
                    joined = jnp.zeros((8, LANES), jnp.float32)
                    for i, tail in zip(slots, tails):
                        near = pltpu.roll(tail[8:16], lax.rem(i + QUAD - g % QUAD, QUAD) * ROWS, 1)
                        joined = jnp.where(slot == i, near, joined)
                    strength[at, 8 * g : 8 * (g + 1), :] = joined + MID

    top = pl.multiple_of(step * STEP_FIELDS * z.span, 16)
    for offset in range(z.regions):
        if offset // z.makers in z.early + z.later:
            continue
        for quad in range(z.quads):
            values = blocks[offset][quad, pl.ds(top, STEP_FIELDS * z.span), :].astype(jnp.float32)
            for f in range(STEP_FIELDS):
                padded[offset // z.makers, f, tile_of(offset, quad), 8 : 8 + z.span, :] = values[
                    f * z.span : (f + 1) * z.span
                ]
    tiles = rows // LANES
    for sample in range(SAMPLES):
        if sample in z.early + z.later:
            continue
        for f in range(STEP_FIELDS):
            low = 2 * (step * STEP_FIELDS + f)
            for t in range(tiles):
                padded[sample, f, t, 7:8, :] = edges[sample, t, pl.ds(low, 1), :]
                padded[sample, f, t, 8 + z.width : 9 + z.width, :] = edges[sample, t, pl.ds(low + 1, 1), :]
    for f, low in ((f, low) for f in range(STEP_FIELDS) for low in range(0, z.width, 16)):
        high = min(low + 16, z.width)
        smoothed = [[] for _ in range(tiles)]
        for sample in range(SAMPLES):
            if sample in z.early + z.later:
                samples, ready = (z.early, early) if sample in z.early else (z.later, later)
                own = (samples.index(sample), step * STEP_FIELDS + f)
                found = [[ready[kind, *own, t, low:high, :] for kind in range(2)] for t in range(tiles)]
            else:
                found = differences(padded.at[sample, f], low, high - low, tiles)
            for t, (here, difference) in enumerate(found):
                smooth = here + strength[t, low:high, :] * difference
                smoothed[t].append(smooth.astype(jnp.bfloat16))
        for t, members in enumerate(smoothed):
            lanes = slice(LANES * t, LANES * (t + 1))
            values = [member.astype(jnp.float32) for member in members]
            target = analysis[f, low:high, lanes].astype(jnp.float32)
            error = sum(jnp.abs(value - target) for value in values) * (1.0 / SAMPLES)
            average = sum(values) * (1.0 / SAMPLES)
            variance = sum((value - average) ** 2 for value in values) * (1.0 / (SAMPLES - 1.0))
            ranked = list(members)
            for pairs in SORT_STEPS:
                for a, b in pairs:
                    ranked[a], ranked[b] = jnp.minimum(ranked[a], ranked[b]), jnp.maximum(ranked[a], ranked[b])
            ranked = [member.astype(jnp.float32) for member in ranked]
            pairs = sum(
                (2 * k - SAMPLES + 1.0) * (ranked[k] - ranked[SAMPLES - 1 - k])
                for k in range(SAMPLES // 2, SAMPLES)
            )
            crps[f, low:high, lanes] = (error - pairs * (1.0 / (SAMPLES * SAMPLES))).astype(jnp.bfloat16)
            spread[0, f, low:high, lanes] = variance.astype(jnp.bfloat16)
            spread[1, f, low:high, lanes] = ((average - target) ** 2).astype(jnp.bfloat16)


def score(z, place, blocks, early, later, analysis):
    width, rows = z.width, z.rows
    return pl.pallas_call(
        functools.partial(score_kernel, z),
        out_shape=[
            jax.ShapeDtypeStruct((FIELDS, width, rows), jnp.bfloat16),
            jax.ShapeDtypeStruct((2, FIELDS, width, rows), jnp.bfloat16),
        ],
        grid=(FIELDS // STEP_FIELDS,),
        in_specs=[pl.BlockSpec(memory_space=pltpu.SMEM)]
        + [pl.BlockSpec(memory_space=pltpu.VMEM)] * (z.regions + 2)
        + [pl.BlockSpec((STEP_FIELDS, width, rows), lambda i: (i, 0, 0))],
        out_specs=[
            pl.BlockSpec((STEP_FIELDS, width, rows), lambda i: (i, 0, 0)),
            pl.BlockSpec((2, STEP_FIELDS, width, rows), lambda i: (0, i, 0, 0)),
        ],
        scratch_shapes=[
            pltpu.VMEM((rows // LANES, z.span, LANES), jnp.float32),
            pltpu.VMEM((SAMPLES, rows // LANES, 8, LANES), jnp.float32),
            pltpu.VMEM((SAMPLES, STEP_FIELDS, rows // LANES, z.span + 16, LANES), jnp.float32),
        ],
        compiler_params=pltpu.CompilerParams(vmem_limit_bytes=VMEM),
        name="score",
    )(place, *blocks, early, later, analysis)


def shards(patch_tiles, slot_lists, blend_table, smoothing, analysis):
    z = Sizes(lax.axis_size("region"))
    place = lax.axis_index("region").reshape(1)
    turns = [
        [(i, i - i % z.makers + (i + k) % z.makers) for i in range(z.regions)] for k in range(1, z.makers)
    ]
    tiles = patch_tiles.reshape(z.regions, CAP, FIELDS, PAIRS * TILES, LANES)
    tiles = jnp.swapaxes(tiles, 2, 3).reshape(z.regions, CAP, LINES, LANES)
    lists = jnp.transpose(slot_lists, (2, 1, 0))
    received = [lax.ppermute(item, "region", turn) for item, turn in zip(pack(z, place, tiles), turns)]
    lists = [lists] + [lax.ppermute(lists, "region", turn) for turn in turns]
    shares = own_share(z, place, lists[0], tiles, blend_table)
    shares = [*shares, strength_blocks(z, smoothing, shares[-1])]
    blocks = join(z, place, lists, received, shares)
    def swapped(block, offset):
        return lax.ppermute(block, "region", [(i, i ^ offset) for i in range(z.regions)])

    moved = [blocks[0]] + [swapped(block, offset) for block, offset in zip(blocks[1:-1], z.offsets[1:-1])]
    def blocks_of(samples):
        return [moved[z.offsets.index(sample * z.makers + part)] for sample in samples for part in range(z.makers)]

    last, early = early_differences(z, z.early, place, blocks_of(z.early), [blocks[-1]])
    (later,) = early_differences(z, z.later, place, blocks_of(z.later))
    moved.append(swapped(last, z.offsets[-1]))
    outs = score(z, place, moved, early, later, jnp.swapaxes(analysis, 1, 2))
    return tuple(jnp.swapaxes(item, -1, -2) for item in outs)


def solution(mesh):
    return jax.shard_map(
        shards,
        mesh=mesh,
        in_specs=(
            P(("groups", "region"), None, None, None),
            P(("groups", "region"), None, None),
            P(),
            P("region", None),
            P(None, "groups", "region"),
        ),
        out_specs=(P(None, "groups", "region"), P(None, None, "groups", "region")),
        check_vma=False,
    )
```

```python
import functools

import jax
import jax.numpy as jnp
from jax import lax
from jax.experimental import pallas as pl
from jax.experimental.pallas import tpu as pltpu
from jax.sharding import PartitionSpec as P

SAMPLES = 8
FIELDS = 4
PATCH = 448
CAP = 2
ROWS = 32
COLS = 896
PAIRS = ROWS // 2
LINES = FIELDS * ROWS * PATCH // 128
LANES = 128
TILES = COLS // LANES
QUAD = LANES // ROWS
MID = 0.11
VMEM = 40 * 1024 * 1024
PACK_VMEM = 52 * 1024 * 1024
MOST_VMEM = 48 * 1024 * 1024


def round_up(value, step):
    return -(-value // step) * step


def swap_order(regions):
    half, quarter = regions // 2, regions // 4
    far = [offset for i in range(quarter) for offset in (half + quarter + i, half + i)]
    near = list(range(1, half))
    return [0] + [item for pair in zip(near + [None], far) for item in pair if item is not None]


class Sizes:
    def __init__(self, regions):
        self.regions = regions
        self.makers = regions // SAMPLES
        self.block = regions // self.makers
        self.quads = self.block // QUAD
        self.width = COLS // regions
        self.span = round_up(self.width, 8)
        self.rows = regions * ROWS
        self.main = round_up(FIELDS * self.span, 16)
        self.offsets = swap_order(regions)
        arrived = self.offsets[: regions - 5]
        groups = [range(sample * self.makers, (sample + 1) * self.makers) for sample in range(SAMPLES)]
        self.early = [sample for sample, group in enumerate(groups) if all(k in arrived for k in group)]
        self.later = [
            sample
            for sample, group in enumerate(groups)
            if sample not in self.early and self.offsets[-1] not in group
        ]
        self.sent = self.main + 16


def stage(staged, tile):
    staged[...] = tile.astype(jnp.float32)


def staged_tile(staged, field, t):
    return staged[pl.ds(FIELDS * t + field, PAIRS, stride=FIELDS * TILES), :]


def weight_tile(weights, kind, t):
    return weights[t, pl.ds(pl.multiple_of(kind * PAIRS, PAIRS), PAIRS), :]


SLOTS = TILES + 2


def place_side(tile, column):
    pairs = jnp.concatenate([tile(t) for t in range(TILES)], 1)
    turned = pltpu.roll(pairs, PATCH, 1)
    lane = lax.broadcasted_iota(jnp.int32, pairs.shape, 1)
    left = (lane < PATCH) & (column == 0)
    right = (lane >= PATCH) & (column != 0)
    even = jnp.where(left, pairs, jnp.where(right, turned, 0.0))
    odd = jnp.where(left, turned, jnp.where(right, pairs, 0.0))
    return [[rows[:, LANES * t : LANES * (t + 1)] for t in range(TILES)] for rows in (even, odd)]


def add_any(sums, tile, column):
    lane = lax.broadcasted_iota(jnp.int32, (PAIRS, LANES), 1)
    middle = PATCH // LANES
    split = PATCH % LANES
    for parity in range(2):
        first = middle * parity
        start = column if parity == 0 else column + COLS - PATCH
        shift = lax.rem(start, LANES)
        at = lax.div(start, LANES) + first + 1 - (TILES if parity else 0)
        turned = []
        for t in range(first, first + middle + 1):
            piece = tile(t)
            if t == middle:
                piece = jnp.where((lane >= split) if parity else (lane < split), piece, 0.0)
            turned.append(pltpu.roll(piece, shift, 1))
        none = jnp.zeros((PAIRS, LANES), jnp.float32)
        for v in range(middle + 2):
            low = turned[v - 1] if v else none
            high = turned[v] if v <= middle else none
            sums[parity, at + v] = sums[parity, at + v] + jnp.where(lane < shift, low, high)


def place_all(side, sums, items):
    if side:
        placed = [place_side(*item) for item in items]
        return [[sum(item[parity][t] for item in placed) for t in range(TILES)] for parity in range(2)]
    for parity in range(2):
        for t in range(SLOTS):
            sums[parity, t] = jnp.zeros((PAIRS, LANES), jnp.float32)
    for item in items:
        add_any(sums, *item)
    return [[sums[parity, t + 1] for t in range(TILES)] for parity in range(2)]


def each_region(z, heavy, body):
    for i in range(QUAD):
        if z.makers == 2:
            body(i, True, range(1))
        else:
            pl.when(jnp.logical_not(heavy(i)))(functools.partial(body, i, False, range(1)))

    def again(i, carry):
        pl.when(heavy(i))(functools.partial(body, i, False, range(CAP)))
        return carry

    lax.fori_loop(0, QUAD, again, 0)


def staged_index(i, side, maker, slot, others):
    return i * others + maker if side else QUAD * others + maker * CAP + slot


def pack_kernel(z, place, tiles, *refs):
    packed, sems = refs[:-1], refs[-1]
    part = lax.rem(place[0], z.makers)
    copies = []
    for k, target in enumerate(packed):
        first = lax.rem(part + k + 1, z.makers) * z.block
        for j in range(z.block):
            copies.append(pltpu.make_async_copy(tiles.at[first + j], target.at[j], sems.at[k, j]))
    for copy in copies:
        copy.start()
    for copy in copies:
        copy.wait()


def pack(z, place, tiles):
    shape = jax.ShapeDtypeStruct((z.block, *tiles.shape[1:]), tiles.dtype)
    return pl.pallas_call(
        functools.partial(pack_kernel, z),
        out_shape=[shape] * (z.makers - 1),
        in_specs=[pl.BlockSpec(memory_space=pltpu.SMEM), pl.BlockSpec(memory_space=pltpu.HBM)],
        out_specs=[pl.BlockSpec(memory_space=pltpu.VMEM)] * (z.makers - 1),
        scratch_shapes=[pltpu.SemaphoreType.DMA((z.makers - 1, z.block))],
        compiler_params=pltpu.CompilerParams(vmem_limit_bytes=PACK_VMEM),
        name="pack",
    )(place, tiles)


def own_kernel(z, place, lists, tiles, table_hbm, *refs):
    half, (total, weights, landed, staged, sums, table, sems) = refs[:FIELDS], refs[FIELDS:]
    first = lax.rem(place[0], z.makers) * z.block

    def fetch(j):
        return pltpu.make_async_copy(tiles.at[first + j], landed.at[j], sems.at[j])

    fetch_table = pltpu.make_async_copy(table_hbm, table, sems.at[z.block])
    fetch_table.start()
    for j in range(z.block):
        fetch(j).start()
    fetch_table.wait()
    kinds = table.shape[0]
    for k in range(PAIRS):
        for t in range(TILES):
            at = COLS * k + LANES * t
            for low in range(0, kinds, 8):
                count = min(8, kinds - low)
                weights[t, pl.ds(PAIRS * low + k, count, stride=PAIRS), :] = table[
                    low : low + count, at : at + LANES
                ]

    def group(quad, carry):
        for i in range(QUAD):
            fetch(quad * QUAD + i).wait()

        def body(i, side, slots):
            j = quad * QUAD + i

            def weight_item(slot):
                column, kind = (lists[entry, slot, first + j] for entry in (1, 2))
                return functools.partial(weight_tile, weights, kind), column

            def field_item(field, slot):
                weight, column = weight_item(slot)
                own = staged.at[staged_index(i, side, 0, slot, 1)]
                return lambda t: staged_tile(own, field, t) * weight(t), column

            for slot in slots:
                stage(staged.at[staged_index(i, side, 0, slot, 1)], landed[j, slot])
            for index in range(FIELDS + 1):
                items = [field_item(index, slot) if index < FIELDS else weight_item(slot) for slot in slots]
                pieces = place_all(side, sums.at[index], items)
                target = half[index] if index < FIELDS else total
                for parity in range(2):
                    for t in range(TILES):
                        target[j, parity, t] = pieces[parity][t]

        each_region(z, lambda i: lists[0, 1, first + quad * QUAD + i] >= 0, body)
        return carry

    lax.fori_loop(0, z.quads, group, 0)


def own_share(z, place, lists, tiles, table):
    smem = pl.BlockSpec(memory_space=pltpu.SMEM)
    vmem = pl.BlockSpec(memory_space=pltpu.VMEM)
    hbm = pl.BlockSpec(memory_space=pltpu.HBM)
    kinds = round_up(table.shape[0], 8)
    return pl.pallas_call(
        functools.partial(own_kernel, z),
        out_shape=[
            *[jax.ShapeDtypeStruct((z.block, 2, TILES, PAIRS, LANES), jnp.float32)] * (FIELDS + 1),
            jax.ShapeDtypeStruct((TILES, kinds * PAIRS, LANES), jnp.float32),
        ],
        in_specs=[smem, smem, hbm, hbm],
        out_specs=[vmem] * (FIELDS + 2),
        scratch_shapes=[
            pltpu.VMEM((z.block, CAP, LINES, LANES), jnp.bfloat16),
            pltpu.VMEM((QUAD + CAP, LINES, LANES), jnp.float32),
            pltpu.VMEM((FIELDS + 1, 2, SLOTS, PAIRS, LANES), jnp.float32),
            pltpu.VMEM(table.shape, jnp.float32),
            pltpu.SemaphoreType.DMA((z.block + 1,)),
        ],
        compiler_params=pltpu.CompilerParams(vmem_limit_bytes=MOST_VMEM),
        cost_estimate=pl.CostEstimate(flops=5_000_000, bytes_accessed=8_000_000, transcendentals=0),
        name="own_share",
    )(place, lists, tiles, table)


def strength_kernel(z, smoothing, _, strength):
    turned_strength = jnp.transpose(smoothing[...] - MID)
    for dest in range(z.regions):
        for g in range(z.span // 8):
            top = z.width * dest + 8 * g
            count, at = min(8, COLS - top), ROWS * (g % QUAD)
            strength[dest, g // QUAD, 0:count, at : at + ROWS] = turned_strength[top : top + count]


def strength_blocks(z, smoothing, before):
    return pl.pallas_call(
        functools.partial(strength_kernel, z),
        out_shape=jax.ShapeDtypeStruct((z.regions, z.quads, 8, LANES), jnp.float32),
        in_specs=[pl.BlockSpec(memory_space=pltpu.VMEM), pl.BlockSpec(memory_space=pl.ANY)],
        out_specs=pl.BlockSpec(memory_space=pltpu.VMEM),
        compiler_params=pltpu.CompilerParams(vmem_limit_bytes=VMEM),
        name="strength_blocks",
    )(smoothing, before)


def join_kernel(z, *refs):
    place, lists, refs = refs[0], refs[1 : 1 + z.makers], refs[1 + z.makers :]
    received, refs = refs[: z.makers - 1], refs[z.makers - 1 :]
    half, (total, weights, strength), outs = refs[:FIELDS], refs[FIELDS : FIELDS + 3], refs[FIELDS + 3 : -5]
    staged, sums, lines, turned, edges = refs[-5:]
    me = place[0]
    first = lax.rem(me, z.makers) * z.block
    row, column = (lax.broadcasted_iota(jnp.int32, (LANES, LANES), axis) for axis in (0, 1))
    identity = (row == column).astype(jnp.bfloat16)

    for quad in range(z.quads):

        def body(i, side, slots):
            j = quad * QUAD + i
            sources = [(maker, slot) for maker in range(1, z.makers) for slot in slots]

            def staged_of(maker, slot):
                return staged.at[staged_index(i, side, maker - 1, slot, z.makers - 1)]

            def weight_item(maker, slot):
                column, kind = (lists[maker][entry, slot, first + j] for entry in (1, 2))
                return functools.partial(weight_tile, weights, kind), column

            def field_item(field, maker, slot):
                weight, column = weight_item(maker, slot)
                return lambda t: staged_tile(staged_of(maker, slot), field, t) * weight(t), column

            for maker, slot in sources:
                stage(staged_of(maker, slot), received[maker - 1][j, slot])
            others = place_all(side, sums.at[FIELDS], [weight_item(*source) for source in sources])
            inverse = [[1.0 / (total[j, parity, t] + others[parity][t]) for t in range(TILES)] for parity in range(2)]
            for field in range(FIELDS):
                pieces = place_all(side, sums.at[field], [field_item(field, *source) for source in sources])
                for parity in range(2):
                    for t in range(TILES):
                        lines[field, t, pl.ds(ROWS * i + parity, PAIRS, stride=2), :] = (
                            half[field][j, parity, t] + pieces[parity][t]
                        ) * inverse[parity][t]

        each_region(z, lambda i: lists[0][0, 1, first + quad * QUAD + i] >= 0, body)
        for t in range(TILES):
            for field in range(FIELDS):
                here = slice(LANES * t, LANES * (t + 1))
                if field % 2:
                    turned[field, here, :] = jnp.transpose(lines[field, t])
                else:
                    turned[field, here, :] = lax.dot_general(
                        identity,
                        lines[field, t].astype(jnp.bfloat16),
                        (((1,), (1,)), ((), ())),
                        preferred_element_type=jnp.float32,
                    )
        for i, (out, offset) in enumerate(zip(outs, z.offsets)):
            dest = me ^ offset
            top = dest * z.width
            if z.width % 8 == 0:
                top = pl.multiple_of(top, 8)
            ends = (jnp.maximum(top - 1, 0), jnp.minimum(top + z.width, COLS - 1))
            for field in range(FIELDS):
                for side, end in enumerate(ends):
                    edges[i, 2 * field + side : 2 * field + side + 1, :] = turned[field, pl.ds(end, 1), :]
            for low in range(0, FIELDS, 2):
                block = [turned[field, pl.ds(top, z.span), :] for field in (low, low + 1)]
                out[quad, low * z.span : (low + 2) * z.span, :] = jnp.concatenate(block, 0).astype(jnp.bfloat16)
            tail = jnp.concatenate([edges[i], strength[dest, quad]], 0)
            out[quad, z.main : z.sent, :] = tail.astype(jnp.bfloat16)


def join(z, place, lists, received, shares):
    smem = pl.BlockSpec(memory_space=pltpu.SMEM)
    vmem = pl.BlockSpec(memory_space=pltpu.VMEM)
    shape = (z.quads, z.sent, LANES)
    return pl.pallas_call(
        functools.partial(join_kernel, z),
        out_shape=[jax.ShapeDtypeStruct(shape, jnp.bfloat16)] * z.regions,
        in_specs=[smem] * (1 + z.makers) + [vmem] * (z.makers - 1 + len(shares)),
        out_specs=[vmem] * z.regions,
        scratch_shapes=[
            pltpu.VMEM(((QUAD + CAP) * (z.makers - 1), LINES, LANES), jnp.float32),
            pltpu.VMEM((FIELDS + 1, 2, SLOTS, PAIRS, LANES), jnp.float32),
            pltpu.VMEM((FIELDS, TILES, LANES, LANES), jnp.float32),
            pltpu.VMEM((FIELDS, COLS + 8, LANES), jnp.float32),
            pltpu.VMEM((z.regions, 8, LANES), jnp.float32),
        ],
        compiler_params=pltpu.CompilerParams(vmem_limit_bytes=VMEM),
        cost_estimate=pl.CostEstimate(flops=5_000_000, bytes_accessed=8_000_000, transcendentals=0),
        name="join",
    )(place, *lists, *received, *shares)


SORT_STEPS = (
    ((0, 1), (2, 3), (4, 5), (6, 7)),
    ((0, 2), (1, 3), (4, 6), (5, 7)),
    ((1, 2), (5, 6)),
    ((0, 4), (1, 5), (2, 6), (3, 7)),
    ((2, 4), (3, 5)),
    ((1, 2), (3, 4), (5, 6)),
)
STEP_FIELDS = 2


def differences(field, low, count, tiles):
    lane = lax.broadcasted_iota(jnp.int32, (count, LANES), 1)
    pieces = [field[t, 8 + low : 8 + low + count, :] for t in range(tiles)]
    later = [pltpu.roll(piece, 1, 1) for piece in pieces]
    sooner = [pltpu.roll(piece, LANES - 1, 1) for piece in pieces]
    results = []
    for t, here in enumerate(pieces):
        above = jnp.where(lane == 0, later[t - 1] if t else here, later[t])
        below = jnp.where(lane == LANES - 1, sooner[t + 1] if t + 1 < tiles else here, sooner[t])
        sides = field[t, 7 + low : 7 + low + count, :] + field[t, 9 + low : 9 + low + count, :]
        results.append((here, above + below + sides - 4.0 * here))
    return results


def early_kernel(z, samples, place, *refs):
    offsets = [sample * z.makers + part for sample in samples for part in range(z.makers)]
    blocks = dict(zip(offsets, refs))
    results, edges, padded = refs[-3:]
    me = place[0]
    tiles = z.rows // LANES
    for offset in offsets:
        index = samples.index(offset // z.makers)
        for quad in range(z.quads):
            tile = lax.rem(me ^ offset, z.makers) * z.quads + quad
            values = blocks[offset][quad, 0 : z.main, :].astype(jnp.float32)
            tail = blocks[offset][quad, z.main : z.sent, :].astype(jnp.float32)
            for field in range(FIELDS):
                target = padded.at[index, field, tile]
                target[8 : 8 + z.span, :] = values[field * z.span : (field + 1) * z.span]
            edges[index, tile] = tail[0:8]

    def one_field(field, carry):
        for index in range(len(samples)):
            for t in range(tiles):
                padded[index, field, t, 7:8, :] = edges[index, t, pl.ds(2 * field, 1), :]
                padded[index, field, t, 8 + z.width : 9 + z.width, :] = edges[index, t, pl.ds(2 * field + 1, 1), :]
            for low in range(0, z.width, 8):
                count = min(8, z.width - low)
                found = differences(padded.at[index, field], low, count, tiles)
                for t, pair in enumerate(found):
                    for kind, rows in enumerate(pair):
                        results[kind, index, field, t, low : low + count, :] = rows
        return carry

    lax.fori_loop(0, FIELDS, one_field, 0)


def early_differences(z, samples, place, blocks, last=()):
    tiles = z.rows // LANES
    vmem, anywhere = pl.BlockSpec(memory_space=pltpu.VMEM), pl.BlockSpec(memory_space=pl.ANY)
    shape = (2, len(samples), FIELDS, tiles, z.span, LANES)
    return pl.pallas_call(
        functools.partial(early_kernel, z, samples),
        out_shape=[jax.ShapeDtypeStruct(item.shape, item.dtype) for item in last]
        + [jax.ShapeDtypeStruct(shape, jnp.float32)],
        in_specs=[pl.BlockSpec(memory_space=pltpu.SMEM)] + [vmem] * len(blocks) + [anywhere] * len(last),
        out_specs=[anywhere] * len(last) + [vmem],
        scratch_shapes=[
            pltpu.VMEM((len(samples), tiles, 8, LANES), jnp.float32),
            pltpu.VMEM((len(samples), FIELDS, tiles, z.span + 16, LANES), jnp.float32),
        ],
        input_output_aliases={1 + len(blocks) + i: i for i in range(len(last))},
        compiler_params=pltpu.CompilerParams(vmem_limit_bytes=VMEM),
        cost_estimate=pl.CostEstimate(flops=5_000_000, bytes_accessed=4_000_000, transcendentals=0),
        name="early_differences",
    )(place, *blocks, *last)


def score_kernel(z, place, *refs):
    blocks = dict(zip(z.offsets, refs))
    early, later, analysis, crps, spread, strength, edges, padded = refs[z.regions :]
    me = place[0]
    step = pl.program_id(0)
    rows = z.rows

    def tile_of(offset, quad):
        return lax.rem(me ^ offset, z.makers) * z.quads + quad

    @pl.when(step == 0)
    def _():
        slot = lax.broadcasted_iota(jnp.int32, (8, LANES), 1) // ROWS
        for low in range(0, z.regions, QUAD):
            offsets = range(low, low + QUAD)
            slots = [lax.rem(me ^ offset, QUAD) for offset in offsets]
            at = lax.div(me ^ low, QUAD)
            for quad in range(z.quads):
                tails = [blocks[offset][quad, z.main : z.sent, :].astype(jnp.float32) for offset in offsets]
                for offset, tail in zip(offsets, tails):
                    edges[offset // z.makers, tile_of(offset, quad)] = tail[0:8]
                for g in range(quad * QUAD, min((quad + 1) * QUAD, z.span // 8)):
                    joined = jnp.zeros((8, LANES), jnp.float32)
                    for i, tail in zip(slots, tails):
                        near = pltpu.roll(tail[8:16], lax.rem(i + QUAD - g % QUAD, QUAD) * ROWS, 1)
                        joined = jnp.where(slot == i, near, joined)
                    strength[at, 8 * g : 8 * (g + 1), :] = joined + MID

    top = pl.multiple_of(step * STEP_FIELDS * z.span, 16)
    for offset in range(z.regions):
        if offset // z.makers in z.early + z.later:
            continue
        for quad in range(z.quads):
            values = blocks[offset][quad, pl.ds(top, STEP_FIELDS * z.span), :].astype(jnp.float32)
            for f in range(STEP_FIELDS):
                padded[offset // z.makers, f, tile_of(offset, quad), 8 : 8 + z.span, :] = values[
                    f * z.span : (f + 1) * z.span
                ]
    tiles = rows // LANES
    for sample in range(SAMPLES):
        if sample in z.early + z.later:
            continue
        for f in range(STEP_FIELDS):
            low = 2 * (step * STEP_FIELDS + f)
            for t in range(tiles):
                padded[sample, f, t, 7:8, :] = edges[sample, t, pl.ds(low, 1), :]
                padded[sample, f, t, 8 + z.width : 9 + z.width, :] = edges[sample, t, pl.ds(low + 1, 1), :]
    for f, low in ((f, low) for f in range(STEP_FIELDS) for low in range(0, z.width, 16)):
        high = min(low + 16, z.width)
        smoothed = [[] for _ in range(tiles)]
        for sample in range(SAMPLES):
            if sample in z.early + z.later:
                samples, ready = (z.early, early) if sample in z.early else (z.later, later)
                own = (samples.index(sample), step * STEP_FIELDS + f)
                found = [[ready[kind, *own, t, low:high, :] for kind in range(2)] for t in range(tiles)]
            else:
                found = differences(padded.at[sample, f], low, high - low, tiles)
            for t, (here, difference) in enumerate(found):
                smooth = here + strength[t, low:high, :] * difference
                smoothed[t].append(smooth.astype(jnp.bfloat16))
        for t, members in enumerate(smoothed):
            lanes = slice(LANES * t, LANES * (t + 1))
            values = [member.astype(jnp.float32) for member in members]
            target = analysis[f, low:high, lanes].astype(jnp.float32)
            error = sum(jnp.abs(value - target) for value in values) * (1.0 / SAMPLES)
            average = sum(values) * (1.0 / SAMPLES)
            variance = sum((value - average) ** 2 for value in values) * (1.0 / (SAMPLES - 1.0))
            ranked = list(members)
            for pairs in SORT_STEPS:
                for a, b in pairs:
                    ranked[a], ranked[b] = jnp.minimum(ranked[a], ranked[b]), jnp.maximum(ranked[a], ranked[b])
            ranked = [member.astype(jnp.float32) for member in ranked]
            pairs = sum(
                (2 * k - SAMPLES + 1.0) * (ranked[k] - ranked[SAMPLES - 1 - k])
                for k in range(SAMPLES // 2, SAMPLES)
            )
            crps[f, low:high, lanes] = (error - pairs * (1.0 / (SAMPLES * SAMPLES))).astype(jnp.bfloat16)
            spread[0, f, low:high, lanes] = variance.astype(jnp.bfloat16)
            spread[1, f, low:high, lanes] = ((average - target) ** 2).astype(jnp.bfloat16)


def score(z, place, blocks, early, later, analysis):
    width, rows = z.width, z.rows
    return pl.pallas_call(
        functools.partial(score_kernel, z),
        out_shape=[
            jax.ShapeDtypeStruct((FIELDS, width, rows), jnp.bfloat16),
            jax.ShapeDtypeStruct((2, FIELDS, width, rows), jnp.bfloat16),
        ],
        grid=(FIELDS // STEP_FIELDS,),
        in_specs=[pl.BlockSpec(memory_space=pltpu.SMEM)]
        + [pl.BlockSpec(memory_space=pltpu.VMEM)] * (z.regions + 2)
        + [pl.BlockSpec((STEP_FIELDS, width, rows), lambda i: (i, 0, 0))],
        out_specs=[
            pl.BlockSpec((STEP_FIELDS, width, rows), lambda i: (i, 0, 0)),
            pl.BlockSpec((2, STEP_FIELDS, width, rows), lambda i: (0, i, 0, 0)),
        ],
        scratch_shapes=[
            pltpu.VMEM((rows // LANES, z.span, LANES), jnp.float32),
            pltpu.VMEM((SAMPLES, rows // LANES, 8, LANES), jnp.float32),
            pltpu.VMEM((SAMPLES, STEP_FIELDS, rows // LANES, z.span + 16, LANES), jnp.float32),
        ],
        compiler_params=pltpu.CompilerParams(vmem_limit_bytes=VMEM),
        name="score",
    )(place, *blocks, early, later, analysis)


def shards(patch_tiles, slot_lists, blend_table, smoothing, analysis):
    z = Sizes(lax.axis_size("region"))
    place = lax.axis_index("region").reshape(1)
    turns = [
        [(i, i - i % z.makers + (i + k) % z.makers) for i in range(z.regions)] for k in range(1, z.makers)
    ]
    tiles = patch_tiles.reshape(z.regions, CAP, FIELDS, PAIRS * TILES, LANES)
    tiles = jnp.swapaxes(tiles, 2, 3).reshape(z.regions, CAP, LINES, LANES)
    lists = jnp.transpose(slot_lists, (2, 1, 0))
    received = [lax.ppermute(item, "region", turn) for item, turn in zip(pack(z, place, tiles), turns)]
    lists = [lists] + [lax.ppermute(lists, "region", turn) for turn in turns]
    shares = own_share(z, place, lists[0], tiles, blend_table)
    shares = [*shares, strength_blocks(z, smoothing, shares[-1])]
    blocks = join(z, place, lists, received, shares)
    def swapped(block, offset):
        return lax.ppermute(block, "region", [(i, i ^ offset) for i in range(z.regions)])

    moved = [blocks[0]] + [swapped(block, offset) for block, offset in zip(blocks[1:-1], z.offsets[1:-1])]
    def blocks_of(samples):
        return [moved[z.offsets.index(sample * z.makers + part)] for sample in samples for part in range(z.makers)]

    last, early = early_differences(z, z.early, place, blocks_of(z.early), [blocks[-1]])
    (later,) = early_differences(z, z.later, place, blocks_of(z.later))
    moved.append(swapped(last, z.offsets[-1]))
    outs = score(z, place, moved, early, later, jnp.swapaxes(analysis, 1, 2))
    return tuple(jnp.swapaxes(item, -1, -2) for item in outs)


def solution(mesh):
    return jax.shard_map(
        shards,
        mesh=mesh,
        in_specs=(
            P(("groups", "region"), None, None, None),
            P(("groups", "region"), None, None),
            P(),
            P("region", None),
            P(None, "groups", "region"),
        ),
        out_specs=(P(None, "groups", "region"), P(None, None, "groups", "region")),
        check_vma=False,
    )
```
